32 devices in a mesh: dp: 4 (over z), ctx: 2 (over y), tp: 4 (over x, core).
Axes of the slice: x: 2, y: 2, z: 4, core: 2. Of those that a mesh axis runs over, the one named last changes fastest.
Arguments:
- tokens: bfloat16 [8192, 1152], P(('dp', 'ctx'), 'tp'), may hold values from -6 to 6
- out_grad: bfloat16 [8192, 1152], P(('dp', 'ctx'), 'tp'), may hold values from -6 to 6
- w_query: bfloat16 [1152, 1024], P(None, 'tp'), may hold values from -0.1875 to 0.1875
- w_key: bfloat16 [1152, 256], replicated, may hold values from -0.1875 to 0.1875
- w_value: bfloat16 [1152, 256], replicated, may hold values from -0.1875 to 0.1875
- w_out: bfloat16 [1024, 1152], P('tp'), may hold values from -0.1875 to 0.1875
- w_gate: bfloat16 [1152, 6912], P(None, 'tp'), may hold values from -0.1875 to 0.1875
- w_up: bfloat16 [1152, 6912], P(None, 'tp'), may hold values from -0.1875 to 0.1875
- w_down: bfloat16 [6912, 1152], P('tp'), may hold values from -0.078125 to 0.078125
- gain_in: bfloat16 [1152], replicated, may hold values from 0.25 to 1.75
- gain_post_attn: bfloat16 [1152], replicated, may hold values from 0.25 to 1.75
- gain_pre_ffn: bfloat16 [1152], replicated, may hold values from 0.25 to 1.75
- gain_post_ffn: bfloat16 [1152], replicated, may hold values from 0.25 to 1.75
- gain_query: bfloat16 [256], replicated, may hold values from 0.25 to 1.75
- gain_key: bfloat16 [256], replicated, may hold values from 0.25 to 1.75
- bucket_lengths: int32 [4, 2], P('dp'), may hold values from 1024 to 1024, as said below
- true_lengths: int32 [4, 2], P('dp'), may hold values from 768 to 1024, as said below
Outputs:
- out: bfloat16 [8192, 1152], P(('dp', 'ctx'), 'tp')
- x_grad: bfloat16 [8192, 1152], P(('dp', 'ctx'), 'tp')
- w_query_grad: float32 [1152, 1024], P(None, 'tp')
- w_key_grad: float32 [1152, 256], replicated
- w_value_grad: float32 [1152, 256], replicated
- w_out_grad: float32 [1024, 1152], P('tp')
- w_gate_grad: float32 [1152, 6912], P(None, 'tp')
- w_up_grad: float32 [1152, 6912], P(None, 'tp')
- w_down_grad: float32 [6912, 1152], P('tp')
- gain_in_grad: float32 [1152], replicated
- gain_post_attn_grad: float32 [1152], replicated
- gain_pre_ffn_grad: float32 [1152], replicated
- gain_post_ffn_grad: float32 [1152], replicated
- gain_query_grad: float32 [256], replicated
- gain_key_grad: float32 [256], replicated
The draws below stay inside these ranges and needn't reach their ends.
Inputs may be any that keep to these rules, and one draw needn't show every extreme that they name: `bucket_lengths`: in each group the 2 bucket lengths, in stream order, add up to 2048; each is a multiple of 512; the first or the last is 1024 or longer; some group has a bucket of length 1024 and one of length 1024. `true_lengths`: each is its bucket's length less 0 to 256 padding positions at the bucket's end; in each group the bucket of length 1024 or more that stands first or last has no padding, and each other bucket of length 1024 has 256.
All inputs are finite; a program needn't handle non-finite values.
Results may differ from the reference program's by a relative error of at most 0.03.
Values may be sent and summed in bfloat16 or wider, within the bound.
A program may use at most 320 MiB of HBM per device.

```python
from functools import partial
import jax
import jax.numpy as jnp
from jax import lax

D = 1152
HEADS = 4
HD = 256
FF = 6912
TOK_DEV = 1024
QBLK = 512
GROUPS = 4
GROUP_TOK = 2048
TOKENS = 8192
SLOTS = 2
MINSEQ = 1024
N_CTX = 2
N_TP = 4


def bucket_plan(key):
    half_group = GROUP_TOK // 2
    unit_rows = TOK_DEV // 2
    others = SLOTS - 1
    anchor_most = (GROUP_TOK - others * MINSEQ - half_group) // unit_rows
    anchor_units = jax.random.randint(jax.random.fold_in(key, 21), (GROUPS, 1), 0, anchor_most + 1)
    widest_group = jax.random.randint(jax.random.fold_in(key, 22), (), 0, GROUPS)
    group_ids = jnp.arange(GROUPS, dtype=jnp.int32)[:, None]
    anchor_units = jnp.where(group_ids == widest_group, anchor_most, anchor_units).astype(jnp.int32)
    anchor = (half_group + unit_rows * anchor_units).astype(jnp.int32)
    spare_units = ((GROUP_TOK - anchor - others * MINSEQ) // unit_rows).astype(jnp.int32)
    cut_points = jax.random.randint(jax.random.fold_in(key, 12), (GROUPS, others - 1), 0, spare_units + 1)
    cut_points = jnp.sort(cut_points, axis=1).astype(jnp.int32)
    cut_side = jax.random.randint(jax.random.fold_in(key, 13), (GROUPS, 1), 0, 2)
    column_ids = jnp.arange(others - 1, dtype=jnp.int32)[None, :]
    forced_low = (cut_side == 0) & (column_ids == 0)
    forced_high = (cut_side == 1) & (column_ids == others - 2)
    spare_wide = jnp.broadcast_to(spare_units, cut_points.shape)
    cut_points = jnp.where(forced_low, 0, jnp.where(forced_high, spare_wide, cut_points)).astype(jnp.int32)
    edge_points = jnp.concatenate([jnp.zeros((GROUPS, 1), jnp.int32), cut_points, spare_units], axis=1)
    pieces = MINSEQ + unit_rows * (edge_points[:, 1:] - edge_points[:, :-1])
    anchor_side = jax.random.randint(jax.random.fold_in(key, 11), (GROUPS, 1), 0, 2)
    leading = jnp.concatenate([anchor, pieces], axis=1)
    trailing = jnp.concatenate([pieces, anchor], axis=1)
    plan = jnp.where(anchor_side == 1, leading, trailing).astype(jnp.int32)
    slot_ids = jnp.arange(SLOTS, dtype=jnp.int32)[None, :]
    anchor_slot = jnp.where(anchor_side == 1, slot_ids == 0, slot_ids == SLOTS - 1)
    return (plan, anchor_slot)


def draw_bucket_lengths(key, part):
    plan, anchor_slot = bucket_plan(key)
    return plan


def draw_true_lengths(key, part):
    plan, anchor_slot = bucket_plan(key)
    key = jax.random.fold_in(key, 5)
    padding = jax.random.randint(key, (GROUPS, SLOTS), 0, TOK_DEV // 4 + 1)
    padding = jnp.where(plan == MINSEQ, TOK_DEV // 4, padding)
    padding = jnp.where(anchor_slot, 0, padding)
    return (plan - padding).astype(jnp.int32)


def level_of(stream_key, extent, shards, smallest, largest):
    def one(dim, blocks):
        steps = jax.random.uniform(jax.random.fold_in(jax.random.fold_in(stream_key, 6), dim), (blocks,), jnp.float32, smallest / len(shards), largest / len(shards))
        return jnp.repeat(jnp.exp(steps), extent[dim] // blocks).reshape((-1,) + (1,) * (len(extent) - dim - 1))

    factor_of = one(*shards[0])
    for cut in shards[1:]:
        factor_of = factor_of * one(*cut)
    return factor_of


def centred(own_key, dims, width, most, shards=(), kind=jnp.bfloat16):
    drawn = jax.random.normal(own_key, dims, jnp.float32) * width
    if len(shards) > 0:
        drawn = level_of(own_key, dims, shards, -0.22, 0.18) * drawn
    return jnp.clip(drawn, min=-most, max=most).astype(kind)


def setup_inputs(seed: int = 0) -> dict:
    keys = jax.random.split(jax.random.key(seed), 18)
    return {
        "tokens": centred(keys[0], (TOKENS, D), 1.0, 6.0, ((0, 8), (1, 4))),
        "out_grad": centred(keys[1], (TOKENS, D), 1.0, 6.0, ((0, 8), (1, 4))),
        "w_query": centred(keys[2], (D, HEADS * HD), D ** -0.5, 0.1875, ((1, 4),)),
        "w_key": centred(keys[3], (D, HD), D ** -0.5, 0.1875),
        "w_value": centred(keys[4], (D, HD), D ** -0.5, 0.1875),
        "w_out": centred(keys[5], (HEADS * HD, D), (HEADS * HD) ** -0.5, 0.1875, ((0, 4),)),
        "w_gate": centred(keys[6], (D, FF), D ** -0.5, 0.1875, ((1, 4),)),
        "w_up": centred(keys[7], (D, FF), D ** -0.5, 0.1875, ((1, 4),)),
        "w_down": centred(keys[8], (FF, D), FF ** -0.5, 0.078125, ((0, 4),)),
        "gain_in": jnp.clip(1.0 + 0.15 * jax.random.normal(keys[9], (D,), jnp.float32), 0.25, 1.75).astype(jnp.bfloat16),
        "gain_post_attn": jnp.clip(1.0 + 0.15 * jax.random.normal(keys[10], (D,), jnp.float32), 0.25, 1.75).astype(jnp.bfloat16),
        "gain_pre_ffn": jnp.clip(1.0 + 0.15 * jax.random.normal(keys[11], (D,), jnp.float32), 0.25, 1.75).astype(jnp.bfloat16),
        "gain_post_ffn": jnp.clip(1.0 + 0.15 * jax.random.normal(keys[12], (D,), jnp.float32), 0.25, 1.75).astype(jnp.bfloat16),
        "gain_query": jnp.clip(1.0 + 0.15 * jax.random.normal(keys[13], (HD,), jnp.float32), 0.25, 1.75).astype(jnp.bfloat16),
        "gain_key": jnp.clip(1.0 + 0.15 * jax.random.normal(keys[14], (HD,), jnp.float32), 0.25, 1.75).astype(jnp.bfloat16),
        "bucket_lengths": draw_bucket_lengths(jax.random.fold_in(keys[17], 71), 0),
        "true_lengths": draw_true_lengths(jax.random.fold_in(keys[17], 71), 0),
    }


@jax.custom_vjp
def low(v):
    return lax.optimization_barrier(v.astype(jnp.bfloat16)).astype(jnp.float32)

@jax.custom_vjp
def low_back(v):
    return v

def low_keep(v):
    return (low(v), None)

def low_pass(kept, grad):
    return (grad,)

def back_keep(v):
    return (v, None)

def back_low(kept, grad):
    return (low(grad),)
low.defvjp(low_keep, low_pass)
low_back.defvjp(back_keep, back_low)
HIGHEST = lax.Precision.HIGHEST
EPSILON = 1e-06
ROPE_BASE = 1000000.0
MASKED = -1e+30

def matmul(left, right):
    return jnp.dot(left, right, precision=HIGHEST, preferred_element_type=jnp.float32)

def rms_norm(values, gain):
    return values * lax.rsqrt(lax.optimization_barrier(jnp.mean(values * values, axis=-1, keepdims=True)) + EPSILON) * gain

def rotate(values, cosine_table, sine_table):
    half_dim = values.shape[-1] // 2
    turned = jnp.concatenate([-values[..., half_dim:], values[..., :half_dim]], axis=-1)
    return values * cosine_table + turned * sine_table

def rope_tables(seq_pos, head_dim):
    freq_index = jnp.arange(head_dim // 2, dtype=jnp.float32)
    inverse = ROPE_BASE ** (-2.0 * freq_index / head_dim)
    angles = seq_pos.astype(jnp.float32)[:, None] * inverse[None, :]
    angles = jnp.concatenate([angles, angles], axis=-1)
    return (jnp.cos(angles), jnp.sin(angles))

def stream_layout(bucket_row, true_row, tok_dev, n_ctx):
    group_rows = tok_dev * n_ctx
    half_shard = tok_dev // 2
    row_ids = jnp.arange(group_rows, dtype=jnp.int32)
    device = row_ids // tok_dev
    half_index = row_ids % tok_dev // half_shard
    block_ids = jnp.where(half_index == 0, device, 2 * n_ctx - 1 - device)
    stream_pos = (block_ids * half_shard + row_ids % half_shard).astype(jnp.int32)
    starts = (jnp.cumsum(bucket_row) - bucket_row).astype(jnp.int32)
    ends = (starts + bucket_row).astype(jnp.int32)
    inside = ((stream_pos[:, None] >= starts[None, :]) & (stream_pos[:, None] < ends[None, :])).astype(jnp.int32)
    slot_ids = jnp.arange(bucket_row.shape[0], dtype=jnp.int32)
    seq_ids = lax.optimization_barrier(jnp.sum(inside * slot_ids[None, :], axis=1)).astype(jnp.int32)
    seq_pos = (stream_pos - lax.optimization_barrier(jnp.sum(inside * starts[None, :], axis=1))).astype(jnp.int32)
    is_valid = (seq_pos < lax.optimization_barrier(jnp.sum(inside * true_row[None, :], axis=1))).astype(jnp.int32)
    return (seq_ids, stream_pos, seq_pos, is_valid)

def attend_block(block_item, key_rows, value_rows, key_seq, key_pos, key_valid):
    query_block, query_seq, query_pos = block_item
    score_scale = HD ** (-0.5)
    scores = low_back(jnp.einsum('qhd,kd->hqk', query_block, key_rows, precision=HIGHEST) * score_scale)
    allowed = (key_valid[None, :] == 1) & (key_seq[None, :] == query_seq[:, None]) & (key_pos[None, :] <= query_pos[:, None])
    scores = jnp.where(allowed[None], scores, MASKED)
    row_max = lax.optimization_barrier(jnp.max(scores, axis=-1, keepdims=True))
    exp_scores = jnp.exp(scores - row_max)
    prob_rows = low(exp_scores / lax.optimization_barrier(jnp.sum(exp_scores, axis=-1, keepdims=True)))
    return jnp.einsum('hqk,kd->qhd', prob_rows, value_rows, precision=HIGHEST)

def group_layer(inputs, weights, layout):
    w_query, w_key, w_value, w_out, w_gate, w_up, w_down, gain_in, gain_post_attn, gain_pre_ffn, gain_post_ffn, gain_query, gain_key = weights
    seq_ids, stream_pos, seq_pos, is_valid = layout
    cosine_table, sine_table = rope_tables(seq_pos, HD)
    normed_in = low(rms_norm(inputs, gain_in))
    query_all = low_back(matmul(normed_in, w_query))
    key_raw = matmul(normed_in, w_key)
    value_raw = matmul(normed_in, w_value)
    group_heads = HEADS // N_TP
    blocks = GROUP_TOK // QBLK
    attention = jnp.zeros((GROUP_TOK, D), jnp.float32)
    for tp_part in range(N_TP):
        key_copy = low_back(key_raw)
        value_copy = low_back(value_raw)
        key_rows = low(rotate(rms_norm(key_copy, gain_key), cosine_table, sine_table))
        value_rows = low(value_copy)
        columns = group_heads * HD
        query_group = query_all[:, tp_part * columns:(tp_part + 1) * columns].reshape(GROUP_TOK, group_heads, HD)
        query_group = low(rotate(rms_norm(query_group, gain_query), cosine_table[:, None, :], sine_table[:, None, :]))
        block_fn = jax.checkpoint(partial(attend_block, key_rows=key_rows, value_rows=value_rows, key_seq=seq_ids, key_pos=stream_pos, key_valid=is_valid))
        attended = lax.map(block_fn, (query_group.reshape(blocks, QBLK, group_heads, HD), seq_ids.reshape(blocks, QBLK), stream_pos.reshape(blocks, QBLK)))
        attended = low(low_back(attended.reshape(GROUP_TOK, columns)))
        attention = attention + low(matmul(attended, w_out[tp_part * columns:(tp_part + 1) * columns]))
    attention = low_back(attention)
    residual = inputs + rms_norm(attention, gain_post_attn)
    normed_mid = low(rms_norm(residual, gain_pre_ffn))
    gate_out = low_back(matmul(normed_mid, w_gate))
    up_out = low_back(matmul(normed_mid, w_up))
    hidden = low(jax.nn.gelu(gate_out, approximate=True) * up_out)
    ffn_cols = FF // N_TP
    ffn_branch = jnp.zeros((GROUP_TOK, D), jnp.float32)
    for tp_part in range(N_TP):
        ffn_branch = ffn_branch + low(matmul(hidden[:, tp_part * ffn_cols:(tp_part + 1) * ffn_cols], w_down[tp_part * ffn_cols:(tp_part + 1) * ffn_cols]))
    ffn_branch = low_back(ffn_branch)
    return residual + rms_norm(ffn_branch, gain_post_ffn)

def add_up(first, second):
    return first + second

def reference(tokens, out_grad, w_query, w_key, w_value, w_out, w_gate, w_up, w_down, gain_in, gain_post_attn, gain_pre_ffn, gain_post_ffn, gain_query, gain_key, bucket_lengths, true_lengths):
    weights = tuple((tensor.astype(jnp.float32) for tensor in (w_query, w_key, w_value, w_out, w_gate, w_up, w_down, gain_in, gain_post_attn, gain_pre_ffn, gain_post_ffn, gain_query, gain_key)))
    group_inputs = tokens.astype(jnp.float32).reshape(GROUPS, GROUP_TOK, D)
    group_cots = out_grad.astype(jnp.float32).reshape(GROUPS, GROUP_TOK, D)

    def one_group(running, group_item):
        inputs, cotangent, bucket_row, true_row = group_item
        layout = stream_layout(bucket_row, true_row, TOK_DEV, N_CTX)
        outputs, pullback = jax.vjp(partial(group_layer, layout=layout), inputs, weights)
        input_cot, weight_cot = pullback(cotangent)
        running = jax.tree.map(add_up, running, weight_cot)
        return (running, (outputs.astype(jnp.bfloat16), input_cot.astype(jnp.bfloat16)))
    start_grads = jax.tree.map(jnp.zeros_like, weights)
    grads, (outputs, input_cots) = lax.scan(one_group, start_grads, (group_inputs, group_cots, bucket_lengths, true_lengths))
    return (outputs.reshape(TOKENS, D), input_cots.reshape(TOKENS, D), grads[0], grads[1], grads[2], grads[3], grads[4], grads[5], grads[6], grads[7], grads[8], grads[9], grads[10], grads[11], grads[12])
```

```python
from functools import partial

import jax
import jax.numpy as jnp
from jax import lax
from jax.sharding import PartitionSpec as P

QBLK = 512


EPSILON = 1e-06
ROPE_BASE = 1000000.0
MASKED = -1e30


def contract(left, right, left_dim, right_dim):
    return lax.dot_general(
        left, right, (((left_dim,), (right_dim,)), ((), ())), preferred_element_type=jnp.float32
    )


def rms_norm(values, gain):
    return values * lax.rsqrt(jnp.mean(values * values, axis=-1, keepdims=True) + EPSILON) * gain


def rotate(values, cosine_table, sine_table):
    half_dim = values.shape[-1] // 2
    turned = jnp.concatenate([-values[..., half_dim:], values[..., :half_dim]], axis=-1)
    return values * cosine_table + turned * sine_table


def rope_tables(seq_pos, head_dim):
    freq_index = jnp.arange(head_dim // 2, dtype=jnp.float32)
    inverse = ROPE_BASE ** (-2.0 * freq_index / head_dim)
    angles = seq_pos.astype(jnp.float32)[:, None] * inverse[None, :]
    angles = jnp.concatenate([angles, angles], axis=-1)
    return (jnp.cos(angles), jnp.sin(angles))


def stream_layout(bucket_row, true_row, tok_dev, n_ctx):
    group_rows = tok_dev * n_ctx
    half_shard = tok_dev // 2
    row_ids = jnp.arange(group_rows, dtype=jnp.int32)
    device = row_ids // tok_dev
    half_index = row_ids % tok_dev // half_shard
    block_ids = jnp.where(half_index == 0, device, 2 * n_ctx - 1 - device)
    stream_pos = block_ids * half_shard + row_ids % half_shard
    starts = jnp.cumsum(bucket_row) - bucket_row
    ends = starts + bucket_row
    inside = (
        (stream_pos[:, None] >= starts[None, :]) & (stream_pos[:, None] < ends[None, :])
    ).astype(jnp.int32)
    slot_ids = jnp.arange(bucket_row.shape[0], dtype=jnp.int32)
    seq_ids = jnp.sum(inside * slot_ids[None, :], axis=1)
    seq_pos = stream_pos - jnp.sum(inside * starts[None, :], axis=1)
    is_valid = (seq_pos < jnp.sum(inside * true_row[None, :], axis=1)).astype(jnp.int32)
    return (seq_ids, stream_pos, seq_pos, is_valid)


def shape_heads(query_raw, key_raw, gain_q, gain_k, cosine_table, sine_table):
    query_heads = query_raw.reshape(query_raw.shape[0], -1, key_raw.shape[1])
    query_rot = rotate(
        rms_norm(query_heads, gain_q), cosine_table[:, None, :], sine_table[:, None, :]
    )
    key_rot = rotate(rms_norm(key_raw, gain_k), cosine_table, sine_table)
    return (query_rot, key_rot)


def geglu(gate_in, up_in):
    return jax.nn.gelu(gate_in, approximate=True) * up_in


def shards(
    tokens,
    out_grad,
    w_query,
    w_key,
    w_value,
    w_out,
    w_gate,
    w_up,
    w_down,
    gain_in,
    gain_post_attn,
    gain_pre_ffn,
    gain_post_ffn,
    gain_query,
    gain_key,
    bucket_lengths,
    true_lengths,
):
    n_ctx = lax.axis_size("ctx")
    ctx_index = lax.axis_index("ctx")
    tp_index = lax.axis_index("tp")
    rows_dev = tokens.shape[0]
    feature_cols = tokens.shape[1]
    head_dim = w_key.shape[1]
    head_count = w_query.shape[1] // head_dim
    group_rows = rows_dev * n_ctx
    blocks = rows_dev // QBLK
    score_scale = head_dim ** (-0.5)
    gain_in32, gain_pa32, gain_pf32, gain_pff32, gain_q32, gain_k32 = [
        tensor.astype(jnp.float32)
        for tensor in (gain_in, gain_post_attn, gain_pre_ffn, gain_post_ffn, gain_query, gain_key)
    ]
    input_full, cot_full = (
        lax.all_gather(tokens, "tp", axis=1, tiled=True),
        lax.all_gather(out_grad, "tp", axis=1, tiled=True),
    )
    inputs = input_full.astype(jnp.float32)
    seq_all, spos_all, rpos_all, valid_all = stream_layout(
        bucket_lengths[0], true_lengths[0], rows_dev, n_ctx
    )
    first_row = ctx_index * rows_dev
    seq_local = lax.dynamic_slice_in_dim(seq_all, first_row, rows_dev)
    spos_local = lax.dynamic_slice_in_dim(spos_all, first_row, rows_dev)
    rpos_local = lax.dynamic_slice_in_dim(rpos_all, first_row, rows_dev)
    cosine_table, sine_table = rope_tables(rpos_local, head_dim)
    normed_in, pull_in = jax.vjp(rms_norm, inputs, gain_in32)
    normed_in16 = normed_in.astype(jnp.bfloat16)
    query_raw = jnp.dot(normed_in16, w_query, preferred_element_type=jnp.float32)
    key_raw = jnp.dot(normed_in16, w_key, preferred_element_type=jnp.float32)
    value_raw = jnp.dot(normed_in16, w_value, preferred_element_type=jnp.float32)
    (query_rot, key_rot), rope_pull = jax.vjp(
        partial(shape_heads, cosine_table=cosine_table, sine_table=sine_table),
        query_raw,
        key_raw,
        gain_q32,
        gain_k32,
    )
    query16 = query_rot.astype(jnp.bfloat16)
    key16 = key_rot.astype(jnp.bfloat16)
    value16 = value_raw.astype(jnp.bfloat16)
    key_group, value_group = (
        lax.all_gather(key16, "ctx", axis=0, tiled=True),
        lax.all_gather(value16, "ctx", axis=0, tiled=True),
    )

    def allowed_mask(seq_rows, spos_rows):
        return (
            (valid_all[None, :] == 1)
            & (seq_all[None, :] == seq_rows[:, None])
            & (spos_all[None, :] <= spos_rows[:, None])
        )

    query_blocks = query16.reshape(blocks, QBLK, head_count, head_dim)
    seq_blocks = seq_local.reshape(blocks, QBLK)
    spos_blocks = spos_local.reshape(blocks, QBLK)

    def forward_block(block_item):
        query_block, seq_rows, spos_rows = block_item
        scores = (
            jnp.einsum("qhd,kd->hqk", query_block, key_group, preferred_element_type=jnp.float32)
            * score_scale
        )
        scores = jnp.where(allowed_mask(seq_rows, spos_rows)[None], scores, MASKED)
        row_max = jnp.max(scores, axis=-1, keepdims=True)
        exp_scores = jnp.exp(scores - row_max)
        row_total = jnp.sum(exp_scores, axis=-1, keepdims=True)
        prob_rows = (exp_scores / row_total).astype(jnp.bfloat16)
        output = jnp.einsum(
            "hqk,kd->qhd", prob_rows, value_group, preferred_element_type=jnp.float32
        )
        return (output, (row_max + jnp.log(row_total))[..., 0])

    attended, log_norm = lax.map(forward_block, (query_blocks, seq_blocks, spos_blocks))
    attended16 = attended.reshape(rows_dev, head_count * head_dim).astype(jnp.bfloat16)
    attention = lax.psum(
        jnp.dot(attended16, w_out, preferred_element_type=jnp.float32).astype(jnp.bfloat16), "tp"
    ).astype(jnp.float32)
    post_attn, pull_post_attn = jax.vjp(rms_norm, attention, gain_pa32)
    residual = inputs + post_attn
    normed_mid, pull_pre_ffn = jax.vjp(rms_norm, residual, gain_pf32)
    mid16 = normed_mid.astype(jnp.bfloat16)
    gate_out = jnp.dot(mid16, w_gate, preferred_element_type=jnp.float32)
    up_out = jnp.dot(mid16, w_up, preferred_element_type=jnp.float32)
    hidden, pull_geglu = jax.vjp(geglu, gate_out, up_out)
    hidden16 = hidden.astype(jnp.bfloat16)
    ffn_branch = lax.psum(
        jnp.dot(hidden16, w_down, preferred_element_type=jnp.float32).astype(jnp.bfloat16), "tp"
    ).astype(jnp.float32)
    post_ffn, pull_post_ffn = jax.vjp(rms_norm, ffn_branch, gain_pff32)
    outputs = residual + post_ffn
    out_rows = lax.dynamic_slice_in_dim(outputs, tp_index * feature_cols, feature_cols, 1).astype(
        jnp.bfloat16
    )
    cotangent = cot_full.astype(jnp.float32)
    d_ffn, d_gain_post_ffn = pull_post_ffn(cotangent)
    d_ffn16 = d_ffn.astype(jnp.bfloat16)
    d_hidden = contract(d_ffn16, w_down, 1, 1)
    grad_down = contract(hidden16, d_ffn16, 0, 0)
    d_gate, d_up = pull_geglu(d_hidden)
    d_gate16 = d_gate.astype(jnp.bfloat16)
    d_up16 = d_up.astype(jnp.bfloat16)
    grad_gate = contract(mid16, d_gate16, 0, 0)
    grad_up = contract(mid16, d_up16, 0, 0)
    d_mid = lax.psum(
        (contract(d_gate16, w_gate, 1, 1) + contract(d_up16, w_up, 1, 1)).astype(jnp.bfloat16), "tp"
    ).astype(jnp.float32)
    d_res_norm, d_gain_pre_ffn = pull_pre_ffn(d_mid)
    d_resid = cotangent + d_res_norm
    d_attn, d_gain_post_attn = pull_post_attn(d_resid)
    d_attn16 = d_attn.astype(jnp.bfloat16)
    d_attended16 = contract(d_attn16, w_out, 1, 1).astype(jnp.bfloat16)
    grad_out = contract(attended16, d_attn16, 0, 0)
    key_back, value_back = (key_group, value_group)

    def backward_block(running, block_item):
        key_sum, value_sum = running
        query_block, dout_block, lse_block, seq_rows, spos_rows = block_item
        scores = (
            jnp.einsum("qhd,kd->hqk", query_block, key_back, preferred_element_type=jnp.float32)
            * score_scale
        )
        scores = jnp.where(allowed_mask(seq_rows, spos_rows)[None], scores, MASKED)
        prob_rows = jnp.exp(scores - lse_block[..., None])
        prob16 = prob_rows.astype(jnp.bfloat16)
        d_probs = jnp.einsum(
            "qhd,kd->hqk", dout_block, value_back, preferred_element_type=jnp.float32
        )
        row_inner = jnp.sum(prob_rows * d_probs, axis=-1, keepdims=True)
        d_scores16 = (prob_rows * (d_probs - row_inner)).astype(jnp.bfloat16)
        d_query = (
            jnp.einsum("hqk,kd->qhd", d_scores16, key_back, preferred_element_type=jnp.float32)
            * score_scale
        )
        key_sum = (
            key_sum
            + jnp.einsum("hqk,qhd->kd", d_scores16, query_block, preferred_element_type=jnp.float32)
            * score_scale
        )
        value_sum = value_sum + jnp.einsum(
            "hqk,qhd->kd", prob16, dout_block, preferred_element_type=jnp.float32
        )
        return ((key_sum, value_sum), d_query)

    zero_rows = jnp.zeros((group_rows, head_dim), jnp.float32)
    (key_sum, value_sum), d_query_blocks = lax.scan(
        backward_block,
        (zero_rows, zero_rows),
        (
            query_blocks,
            d_attended16.reshape(blocks, QBLK, head_count, head_dim),
            log_norm,
            seq_blocks,
            spos_blocks,
        ),
    )
    d_key_rot, d_value = (
        lax.psum_scatter(
            key_sum.astype(jnp.bfloat16), "ctx", scatter_dimension=0, tiled=True
        ).astype(jnp.float32),
        lax.psum_scatter(
            value_sum.astype(jnp.bfloat16), "ctx", scatter_dimension=0, tiled=True
        ).astype(jnp.float32),
    )
    d_query_raw, d_key_raw, d_gain_query, d_gain_key = rope_pull(
        (d_query_blocks.reshape(rows_dev, head_count, head_dim), d_key_rot)
    )
    d_query16 = d_query_raw.astype(jnp.bfloat16)
    d_key16 = d_key_raw.astype(jnp.bfloat16)
    d_value16 = d_value.astype(jnp.bfloat16)
    grad_query = contract(normed_in16, d_query16, 0, 0)
    grad_key = contract(normed_in16, d_key16, 0, 0)
    grad_value = contract(normed_in16, d_value16, 0, 0)
    d_normed_part = (
        contract(d_query16, w_query, 1, 1)
        + contract(d_key16, w_key, 1, 1)
        + contract(d_value16, w_value, 1, 1)
    )
    d_normed_in = lax.psum(d_normed_part.astype(jnp.bfloat16), "tp").astype(jnp.float32)
    d_in_norm, d_gain_in = pull_in(d_normed_in)
    d_inputs = d_resid + d_in_norm
    grad_rows = lax.dynamic_slice_in_dim(d_inputs, tp_index * feature_cols, feature_cols, 1).astype(
        jnp.bfloat16
    )
    sharded = (
        grad_query,
        grad_out,
        grad_gate,
        grad_up,
        grad_down,
        d_gain_in,
        d_gain_post_attn,
        d_gain_pre_ffn,
        d_gain_post_ffn,
    )
    reduced = (
        lax.psum_scatter(
            sharded[0].astype(jnp.bfloat16), ("dp", "ctx"), scatter_dimension=0, tiled=True
        ).astype(jnp.float32),
        lax.psum_scatter(
            sharded[1].astype(jnp.bfloat16), ("dp", "ctx"), scatter_dimension=1, tiled=True
        ).astype(jnp.float32),
        lax.psum_scatter(
            sharded[2].astype(jnp.bfloat16), ("dp", "ctx"), scatter_dimension=0, tiled=True
        ).astype(jnp.float32),
        lax.psum_scatter(
            sharded[3].astype(jnp.bfloat16), ("dp", "ctx"), scatter_dimension=0, tiled=True
        ).astype(jnp.float32),
        lax.psum_scatter(
            sharded[4].astype(jnp.bfloat16), ("dp", "ctx"), scatter_dimension=1, tiled=True
        ).astype(jnp.float32),
        lax.psum_scatter(
            sharded[5].astype(jnp.bfloat16), ("dp", "ctx"), scatter_dimension=0, tiled=True
        ).astype(jnp.float32),
        lax.psum_scatter(
            sharded[6].astype(jnp.bfloat16), ("dp", "ctx"), scatter_dimension=0, tiled=True
        ).astype(jnp.float32),
        lax.psum_scatter(
            sharded[7].astype(jnp.bfloat16), ("dp", "ctx"), scatter_dimension=0, tiled=True
        ).astype(jnp.float32),
        lax.psum_scatter(
            sharded[8].astype(jnp.bfloat16), ("dp", "ctx"), scatter_dimension=0, tiled=True
        ).astype(jnp.float32),
    )
    summed = (
        lax.all_gather(reduced[0].astype(jnp.bfloat16), ("dp", "ctx"), axis=0, tiled=True).astype(
            jnp.float32
        ),
        lax.all_gather(reduced[1].astype(jnp.bfloat16), ("dp", "ctx"), axis=1, tiled=True).astype(
            jnp.float32
        ),
        lax.all_gather(reduced[2].astype(jnp.bfloat16), ("dp", "ctx"), axis=0, tiled=True).astype(
            jnp.float32
        ),
        lax.all_gather(reduced[3].astype(jnp.bfloat16), ("dp", "ctx"), axis=0, tiled=True).astype(
            jnp.float32
        ),
        lax.all_gather(reduced[4].astype(jnp.bfloat16), ("dp", "ctx"), axis=1, tiled=True).astype(
            jnp.float32
        ),
        lax.all_gather(reduced[5].astype(jnp.bfloat16), ("dp", "ctx"), axis=0, tiled=True).astype(
            jnp.float32
        ),
        lax.all_gather(reduced[6].astype(jnp.bfloat16), ("dp", "ctx"), axis=0, tiled=True).astype(
            jnp.float32
        ),
        lax.all_gather(reduced[7].astype(jnp.bfloat16), ("dp", "ctx"), axis=0, tiled=True).astype(
            jnp.float32
        ),
        lax.all_gather(reduced[8].astype(jnp.bfloat16), ("dp", "ctx"), axis=0, tiled=True).astype(
            jnp.float32
        ),
    )
    shared = lax.psum((grad_key, grad_value, d_gain_query, d_gain_key), ("dp", "ctx", "tp"))
    return (
        out_rows,
        grad_rows,
        summed[0],
        shared[0],
        shared[1],
        summed[1],
        summed[2],
        summed[3],
        summed[4],
        summed[5],
        summed[6],
        summed[7],
        summed[8],
        shared[2],
        shared[3],
    )


MESH_PAIR = ((0, 1), (1, 0))
XOR1 = ((0, 1), (1, 0), (2, 3), (3, 2))
XOR2 = ((0, 2), (2, 0), (1, 3), (3, 1))
OUTER_IN = ((0, 1), (3, 2))
INNER = ((1, 2), (2, 1))
INNER_OUT = ((1, 0), (2, 3))
INNER_Y = ((2, 3), (3, 2), (4, 5), (5, 4))
F32 = jnp.float32
BF16 = jnp.bfloat16


def add16(left, right):
    return (left.astype(F32) + right.astype(F32)).astype(BF16)


def halves(values, index):
    size = values.shape[0] // 2
    own = lax.dynamic_slice_in_dim(values, index * size, size)
    other = lax.dynamic_slice_in_dim(values, (1 - index) * size, size)
    return own, other


def join(own, other, index):
    first = jnp.where(index == 0, own, other)
    second = jnp.where(index == 0, other, own)
    return jnp.concatenate([first, second], axis=0)


def tp_sum(values):
    odd = lax.axis_index("tp") % 2
    own, other = halves(values, odd)
    own = add16(own, lax.ppermute(other, "tp", XOR1))
    own = add16(own, lax.ppermute(own, "tp", XOR2))
    return join(own, lax.ppermute(own, "tp", XOR1), odd)


def tp_gather(part):
    tp_index = lax.axis_index("tp")
    near = lax.ppermute(part, "tp", XOR1)
    far = lax.ppermute(part, "tp", XOR2)
    both = lax.ppermute(far, "tp", XOR1)
    blocks = (part, near, far, both)
    return jnp.concatenate(
        [lax.select_n(tp_index ^ j, *blocks) for j in range(4)], axis=1
    )


def sum_y_first(grad):
    ctx_index, dp_index = lax.axis_index("ctx"), lax.axis_index("dp")
    own, other = halves(grad, ctx_index)
    own = add16(own, lax.ppermute(other, "ctx", MESH_PAIR))
    own = add16(own, lax.ppermute(own, "dp", OUTER_IN))
    own = add16(own, lax.ppermute(own, "dp", INNER))
    inner = (dp_index == 1) | (dp_index == 2)
    own = jnp.where(inner, own, lax.ppermute(own, "dp", INNER_OUT))
    return join(own, lax.ppermute(own, "ctx", MESH_PAIR), ctx_index)


def sum_z_first(grad):
    dp_index = lax.axis_index("dp")
    upper = dp_index // 2
    grad = add16(grad, lax.ppermute(grad, "dp", OUTER_IN))
    own, other = halves(grad, upper)
    own = add16(own, lax.ppermute(other, "dp", INNER))
    own = add16(own, lax.ppermute(own, ("dp", "ctx"), INNER_Y))
    whole = join(own, lax.ppermute(own, "dp", INNER), upper)
    inner = (dp_index == 1) | (dp_index == 2)
    return jnp.where(inner, whole, lax.ppermute(whole, "dp", INNER_OUT))


def sum_all(values):
    for axis, pairs in (
        ("tp", XOR1), ("tp", XOR2), ("ctx", MESH_PAIR), ("dp", XOR1), ("dp", XOR2)
    ):
        values = values + lax.ppermute(values, axis, pairs)
    return values


def scale_of(values):
    return lax.rsqrt(jnp.mean(values * values, axis=-1, keepdims=True) + EPSILON)


def rms_back(values, gain, cotangent):
    scale = scale_of(values)
    weighted = gain * cotangent
    inner = jnp.mean(values * weighted, axis=-1, keepdims=True)
    back = scale * weighted - values * (scale * scale * scale * inner)
    return back, jnp.sum(cotangent * values * scale, axis=0)


def rotate_back(values, cosine_table, sine_table):
    half_dim = values.shape[-1] // 2
    turned = values * sine_table
    turned = jnp.concatenate([turned[..., half_dim:], -turned[..., :half_dim]], axis=-1)
    return values * cosine_table + turned


def positions(block, rows, bucket_row, true_row):
    stream_pos = block * rows + jnp.arange(rows, dtype=jnp.int32)
    starts = jnp.cumsum(bucket_row) - bucket_row
    ends = starts + bucket_row
    inside = (
        (stream_pos[:, None] >= starts[None, :]) & (stream_pos[:, None] < ends[None, :])
    ).astype(jnp.int32)
    slot_ids = jnp.arange(bucket_row.shape[0], dtype=jnp.int32)
    seq_id = jnp.sum(inside * slot_ids[None, :], axis=1)
    seq_pos = stream_pos - jnp.sum(inside * starts[None, :], axis=1)
    is_valid = (seq_pos < jnp.sum(inside * true_row[None, :], axis=1)).astype(jnp.int32)
    return seq_id, stream_pos, seq_pos, is_valid


def allowed_pairs(query_layout, key_layout):
    return (
        (key_layout[3][None, :] == 1)
        & (key_layout[0][None, :] == query_layout[0][:, None])
        & (key_layout[1][None, :] <= query_layout[1][:, None])
    )


def attend(query16, key16, value16, allowed, score_scale):
    scores = contract(query16, key16, 1, 1) * score_scale
    scores = jnp.where(allowed, scores, MASKED)
    exp_scores = jnp.exp(scores - jnp.max(scores, axis=-1, keepdims=True))
    probs = exp_scores / jnp.sum(exp_scores, axis=-1, keepdims=True)
    attended = jnp.dot(probs.astype(BF16), value16, preferred_element_type=F32)
    return probs, attended.astype(BF16)


def attend_back(query16, key16, value16, probs, d_attended16, score_scale):
    d_probs = contract(d_attended16, value16, 1, 1)
    inner = jnp.sum(probs * d_probs, axis=-1, keepdims=True)
    d_scores16 = (probs * (d_probs - inner)).astype(BF16)
    d_query = jnp.dot(d_scores16, key16, preferred_element_type=F32) * score_scale
    d_key = contract(d_scores16, query16, 0, 0) * score_scale
    d_value = contract(probs.astype(BF16), d_attended16, 0, 0)
    return d_query, d_key, d_value


def paired_shards(
    tokens,
    out_grad,
    w_query,
    w_key,
    w_value,
    w_out,
    w_gate,
    w_up,
    w_down,
    gain_in,
    gain_post_attn,
    gain_pre_ffn,
    gain_post_ffn,
    gain_query,
    gain_key,
    bucket_lengths,
    true_lengths,
):
    ctx_index, tp_index = lax.axis_index("ctx"), lax.axis_index("tp")
    rows = tokens.shape[0] // 2
    feature_cols = tokens.shape[1]
    head_dim = w_key.shape[1]
    score_scale = head_dim ** (-0.5)
    g_in, g_pa, g_pf, g_pff, g_q, g_k = [
        gain.astype(F32)
        for gain in (gain_in, gain_post_attn, gain_pre_ffn, gain_post_ffn, gain_query, gain_key)
    ]
    both = range(2)
    token_parts = halves(tokens, ctx_index)
    cot_parts = halves(out_grad, ctx_index)
    w_qkv = jnp.concatenate([w_query, w_key, w_value], axis=1)

    blocks = (2 * ctx_index, 3 - 2 * ctx_index, 2 - 2 * ctx_index)
    layouts = [positions(b, rows, bucket_lengths[0], true_lengths[0]) for b in blocks]
    tables = [rope_tables(layouts[i][2], head_dim) for i in both]
    key_layout = [jnp.concatenate([a, b]) for a, b in zip(layouts[2], layouts[1])]
    allowed = [allowed_pairs(layouts[0], layouts[0]), allowed_pairs(layouts[1], key_layout)]

    inputs16 = [tp_gather(part) for part in token_parts]
    cots16 = [tp_gather(part) for part in cot_parts]
    inputs = [values.astype(F32) for values in inputs16]
    normed16 = [rms_norm(values, g_in).astype(BF16) for values in inputs]
    raw = [jnp.dot(values, w_qkv, preferred_element_type=F32) for values in normed16]
    query_raw = [values[:, :head_dim] for values in raw]
    key_raw = [values[:, head_dim : 2 * head_dim] for values in raw]
    value16 = [values[:, 2 * head_dim :].astype(BF16) for values in raw]
    query16 = [rotate(rms_norm(query_raw[i], g_q), *tables[i]).astype(BF16) for i in both]
    key16 = [rotate(rms_norm(key_raw[i], g_k), *tables[i]).astype(BF16) for i in both]
    far_key, far_value = [
        lax.ppermute(values, "ctx", MESH_PAIR) for values in (key16[0], value16[0])
    ]
    keys = [key16[0], jnp.concatenate([far_key, key16[1]], axis=0)]
    values_ = [value16[0], jnp.concatenate([far_value, value16[1]], axis=0)]

    probs, attended16, attention, residual, mid16 = [], [], [], [], []
    hidden16, gate, up, ffn = [], [], [], []
    for i in both:
        p, a = attend(query16[i], keys[i], values_[i], allowed[i], score_scale)
        probs.append(p)
        attended16.append(a)
    for i in both:
        part = jnp.dot(attended16[i], w_out, preferred_element_type=F32).astype(BF16)
        attention.append(tp_sum(part).astype(F32))
        residual.append(inputs[i] + rms_norm(attention[i], g_pa))
        mid16.append(rms_norm(residual[i], g_pf).astype(BF16))
        gate.append(jnp.dot(mid16[i], w_gate, preferred_element_type=F32).astype(BF16))
        up.append(jnp.dot(mid16[i], w_up, preferred_element_type=F32).astype(BF16))
        hidden16.append(geglu(gate[i].astype(F32), up[i].astype(F32)).astype(BF16))
        part = jnp.dot(hidden16[i], w_down, preferred_element_type=F32).astype(BF16)
        ffn.append(tp_sum(part).astype(F32))

    out_parts, d_ffn16, d_gate16, d_up16 = [], [], [], []
    gain_sums = []
    cots = [values.astype(F32) for values in cots16]
    for i in both:
        outputs = residual[i] + rms_norm(ffn[i], g_pff)
        out_parts.append(
            lax.dynamic_slice_in_dim(outputs, tp_index * feature_cols, feature_cols, 1).astype(BF16)
        )
        d_ffn, d_pff = rms_back(ffn[i], g_pff, cots[i])
        d_ffn16.append(d_ffn.astype(BF16))
        d_hidden = contract(d_ffn16[i], w_down, 1, 1)
        gate32, up32 = gate[i].astype(F32), up[i].astype(F32)
        _, pull = jax.vjp(geglu, gate32, up32)
        d_gate, d_up = pull(d_hidden)
        d_gate16.append(d_gate.astype(BF16))
        d_up16.append(d_up.astype(BF16))
        gain_sums.append(d_pff)
    hidden_all, mid_all, d_ffn_all, d_gate_all, d_up_all = [
        jnp.concatenate(pair, axis=0) for pair in (hidden16, mid16, d_ffn16, d_gate16, d_up16)
    ]
    grad_down = contract(hidden_all, d_ffn_all, 0, 0).astype(BF16)
    grad_gate = contract(mid_all, d_gate_all, 0, 0).astype(BF16)
    grad_up = contract(mid_all, d_up_all, 0, 0).astype(BF16)

    def summed(grad):
        size = grad.shape[0] // 2
        return jnp.concatenate([sum_y_first(grad[:size]), sum_z_first(grad[size:])], axis=0).astype(
            F32
        )

    down_sum, gate_sum, up_sum = summed(grad_down), summed(grad_gate), summed(grad_up)

    d_resid, d_attn16, d_attended16 = [], [], []
    pf_sums, pa_sums = [], []
    for i in both:
        part = contract(d_gate16[i], w_gate, 1, 1) + contract(d_up16[i], w_up, 1, 1)
        d_mid = tp_sum(part.astype(BF16)).astype(F32)
        d_norm, d_pf = rms_back(residual[i], g_pf, d_mid)
        d_resid.append(cots[i] + d_norm)
        d_attn, d_pa = rms_back(attention[i], g_pa, d_resid[i])
        d_attn16.append(d_attn.astype(BF16))
        d_attended16.append(contract(d_attn16[i], w_out, 1, 1).astype(BF16))
        pf_sums.append(d_pf)
        pa_sums.append(d_pa)
    grad_out = contract(
        jnp.concatenate(attended16, axis=0), jnp.concatenate(d_attn16, axis=0), 0, 0
    ).astype(BF16)
    out_sum = sum_y_first(grad_out).astype(F32)

    d_query, d_key, d_value = [], [], []
    for i in both:
        dq, dk, dv = attend_back(
            query16[i], keys[i], values_[i], probs[i], d_attended16[i], score_scale
        )
        d_query.append(dq)
        d_key.append(dk)
        d_value.append(dv)
    far_dk = lax.ppermute(d_key[1][:rows].astype(BF16), "ctx", MESH_PAIR)
    far_dv = lax.ppermute(d_value[1][:rows].astype(BF16), "ctx", MESH_PAIR)
    d_key = [d_key[0] + far_dk.astype(F32), d_key[1][rows:]]
    d_value = [d_value[0] + far_dv.astype(F32), d_value[1][rows:]]

    w_blocks = w_qkv.reshape(4, feature_cols, w_qkv.shape[1])
    w_near = [
        lax.dynamic_index_in_dim(w_blocks, tp_index ^ j, keepdims=False) for j in range(4)
    ]
    g_in_own = lax.dynamic_slice_in_dim(g_in, tp_index * feature_cols, feature_cols)
    d_qkv16, x_parts, q_sums, k_sums, in_sums = [], [], [], [], []
    for i in both:
        dq, d_gq = rms_back(query_raw[i], g_q, rotate_back(d_query[i], *tables[i]))
        dk, d_gk = rms_back(key_raw[i], g_k, rotate_back(d_key[i], *tables[i]))
        q_sums.append(d_gq)
        k_sums.append(d_gk)
        d_qkv16.append(jnp.concatenate([dq, dk, d_value[i]], axis=1).astype(BF16))
        parts = [contract(d_qkv16[i], w, 1, 1).astype(BF16) for w in w_near]
        near = lax.ppermute(jnp.stack([parts[1], parts[3]]), "tp", XOR1)
        mine = add16(parts[0], near[0])
        theirs = add16(parts[2], near[1])
        u = add16(mine, lax.ppermute(theirs, "tp", XOR2)).astype(F32)
        own_in = token_parts[i].astype(F32)
        weighted = g_in_own * u
        inner = jnp.sum(own_in * weighted, axis=-1)
        inner = inner + lax.ppermute(inner, "tp", XOR1)
        inner = inner + lax.ppermute(inner, "tp", XOR2)
        inner = inner[:, None] / (4 * feature_cols)
        scale = scale_of(inputs[i])
        d_in = scale * weighted - own_in * (scale * scale * scale * inner)
        resid_own = lax.dynamic_slice_in_dim(d_resid[i], tp_index * feature_cols, feature_cols, 1)
        x_parts.append((resid_own + d_in).astype(BF16))
        in_sums.append(jnp.sum(u * own_in * scale, axis=0))
    grad_qkv = contract(
        jnp.concatenate(normed16, axis=0), jnp.concatenate(d_qkv16, axis=0), 0, 0
    ).astype(BF16)
    query_sum = sum_y_first(grad_qkv[:, :head_dim]).astype(F32)
    kv_blocks = grad_qkv[:, head_dim:].reshape(4, feature_cols, 2 * head_dim)
    kv = [lax.dynamic_index_in_dim(kv_blocks, tp_index ^ j, keepdims=False) for j in range(4)]
    near = lax.ppermute(jnp.stack([kv[1], kv[3]]), "tp", XOR1)
    mine, theirs = add16(kv[0], near[0]), add16(kv[2], near[1])
    mine = add16(mine, lax.ppermute(theirs, "tp", XOR2))
    mine = sum_y_first(mine)
    far = lax.ppermute(mine, "tp", XOR2)
    near = lax.ppermute(jnp.stack([mine, far]), "tp", XOR1)
    kv_all = (mine, near[0], far, near[1])
    kv_sum = jnp.concatenate(
        [lax.select_n(tp_index ^ j, *kv_all) for j in range(4)], axis=0
    ).astype(F32)

    width = 4 * feature_cols
    in_full = lax.dynamic_update_slice_in_dim(
        jnp.zeros((width,), F32), in_sums[0] + in_sums[1], tp_index * feature_cols, 0
    )
    shared = [0.25 * (pair[0] + pair[1]) for pair in (pa_sums, pf_sums, gain_sums)]
    small = sum_all(
        jnp.concatenate([in_full, *shared, q_sums[0] + q_sums[1], k_sums[0] + k_sums[1]]).reshape(
            -1, 128
        )
    ).reshape(-1)
    gains = [small[j * width : (j + 1) * width] for j in range(4)]
    gain_q_sum = small[4 * width : 4 * width + head_dim]
    gain_k_sum = small[4 * width + head_dim :]
    return (
        join(*out_parts, ctx_index),
        join(*x_parts, ctx_index),
        query_sum,
        kv_sum[:, :head_dim],
        kv_sum[:, head_dim:],
        out_sum,
        gate_sum,
        up_sum,
        down_sum,
        gains[0],
        gains[1],
        gains[2],
        gains[3],
        gain_q_sum,
        gain_k_sum,
    )


def solution(mesh):
    def layer(*args):
        tokens, bucket_lengths = args[0], args[-2]
        sizes = mesh.shape
        group_rows = tokens.shape[0] // sizes["dp"]
        paired = (sizes["dp"], sizes["ctx"], sizes["tp"]) == (4, 2, 4) and (
            group_rows == 1024 * bucket_lengths.shape[1] == 2048
        )
        return mapped(paired_shards if paired else shards)(*args)

    def mapped(body):
        return jax.shard_map(
            body,
            mesh=mesh,
            in_specs=(
                P(("dp", "ctx"), "tp"),
                P(("dp", "ctx"), "tp"),
                P(None, "tp"),
                P(),
                P(),
                P("tp", None),
                P(None, "tp"),
                P(None, "tp"),
                P("tp", None),
                P(),
                P(),
                P(),
                P(),
                P(),
                P(),
                P("dp", None),
                P("dp", None),
            ),
            out_specs=(
                P(("dp", "ctx"), "tp"),
                P(("dp", "ctx"), "tp"),
                P(None, "tp"),
                P(),
                P(),
                P("tp", None),
                P(None, "tp"),
                P(None, "tp"),
                P("tp", None),
                P(),
                P(),
                P(),
                P(),
                P(),
                P(),
            ),
            check_vma=False,
        )

    return layer
```

```python
from functools import partial

import jax
import jax.numpy as jnp
from jax import lax
from jax.experimental import pallas as pl
from jax.experimental.pallas import tpu as pltpu
from jax.sharding import PartitionSpec as P

QBLK = 512


EPSILON = 1e-06
ROPE_BASE = 1000000.0
MASKED = -1e30


def contract(left, right, left_dim, right_dim):
    return lax.dot_general(
        left, right, (((left_dim,), (right_dim,)), ((), ())), preferred_element_type=jnp.float32
    )


def rms_norm(values, gain):
    return values * lax.rsqrt(jnp.mean(values * values, axis=-1, keepdims=True) + EPSILON) * gain


def rotate(values, cosine_table, sine_table):
    half_dim = values.shape[-1] // 2
    turned = jnp.concatenate([-values[..., half_dim:], values[..., :half_dim]], axis=-1)
    return values * cosine_table + turned * sine_table


def rope_tables(seq_pos, head_dim):
    freq_index = jnp.arange(head_dim // 2, dtype=jnp.float32)
    inverse = ROPE_BASE ** (-2.0 * freq_index / head_dim)
    angles = seq_pos.astype(jnp.float32)[:, None] * inverse[None, :]
    angles = jnp.concatenate([angles, angles], axis=-1)
    return (jnp.cos(angles), jnp.sin(angles))


def stream_layout(bucket_row, true_row, tok_dev, n_ctx):
    group_rows = tok_dev * n_ctx
    half_shard = tok_dev // 2
    row_ids = jnp.arange(group_rows, dtype=jnp.int32)
    device = row_ids // tok_dev
    half_index = row_ids % tok_dev // half_shard
    block_ids = jnp.where(half_index == 0, device, 2 * n_ctx - 1 - device)
    stream_pos = block_ids * half_shard + row_ids % half_shard
    starts = jnp.cumsum(bucket_row) - bucket_row
    ends = starts + bucket_row
    inside = (
        (stream_pos[:, None] >= starts[None, :]) & (stream_pos[:, None] < ends[None, :])
    ).astype(jnp.int32)
    slot_ids = jnp.arange(bucket_row.shape[0], dtype=jnp.int32)
    seq_ids = jnp.sum(inside * slot_ids[None, :], axis=1)
    seq_pos = stream_pos - jnp.sum(inside * starts[None, :], axis=1)
    is_valid = (seq_pos < jnp.sum(inside * true_row[None, :], axis=1)).astype(jnp.int32)
    return (seq_ids, stream_pos, seq_pos, is_valid)


def shape_heads(query_raw, key_raw, gain_q, gain_k, cosine_table, sine_table):
    query_heads = query_raw.reshape(query_raw.shape[0], -1, key_raw.shape[1])
    query_rot = rotate(
        rms_norm(query_heads, gain_q), cosine_table[:, None, :], sine_table[:, None, :]
    )
    key_rot = rotate(rms_norm(key_raw, gain_k), cosine_table, sine_table)
    return (query_rot, key_rot)


def geglu(gate_in, up_in):
    return jax.nn.gelu(gate_in, approximate=True) * up_in


def shards(
    tokens,
    out_grad,
    w_query,
    w_key,
    w_value,
    w_out,
    w_gate,
    w_up,
    w_down,
    gain_in,
    gain_post_attn,
    gain_pre_ffn,
    gain_post_ffn,
    gain_query,
    gain_key,
    bucket_lengths,
    true_lengths,
):
    n_ctx = lax.axis_size("ctx")
    ctx_index = lax.axis_index("ctx")
    tp_index = lax.axis_index("tp")
    rows_dev = tokens.shape[0]
    feature_cols = tokens.shape[1]
    head_dim = w_key.shape[1]
    head_count = w_query.shape[1] // head_dim
    group_rows = rows_dev * n_ctx
    blocks = rows_dev // QBLK
    score_scale = head_dim ** (-0.5)
    gain_in32, gain_pa32, gain_pf32, gain_pff32, gain_q32, gain_k32 = [
        tensor.astype(jnp.float32)
        for tensor in (gain_in, gain_post_attn, gain_pre_ffn, gain_post_ffn, gain_query, gain_key)
    ]
    input_full, cot_full = (
        lax.all_gather(tokens, "tp", axis=1, tiled=True),
        lax.all_gather(out_grad, "tp", axis=1, tiled=True),
    )
    inputs = input_full.astype(jnp.float32)
    seq_all, spos_all, rpos_all, valid_all = stream_layout(
        bucket_lengths[0], true_lengths[0], rows_dev, n_ctx
    )
    first_row = ctx_index * rows_dev
    seq_local = lax.dynamic_slice_in_dim(seq_all, first_row, rows_dev)
    spos_local = lax.dynamic_slice_in_dim(spos_all, first_row, rows_dev)
    rpos_local = lax.dynamic_slice_in_dim(rpos_all, first_row, rows_dev)
    cosine_table, sine_table = rope_tables(rpos_local, head_dim)
    normed_in, pull_in = jax.vjp(rms_norm, inputs, gain_in32)
    normed_in16 = normed_in.astype(jnp.bfloat16)
    query_raw = jnp.dot(normed_in16, w_query, preferred_element_type=jnp.float32)
    key_raw = jnp.dot(normed_in16, w_key, preferred_element_type=jnp.float32)
    value_raw = jnp.dot(normed_in16, w_value, preferred_element_type=jnp.float32)
    (query_rot, key_rot), rope_pull = jax.vjp(
        partial(shape_heads, cosine_table=cosine_table, sine_table=sine_table),
        query_raw,
        key_raw,
        gain_q32,
        gain_k32,
    )
    query16 = query_rot.astype(jnp.bfloat16)
    key16 = key_rot.astype(jnp.bfloat16)
    value16 = value_raw.astype(jnp.bfloat16)
    key_group, value_group = (
        lax.all_gather(key16, "ctx", axis=0, tiled=True),
        lax.all_gather(value16, "ctx", axis=0, tiled=True),
    )

    def allowed_mask(seq_rows, spos_rows):
        return (
            (valid_all[None, :] == 1)
            & (seq_all[None, :] == seq_rows[:, None])
            & (spos_all[None, :] <= spos_rows[:, None])
        )

    query_blocks = query16.reshape(blocks, QBLK, head_count, head_dim)
    seq_blocks = seq_local.reshape(blocks, QBLK)
    spos_blocks = spos_local.reshape(blocks, QBLK)

    def forward_block(block_item):
        query_block, seq_rows, spos_rows = block_item
        scores = (
            jnp.einsum("qhd,kd->hqk", query_block, key_group, preferred_element_type=jnp.float32)
            * score_scale
        )
        scores = jnp.where(allowed_mask(seq_rows, spos_rows)[None], scores, MASKED)
        row_max = jnp.max(scores, axis=-1, keepdims=True)
        exp_scores = jnp.exp(scores - row_max)
        row_total = jnp.sum(exp_scores, axis=-1, keepdims=True)
        prob_rows = (exp_scores / row_total).astype(jnp.bfloat16)
        output = jnp.einsum(
            "hqk,kd->qhd", prob_rows, value_group, preferred_element_type=jnp.float32
        )
        return (output, (row_max + jnp.log(row_total))[..., 0])

    attended, log_norm = lax.map(forward_block, (query_blocks, seq_blocks, spos_blocks))
    attended16 = attended.reshape(rows_dev, head_count * head_dim).astype(jnp.bfloat16)
    attention = lax.psum(
        jnp.dot(attended16, w_out, preferred_element_type=jnp.float32).astype(jnp.bfloat16), "tp"
    ).astype(jnp.float32)
    post_attn, pull_post_attn = jax.vjp(rms_norm, attention, gain_pa32)
    residual = inputs + post_attn
    normed_mid, pull_pre_ffn = jax.vjp(rms_norm, residual, gain_pf32)
    mid16 = normed_mid.astype(jnp.bfloat16)
    gate_out = jnp.dot(mid16, w_gate, preferred_element_type=jnp.float32)
    up_out = jnp.dot(mid16, w_up, preferred_element_type=jnp.float32)
    hidden, pull_geglu = jax.vjp(geglu, gate_out, up_out)
    hidden16 = hidden.astype(jnp.bfloat16)
    ffn_branch = lax.psum(
        jnp.dot(hidden16, w_down, preferred_element_type=jnp.float32).astype(jnp.bfloat16), "tp"
    ).astype(jnp.float32)
    post_ffn, pull_post_ffn = jax.vjp(rms_norm, ffn_branch, gain_pff32)
    outputs = residual + post_ffn
    out_rows = lax.dynamic_slice_in_dim(outputs, tp_index * feature_cols, feature_cols, 1).astype(
        jnp.bfloat16
    )
    cotangent = cot_full.astype(jnp.float32)
    d_ffn, d_gain_post_ffn = pull_post_ffn(cotangent)
    d_ffn16 = d_ffn.astype(jnp.bfloat16)
    d_hidden = contract(d_ffn16, w_down, 1, 1)
    grad_down = contract(hidden16, d_ffn16, 0, 0)
    d_gate, d_up = pull_geglu(d_hidden)
    d_gate16 = d_gate.astype(jnp.bfloat16)
    d_up16 = d_up.astype(jnp.bfloat16)
    grad_gate = contract(mid16, d_gate16, 0, 0)
    grad_up = contract(mid16, d_up16, 0, 0)
    d_mid = lax.psum(
        (contract(d_gate16, w_gate, 1, 1) + contract(d_up16, w_up, 1, 1)).astype(jnp.bfloat16), "tp"
    ).astype(jnp.float32)
    d_res_norm, d_gain_pre_ffn = pull_pre_ffn(d_mid)
    d_resid = cotangent + d_res_norm
    d_attn, d_gain_post_attn = pull_post_attn(d_resid)
    d_attn16 = d_attn.astype(jnp.bfloat16)
    d_attended16 = contract(d_attn16, w_out, 1, 1).astype(jnp.bfloat16)
    grad_out = contract(attended16, d_attn16, 0, 0)
    key_back, value_back = (key_group, value_group)

    def backward_block(running, block_item):
        key_sum, value_sum = running
        query_block, dout_block, lse_block, seq_rows, spos_rows = block_item
        scores = (
            jnp.einsum("qhd,kd->hqk", query_block, key_back, preferred_element_type=jnp.float32)
            * score_scale
        )
        scores = jnp.where(allowed_mask(seq_rows, spos_rows)[None], scores, MASKED)
        prob_rows = jnp.exp(scores - lse_block[..., None])
        prob16 = prob_rows.astype(jnp.bfloat16)
        d_probs = jnp.einsum(
            "qhd,kd->hqk", dout_block, value_back, preferred_element_type=jnp.float32
        )
        row_inner = jnp.sum(prob_rows * d_probs, axis=-1, keepdims=True)
        d_scores16 = (prob_rows * (d_probs - row_inner)).astype(jnp.bfloat16)
        d_query = (
            jnp.einsum("hqk,kd->qhd", d_scores16, key_back, preferred_element_type=jnp.float32)
            * score_scale
        )
        key_sum = (
            key_sum
            + jnp.einsum("hqk,qhd->kd", d_scores16, query_block, preferred_element_type=jnp.float32)
            * score_scale
        )
        value_sum = value_sum + jnp.einsum(
            "hqk,qhd->kd", prob16, dout_block, preferred_element_type=jnp.float32
        )
        return ((key_sum, value_sum), d_query)

    zero_rows = jnp.zeros((group_rows, head_dim), jnp.float32)
    (key_sum, value_sum), d_query_blocks = lax.scan(
        backward_block,
        (zero_rows, zero_rows),
        (
            query_blocks,
            d_attended16.reshape(blocks, QBLK, head_count, head_dim),
            log_norm,
            seq_blocks,
            spos_blocks,
        ),
    )
    d_key_rot, d_value = (
        lax.psum_scatter(
            key_sum.astype(jnp.bfloat16), "ctx", scatter_dimension=0, tiled=True
        ).astype(jnp.float32),
        lax.psum_scatter(
            value_sum.astype(jnp.bfloat16), "ctx", scatter_dimension=0, tiled=True
        ).astype(jnp.float32),
    )
    d_query_raw, d_key_raw, d_gain_query, d_gain_key = rope_pull(
        (d_query_blocks.reshape(rows_dev, head_count, head_dim), d_key_rot)
    )
    d_query16 = d_query_raw.astype(jnp.bfloat16)
    d_key16 = d_key_raw.astype(jnp.bfloat16)
    d_value16 = d_value.astype(jnp.bfloat16)
    grad_query = contract(normed_in16, d_query16, 0, 0)
    grad_key = contract(normed_in16, d_key16, 0, 0)
    grad_value = contract(normed_in16, d_value16, 0, 0)
    d_normed_part = (
        contract(d_query16, w_query, 1, 1)
        + contract(d_key16, w_key, 1, 1)
        + contract(d_value16, w_value, 1, 1)
    )
    d_normed_in = lax.psum(d_normed_part.astype(jnp.bfloat16), "tp").astype(jnp.float32)
    d_in_norm, d_gain_in = pull_in(d_normed_in)
    d_inputs = d_resid + d_in_norm
    grad_rows = lax.dynamic_slice_in_dim(d_inputs, tp_index * feature_cols, feature_cols, 1).astype(
        jnp.bfloat16
    )
    sharded = (
        grad_query,
        grad_out,
        grad_gate,
        grad_up,
        grad_down,
        d_gain_in,
        d_gain_post_attn,
        d_gain_pre_ffn,
        d_gain_post_ffn,
    )
    reduced = (
        lax.psum_scatter(
            sharded[0].astype(jnp.bfloat16), ("dp", "ctx"), scatter_dimension=0, tiled=True
        ).astype(jnp.float32),
        lax.psum_scatter(
            sharded[1].astype(jnp.bfloat16), ("dp", "ctx"), scatter_dimension=1, tiled=True
        ).astype(jnp.float32),
        lax.psum_scatter(
            sharded[2].astype(jnp.bfloat16), ("dp", "ctx"), scatter_dimension=0, tiled=True
        ).astype(jnp.float32),
        lax.psum_scatter(
            sharded[3].astype(jnp.bfloat16), ("dp", "ctx"), scatter_dimension=0, tiled=True
        ).astype(jnp.float32),
        lax.psum_scatter(
            sharded[4].astype(jnp.bfloat16), ("dp", "ctx"), scatter_dimension=1, tiled=True
        ).astype(jnp.float32),
        lax.psum_scatter(
            sharded[5].astype(jnp.bfloat16), ("dp", "ctx"), scatter_dimension=0, tiled=True
        ).astype(jnp.float32),
        lax.psum_scatter(
            sharded[6].astype(jnp.bfloat16), ("dp", "ctx"), scatter_dimension=0, tiled=True
        ).astype(jnp.float32),
        lax.psum_scatter(
            sharded[7].astype(jnp.bfloat16), ("dp", "ctx"), scatter_dimension=0, tiled=True
        ).astype(jnp.float32),
        lax.psum_scatter(
            sharded[8].astype(jnp.bfloat16), ("dp", "ctx"), scatter_dimension=0, tiled=True
        ).astype(jnp.float32),
    )
    summed = (
        lax.all_gather(reduced[0].astype(jnp.bfloat16), ("dp", "ctx"), axis=0, tiled=True).astype(
            jnp.float32
        ),
        lax.all_gather(reduced[1].astype(jnp.bfloat16), ("dp", "ctx"), axis=1, tiled=True).astype(
            jnp.float32
        ),
        lax.all_gather(reduced[2].astype(jnp.bfloat16), ("dp", "ctx"), axis=0, tiled=True).astype(
            jnp.float32
        ),
        lax.all_gather(reduced[3].astype(jnp.bfloat16), ("dp", "ctx"), axis=0, tiled=True).astype(
            jnp.float32
        ),
        lax.all_gather(reduced[4].astype(jnp.bfloat16), ("dp", "ctx"), axis=1, tiled=True).astype(
            jnp.float32
        ),
        lax.all_gather(reduced[5].astype(jnp.bfloat16), ("dp", "ctx"), axis=0, tiled=True).astype(
            jnp.float32
        ),
        lax.all_gather(reduced[6].astype(jnp.bfloat16), ("dp", "ctx"), axis=0, tiled=True).astype(
            jnp.float32
        ),
        lax.all_gather(reduced[7].astype(jnp.bfloat16), ("dp", "ctx"), axis=0, tiled=True).astype(
            jnp.float32
        ),
        lax.all_gather(reduced[8].astype(jnp.bfloat16), ("dp", "ctx"), axis=0, tiled=True).astype(
            jnp.float32
        ),
    )
    shared = lax.psum((grad_key, grad_value, d_gain_query, d_gain_key), ("dp", "ctx", "tp"))
    return (
        out_rows,
        grad_rows,
        summed[0],
        shared[0],
        shared[1],
        summed[1],
        summed[2],
        summed[3],
        summed[4],
        summed[5],
        summed[6],
        summed[7],
        summed[8],
        shared[2],
        shared[3],
    )


MESH_PAIR = ((0, 1), (1, 0))
XOR1 = ((0, 1), (1, 0), (2, 3), (3, 2))
XOR2 = ((0, 2), (2, 0), (1, 3), (3, 1))
MESH = pl.DeviceIdType.MESH
F32 = jnp.float32
BF16 = jnp.bfloat16


def add16(left, right):
    return (left.astype(F32) + right.astype(F32)).astype(BF16)


def halves(values, index):
    size = values.shape[0] // 2
    own = lax.dynamic_slice_in_dim(values, index * size, size)
    other = lax.dynamic_slice_in_dim(values, (1 - index) * size, size)
    return own, other


def join(own, other, index):
    first = jnp.where(index == 0, own, other)
    second = jnp.where(index == 0, other, own)
    return jnp.concatenate([first, second], axis=0)


def tp_sum(values):
    odd = lax.axis_index("tp") % 2
    own, other = halves(values, odd)
    own = add16(own, lax.ppermute(other, "tp", XOR1))
    own = add16(own, lax.ppermute(own, "tp", XOR2))
    return join(own, lax.ppermute(own, "tp", XOR1), odd)


def tp_gather(part):
    tp_index = lax.axis_index("tp")
    near = lax.ppermute(part, "tp", XOR1)
    far = lax.ppermute(part, "tp", XOR2)
    both = lax.ppermute(far, "tp", XOR1)
    blocks = (part, near, far, both)
    return jnp.concatenate(
        [lax.select_n(tp_index ^ j, *blocks) for j in range(4)], axis=1
    )


def sum_all(values):
    for axis, pairs in (
        ("tp", XOR1), ("tp", XOR2), ("ctx", MESH_PAIR), ("dp", XOR1), ("dp", XOR2)
    ):
        values = values + lax.ppermute(values, axis, pairs)
    return values


def grid_sum_kernel(s, K, L, g, out, Y2, Z2, M2, Z1, M1, Y1, *sems):
    sy2, sz2, sm2, sfo, sfy, sz1, sm1, sy1, sfm, sfa, sfb = sems[:11]
    ry2, rz2, rm2, rfo, rfy, rz1, rm1, ry1, rfm, rfa, rfb = sems[11:]
    dp, ctx, tp = lax.axis_index("dp"), lax.axis_index("ctx"), lax.axis_index("tp")
    upper = dp // 2
    outer = (dp == 0) | (dp == 3)
    inner = jnp.logical_not(outer)
    zn = jnp.where(dp < 2, 1 - dp, 5 - dp)
    zm = 3 - dp
    ypeer, zpeer, mpeer = (dp, 1 - ctx, tp), (zn, ctx, tp), (zm, ctx, tp)
    bar = pltpu.get_barrier_semaphore()
    pl.semaphore_signal(bar, inc=1, device_id=ypeer, device_id_type=MESH)
    pl.semaphore_signal(bar, inc=1, device_id=zpeer, device_id_type=MESH)
    pl.when(inner)(lambda: pl.semaphore_signal(bar, inc=1, device_id=mpeer, device_id_type=MESH))
    pl.semaphore_wait(bar, jnp.where(inner, 3, 2))
    base1 = 2 * s * K
    def rows2(k, h): return pl.ds(pl.multiple_of((2 * k + h) * s, s), s)
    def rows1(k, h): return pl.ds(pl.multiple_of(base1 + (2 * k + h) * s, s), s)
    def pair1(k): return pl.ds(pl.multiple_of(base1 + 2 * k * s, s), 2 * s)
    def slot(k, n=1): return pl.ds(pl.multiple_of(k * n * s, s), n * s)
    def half1(k, h): return pl.ds(pl.multiple_of((2 * k + h) * s, s), s)
    def cp(src, dst, ss, rs, k, dev):
        return pltpu.make_async_remote_copy(src_ref=src, dst_ref=dst, send_sem=ss.at[k], recv_sem=rs.at[k], device_id=dev, device_id_type=MESH)
    def c_y2(k): return cp(g.at[rows2(k, 1 - ctx)], Y2.at[slot(k)], sy2, ry2, k, ypeer)
    def c_z2(k): return cp(Y2.at[slot(k)], Z2.at[slot(k)], sz2, rz2, k, zpeer)
    def c_m2(k): return cp(Z2.at[slot(k)], M2.at[slot(k)], sm2, rm2, k, mpeer)
    def c_fo(k): return cp(out.at[rows2(k, ctx)], out.at[rows2(k, ctx)], sfo, rfo, k, zpeer)
    def c_fy(k): return cp(out.at[rows2(k, ctx)], out.at[rows2(k, ctx)], sfy, rfy, k, ypeer)
    def c_z1(k): return cp(g.at[pair1(k)], Z1.at[slot(k, 2)], sz1, rz1, k, zpeer)
    def c_m1(k): return cp(Z1.at[half1(k, 1 - upper)], M1.at[slot(k)], sm1, rm1, k, mpeer)
    def c_y1(k): return cp(M1.at[slot(k)], Y1.at[slot(k)], sy1, ry1, k, ypeer)
    def c_fm(k): return cp(out.at[rows1(k, upper)], out.at[rows1(k, upper)], sfm, rfm, k, mpeer)
    def c_fa(k): return cp(out.at[rows1(k, upper)], out.at[rows1(k, upper)], sfa, rfa, k, zpeer)
    def c_fb(k): return cp(out.at[rows1(k, 1 - upper)], out.at[rows1(k, 1 - upper)], sfb, rfb, k, zpeer)
    def add(a, b): return (a.astype(F32) + b.astype(F32)).astype(BF16)
    def at(t, lag, cond, fn):
        k = t - lag
        pl.when(cond & (k >= 0) & (k < K))(lambda: fn(k))
    yes = dp >= 0
    def a2(k):
        c_y2(k).start()
    def a1(k):
        c_z1(k).start()
    def b2(k):
        c_y2(k).wait_recv()
        Y2[slot(k)] = add(Y2[slot(k)], g[rows2(k, ctx)])
        pl.when(outer)(lambda: c_z2(k).start())
    def b1(k):
        c_z1(k).wait_recv()
        Z1[slot(k, 2)] = add(Z1[slot(k, 2)], g[pair1(k)])
        c_m1(k).start()
    def c2(k):
        c_z2(k).wait_recv()
        Z2[slot(k)] = add(Z2[slot(k)], Y2[slot(k)])
        c_m2(k).start()
    def c1(k):
        c_m1(k).wait_recv()
        M1[slot(k)] = add(M1[slot(k)], Z1[half1(k, upper)])
        c_y1(k).start()
    def d2(k):
        c_m2(k).wait_recv()
        out[rows2(k, ctx)] = add(M2[slot(k)], Z2[slot(k)])
        c_fo(k).start()
        c_fy(k).start()
    def d1(k):
        c_y1(k).wait_recv()
        out[rows1(k, upper)] = add(Y1[slot(k)], M1[slot(k)])
        c_fm(k).start()
        c_fa(k).start()
    def e2(k):
        c_fo(k).wait_recv()
        c_fy(k).start()
    def e1(k):
        c_fm(k).wait_recv()
        c_fb(k).start()
    def f2(k):
        c_fy(k).wait_recv()
        c_y2(k).wait_send()
        c_fy(k).wait_send()
    def f2o(k):
        c_z2(k).wait_send()
    def f2i(k):
        c_m2(k).wait_send()
        c_fo(k).wait_send()
    def f1o(k):
        c_fa(k).wait_recv()
        c_fb(k).wait_recv()
        c_z1(k).wait_send()
    def f1i(k):
        c_m1(k).wait_send()
        c_y1(k).wait_send()
        c_fm(k).wait_send()
        c_fa(k).wait_send()
        c_fb(k).wait_send()
    def body(t, carry):
        at(t, 5 * L, yes, f2)
        at(t, 5 * L, outer, f2o)
        at(t, 5 * L, inner, f2i)
        at(t, 5 * L, outer, f1o)
        at(t, 5 * L, inner, f1i)
        at(t, 4 * L, outer, e2)
        at(t, 4 * L, inner, e1)
        at(t, 3 * L, inner, d2)
        at(t, 3 * L, inner, d1)
        at(t, 2 * L, inner, c2)
        at(t, 2 * L, inner, c1)
        at(t, L, yes, b2)
        at(t, L, inner, b1)
        at(t, 0, yes, a2)
        at(t, 0, outer, a1)
        return carry
    lax.fori_loop(0, K + 5 * L, body, 0)

def grid_sum(grads):
    step_rows, lag = 48, 1
    rows, width = grads.shape
    steps = rows // (4 * step_rows)

    def slots(n):
        return pltpu.VMEM((n * step_rows * steps, width), BF16)

    return pl.pallas_call(
        partial(grid_sum_kernel, step_rows, steps, lag),
        out_shape=jax.ShapeDtypeStruct(grads.shape, BF16),
        in_specs=[pl.BlockSpec(memory_space=pltpu.VMEM)],
        out_specs=pl.BlockSpec(memory_space=pltpu.VMEM),
        scratch_shapes=[slots(n) for n in (1, 1, 1, 2, 1, 1)]
        + [pltpu.SemaphoreType.DMA((steps,)) for _ in range(22)],
        name="grid_sum",
        compiler_params=pltpu.CompilerParams(
            collective_id=1, has_side_effects=True, vmem_limit_bytes=62 << 20
        ),
    )(grads)


def scale_of(values):
    return lax.rsqrt(jnp.mean(values * values, axis=-1, keepdims=True) + EPSILON)


def rms_back(values, gain, cotangent):
    scale = scale_of(values)
    weighted = gain * cotangent
    inner = jnp.mean(values * weighted, axis=-1, keepdims=True)
    back = scale * weighted - values * (scale * scale * scale * inner)
    return back, jnp.sum(cotangent * values * scale, axis=0)


def rotate_back(values, cosine_table, sine_table):
    half_dim = values.shape[-1] // 2
    turned = values * sine_table
    turned = jnp.concatenate([turned[..., half_dim:], -turned[..., :half_dim]], axis=-1)
    return values * cosine_table + turned


def positions(block, rows, bucket_row, true_row):
    stream_pos = block * rows + jnp.arange(rows, dtype=jnp.int32)
    starts = jnp.cumsum(bucket_row) - bucket_row
    ends = starts + bucket_row
    inside = (
        (stream_pos[:, None] >= starts[None, :]) & (stream_pos[:, None] < ends[None, :])
    ).astype(jnp.int32)
    slot_ids = jnp.arange(bucket_row.shape[0], dtype=jnp.int32)
    seq_id = jnp.sum(inside * slot_ids[None, :], axis=1)
    seq_pos = stream_pos - jnp.sum(inside * starts[None, :], axis=1)
    is_valid = (seq_pos < jnp.sum(inside * true_row[None, :], axis=1)).astype(jnp.int32)
    return seq_id, stream_pos, seq_pos, is_valid


def allowed_pairs(query_layout, key_layout):
    return (
        (key_layout[3][None, :] == 1)
        & (key_layout[0][None, :] == query_layout[0][:, None])
        & (key_layout[1][None, :] <= query_layout[1][:, None])
    )


def attend(query16, key16, value16, allowed, score_scale):
    scores = contract(query16, key16, 1, 1) * score_scale
    scores = jnp.where(allowed, scores, MASKED)
    exp_scores = jnp.exp(scores - jnp.max(scores, axis=-1, keepdims=True))
    probs = exp_scores / jnp.sum(exp_scores, axis=-1, keepdims=True)
    attended = jnp.dot(probs.astype(BF16), value16, preferred_element_type=F32)
    return probs, attended.astype(BF16)


def attend_back(query16, key16, value16, probs, d_attended16, score_scale):
    d_probs = contract(d_attended16, value16, 1, 1)
    inner = jnp.sum(probs * d_probs, axis=-1, keepdims=True)
    d_scores16 = (probs * (d_probs - inner)).astype(BF16)
    d_query = jnp.dot(d_scores16, key16, preferred_element_type=F32) * score_scale
    d_key = contract(d_scores16, query16, 0, 0) * score_scale
    d_value = contract(probs.astype(BF16), d_attended16, 0, 0)
    return d_query, d_key, d_value


def paired_shards(
    tokens,
    out_grad,
    w_query,
    w_key,
    w_value,
    w_out,
    w_gate,
    w_up,
    w_down,
    gain_in,
    gain_post_attn,
    gain_pre_ffn,
    gain_post_ffn,
    gain_query,
    gain_key,
    bucket_lengths,
    true_lengths,
):
    ctx_index, tp_index = lax.axis_index("ctx"), lax.axis_index("tp")
    rows = tokens.shape[0] // 2
    feature_cols = tokens.shape[1]
    head_dim = w_key.shape[1]
    score_scale = head_dim ** (-0.5)
    g_in, g_pa, g_pf, g_pff, g_q, g_k = [
        gain.astype(F32)
        for gain in (gain_in, gain_post_attn, gain_pre_ffn, gain_post_ffn, gain_query, gain_key)
    ]
    both = range(2)
    token_parts = halves(tokens, ctx_index)
    cot_parts = halves(out_grad, ctx_index)
    w_qkv = jnp.concatenate([w_query, w_key, w_value], axis=1)

    blocks = (2 * ctx_index, 3 - 2 * ctx_index, 2 - 2 * ctx_index)
    layouts = [positions(b, rows, bucket_lengths[0], true_lengths[0]) for b in blocks]
    tables = [rope_tables(layouts[i][2], head_dim) for i in both]
    key_layout = [jnp.concatenate([a, b]) for a, b in zip(layouts[2], layouts[1])]
    allowed = [allowed_pairs(layouts[0], layouts[0]), allowed_pairs(layouts[1], key_layout)]

    inputs16 = [tp_gather(part) for part in token_parts]
    cots16 = [tp_gather(part) for part in cot_parts]
    inputs = [values.astype(F32) for values in inputs16]
    normed16 = [rms_norm(values, g_in).astype(BF16) for values in inputs]
    raw = [jnp.dot(values, w_qkv, preferred_element_type=F32) for values in normed16]
    query_raw = [values[:, :head_dim] for values in raw]
    key_raw = [values[:, head_dim : 2 * head_dim] for values in raw]
    value16 = [values[:, 2 * head_dim :].astype(BF16) for values in raw]
    query16 = [rotate(rms_norm(query_raw[i], g_q), *tables[i]).astype(BF16) for i in both]
    key16 = [rotate(rms_norm(key_raw[i], g_k), *tables[i]).astype(BF16) for i in both]
    far_key, far_value = [
        lax.ppermute(values, "ctx", MESH_PAIR) for values in (key16[0], value16[0])
    ]
    keys = [key16[0], jnp.concatenate([far_key, key16[1]], axis=0)]
    values_ = [value16[0], jnp.concatenate([far_value, value16[1]], axis=0)]

    probs, attended16, attention, residual, mid16 = [], [], [], [], []
    hidden16, gate, up, ffn = [], [], [], []
    for i in both:
        p, a = attend(query16[i], keys[i], values_[i], allowed[i], score_scale)
        probs.append(p)
        attended16.append(a)
    for i in both:
        part = jnp.dot(attended16[i], w_out, preferred_element_type=F32).astype(BF16)
        attention.append(tp_sum(part).astype(F32))
        residual.append(inputs[i] + rms_norm(attention[i], g_pa))
        mid16.append(rms_norm(residual[i], g_pf).astype(BF16))
        gate.append(jnp.dot(mid16[i], w_gate, preferred_element_type=F32).astype(BF16))
        up.append(jnp.dot(mid16[i], w_up, preferred_element_type=F32).astype(BF16))
        hidden16.append(geglu(gate[i].astype(F32), up[i].astype(F32)).astype(BF16))
        part = jnp.dot(hidden16[i], w_down, preferred_element_type=F32).astype(BF16)
        ffn.append(tp_sum(part).astype(F32))

    out_parts, d_ffn16, d_gate16, d_up16 = [], [], [], []
    gain_sums = []
    cots = [values.astype(F32) for values in cots16]
    for i in both:
        outputs = residual[i] + rms_norm(ffn[i], g_pff)
        out_parts.append(
            lax.dynamic_slice_in_dim(outputs, tp_index * feature_cols, feature_cols, 1).astype(BF16)
        )
        d_ffn, d_pff = rms_back(ffn[i], g_pff, cots[i])
        d_ffn16.append(d_ffn.astype(BF16))
        d_hidden = contract(d_ffn16[i], w_down, 1, 1)
        gate32, up32 = gate[i].astype(F32), up[i].astype(F32)
        _, pull = jax.vjp(geglu, gate32, up32)
        d_gate, d_up = pull(d_hidden)
        d_gate16.append(d_gate.astype(BF16))
        d_up16.append(d_up.astype(BF16))
        gain_sums.append(d_pff)
    hidden_all, mid_all, d_ffn_all, d_gate_all, d_up_all = [
        jnp.concatenate(pair, axis=0) for pair in (hidden16, mid16, d_ffn16, d_gate16, d_up16)
    ]
    grad_down = contract(hidden_all, d_ffn_all, 0, 0).astype(BF16)
    grad_gate = contract(d_gate_all, mid_all, 0, 0).astype(BF16)
    grad_up = contract(d_up_all, mid_all, 0, 0).astype(BF16)

    d_resid, d_attn16, d_attended16 = [], [], []
    pf_sums, pa_sums = [], []
    for i in both:
        part = contract(d_gate16[i], w_gate, 1, 1) + contract(d_up16[i], w_up, 1, 1)
        d_mid = tp_sum(part.astype(BF16)).astype(F32)
        d_norm, d_pf = rms_back(residual[i], g_pf, d_mid)
        d_resid.append(cots[i] + d_norm)
        d_attn, d_pa = rms_back(attention[i], g_pa, d_resid[i])
        d_attn16.append(d_attn.astype(BF16))
        d_attended16.append(contract(d_attn16[i], w_out, 1, 1).astype(BF16))
        pf_sums.append(d_pf)
        pa_sums.append(d_pa)
    grad_out = contract(
        jnp.concatenate(attended16, axis=0), jnp.concatenate(d_attn16, axis=0), 0, 0
    ).astype(BF16)

    d_query, d_key, d_value = [], [], []
    for i in both:
        dq, dk, dv = attend_back(
            query16[i], keys[i], values_[i], probs[i], d_attended16[i], score_scale
        )
        d_query.append(dq)
        d_key.append(dk)
        d_value.append(dv)
    far_dk = lax.ppermute(d_key[1][:rows].astype(BF16), "ctx", MESH_PAIR)
    far_dv = lax.ppermute(d_value[1][:rows].astype(BF16), "ctx", MESH_PAIR)
    d_key = [d_key[0] + far_dk.astype(F32), d_key[1][rows:]]
    d_value = [d_value[0] + far_dv.astype(F32), d_value[1][rows:]]

    w_blocks = w_qkv.reshape(4, feature_cols, w_qkv.shape[1])
    w_near = [
        lax.dynamic_index_in_dim(w_blocks, tp_index ^ j, keepdims=False) for j in range(4)
    ]
    g_in_own = lax.dynamic_slice_in_dim(g_in, tp_index * feature_cols, feature_cols)
    d_qkv16, x_parts, q_sums, k_sums, in_sums = [], [], [], [], []
    for i in both:
        dq, d_gq = rms_back(query_raw[i], g_q, rotate_back(d_query[i], *tables[i]))
        dk, d_gk = rms_back(key_raw[i], g_k, rotate_back(d_key[i], *tables[i]))
        q_sums.append(d_gq)
        k_sums.append(d_gk)
        d_qkv16.append(jnp.concatenate([dq, dk, d_value[i]], axis=1).astype(BF16))
        parts = [contract(d_qkv16[i], w, 1, 1).astype(BF16) for w in w_near]
        near = lax.ppermute(jnp.stack([parts[1], parts[3]]), "tp", XOR1)
        mine = add16(parts[0], near[0])
        theirs = add16(parts[2], near[1])
        u = add16(mine, lax.ppermute(theirs, "tp", XOR2)).astype(F32)
        own_in = token_parts[i].astype(F32)
        weighted = g_in_own * u
        inner = jnp.sum(own_in * weighted, axis=-1)
        inner = inner + lax.ppermute(inner, "tp", XOR1)
        inner = inner + lax.ppermute(inner, "tp", XOR2)
        inner = inner[:, None] / (4 * feature_cols)
        scale = scale_of(inputs[i])
        d_in = scale * weighted - own_in * (scale * scale * scale * inner)
        resid_own = lax.dynamic_slice_in_dim(d_resid[i], tp_index * feature_cols, feature_cols, 1)
        x_parts.append((resid_own + d_in).astype(BF16))
        in_sums.append(jnp.sum(u * own_in * scale, axis=0))
    grad_qkv = contract(
        jnp.concatenate(d_qkv16, axis=0), jnp.concatenate(normed16, axis=0), 0, 0
    ).astype(BF16)
    grad_query = grad_qkv[:head_dim]
    kv_blocks = grad_qkv[head_dim:].reshape(4, head_dim // 2, -1)
    kv = [lax.dynamic_index_in_dim(kv_blocks, tp_index ^ j, keepdims=False) for j in range(4)]
    near = lax.ppermute(jnp.stack([kv[1], kv[3]]), "tp", XOR1)
    mine, theirs = add16(kv[0], near[0]), add16(kv[2], near[1])
    grad_kv = add16(mine, lax.ppermute(theirs, "tp", XOR2))
    grads = [grad_down, grad_gate, grad_up, grad_out, grad_query, grad_kv]
    sizes = [grad.shape[0] for grad in grads]
    spare = -sum(sizes) % 192
    grads.append(jnp.zeros((spare, grad_down.shape[1]), BF16))
    sums = grid_sum(jnp.concatenate(grads, axis=0))
    ends = [sum(sizes[: j + 1]) for j in range(6)]
    down_sum, gate_sum, up_sum, out_sum, query_sum, mine = [
        sums[end - size : end] for size, end in zip(sizes, ends)
    ]
    far = lax.ppermute(mine, "tp", XOR2)
    near = lax.ppermute(jnp.stack([mine, far]), "tp", XOR1)
    kv_all = (mine, near[0], far, near[1])
    kv_sum = jnp.concatenate(
        [lax.select_n(tp_index ^ j, *kv_all) for j in range(4)], axis=0
    ).astype(F32).T

    width = 4 * feature_cols
    in_full = lax.dynamic_update_slice_in_dim(
        jnp.zeros((width,), F32), in_sums[0] + in_sums[1], tp_index * feature_cols, 0
    )
    shared = [0.25 * (pair[0] + pair[1]) for pair in (pa_sums, pf_sums, gain_sums)]
    small = sum_all(
        jnp.concatenate([in_full, *shared, q_sums[0] + q_sums[1], k_sums[0] + k_sums[1]]).reshape(
            -1, 128
        )
    ).reshape(-1)
    gains = [small[j * width : (j + 1) * width] for j in range(4)]
    gain_q_sum = small[4 * width : 4 * width + head_dim]
    gain_k_sum = small[4 * width + head_dim :]
    return (
        join(*out_parts, ctx_index),
        join(*x_parts, ctx_index),
        query_sum.astype(F32).T,
        kv_sum[:, :head_dim],
        kv_sum[:, head_dim:],
        out_sum.astype(F32),
        gate_sum.astype(F32).T,
        up_sum.astype(F32).T,
        down_sum.astype(F32),
        gains[0],
        gains[1],
        gains[2],
        gains[3],
        gain_q_sum,
        gain_k_sum,
    )


def solution(mesh):
    def layer(*args):
        tokens, bucket_lengths = args[0], args[-2]
        sizes = mesh.shape
        group_rows = tokens.shape[0] // sizes["dp"]
        paired = (sizes["dp"], sizes["ctx"], sizes["tp"]) == (4, 2, 4) and (
            group_rows == 1024 * bucket_lengths.shape[1] == 2048
        )
        return mapped(paired_shards if paired else shards)(*args)

    def mapped(body):
        return jax.shard_map(
            body,
            mesh=mesh,
            in_specs=(
                P(("dp", "ctx"), "tp"),
                P(("dp", "ctx"), "tp"),
                P(None, "tp"),
                P(),
                P(),
                P("tp", None),
                P(None, "tp"),
                P(None, "tp"),
                P("tp", None),
                P(),
                P(),
                P(),
                P(),
                P(),
                P(),
                P("dp", None),
                P("dp", None),
            ),
            out_specs=(
                P(("dp", "ctx"), "tp"),
                P(("dp", "ctx"), "tp"),
                P(None, "tp"),
                P(),
                P(),
                P("tp", None),
                P(None, "tp"),
                P(None, "tp"),
                P("tp", None),
                P(),
                P(),
                P(),
                P(),
                P(),
                P(),
            ),
            check_vma=False,
        )

    return layer
```

```python
import math
from functools import partial

import jax
import jax.numpy as jnp
from jax import lax
from jax.experimental import pallas as pl
from jax.experimental.pallas import tpu as pltpu
from jax.sharding import PartitionSpec as P

QBLK = 512


EPSILON = 1e-06
ROPE_BASE = 1000000.0
MASKED = -1e30


def contract(left, right, left_dim, right_dim):
    return lax.dot_general(
        left, right, (((left_dim,), (right_dim,)), ((), ())), preferred_element_type=jnp.float32
    )


def rms_norm(values, gain):
    return values * lax.rsqrt(jnp.mean(values * values, axis=-1, keepdims=True) + EPSILON) * gain


def rotate(values, cosine_table, sine_table):
    half_dim = values.shape[-1] // 2
    turned = jnp.concatenate([-values[..., half_dim:], values[..., :half_dim]], axis=-1)
    return values * cosine_table + turned * sine_table


def rope_tables(seq_pos, head_dim):
    freq_index = jnp.arange(head_dim // 2, dtype=jnp.float32)
    inverse = ROPE_BASE ** (-2.0 * freq_index / head_dim)
    angles = seq_pos.astype(jnp.float32)[:, None] * inverse[None, :]
    angles = jnp.concatenate([angles, angles], axis=-1)
    return (jnp.cos(angles), jnp.sin(angles))


def stream_layout(bucket_row, true_row, tok_dev, n_ctx):
    group_rows = tok_dev * n_ctx
    half_shard = tok_dev // 2
    row_ids = jnp.arange(group_rows, dtype=jnp.int32)
    device = row_ids // tok_dev
    half_index = row_ids % tok_dev // half_shard
    block_ids = jnp.where(half_index == 0, device, 2 * n_ctx - 1 - device)
    stream_pos = block_ids * half_shard + row_ids % half_shard
    starts = jnp.cumsum(bucket_row) - bucket_row
    ends = starts + bucket_row
    inside = (
        (stream_pos[:, None] >= starts[None, :]) & (stream_pos[:, None] < ends[None, :])
    ).astype(jnp.int32)
    slot_ids = jnp.arange(bucket_row.shape[0], dtype=jnp.int32)
    seq_ids = jnp.sum(inside * slot_ids[None, :], axis=1)
    seq_pos = stream_pos - jnp.sum(inside * starts[None, :], axis=1)
    is_valid = (seq_pos < jnp.sum(inside * true_row[None, :], axis=1)).astype(jnp.int32)
    return (seq_ids, stream_pos, seq_pos, is_valid)


def shape_heads(query_raw, key_raw, gain_q, gain_k, cosine_table, sine_table):
    query_heads = query_raw.reshape(query_raw.shape[0], -1, key_raw.shape[1])
    query_rot = rotate(
        rms_norm(query_heads, gain_q), cosine_table[:, None, :], sine_table[:, None, :]
    )
    key_rot = rotate(rms_norm(key_raw, gain_k), cosine_table, sine_table)
    return (query_rot, key_rot)


def geglu(gate_in, up_in):
    return jax.nn.gelu(gate_in, approximate=True) * up_in


def shards(
    tokens,
    out_grad,
    w_query,
    w_key,
    w_value,
    w_out,
    w_gate,
    w_up,
    w_down,
    gain_in,
    gain_post_attn,
    gain_pre_ffn,
    gain_post_ffn,
    gain_query,
    gain_key,
    bucket_lengths,
    true_lengths,
):
    n_ctx = lax.axis_size("ctx")
    ctx_index = lax.axis_index("ctx")
    tp_index = lax.axis_index("tp")
    rows_dev = tokens.shape[0]
    feature_cols = tokens.shape[1]
    head_dim = w_key.shape[1]
    head_count = w_query.shape[1] // head_dim
    group_rows = rows_dev * n_ctx
    blocks = rows_dev // QBLK
    score_scale = head_dim ** (-0.5)
    gain_in32, gain_pa32, gain_pf32, gain_pff32, gain_q32, gain_k32 = [
        tensor.astype(jnp.float32)
        for tensor in (gain_in, gain_post_attn, gain_pre_ffn, gain_post_ffn, gain_query, gain_key)
    ]
    input_full, cot_full = (
        lax.all_gather(tokens, "tp", axis=1, tiled=True),
        lax.all_gather(out_grad, "tp", axis=1, tiled=True),
    )
    inputs = input_full.astype(jnp.float32)
    seq_all, spos_all, rpos_all, valid_all = stream_layout(
        bucket_lengths[0], true_lengths[0], rows_dev, n_ctx
    )
    first_row = ctx_index * rows_dev
    seq_local = lax.dynamic_slice_in_dim(seq_all, first_row, rows_dev)
    spos_local = lax.dynamic_slice_in_dim(spos_all, first_row, rows_dev)
    rpos_local = lax.dynamic_slice_in_dim(rpos_all, first_row, rows_dev)
    cosine_table, sine_table = rope_tables(rpos_local, head_dim)
    normed_in, pull_in = jax.vjp(rms_norm, inputs, gain_in32)
    normed_in16 = normed_in.astype(jnp.bfloat16)
    query_raw = jnp.dot(normed_in16, w_query, preferred_element_type=jnp.float32)
    key_raw = jnp.dot(normed_in16, w_key, preferred_element_type=jnp.float32)
    value_raw = jnp.dot(normed_in16, w_value, preferred_element_type=jnp.float32)
    (query_rot, key_rot), rope_pull = jax.vjp(
        partial(shape_heads, cosine_table=cosine_table, sine_table=sine_table),
        query_raw,
        key_raw,
        gain_q32,
        gain_k32,
    )
    query16 = query_rot.astype(jnp.bfloat16)
    key16 = key_rot.astype(jnp.bfloat16)
    value16 = value_raw.astype(jnp.bfloat16)
    key_group, value_group = (
        lax.all_gather(key16, "ctx", axis=0, tiled=True),
        lax.all_gather(value16, "ctx", axis=0, tiled=True),
    )

    def allowed_mask(seq_rows, spos_rows):
        return (
            (valid_all[None, :] == 1)
            & (seq_all[None, :] == seq_rows[:, None])
            & (spos_all[None, :] <= spos_rows[:, None])
        )

    query_blocks = query16.reshape(blocks, QBLK, head_count, head_dim)
    seq_blocks = seq_local.reshape(blocks, QBLK)
    spos_blocks = spos_local.reshape(blocks, QBLK)

    def forward_block(block_item):
        query_block, seq_rows, spos_rows = block_item
        scores = (
            jnp.einsum("qhd,kd->hqk", query_block, key_group, preferred_element_type=jnp.float32)
            * score_scale
        )
        scores = jnp.where(allowed_mask(seq_rows, spos_rows)[None], scores, MASKED)
        row_max = jnp.max(scores, axis=-1, keepdims=True)
        exp_scores = jnp.exp(scores - row_max)
        row_total = jnp.sum(exp_scores, axis=-1, keepdims=True)
        prob_rows = (exp_scores / row_total).astype(jnp.bfloat16)
        output = jnp.einsum(
            "hqk,kd->qhd", prob_rows, value_group, preferred_element_type=jnp.float32
        )
        return (output, (row_max + jnp.log(row_total))[..., 0])

    attended, log_norm = lax.map(forward_block, (query_blocks, seq_blocks, spos_blocks))
    attended16 = attended.reshape(rows_dev, head_count * head_dim).astype(jnp.bfloat16)
    attention = lax.psum(
        jnp.dot(attended16, w_out, preferred_element_type=jnp.float32).astype(jnp.bfloat16), "tp"
    ).astype(jnp.float32)
    post_attn, pull_post_attn = jax.vjp(rms_norm, attention, gain_pa32)
    residual = inputs + post_attn
    normed_mid, pull_pre_ffn = jax.vjp(rms_norm, residual, gain_pf32)
    mid16 = normed_mid.astype(jnp.bfloat16)
    gate_out = jnp.dot(mid16, w_gate, preferred_element_type=jnp.float32)
    up_out = jnp.dot(mid16, w_up, preferred_element_type=jnp.float32)
    hidden, pull_geglu = jax.vjp(geglu, gate_out, up_out)
    hidden16 = hidden.astype(jnp.bfloat16)
    ffn_branch = lax.psum(
        jnp.dot(hidden16, w_down, preferred_element_type=jnp.float32).astype(jnp.bfloat16), "tp"
    ).astype(jnp.float32)
    post_ffn, pull_post_ffn = jax.vjp(rms_norm, ffn_branch, gain_pff32)
    outputs = residual + post_ffn
    out_rows = lax.dynamic_slice_in_dim(outputs, tp_index * feature_cols, feature_cols, 1).astype(
        jnp.bfloat16
    )
    cotangent = cot_full.astype(jnp.float32)
    d_ffn, d_gain_post_ffn = pull_post_ffn(cotangent)
    d_ffn16 = d_ffn.astype(jnp.bfloat16)
    d_hidden = contract(d_ffn16, w_down, 1, 1)
    grad_down = contract(hidden16, d_ffn16, 0, 0)
    d_gate, d_up = pull_geglu(d_hidden)
    d_gate16 = d_gate.astype(jnp.bfloat16)
    d_up16 = d_up.astype(jnp.bfloat16)
    grad_gate = contract(mid16, d_gate16, 0, 0)
    grad_up = contract(mid16, d_up16, 0, 0)
    d_mid = lax.psum(
        (contract(d_gate16, w_gate, 1, 1) + contract(d_up16, w_up, 1, 1)).astype(jnp.bfloat16), "tp"
    ).astype(jnp.float32)
    d_res_norm, d_gain_pre_ffn = pull_pre_ffn(d_mid)
    d_resid = cotangent + d_res_norm
    d_attn, d_gain_post_attn = pull_post_attn(d_resid)
    d_attn16 = d_attn.astype(jnp.bfloat16)
    d_attended16 = contract(d_attn16, w_out, 1, 1).astype(jnp.bfloat16)
    grad_out = contract(attended16, d_attn16, 0, 0)
    key_back, value_back = (key_group, value_group)

    def backward_block(running, block_item):
        key_sum, value_sum = running
        query_block, dout_block, lse_block, seq_rows, spos_rows = block_item
        scores = (
            jnp.einsum("qhd,kd->hqk", query_block, key_back, preferred_element_type=jnp.float32)
            * score_scale
        )
        scores = jnp.where(allowed_mask(seq_rows, spos_rows)[None], scores, MASKED)
        prob_rows = jnp.exp(scores - lse_block[..., None])
        prob16 = prob_rows.astype(jnp.bfloat16)
        d_probs = jnp.einsum(
            "qhd,kd->hqk", dout_block, value_back, preferred_element_type=jnp.float32
        )
        row_inner = jnp.sum(prob_rows * d_probs, axis=-1, keepdims=True)
        d_scores16 = (prob_rows * (d_probs - row_inner)).astype(jnp.bfloat16)
        d_query = (
            jnp.einsum("hqk,kd->qhd", d_scores16, key_back, preferred_element_type=jnp.float32)
            * score_scale
        )
        key_sum = (
            key_sum
            + jnp.einsum("hqk,qhd->kd", d_scores16, query_block, preferred_element_type=jnp.float32)
            * score_scale
        )
        value_sum = value_sum + jnp.einsum(
            "hqk,qhd->kd", prob16, dout_block, preferred_element_type=jnp.float32
        )
        return ((key_sum, value_sum), d_query)

    zero_rows = jnp.zeros((group_rows, head_dim), jnp.float32)
    (key_sum, value_sum), d_query_blocks = lax.scan(
        backward_block,
        (zero_rows, zero_rows),
        (
            query_blocks,
            d_attended16.reshape(blocks, QBLK, head_count, head_dim),
            log_norm,
            seq_blocks,
            spos_blocks,
        ),
    )
    d_key_rot, d_value = (
        lax.psum_scatter(
            key_sum.astype(jnp.bfloat16), "ctx", scatter_dimension=0, tiled=True
        ).astype(jnp.float32),
        lax.psum_scatter(
            value_sum.astype(jnp.bfloat16), "ctx", scatter_dimension=0, tiled=True
        ).astype(jnp.float32),
    )
    d_query_raw, d_key_raw, d_gain_query, d_gain_key = rope_pull(
        (d_query_blocks.reshape(rows_dev, head_count, head_dim), d_key_rot)
    )
    d_query16 = d_query_raw.astype(jnp.bfloat16)
    d_key16 = d_key_raw.astype(jnp.bfloat16)
    d_value16 = d_value.astype(jnp.bfloat16)
    grad_query = contract(normed_in16, d_query16, 0, 0)
    grad_key = contract(normed_in16, d_key16, 0, 0)
    grad_value = contract(normed_in16, d_value16, 0, 0)
    d_normed_part = (
        contract(d_query16, w_query, 1, 1)
        + contract(d_key16, w_key, 1, 1)
        + contract(d_value16, w_value, 1, 1)
    )
    d_normed_in = lax.psum(d_normed_part.astype(jnp.bfloat16), "tp").astype(jnp.float32)
    d_in_norm, d_gain_in = pull_in(d_normed_in)
    d_inputs = d_resid + d_in_norm
    grad_rows = lax.dynamic_slice_in_dim(d_inputs, tp_index * feature_cols, feature_cols, 1).astype(
        jnp.bfloat16
    )
    sharded = (
        grad_query,
        grad_out,
        grad_gate,
        grad_up,
        grad_down,
        d_gain_in,
        d_gain_post_attn,
        d_gain_pre_ffn,
        d_gain_post_ffn,
    )
    reduced = (
        lax.psum_scatter(
            sharded[0].astype(jnp.bfloat16), ("dp", "ctx"), scatter_dimension=0, tiled=True
        ).astype(jnp.float32),
        lax.psum_scatter(
            sharded[1].astype(jnp.bfloat16), ("dp", "ctx"), scatter_dimension=1, tiled=True
        ).astype(jnp.float32),
        lax.psum_scatter(
            sharded[2].astype(jnp.bfloat16), ("dp", "ctx"), scatter_dimension=0, tiled=True
        ).astype(jnp.float32),
        lax.psum_scatter(
            sharded[3].astype(jnp.bfloat16), ("dp", "ctx"), scatter_dimension=0, tiled=True
        ).astype(jnp.float32),
        lax.psum_scatter(
            sharded[4].astype(jnp.bfloat16), ("dp", "ctx"), scatter_dimension=1, tiled=True
        ).astype(jnp.float32),
        lax.psum_scatter(
            sharded[5].astype(jnp.bfloat16), ("dp", "ctx"), scatter_dimension=0, tiled=True
        ).astype(jnp.float32),
        lax.psum_scatter(
            sharded[6].astype(jnp.bfloat16), ("dp", "ctx"), scatter_dimension=0, tiled=True
        ).astype(jnp.float32),
        lax.psum_scatter(
            sharded[7].astype(jnp.bfloat16), ("dp", "ctx"), scatter_dimension=0, tiled=True
        ).astype(jnp.float32),
        lax.psum_scatter(
            sharded[8].astype(jnp.bfloat16), ("dp", "ctx"), scatter_dimension=0, tiled=True
        ).astype(jnp.float32),
    )
    summed = (
        lax.all_gather(reduced[0].astype(jnp.bfloat16), ("dp", "ctx"), axis=0, tiled=True).astype(
            jnp.float32
        ),
        lax.all_gather(reduced[1].astype(jnp.bfloat16), ("dp", "ctx"), axis=1, tiled=True).astype(
            jnp.float32
        ),
        lax.all_gather(reduced[2].astype(jnp.bfloat16), ("dp", "ctx"), axis=0, tiled=True).astype(
            jnp.float32
        ),
        lax.all_gather(reduced[3].astype(jnp.bfloat16), ("dp", "ctx"), axis=0, tiled=True).astype(
            jnp.float32
        ),
        lax.all_gather(reduced[4].astype(jnp.bfloat16), ("dp", "ctx"), axis=1, tiled=True).astype(
            jnp.float32
        ),
        lax.all_gather(reduced[5].astype(jnp.bfloat16), ("dp", "ctx"), axis=0, tiled=True).astype(
            jnp.float32
        ),
        lax.all_gather(reduced[6].astype(jnp.bfloat16), ("dp", "ctx"), axis=0, tiled=True).astype(
            jnp.float32
        ),
        lax.all_gather(reduced[7].astype(jnp.bfloat16), ("dp", "ctx"), axis=0, tiled=True).astype(
            jnp.float32
        ),
        lax.all_gather(reduced[8].astype(jnp.bfloat16), ("dp", "ctx"), axis=0, tiled=True).astype(
            jnp.float32
        ),
    )
    shared = lax.psum((grad_key, grad_value, d_gain_query, d_gain_key), ("dp", "ctx", "tp"))
    return (
        out_rows,
        grad_rows,
        summed[0],
        shared[0],
        shared[1],
        summed[1],
        summed[2],
        summed[3],
        summed[4],
        summed[5],
        summed[6],
        summed[7],
        summed[8],
        shared[2],
        shared[3],
    )


MESH_PAIR = ((0, 1), (1, 0))
XOR1 = ((0, 1), (1, 0), (2, 3), (3, 2))
XOR2 = ((0, 2), (2, 0), (1, 3), (3, 1))
MESH = pl.DeviceIdType.MESH
GELU_SCALE = math.sqrt(2.0 / math.pi)
F32 = jnp.float32
BF16 = jnp.bfloat16


def add16(left, right):
    return (left.astype(F32) + right.astype(F32)).astype(BF16)


def halves(values, index):
    size = values.shape[0] // 2
    own = lax.dynamic_slice_in_dim(values, index * size, size)
    other = lax.dynamic_slice_in_dim(values, (1 - index) * size, size)
    return own, other


def join(own, other, index):
    first = jnp.where(index == 0, own, other)
    second = jnp.where(index == 0, other, own)
    return jnp.concatenate([first, second], axis=0)


def tp_sum(values):
    odd = lax.axis_index("tp") % 2
    own, other = halves(values, odd)
    own = add16(own, lax.ppermute(other, "tp", XOR1))
    own = add16(own, lax.ppermute(own, "tp", XOR2))
    return join(own, lax.ppermute(own, "tp", XOR1), odd)


def tp_gather(part):
    tp_index = lax.axis_index("tp")
    near = lax.ppermute(part, "tp", XOR1)
    far = lax.ppermute(part, "tp", XOR2)
    both = lax.ppermute(far, "tp", XOR1)
    blocks = (part, near, far, both)
    return jnp.concatenate(
        [lax.select_n(tp_index ^ j, *blocks) for j in range(4)], axis=1
    )


def sum_all(values):
    for axis, pairs in (
        ("tp", XOR1), ("tp", XOR2), ("ctx", MESH_PAIR), ("dp", XOR1), ("dp", XOR2)
    ):
        values = values + lax.ppermute(values, axis, pairs)
    return values


def grid_sum_kernel(s, K, L, g, out, Y2, Z2, M2, Z1, M1, Y1, *sems):
    sy2, sz2, sm2, sfo, sfy, sz1, sm1, sy1, sfm, sfa, sfb = sems[:11]
    ry2, rz2, rm2, rfo, rfy, rz1, rm1, ry1, rfm, rfa, rfb = sems[11:]
    dp, ctx, tp = lax.axis_index("dp"), lax.axis_index("ctx"), lax.axis_index("tp")
    upper = dp // 2
    outer = (dp == 0) | (dp == 3)
    inner = jnp.logical_not(outer)
    zn = jnp.where(dp < 2, 1 - dp, 5 - dp)
    zm = 3 - dp
    ypeer, zpeer, mpeer = (dp, 1 - ctx, tp), (zn, ctx, tp), (zm, ctx, tp)
    bar = pltpu.get_barrier_semaphore()
    pl.semaphore_signal(bar, inc=1, device_id=ypeer, device_id_type=MESH)
    pl.semaphore_signal(bar, inc=1, device_id=zpeer, device_id_type=MESH)
    pl.when(inner)(lambda: pl.semaphore_signal(bar, inc=1, device_id=mpeer, device_id_type=MESH))
    pl.semaphore_wait(bar, jnp.where(inner, 3, 2))
    base1 = 2 * s * K
    def rows2(k, h): return pl.ds(pl.multiple_of((2 * k + h) * s, s), s)
    def rows1(k, h): return pl.ds(pl.multiple_of(base1 + (2 * k + h) * s, s), s)
    def pair1(k): return pl.ds(pl.multiple_of(base1 + 2 * k * s, s), 2 * s)
    def slot(k, n=1): return pl.ds(pl.multiple_of(k * n * s, s), n * s)
    def half1(k, h): return pl.ds(pl.multiple_of((2 * k + h) * s, s), s)
    def cp(src, dst, ss, rs, k, dev):
        return pltpu.make_async_remote_copy(src_ref=src, dst_ref=dst, send_sem=ss.at[k], recv_sem=rs.at[k], device_id=dev, device_id_type=MESH)
    def c_y2(k): return cp(g.at[rows2(k, 1 - ctx)], Y2.at[slot(k)], sy2, ry2, k, ypeer)
    def c_z2(k): return cp(Y2.at[slot(k)], Z2.at[slot(k)], sz2, rz2, k, zpeer)
    def c_m2(k): return cp(Z2.at[slot(k)], M2.at[slot(k)], sm2, rm2, k, mpeer)
    def c_fo(k): return cp(out.at[rows2(k, ctx)], out.at[rows2(k, ctx)], sfo, rfo, k, zpeer)
    def c_fy(k): return cp(out.at[rows2(k, ctx)], out.at[rows2(k, ctx)], sfy, rfy, k, ypeer)
    def c_z1(k): return cp(g.at[pair1(k)], Z1.at[slot(k, 2)], sz1, rz1, k, zpeer)
    def c_m1(k): return cp(Z1.at[half1(k, 1 - upper)], M1.at[slot(k)], sm1, rm1, k, mpeer)
    def c_y1(k): return cp(M1.at[slot(k)], Y1.at[slot(k)], sy1, ry1, k, ypeer)
    def c_fm(k): return cp(out.at[rows1(k, upper)], out.at[rows1(k, upper)], sfm, rfm, k, mpeer)
    def c_fa(k): return cp(out.at[rows1(k, upper)], out.at[rows1(k, upper)], sfa, rfa, k, zpeer)
    def c_fb(k): return cp(out.at[rows1(k, 1 - upper)], out.at[rows1(k, 1 - upper)], sfb, rfb, k, zpeer)
    def add(a, b): return (a.astype(F32) + b.astype(F32)).astype(BF16)
    def at(t, lag, cond, fn):
        k = t - lag
        pl.when(cond & (k >= 0) & (k < K))(lambda: fn(k))
    yes = dp >= 0
    def a2(k):
        c_y2(k).start()
    def a1(k):
        c_z1(k).start()
    def b2(k):
        c_y2(k).wait_recv()
        Y2[slot(k)] = add(Y2[slot(k)], g[rows2(k, ctx)])
        pl.when(outer)(lambda: c_z2(k).start())
    def b1(k):
        c_z1(k).wait_recv()
        Z1[slot(k, 2)] = add(Z1[slot(k, 2)], g[pair1(k)])
        c_m1(k).start()
    def c2(k):
        c_z2(k).wait_recv()
        Z2[slot(k)] = add(Z2[slot(k)], Y2[slot(k)])
        c_m2(k).start()
    def c1(k):
        c_m1(k).wait_recv()
        M1[slot(k)] = add(M1[slot(k)], Z1[half1(k, upper)])
        c_y1(k).start()
    def d2(k):
        c_m2(k).wait_recv()
        out[rows2(k, ctx)] = add(M2[slot(k)], Z2[slot(k)])
        c_fo(k).start()
        c_fy(k).start()
    def d1(k):
        c_y1(k).wait_recv()
        out[rows1(k, upper)] = add(Y1[slot(k)], M1[slot(k)])
        c_fm(k).start()
        c_fa(k).start()
    def e2(k):
        c_fo(k).wait_recv()
        c_fy(k).start()
    def e1(k):
        c_fm(k).wait_recv()
        c_fb(k).start()
    def f2(k):
        c_fy(k).wait_recv()
        c_y2(k).wait_send()
        c_fy(k).wait_send()
    def f2o(k):
        c_z2(k).wait_send()
    def f2i(k):
        c_m2(k).wait_send()
        c_fo(k).wait_send()
    def f1o(k):
        c_fa(k).wait_recv()
        c_fb(k).wait_recv()
        c_z1(k).wait_send()
    def f1i(k):
        c_m1(k).wait_send()
        c_y1(k).wait_send()
        c_fm(k).wait_send()
        c_fa(k).wait_send()
        c_fb(k).wait_send()
    def body(t, carry):
        at(t, 5 * L, yes, f2)
        at(t, 5 * L, outer, f2o)
        at(t, 5 * L, inner, f2i)
        at(t, 5 * L, outer, f1o)
        at(t, 5 * L, inner, f1i)
        at(t, 4 * L, outer, e2)
        at(t, 4 * L, inner, e1)
        at(t, 3 * L, inner, d2)
        at(t, 3 * L, inner, d1)
        at(t, 2 * L, inner, c2)
        at(t, 2 * L, inner, c1)
        at(t, L, yes, b2)
        at(t, L, inner, b1)
        at(t, 0, yes, a2)
        at(t, 0, outer, a1)
        return carry
    lax.fori_loop(0, K + 5 * L, body, 0)

def grid_sum(grads):
    step_rows, lag = 48, 1
    rows, width = grads.shape
    steps = rows // (4 * step_rows)

    def slots(n):
        return pltpu.VMEM((n * step_rows * steps, width), BF16)

    return pl.pallas_call(
        partial(grid_sum_kernel, step_rows, steps, lag),
        out_shape=jax.ShapeDtypeStruct(grads.shape, BF16),
        in_specs=[pl.BlockSpec(memory_space=pltpu.VMEM)],
        out_specs=pl.BlockSpec(memory_space=pltpu.VMEM),
        scratch_shapes=[slots(n) for n in (1, 1, 1, 2, 1, 1)]
        + [pltpu.SemaphoreType.DMA((steps,)) for _ in range(22)],
        name="grid_sum",
        compiler_params=pltpu.CompilerParams(
            collective_id=1, has_side_effects=True, vmem_limit_bytes=62 << 20
        ),
    )(grads)


def scale_of(values):
    return lax.rsqrt(jnp.mean(values * values, axis=-1, keepdims=True) + EPSILON)


def rms_back(values, gain, cotangent):
    scale = scale_of(values)
    weighted = gain * cotangent
    inner = jnp.mean(values * weighted, axis=-1, keepdims=True)
    back = scale * weighted - values * (scale * scale * scale * inner)
    return back, jnp.sum(cotangent * values * scale, axis=0)


def rotate_back(values, cosine_table, sine_table):
    half_dim = values.shape[-1] // 2
    turned = values * sine_table
    turned = jnp.concatenate([turned[..., half_dim:], -turned[..., :half_dim]], axis=-1)
    return values * cosine_table + turned


def row_blocks(rows, size, body, carry=None):
    def step(i, state):
        return body(pl.ds(pl.multiple_of(i * size, size), size), state)

    return lax.fori_loop(0, rows // size, step, carry)


def turn_in(source, target, rows):
    for first in range(0, source.shape[0], 128):
        target[rows, first : first + 128] = source[first : first + 128, :].T


def column_tiles(total, size):
    return [(first, min(size, total - first)) for first in range(0, total, size)]


def dot_nn(left, right):
    return jnp.dot(left, right, preferred_element_type=F32)


def dot_nt(left, right):
    return contract(left, right, 1, 1)


def gelu_parts(gate):
    square = gate * gate
    tanh = jnp.tanh(GELU_SCALE * gate * (1.0 + 0.044715 * square))
    half = 0.5 + 0.5 * tanh
    slope = GELU_SCALE * (1.0 + 3.0 * 0.044715 * square)
    return gate * half, half + 0.5 * gate * (1.0 - tanh * tanh) * slope


def forward_kernel(
    real_length, tok, cot, w_q, w_k, w_v, w_o, w_g, w_u, w_d, gains, head_gains, cosines, sines,
    out_t, x16, cot16, n16, raw, q16, kv16, far_kv, att16, attn16, mid16, hid16, dffn16, dg16, du16,
    gain_sum,
    blocks, v_qkv, v_o, v_g, v_u, v_d, part, near, far, ffn16,
    load_sem, own_sem, g_send, g_recv, kv_send, kv_recv, s_send, s_recv,
):
    dp, ctx, tp = lax.axis_index("dp"), lax.axis_index("ctx"), lax.axis_index("tp")
    core_peer = (dp, ctx, tp + 1 - 2 * (tp % 2))
    x_index = (tp + 2) % 4
    x_peer = (dp, ctx, x_index)
    y_peer = (dp, 1 - ctx, tp)
    features, rows = tok.shape[0], tok.shape[1] // 2
    width = 4 * features
    hidden = w_d.shape[0]
    head_dim = w_k.shape[1]
    half = rows // 2
    odd = tp % 2

    loads = [
        pltpu.make_async_copy(source, target, load_sem.at[j])
        for j, (source, target) in enumerate(
            (
                (w_q, v_qkv.at[:, 0:head_dim]),
                (w_k, v_qkv.at[:, head_dim : 2 * head_dim]),
                (w_v, v_qkv.at[:, 2 * head_dim : 3 * head_dim]),
                (w_o, v_o), (w_g, v_g), (w_u, v_u), (w_d, v_d),
            )
        )
    ]
    for copy in loads:
        copy.start()

    def half_of(source, index):
        lane = (ctx if index % 2 == 0 else 1 - ctx) * rows
        return source.at[:, pl.ds(pl.multiple_of(lane, rows), rows)]

    def place(index, owner):
        return blocks.at[index, pl.ds(pl.multiple_of(owner * features, features), features)]

    sources = [half_of(tok, 0), half_of(tok, 1), half_of(cot, 0), half_of(cot, 1)]

    def remote(source, target, send, recv, peer):
        return pltpu.make_async_remote_copy(
            src_ref=source, dst_ref=target, send_sem=send, recv_sem=recv,
            device_id=peer, device_id_type=MESH,
        )

    own = [pltpu.make_async_copy(sources[j], place(j, tp), own_sem.at[j]) for j in range(4)]
    to_x = [
        remote(sources[j], place(j, tp), g_send.at[0, j], g_recv.at[0, j], x_peer) for j in range(4)
    ]
    to_core = [
        remote(sources[j], place(j, tp), g_send.at[1, j], g_recv.at[1, j], core_peer)
        for j in range(4)
    ]
    onward = [
        remote(place(j, x_index), place(j, x_index), g_send.at[2, j], g_recv.at[2, j], core_peer)
        for j in range(4)
    ]
    for copy in own:
        copy.start()
    barrier = pltpu.get_barrier_semaphore()
    for peer in (core_peer, x_peer, y_peer):
        pl.semaphore_signal(barrier, inc=1, device_id=peer, device_id_type=MESH)
    pl.semaphore_wait(barrier, 3)

    for j in range(4):
        to_core[j].start()
    to_x[0].start()
    to_x[1].start()

    def pass_on(j):
        to_x[j].wait_recv()
        onward[j].start()

    def gathered(j):
        own[j].wait()
        to_core[j].wait_recv()
        onward[j].wait_recv()

    def chunk(c):
        return pl.ds(c * rows, rows)

    def project(c):
        turn_in(blocks.at[c], x16, chunk(c))

        def norm(block, _):
            at = pl.ds(c * rows + block.start, block.size)
            values = x16[at, :].astype(F32)
            n16[at, :] = (values * scale_of(values) * gains[0:1, :]).astype(BF16)

        row_blocks(rows, 32, norm)
        for first in range(0, rows, half):
            at = pl.ds(c * rows + first, half)
            tables = pl.ds(c * rows + first, half)
            values = dot_nn(n16[at, :], v_qkv[...])
            raw[at, :] = values[:, : 2 * head_dim]
            cosine, sine = cosines[tables, :], sines[tables, :]
            for j, target in ((0, q16.at[at, :]), (1, kv16.at[at, 0:head_dim])):
                head = values[:, j * head_dim : (j + 1) * head_dim]
                head = head * scale_of(head) * head_gains[j : j + 1, :]
                low, high = head[:, : head_dim // 2], head[:, head_dim // 2 :]
                target[:, : head_dim // 2] = (low * cosine - high * sine).astype(BF16)
                target[:, head_dim // 2 :] = (high * cosine + low * sine).astype(BF16)
            kv16[at, head_dim:] = values[:, 2 * head_dim :].astype(BF16)

    score_scale = head_dim ** (-0.5)

    def attend_rows(c):
        for first in range(0, rows, half):
            at = pl.ds(c * rows + first, half)
            query = q16[at, :]
            row_id = first + lax.broadcasted_iota(jnp.int32, (half, rows), 0)
            key_id = lax.broadcasted_iota(jnp.int32, (half, rows), 1)
            allowed = key_id <= row_id
            if c == 1:
                allowed = allowed & (rows + key_id < real_length[0, 0])
            keys = [(kv16[chunk(c), :head_dim], kv16[chunk(c), head_dim:], allowed)]
            if c == 1:
                keys.append((far_kv[:, :head_dim], far_kv[:, head_dim:], None))
            scores = []
            for key, _, mask in keys:
                score = dot_nt(query, key) * score_scale
                scores.append(score if mask is None else jnp.where(mask, score, MASKED))
            most = scores[0].max(axis=1, keepdims=True)
            for score in scores[1:]:
                most = jnp.maximum(most, score.max(axis=1, keepdims=True))
            exps = [jnp.exp(score - most) for score in scores]
            total = sum(e.sum(axis=1, keepdims=True) for e in exps)
            out = sum(dot_nn((e / total).astype(BF16), k[1]) for e, k in zip(exps, keys))
            att16[at, :] = out.astype(BF16)
        part[c] = dot_nn(att16[chunk(c), :], v_o[...]).astype(BF16)

    def rows_of(index):
        return pl.ds(pl.multiple_of(index * half, half), half)

    def sum_copies(s, target):
        start = pl.multiple_of((s % 2) * rows + odd * half, half)
        final = target.at[pl.ds(start, half)]
        return (
            remote(part.at[s, rows_of(1 - odd)], near.at[s], s_send.at[0, s], s_recv.at[0, s], core_peer),
            remote(near.at[s], far.at[s], s_send.at[1, s], s_recv.at[1, s], x_peer),
            remote(final, final, s_send.at[2, s], s_recv.at[2, s], core_peer),
        )

    def sum_start(s, target):
        sum_copies(s, target)[0].start()

    def sum_cross(s, target):
        copies = sum_copies(s, target)
        copies[0].wait_recv()
        near[s] = add16(part[s, rows_of(odd)], near[s])
        copies[1].start()

    def sum_back(s, target):
        copies = sum_copies(s, target)
        copies[1].wait_recv()
        start = pl.multiple_of((s % 2) * rows + odd * half, half)
        target[pl.ds(start, half), :] = add16(near[s], far[s])
        copies[2].start()
        copies[2].wait_recv()

    def residual(at):
        branch = attn16[at, :].astype(F32)
        return x16[at, :].astype(F32) + branch * scale_of(branch) * gains[1:2, :]

    def middle(c):
        def body(block, _):
            at = pl.ds(c * rows + block.start, block.size)
            values = residual(at)
            mid16[at, :] = (values * scale_of(values) * gains[2:3, :]).astype(BF16)

        row_blocks(rows, 32, body)

    def feed(c):
        for first, size in column_tiles(hidden, 256):
            for low in range(0, rows, half):
                at = pl.ds(c * rows + low, half)
                cols = pl.ds(first, size)
                gate = dot_nt(mid16[at, :], v_g[cols, :])
                up = dot_nt(mid16[at, :], v_u[cols, :])
                act, slope = gelu_parts(gate)
                hid16[at, cols] = (act * up).astype(BF16)
                dg16[at, cols] = (slope * up).astype(BF16)
                du16[at, cols] = act.astype(BF16)
        for first, size in column_tiles(width, 256):
            cols = pl.ds(first, size)
            part[2 + c, :, cols] = dot_nn(hid16[chunk(c), :], v_d[:, cols]).astype(BF16)

    def finish(c):
        turn_in(blocks.at[2 + c], cot16, chunk(c))
        sum_copies(c, attn16)[0].wait_send()
        onward[c].wait_send()

        def body(block, total):
            at = pl.ds(c * rows + block.start, block.size)
            branch = ffn16[at, :].astype(F32)
            scale = scale_of(branch)
            unit = branch * scale
            grad = cot16[at, :].astype(F32)
            part[c, block, :] = (residual(at) + unit * gains[3:4, :]).astype(BF16)
            weighted = grad * gains[3:4, :]
            inner = jnp.mean(unit * weighted, axis=-1, keepdims=True)
            dffn16[at, :] = (scale * (weighted - unit * inner)).astype(BF16)
            return total + (grad * unit).reshape(-1, 8, width).sum(axis=0)

        total = row_blocks(rows, 32, body, jnp.zeros((8, width), F32))
        if c == 0:
            gain_sum[...] = total
        else:
            gain_sum[...] += total
        for first in range(0, width, 128):
            blocks[c, first : first + 128, :] = part[c, :, first : first + 128].T
        lane = (ctx if c == 0 else 1 - ctx) * rows
        mine = blocks[c, pl.ds(pl.multiple_of(tp * features, features), features), :]
        out_t[:, pl.ds(pl.multiple_of(lane, rows), rows)] = mine

    def feed_back(c):
        for first, size in column_tiles(hidden, 256):
            for low in range(0, rows, half):
                at = pl.ds(c * rows + low, half)
                cols = pl.ds(first, size)
                d_hidden = dot_nt(dffn16[at, :], v_d[cols, :])
                dg16[at, cols] = (d_hidden * dg16[at, cols].astype(F32)).astype(BF16)
                du16[at, cols] = (d_hidden * du16[at, cols].astype(F32)).astype(BF16)

    kv_copy = remote(kv16.at[chunk(0)], far_kv, kv_send.at[0], kv_recv.at[0], y_peer)
    pass_on(0)
    for copy in loads[:3]:
        copy.wait()
    gathered(0)
    project(0)
    kv_copy.start()
    pass_on(1)
    to_x[2].start()
    to_x[3].start()
    loads[3].wait()
    attend_rows(0)
    sum_start(0, attn16)
    gathered(1)
    project(1)
    sum_cross(0, attn16)
    kv_copy.wait_recv()
    attend_rows(1)
    sum_start(1, attn16)
    pass_on(2)
    pass_on(3)
    sum_cross(1, attn16)
    sum_back(0, attn16)
    for copy in loads[4:]:
        copy.wait()
    middle(0)
    feed(0)
    sum_start(2, ffn16)
    sum_back(1, attn16)
    middle(1)
    sum_cross(2, ffn16)
    feed(1)
    sum_start(3, ffn16)
    gathered(2)
    gathered(3)
    sum_back(2, ffn16)
    sum_cross(3, ffn16)
    finish(0)
    feed_back(0)
    sum_back(3, ffn16)
    finish(1)
    feed_back(1)
    for group in (to_x, to_core, onward[2:], [kv_copy]):
        for copy in group:
            copy.wait_send()
    for s, target in ((0, attn16), (1, attn16), (2, ffn16), (3, ffn16)):
        for copy in sum_copies(s, target)[1 if s < 2 else 0 :]:
            copy.wait_send()


def forward(real_length, tok_t, cot_t, weights, gains, head_gains, cosines, sines):
    features, rows = tok_t.shape
    half = rows // 2
    width = 4 * features
    hidden = weights[-1].shape[0]
    head_dim = weights[1].shape[1]
    whole = pl.BlockSpec(memory_space=pltpu.VMEM)
    there = pl.BlockSpec(memory_space=pl.ANY)

    def low(*shape):
        return jax.ShapeDtypeStruct(shape, BF16)

    return pl.pallas_call(
        forward_kernel,
        out_shape=(
            low(features, rows), low(rows, width), low(rows, width), low(rows, width),
            jax.ShapeDtypeStruct((rows, 2 * head_dim), F32), low(rows, head_dim),
            low(rows, 2 * head_dim), low(half, 2 * head_dim), low(rows, head_dim),
            low(rows, width), low(rows, width), low(rows, hidden), low(rows, width),
            low(rows, hidden), low(rows, hidden), jax.ShapeDtypeStruct((8, width), F32),
        ),
        in_specs=[pl.BlockSpec(memory_space=pltpu.SMEM)] + [there] * 9 + [whole] * 4,
        out_specs=[whole] * 16,
        scratch_shapes=[
            pltpu.VMEM((4, width, half), BF16),
            pltpu.VMEM((width, 3 * head_dim), BF16),
            pltpu.VMEM((head_dim, width), BF16),
            pltpu.VMEM((hidden, width), BF16),
            pltpu.VMEM((hidden, width), BF16),
            pltpu.VMEM((hidden, width), BF16),
            pltpu.VMEM((4, half, width), BF16),
            pltpu.VMEM((4, half // 2, width), BF16),
            pltpu.VMEM((4, half // 2, width), BF16),
            pltpu.VMEM((rows, width), BF16),
            pltpu.SemaphoreType.DMA((7,)),
            pltpu.SemaphoreType.DMA((4,)),
            pltpu.SemaphoreType.DMA((3, 4)),
            pltpu.SemaphoreType.DMA((3, 4)),
            pltpu.SemaphoreType.DMA((1,)),
            pltpu.SemaphoreType.DMA((1,)),
            pltpu.SemaphoreType.DMA((3, 4)),
            pltpu.SemaphoreType.DMA((3, 4)),
        ],
        name="forward",
        compiler_params=pltpu.CompilerParams(
            collective_id=2, has_side_effects=True, vmem_limit_bytes=63 << 20
        ),
    )(real_length, tok_t, cot_t, *weights, gains, head_gains, cosines, sines)


def positions(block, rows, bucket_row, true_row):
    stream_pos = block * rows + jnp.arange(rows, dtype=jnp.int32)
    starts = jnp.cumsum(bucket_row) - bucket_row
    ends = starts + bucket_row
    inside = (
        (stream_pos[:, None] >= starts[None, :]) & (stream_pos[:, None] < ends[None, :])
    ).astype(jnp.int32)
    slot_ids = jnp.arange(bucket_row.shape[0], dtype=jnp.int32)
    seq_id = jnp.sum(inside * slot_ids[None, :], axis=1)
    seq_pos = stream_pos - jnp.sum(inside * starts[None, :], axis=1)
    is_valid = (seq_pos < jnp.sum(inside * true_row[None, :], axis=1)).astype(jnp.int32)
    return seq_id, stream_pos, seq_pos, is_valid


def allowed_pairs(query_layout, key_layout):
    return (
        (key_layout[3][None, :] == 1)
        & (key_layout[0][None, :] == query_layout[0][:, None])
        & (key_layout[1][None, :] <= query_layout[1][:, None])
    )


def attend(query16, key16, value16, allowed, score_scale):
    scores = contract(query16, key16, 1, 1) * score_scale
    scores = jnp.where(allowed, scores, MASKED)
    exp_scores = jnp.exp(scores - jnp.max(scores, axis=-1, keepdims=True))
    probs = exp_scores / jnp.sum(exp_scores, axis=-1, keepdims=True)
    attended = jnp.dot(probs.astype(BF16), value16, preferred_element_type=F32)
    return probs, attended.astype(BF16)


def attend_back(query16, key16, value16, probs, d_attended16, score_scale):
    d_probs = contract(d_attended16, value16, 1, 1)
    inner = jnp.sum(probs * d_probs, axis=-1, keepdims=True)
    d_scores16 = (probs * (d_probs - inner)).astype(BF16)
    d_query = jnp.dot(d_scores16, key16, preferred_element_type=F32) * score_scale
    d_key = contract(d_scores16, query16, 0, 0) * score_scale
    d_value = contract(probs.astype(BF16), d_attended16, 0, 0)
    return d_query, d_key, d_value


def paired_shards(
    tokens,
    out_grad,
    w_query,
    w_key,
    w_value,
    w_out,
    w_gate,
    w_up,
    w_down,
    gain_in,
    gain_post_attn,
    gain_pre_ffn,
    gain_post_ffn,
    gain_query,
    gain_key,
    bucket_lengths,
    true_lengths,
):
    ctx_index, tp_index = lax.axis_index("ctx"), lax.axis_index("tp")
    rows = tokens.shape[0] // 2
    feature_cols = tokens.shape[1]
    head_dim = w_key.shape[1]
    score_scale = head_dim ** (-0.5)
    g_in, g_pa, g_pf, g_pff, g_q, g_k = [
        gain.astype(F32)
        for gain in (gain_in, gain_post_attn, gain_pre_ffn, gain_post_ffn, gain_query, gain_key)
    ]
    both = range(2)
    width = 4 * feature_cols
    seq_pos = jnp.arange(2 * rows, dtype=jnp.int32)
    cosines, sines = [table[:, : head_dim // 2] for table in rope_tables(seq_pos, head_dim)]
    real_length = lax.dynamic_slice_in_dim(true_lengths, 1 - ctx_index, 1, 1)
    gains = jnp.stack([g_in, g_pa, g_pf, g_pff])
    head_gains = jnp.stack([g_q, g_k])
    weights = (w_query, w_key, w_value, w_out, w_gate.T, w_up.T, w_down)
    (
        out_t, x16, cot16, n16, raw, q16, kv16, far_kv, att16, attn16, mid16, hid16, dffn16, dg16,
        du16, gain_sum,
    ) = forward(
        real_length, tokens.T, out_grad.T, weights, gains, head_gains, cosines, sines
    )

    def two(values):
        return [values[:rows], values[rows:]]

    inputs16, cots16, normed16 = two(x16), two(cot16), two(n16)
    inputs = [values.astype(F32) for values in inputs16]
    cots = [values.astype(F32) for values in cots16]
    query_raw, key_raw = two(raw[:, :head_dim]), two(raw[:, head_dim:])
    query16, key16, value16 = two(q16), two(kv16[:, :head_dim]), two(kv16[:, head_dim:])
    keys = [key16[0], jnp.concatenate([far_kv[:, :head_dim], key16[1]], axis=0)]
    values_ = [value16[0], jnp.concatenate([far_kv[:, head_dim:], value16[1]], axis=0)]
    ids = jnp.arange(rows, dtype=jnp.int32)
    causal = ids[None, :] <= ids[:, None]
    real = causal & (rows + ids[None, :] < real_length[0, 0])
    allowed = [causal, jnp.concatenate([jnp.ones_like(real), real], axis=1)]
    probs = [
        attend(query16[i], keys[i], values_[i], allowed[i], score_scale)[0] for i in both
    ]
    attended16 = two(att16)
    attention = [values.astype(F32) for values in two(attn16)]
    residual = [inputs[i] + rms_norm(attention[i], g_pa) for i in both]
    d_gate16, d_up16 = two(dg16), two(du16)
    tables = [
        [jnp.concatenate([t, t], axis=1) for t in (cosines[at], sines[at])]
        for at in (slice(0, rows), slice(rows, 2 * rows))
    ]
    gain_sums = [jnp.sum(gain_sum, axis=0), 0.0]
    token_parts = halves(tokens, ctx_index)

    grad_down = contract(hid16, dffn16, 0, 0).astype(BF16)
    grad_gate = contract(dg16, mid16, 0, 0).astype(BF16)
    grad_up = contract(du16, mid16, 0, 0).astype(BF16)

    d_resid, d_attn16, d_attended16 = [], [], []
    pf_sums, pa_sums = [], []
    for i in both:
        part = contract(d_gate16[i], w_gate, 1, 1) + contract(d_up16[i], w_up, 1, 1)
        d_mid = tp_sum(part.astype(BF16)).astype(F32)
        d_norm, d_pf = rms_back(residual[i], g_pf, d_mid)
        d_resid.append(cots[i] + d_norm)
        d_attn, d_pa = rms_back(attention[i], g_pa, d_resid[i])
        d_attn16.append(d_attn.astype(BF16))
        d_attended16.append(contract(d_attn16[i], w_out, 1, 1).astype(BF16))
        pf_sums.append(d_pf)
        pa_sums.append(d_pa)
    grad_out = contract(
        att16, jnp.concatenate(d_attn16, axis=0), 0, 0
    ).astype(BF16)

    d_query, d_key, d_value = [], [], []
    for i in both:
        dq, dk, dv = attend_back(
            query16[i], keys[i], values_[i], probs[i], d_attended16[i], score_scale
        )
        d_query.append(dq)
        d_key.append(dk)
        d_value.append(dv)
    far_dk = lax.ppermute(d_key[1][:rows].astype(BF16), "ctx", MESH_PAIR)
    far_dv = lax.ppermute(d_value[1][:rows].astype(BF16), "ctx", MESH_PAIR)
    d_key = [d_key[0] + far_dk.astype(F32), d_key[1][rows:]]
    d_value = [d_value[0] + far_dv.astype(F32), d_value[1][rows:]]

    w_qkv = jnp.concatenate([w_query, w_key, w_value], axis=1)
    w_blocks = w_qkv.reshape(4, feature_cols, w_qkv.shape[1])
    w_near = [
        lax.dynamic_index_in_dim(w_blocks, tp_index ^ j, keepdims=False) for j in range(4)
    ]
    g_in_own = lax.dynamic_slice_in_dim(g_in, tp_index * feature_cols, feature_cols)
    d_qkv16, x_parts, q_sums, k_sums, in_sums = [], [], [], [], []
    for i in both:
        dq, d_gq = rms_back(query_raw[i], g_q, rotate_back(d_query[i], *tables[i]))
        dk, d_gk = rms_back(key_raw[i], g_k, rotate_back(d_key[i], *tables[i]))
        q_sums.append(d_gq)
        k_sums.append(d_gk)
        d_qkv16.append(jnp.concatenate([dq, dk, d_value[i]], axis=1).astype(BF16))
        parts = [contract(d_qkv16[i], w, 1, 1).astype(BF16) for w in w_near]
        near = lax.ppermute(jnp.stack([parts[1], parts[3]]), "tp", XOR1)
        mine = add16(parts[0], near[0])
        theirs = add16(parts[2], near[1])
        u = add16(mine, lax.ppermute(theirs, "tp", XOR2)).astype(F32)
        own_in = token_parts[i].astype(F32)
        weighted = g_in_own * u
        inner = jnp.sum(own_in * weighted, axis=-1)
        inner = inner + lax.ppermute(inner, "tp", XOR1)
        inner = inner + lax.ppermute(inner, "tp", XOR2)
        inner = inner[:, None] / (4 * feature_cols)
        scale = scale_of(inputs[i])
        d_in = scale * weighted - own_in * (scale * scale * scale * inner)
        resid_own = lax.dynamic_slice_in_dim(d_resid[i], tp_index * feature_cols, feature_cols, 1)
        x_parts.append((resid_own + d_in).astype(BF16))
        in_sums.append(jnp.sum(u * own_in * scale, axis=0))
    grad_qkv = contract(
        jnp.concatenate(d_qkv16, axis=0), n16, 0, 0
    ).astype(BF16)
    grad_query = grad_qkv[:head_dim]
    kv_blocks = grad_qkv[head_dim:].reshape(4, head_dim // 2, -1)
    kv = [lax.dynamic_index_in_dim(kv_blocks, tp_index ^ j, keepdims=False) for j in range(4)]
    near = lax.ppermute(jnp.stack([kv[1], kv[3]]), "tp", XOR1)
    mine, theirs = add16(kv[0], near[0]), add16(kv[2], near[1])
    grad_kv = add16(mine, lax.ppermute(theirs, "tp", XOR2))
    grads = [grad_down, grad_gate, grad_up, grad_out, grad_query, grad_kv]
    sizes = [grad.shape[0] for grad in grads]
    spare = -sum(sizes) % 192
    grads.append(jnp.zeros((spare, grad_down.shape[1]), BF16))
    sums = grid_sum(jnp.concatenate(grads, axis=0))
    ends = [sum(sizes[: j + 1]) for j in range(6)]
    down_sum, gate_sum, up_sum, out_sum, query_sum, mine = [
        sums[end - size : end] for size, end in zip(sizes, ends)
    ]
    far = lax.ppermute(mine, "tp", XOR2)
    near = lax.ppermute(jnp.stack([mine, far]), "tp", XOR1)
    kv_all = (mine, near[0], far, near[1])
    kv_sum = jnp.concatenate(
        [lax.select_n(tp_index ^ j, *kv_all) for j in range(4)], axis=0
    ).astype(F32).T

    in_full = lax.dynamic_update_slice_in_dim(
        jnp.zeros((width,), F32), in_sums[0] + in_sums[1], tp_index * feature_cols, 0
    )
    shared = [0.25 * (pair[0] + pair[1]) for pair in (pa_sums, pf_sums, gain_sums)]
    small = sum_all(
        jnp.concatenate([in_full, *shared, q_sums[0] + q_sums[1], k_sums[0] + k_sums[1]]).reshape(
            -1, 128
        )
    ).reshape(-1)
    gains = [small[j * width : (j + 1) * width] for j in range(4)]
    gain_q_sum = small[4 * width : 4 * width + head_dim]
    gain_k_sum = small[4 * width + head_dim :]
    return (
        out_t.T,
        join(*x_parts, ctx_index),
        query_sum.astype(F32).T,
        kv_sum[:, :head_dim],
        kv_sum[:, head_dim:],
        out_sum.astype(F32),
        gate_sum.astype(F32).T,
        up_sum.astype(F32).T,
        down_sum.astype(F32),
        gains[0],
        gains[1],
        gains[2],
        gains[3],
        gain_q_sum,
        gain_k_sum,
    )


def solution(mesh):
    def layer(*args):
        tokens, bucket_lengths = args[0], args[-2]
        sizes = mesh.shape
        group_rows = tokens.shape[0] // sizes["dp"]
        paired = (sizes["dp"], sizes["ctx"], sizes["tp"]) == (4, 2, 4) and (
            group_rows == 1024 * bucket_lengths.shape[1] == 2048
        )
        return mapped(paired_shards if paired else shards)(*args)

    def mapped(body):
        return jax.shard_map(
            body,
            mesh=mesh,
            in_specs=(
                P(("dp", "ctx"), "tp"),
                P(("dp", "ctx"), "tp"),
                P(None, "tp"),
                P(),
                P(),
                P("tp", None),
                P(None, "tp"),
                P(None, "tp"),
                P("tp", None),
                P(),
                P(),
                P(),
                P(),
                P(),
                P(),
                P("dp", None),
                P("dp", None),
            ),
            out_specs=(
                P(("dp", "ctx"), "tp"),
                P(("dp", "ctx"), "tp"),
                P(None, "tp"),
                P(),
                P(),
                P("tp", None),
                P(None, "tp"),
                P(None, "tp"),
                P("tp", None),
                P(),
                P(),
                P(),
                P(),
                P(),
                P(),
            ),
            check_vma=False,
        )

    return layer
```

```python
import math
from functools import partial

import jax
import jax.numpy as jnp
from jax import lax
from jax.experimental import pallas as pl
from jax.experimental.pallas import tpu as pltpu
from jax.sharding import PartitionSpec as P

QBLK = 512


EPSILON = 1e-06
ROPE_BASE = 1000000.0
MASKED = -1e30


def contract(left, right, left_dim, right_dim):
    return lax.dot_general(
        left, right, (((left_dim,), (right_dim,)), ((), ())), preferred_element_type=jnp.float32
    )


def rms_norm(values, gain):
    return values * lax.rsqrt(jnp.mean(values * values, axis=-1, keepdims=True) + EPSILON) * gain


def rotate(values, cosine_table, sine_table):
    half_dim = values.shape[-1] // 2
    turned = jnp.concatenate([-values[..., half_dim:], values[..., :half_dim]], axis=-1)
    return values * cosine_table + turned * sine_table


def rope_tables(seq_pos, head_dim):
    freq_index = jnp.arange(head_dim // 2, dtype=jnp.float32)
    inverse = ROPE_BASE ** (-2.0 * freq_index / head_dim)
    angles = seq_pos.astype(jnp.float32)[:, None] * inverse[None, :]
    angles = jnp.concatenate([angles, angles], axis=-1)
    return (jnp.cos(angles), jnp.sin(angles))


def stream_layout(bucket_row, true_row, tok_dev, n_ctx):
    group_rows = tok_dev * n_ctx
    half_shard = tok_dev // 2
    row_ids = jnp.arange(group_rows, dtype=jnp.int32)
    device = row_ids // tok_dev
    half_index = row_ids % tok_dev // half_shard
    block_ids = jnp.where(half_index == 0, device, 2 * n_ctx - 1 - device)
    stream_pos = block_ids * half_shard + row_ids % half_shard
    starts = jnp.cumsum(bucket_row) - bucket_row
    ends = starts + bucket_row
    inside = (
        (stream_pos[:, None] >= starts[None, :]) & (stream_pos[:, None] < ends[None, :])
    ).astype(jnp.int32)
    slot_ids = jnp.arange(bucket_row.shape[0], dtype=jnp.int32)
    seq_ids = jnp.sum(inside * slot_ids[None, :], axis=1)
    seq_pos = stream_pos - jnp.sum(inside * starts[None, :], axis=1)
    is_valid = (seq_pos < jnp.sum(inside * true_row[None, :], axis=1)).astype(jnp.int32)
    return (seq_ids, stream_pos, seq_pos, is_valid)


def shape_heads(query_raw, key_raw, gain_q, gain_k, cosine_table, sine_table):
    query_heads = query_raw.reshape(query_raw.shape[0], -1, key_raw.shape[1])
    query_rot = rotate(
        rms_norm(query_heads, gain_q), cosine_table[:, None, :], sine_table[:, None, :]
    )
    key_rot = rotate(rms_norm(key_raw, gain_k), cosine_table, sine_table)
    return (query_rot, key_rot)


def geglu(gate_in, up_in):
    return jax.nn.gelu(gate_in, approximate=True) * up_in


def shards(
    tokens,
    out_grad,
    w_query,
    w_key,
    w_value,
    w_out,
    w_gate,
    w_up,
    w_down,
    gain_in,
    gain_post_attn,
    gain_pre_ffn,
    gain_post_ffn,
    gain_query,
    gain_key,
    bucket_lengths,
    true_lengths,
):
    n_ctx = lax.axis_size("ctx")
    ctx_index = lax.axis_index("ctx")
    tp_index = lax.axis_index("tp")
    rows_dev = tokens.shape[0]
    feature_cols = tokens.shape[1]
    head_dim = w_key.shape[1]
    head_count = w_query.shape[1] // head_dim
    group_rows = rows_dev * n_ctx
    blocks = rows_dev // QBLK
    score_scale = head_dim ** (-0.5)
    gain_in32, gain_pa32, gain_pf32, gain_pff32, gain_q32, gain_k32 = [
        tensor.astype(jnp.float32)
        for tensor in (gain_in, gain_post_attn, gain_pre_ffn, gain_post_ffn, gain_query, gain_key)
    ]
    input_full, cot_full = (
        lax.all_gather(tokens, "tp", axis=1, tiled=True),
        lax.all_gather(out_grad, "tp", axis=1, tiled=True),
    )
    inputs = input_full.astype(jnp.float32)
    seq_all, spos_all, rpos_all, valid_all = stream_layout(
        bucket_lengths[0], true_lengths[0], rows_dev, n_ctx
    )
    first_row = ctx_index * rows_dev
    seq_local = lax.dynamic_slice_in_dim(seq_all, first_row, rows_dev)
    spos_local = lax.dynamic_slice_in_dim(spos_all, first_row, rows_dev)
    rpos_local = lax.dynamic_slice_in_dim(rpos_all, first_row, rows_dev)
    cosine_table, sine_table = rope_tables(rpos_local, head_dim)
    normed_in, pull_in = jax.vjp(rms_norm, inputs, gain_in32)
    normed_in16 = normed_in.astype(jnp.bfloat16)
    query_raw = jnp.dot(normed_in16, w_query, preferred_element_type=jnp.float32)
    key_raw = jnp.dot(normed_in16, w_key, preferred_element_type=jnp.float32)
    value_raw = jnp.dot(normed_in16, w_value, preferred_element_type=jnp.float32)
    (query_rot, key_rot), rope_pull = jax.vjp(
        partial(shape_heads, cosine_table=cosine_table, sine_table=sine_table),
        query_raw,
        key_raw,
        gain_q32,
        gain_k32,
    )
    query16 = query_rot.astype(jnp.bfloat16)
    key16 = key_rot.astype(jnp.bfloat16)
    value16 = value_raw.astype(jnp.bfloat16)
    key_group, value_group = (
        lax.all_gather(key16, "ctx", axis=0, tiled=True),
        lax.all_gather(value16, "ctx", axis=0, tiled=True),
    )

    def allowed_mask(seq_rows, spos_rows):
        return (
            (valid_all[None, :] == 1)
            & (seq_all[None, :] == seq_rows[:, None])
            & (spos_all[None, :] <= spos_rows[:, None])
        )

    query_blocks = query16.reshape(blocks, QBLK, head_count, head_dim)
    seq_blocks = seq_local.reshape(blocks, QBLK)
    spos_blocks = spos_local.reshape(blocks, QBLK)

    def forward_block(block_item):
        query_block, seq_rows, spos_rows = block_item
        scores = (
            jnp.einsum("qhd,kd->hqk", query_block, key_group, preferred_element_type=jnp.float32)
            * score_scale
        )
        scores = jnp.where(allowed_mask(seq_rows, spos_rows)[None], scores, MASKED)
        row_max = jnp.max(scores, axis=-1, keepdims=True)
        exp_scores = jnp.exp(scores - row_max)
        row_total = jnp.sum(exp_scores, axis=-1, keepdims=True)
        prob_rows = (exp_scores / row_total).astype(jnp.bfloat16)
        output = jnp.einsum(
            "hqk,kd->qhd", prob_rows, value_group, preferred_element_type=jnp.float32
        )
        return (output, (row_max + jnp.log(row_total))[..., 0])

    attended, log_norm = lax.map(forward_block, (query_blocks, seq_blocks, spos_blocks))
    attended16 = attended.reshape(rows_dev, head_count * head_dim).astype(jnp.bfloat16)
    attention = lax.psum(
        jnp.dot(attended16, w_out, preferred_element_type=jnp.float32).astype(jnp.bfloat16), "tp"
    ).astype(jnp.float32)
    post_attn, pull_post_attn = jax.vjp(rms_norm, attention, gain_pa32)
    residual = inputs + post_attn
    normed_mid, pull_pre_ffn = jax.vjp(rms_norm, residual, gain_pf32)
    mid16 = normed_mid.astype(jnp.bfloat16)
    gate_out = jnp.dot(mid16, w_gate, preferred_element_type=jnp.float32)
    up_out = jnp.dot(mid16, w_up, preferred_element_type=jnp.float32)
    hidden, pull_geglu = jax.vjp(geglu, gate_out, up_out)
    hidden16 = hidden.astype(jnp.bfloat16)
    ffn_branch = lax.psum(
        jnp.dot(hidden16, w_down, preferred_element_type=jnp.float32).astype(jnp.bfloat16), "tp"
    ).astype(jnp.float32)
    post_ffn, pull_post_ffn = jax.vjp(rms_norm, ffn_branch, gain_pff32)
    outputs = residual + post_ffn
    out_rows = lax.dynamic_slice_in_dim(outputs, tp_index * feature_cols, feature_cols, 1).astype(
        jnp.bfloat16
    )
    cotangent = cot_full.astype(jnp.float32)
    d_ffn, d_gain_post_ffn = pull_post_ffn(cotangent)
    d_ffn16 = d_ffn.astype(jnp.bfloat16)
    d_hidden = contract(d_ffn16, w_down, 1, 1)
    grad_down = contract(hidden16, d_ffn16, 0, 0)
    d_gate, d_up = pull_geglu(d_hidden)
    d_gate16 = d_gate.astype(jnp.bfloat16)
    d_up16 = d_up.astype(jnp.bfloat16)
    grad_gate = contract(mid16, d_gate16, 0, 0)
    grad_up = contract(mid16, d_up16, 0, 0)
    d_mid = lax.psum(
        (contract(d_gate16, w_gate, 1, 1) + contract(d_up16, w_up, 1, 1)).astype(jnp.bfloat16), "tp"
    ).astype(jnp.float32)
    d_res_norm, d_gain_pre_ffn = pull_pre_ffn(d_mid)
    d_resid = cotangent + d_res_norm
    d_attn, d_gain_post_attn = pull_post_attn(d_resid)
    d_attn16 = d_attn.astype(jnp.bfloat16)
    d_attended16 = contract(d_attn16, w_out, 1, 1).astype(jnp.bfloat16)
    grad_out = contract(attended16, d_attn16, 0, 0)
    key_back, value_back = (key_group, value_group)

    def backward_block(running, block_item):
        key_sum, value_sum = running
        query_block, dout_block, lse_block, seq_rows, spos_rows = block_item
        scores = (
            jnp.einsum("qhd,kd->hqk", query_block, key_back, preferred_element_type=jnp.float32)
            * score_scale
        )
        scores = jnp.where(allowed_mask(seq_rows, spos_rows)[None], scores, MASKED)
        prob_rows = jnp.exp(scores - lse_block[..., None])
        prob16 = prob_rows.astype(jnp.bfloat16)
        d_probs = jnp.einsum(
            "qhd,kd->hqk", dout_block, value_back, preferred_element_type=jnp.float32
        )
        row_inner = jnp.sum(prob_rows * d_probs, axis=-1, keepdims=True)
        d_scores16 = (prob_rows * (d_probs - row_inner)).astype(jnp.bfloat16)
        d_query = (
            jnp.einsum("hqk,kd->qhd", d_scores16, key_back, preferred_element_type=jnp.float32)
            * score_scale
        )
        key_sum = (
            key_sum
            + jnp.einsum("hqk,qhd->kd", d_scores16, query_block, preferred_element_type=jnp.float32)
            * score_scale
        )
        value_sum = value_sum + jnp.einsum(
            "hqk,qhd->kd", prob16, dout_block, preferred_element_type=jnp.float32
        )
        return ((key_sum, value_sum), d_query)

    zero_rows = jnp.zeros((group_rows, head_dim), jnp.float32)
    (key_sum, value_sum), d_query_blocks = lax.scan(
        backward_block,
        (zero_rows, zero_rows),
        (
            query_blocks,
            d_attended16.reshape(blocks, QBLK, head_count, head_dim),
            log_norm,
            seq_blocks,
            spos_blocks,
        ),
    )
    d_key_rot, d_value = (
        lax.psum_scatter(
            key_sum.astype(jnp.bfloat16), "ctx", scatter_dimension=0, tiled=True
        ).astype(jnp.float32),
        lax.psum_scatter(
            value_sum.astype(jnp.bfloat16), "ctx", scatter_dimension=0, tiled=True
        ).astype(jnp.float32),
    )
    d_query_raw, d_key_raw, d_gain_query, d_gain_key = rope_pull(
        (d_query_blocks.reshape(rows_dev, head_count, head_dim), d_key_rot)
    )
    d_query16 = d_query_raw.astype(jnp.bfloat16)
    d_key16 = d_key_raw.astype(jnp.bfloat16)
    d_value16 = d_value.astype(jnp.bfloat16)
    grad_query = contract(normed_in16, d_query16, 0, 0)
    grad_key = contract(normed_in16, d_key16, 0, 0)
    grad_value = contract(normed_in16, d_value16, 0, 0)
    d_normed_part = (
        contract(d_query16, w_query, 1, 1)
        + contract(d_key16, w_key, 1, 1)
        + contract(d_value16, w_value, 1, 1)
    )
    d_normed_in = lax.psum(d_normed_part.astype(jnp.bfloat16), "tp").astype(jnp.float32)
    d_in_norm, d_gain_in = pull_in(d_normed_in)
    d_inputs = d_resid + d_in_norm
    grad_rows = lax.dynamic_slice_in_dim(d_inputs, tp_index * feature_cols, feature_cols, 1).astype(
        jnp.bfloat16
    )
    sharded = (
        grad_query,
        grad_out,
        grad_gate,
        grad_up,
        grad_down,
        d_gain_in,
        d_gain_post_attn,
        d_gain_pre_ffn,
        d_gain_post_ffn,
    )
    reduced = (
        lax.psum_scatter(
            sharded[0].astype(jnp.bfloat16), ("dp", "ctx"), scatter_dimension=0, tiled=True
        ).astype(jnp.float32),
        lax.psum_scatter(
            sharded[1].astype(jnp.bfloat16), ("dp", "ctx"), scatter_dimension=1, tiled=True
        ).astype(jnp.float32),
        lax.psum_scatter(
            sharded[2].astype(jnp.bfloat16), ("dp", "ctx"), scatter_dimension=0, tiled=True
        ).astype(jnp.float32),
        lax.psum_scatter(
            sharded[3].astype(jnp.bfloat16), ("dp", "ctx"), scatter_dimension=0, tiled=True
        ).astype(jnp.float32),
        lax.psum_scatter(
            sharded[4].astype(jnp.bfloat16), ("dp", "ctx"), scatter_dimension=1, tiled=True
        ).astype(jnp.float32),
        lax.psum_scatter(
            sharded[5].astype(jnp.bfloat16), ("dp", "ctx"), scatter_dimension=0, tiled=True
        ).astype(jnp.float32),
        lax.psum_scatter(
            sharded[6].astype(jnp.bfloat16), ("dp", "ctx"), scatter_dimension=0, tiled=True
        ).astype(jnp.float32),
        lax.psum_scatter(
            sharded[7].astype(jnp.bfloat16), ("dp", "ctx"), scatter_dimension=0, tiled=True
        ).astype(jnp.float32),
        lax.psum_scatter(
            sharded[8].astype(jnp.bfloat16), ("dp", "ctx"), scatter_dimension=0, tiled=True
        ).astype(jnp.float32),
    )
    summed = (
        lax.all_gather(reduced[0].astype(jnp.bfloat16), ("dp", "ctx"), axis=0, tiled=True).astype(
            jnp.float32
        ),
        lax.all_gather(reduced[1].astype(jnp.bfloat16), ("dp", "ctx"), axis=1, tiled=True).astype(
            jnp.float32
        ),
        lax.all_gather(reduced[2].astype(jnp.bfloat16), ("dp", "ctx"), axis=0, tiled=True).astype(
            jnp.float32
        ),
        lax.all_gather(reduced[3].astype(jnp.bfloat16), ("dp", "ctx"), axis=0, tiled=True).astype(
            jnp.float32
        ),
        lax.all_gather(reduced[4].astype(jnp.bfloat16), ("dp", "ctx"), axis=1, tiled=True).astype(
            jnp.float32
        ),
        lax.all_gather(reduced[5].astype(jnp.bfloat16), ("dp", "ctx"), axis=0, tiled=True).astype(
            jnp.float32
        ),
        lax.all_gather(reduced[6].astype(jnp.bfloat16), ("dp", "ctx"), axis=0, tiled=True).astype(
            jnp.float32
        ),
        lax.all_gather(reduced[7].astype(jnp.bfloat16), ("dp", "ctx"), axis=0, tiled=True).astype(
            jnp.float32
        ),
        lax.all_gather(reduced[8].astype(jnp.bfloat16), ("dp", "ctx"), axis=0, tiled=True).astype(
            jnp.float32
        ),
    )
    shared = lax.psum((grad_key, grad_value, d_gain_query, d_gain_key), ("dp", "ctx", "tp"))
    return (
        out_rows,
        grad_rows,
        summed[0],
        shared[0],
        shared[1],
        summed[1],
        summed[2],
        summed[3],
        summed[4],
        summed[5],
        summed[6],
        summed[7],
        summed[8],
        shared[2],
        shared[3],
    )


XOR1 = ((0, 1), (1, 0), (2, 3), (3, 2))
XOR2 = ((0, 2), (2, 0), (1, 3), (3, 1))
MESH = pl.DeviceIdType.MESH
GELU_SCALE = math.sqrt(2.0 / math.pi)
F32 = jnp.float32
BF16 = jnp.bfloat16


def add16(left, right):
    return (left.astype(F32) + right.astype(F32)).astype(BF16)


def scale_of(values):
    return lax.rsqrt(jnp.mean(values * values, axis=-1, keepdims=True) + EPSILON)


def row_blocks(rows, size, body, carry=None):
    def step(i, state):
        return body(pl.ds(pl.multiple_of(i * size, size), size), state)

    return lax.fori_loop(0, rows // size, step, carry)


def turn_in(source, target, rows):
    for first in range(0, source.shape[0], 128):
        target[rows, first : first + 128] = source[first : first + 128, :].T


def column_tiles(total, size):
    return [(first, min(size, total - first)) for first in range(0, total, size)]


def dot_nn(left, right):
    return jnp.dot(left, right, preferred_element_type=F32)


def dot_nt(left, right):
    return contract(left, right, 1, 1)


def gelu_parts(gate):
    square = gate * gate
    tanh = jnp.tanh(GELU_SCALE * gate * (1.0 + 0.044715 * square))
    half = 0.5 + 0.5 * tanh
    slope = GELU_SCALE * (1.0 + 3.0 * 0.044715 * square)
    return gate * half, half + 0.5 * gate * (1.0 - tanh * tanh) * slope


def forward_kernel(
    real_length, tok, cot, w_q, w_k, w_v, w_o, w_g, w_u, w_d, gains, head_gains, cosines, sines,
    out_t, x16, cot16, n16, raw, q16, kv16, far_kv, att16, attn16, mid16, hid16, dffn16, dg16, du16,
    gain_sum,
    blocks, v_qkv, v_o, v_g, v_u, v_d, part, near, far, ffn16,
    load_sem, own_sem, g_send, g_recv, kv_send, kv_recv, s_send, s_recv,
):
    dp, ctx, tp = lax.axis_index("dp"), lax.axis_index("ctx"), lax.axis_index("tp")
    core_peer = (dp, ctx, tp + 1 - 2 * (tp % 2))
    x_index = (tp + 2) % 4
    x_peer = (dp, ctx, x_index)
    y_peer = (dp, 1 - ctx, tp)
    features, rows = tok.shape[0], tok.shape[1] // 2
    width = 4 * features
    hidden = w_d.shape[0]
    head_dim = w_k.shape[1]
    half = rows // 2
    odd = tp % 2

    loads = [
        pltpu.make_async_copy(source, target, load_sem.at[j])
        for j, (source, target) in enumerate(
            (
                (w_q, v_qkv.at[:, 0:head_dim]),
                (w_k, v_qkv.at[:, head_dim : 2 * head_dim]),
                (w_v, v_qkv.at[:, 2 * head_dim : 3 * head_dim]),
                (w_o, v_o), (w_g, v_g), (w_u, v_u), (w_d, v_d),
            )
        )
    ]
    for copy in loads:
        copy.start()

    def half_of(source, index):
        lane = (ctx if index % 2 == 0 else 1 - ctx) * rows
        return source.at[:, pl.ds(pl.multiple_of(lane, rows), rows)]

    def place(index, owner):
        return blocks.at[index, pl.ds(pl.multiple_of(owner * features, features), features)]

    sources = [half_of(tok, 0), half_of(tok, 1), half_of(cot, 0), half_of(cot, 1)]

    def remote(source, target, send, recv, peer):
        return pltpu.make_async_remote_copy(
            src_ref=source, dst_ref=target, send_sem=send, recv_sem=recv,
            device_id=peer, device_id_type=MESH,
        )

    own = [pltpu.make_async_copy(sources[j], place(j, tp), own_sem.at[j]) for j in range(4)]
    to_x = [
        remote(sources[j], place(j, tp), g_send.at[0, j], g_recv.at[0, j], x_peer) for j in range(4)
    ]
    to_core = [
        remote(sources[j], place(j, tp), g_send.at[1, j], g_recv.at[1, j], core_peer)
        for j in range(4)
    ]
    onward = [
        remote(place(j, x_index), place(j, x_index), g_send.at[2, j], g_recv.at[2, j], core_peer)
        for j in range(4)
    ]
    for copy in own:
        copy.start()
    barrier = pltpu.get_barrier_semaphore()
    for peer in (core_peer, x_peer, y_peer):
        pl.semaphore_signal(barrier, inc=1, device_id=peer, device_id_type=MESH)
    pl.semaphore_wait(barrier, 3)

    for j in range(4):
        to_core[j].start()
    to_x[0].start()
    to_x[1].start()

    def pass_on(j):
        to_x[j].wait_recv()
        onward[j].start()

    def gathered(j):
        own[j].wait()
        to_core[j].wait_recv()
        onward[j].wait_recv()

    def chunk(c):
        return pl.ds(c * rows, rows)

    def project(c):
        turn_in(blocks.at[c], x16, chunk(c))

        def norm(block, _):
            at = pl.ds(c * rows + block.start, block.size)
            values = x16[at, :].astype(F32)
            n16[at, :] = (values * scale_of(values) * gains[0:1, :]).astype(BF16)

        row_blocks(rows, 32, norm)
        for first in range(0, rows, half):
            at = pl.ds(c * rows + first, half)
            tables = pl.ds(c * rows + first, half)
            values = dot_nn(n16[at, :], v_qkv[...])
            raw[at, :] = values[:, : 2 * head_dim]
            cosine, sine = cosines[tables, :], sines[tables, :]
            for j, target in ((0, q16.at[at, :]), (1, kv16.at[at, 0:head_dim])):
                head = values[:, j * head_dim : (j + 1) * head_dim]
                head = head * scale_of(head) * head_gains[j : j + 1, :]
                low, high = head[:, : head_dim // 2], head[:, head_dim // 2 :]
                target[:, : head_dim // 2] = (low * cosine - high * sine).astype(BF16)
                target[:, head_dim // 2 :] = (high * cosine + low * sine).astype(BF16)
            kv16[at, head_dim:] = values[:, 2 * head_dim :].astype(BF16)

    score_scale = head_dim ** (-0.5)

    def attend_rows(c):
        for first in range(0, rows, half):
            at = pl.ds(c * rows + first, half)
            query = q16[at, :]
            row_id = first + lax.broadcasted_iota(jnp.int32, (half, rows), 0)
            key_id = lax.broadcasted_iota(jnp.int32, (half, rows), 1)
            allowed = key_id <= row_id
            if c == 1:
                allowed = allowed & (rows + key_id < real_length[0, 0])
            keys = [(kv16[chunk(c), :head_dim], kv16[chunk(c), head_dim:], allowed)]
            if c == 1:
                keys.append((far_kv[:, :head_dim], far_kv[:, head_dim:], None))
            scores = []
            for key, _, mask in keys:
                score = dot_nt(query, key) * score_scale
                scores.append(score if mask is None else jnp.where(mask, score, MASKED))
            most = scores[0].max(axis=1, keepdims=True)
            for score in scores[1:]:
                most = jnp.maximum(most, score.max(axis=1, keepdims=True))
            exps = [jnp.exp(score - most) for score in scores]
            total = sum(e.sum(axis=1, keepdims=True) for e in exps)
            out = sum(dot_nn((e / total).astype(BF16), k[1]) for e, k in zip(exps, keys))
            att16[at, :] = out.astype(BF16)
        part[c] = dot_nn(att16[chunk(c), :], v_o[...]).astype(BF16)

    def rows_of(index):
        return pl.ds(pl.multiple_of(index * half, half), half)

    def sum_copies(s, target):
        start = pl.multiple_of((s % 2) * rows + odd * half, half)
        final = target.at[pl.ds(start, half)]
        return (
            remote(part.at[s, rows_of(1 - odd)], near.at[s], s_send.at[0, s], s_recv.at[0, s], core_peer),
            remote(near.at[s], far.at[s], s_send.at[1, s], s_recv.at[1, s], x_peer),
            remote(final, final, s_send.at[2, s], s_recv.at[2, s], core_peer),
        )

    def sum_start(s, target):
        sum_copies(s, target)[0].start()

    def sum_cross(s, target):
        copies = sum_copies(s, target)
        copies[0].wait_recv()
        near[s] = add16(part[s, rows_of(odd)], near[s])
        copies[1].start()

    def sum_back(s, target):
        copies = sum_copies(s, target)
        copies[1].wait_recv()
        start = pl.multiple_of((s % 2) * rows + odd * half, half)
        target[pl.ds(start, half), :] = add16(near[s], far[s])
        copies[2].start()
        copies[2].wait_recv()

    def residual(at):
        branch = attn16[at, :].astype(F32)
        return x16[at, :].astype(F32) + branch * scale_of(branch) * gains[1:2, :]

    def middle(c):
        def body(block, _):
            at = pl.ds(c * rows + block.start, block.size)
            values = residual(at)
            mid16[at, :] = (values * scale_of(values) * gains[2:3, :]).astype(BF16)

        row_blocks(rows, 32, body)

    def feed(c):
        for first, size in column_tiles(hidden, 256):
            for low in range(0, rows, half):
                at = pl.ds(c * rows + low, half)
                cols = pl.ds(first, size)
                gate = dot_nt(mid16[at, :], v_g[cols, :])
                up = dot_nt(mid16[at, :], v_u[cols, :])
                act, slope = gelu_parts(gate)
                hid16[at, cols] = (act * up).astype(BF16)
                dg16[at, cols] = (slope * up).astype(BF16)
                du16[at, cols] = act.astype(BF16)
        for first, size in column_tiles(width, 256):
            cols = pl.ds(first, size)
            part[2 + c, :, cols] = dot_nn(hid16[chunk(c), :], v_d[:, cols]).astype(BF16)

    def finish(c):
        turn_in(blocks.at[2 + c], cot16, chunk(c))
        sum_copies(c, attn16)[0].wait_send()
        onward[c].wait_send()

        def body(block, total):
            at = pl.ds(c * rows + block.start, block.size)
            branch = ffn16[at, :].astype(F32)
            scale = scale_of(branch)
            unit = branch * scale
            grad = cot16[at, :].astype(F32)
            part[c, block, :] = (residual(at) + unit * gains[3:4, :]).astype(BF16)
            weighted = grad * gains[3:4, :]
            inner = jnp.mean(unit * weighted, axis=-1, keepdims=True)
            dffn16[at, :] = (scale * (weighted - unit * inner)).astype(BF16)
            return total + (grad * unit).reshape(-1, 8, width).sum(axis=0)

        total = row_blocks(rows, 32, body, jnp.zeros((8, width), F32))
        if c == 0:
            gain_sum[...] = total
        else:
            gain_sum[...] += total
        for first in range(0, width, 128):
            blocks[c, first : first + 128, :] = part[c, :, first : first + 128].T
        lane = (ctx if c == 0 else 1 - ctx) * rows
        mine = blocks[c, pl.ds(pl.multiple_of(tp * features, features), features), :]
        out_t[:, pl.ds(pl.multiple_of(lane, rows), rows)] = mine

    def feed_back(c):
        for first, size in column_tiles(hidden, 256):
            for low in range(0, rows, half):
                at = pl.ds(c * rows + low, half)
                cols = pl.ds(first, size)
                d_hidden = dot_nt(dffn16[at, :], v_d[cols, :])
                dg16[at, cols] = (d_hidden * dg16[at, cols].astype(F32)).astype(BF16)
                du16[at, cols] = (d_hidden * du16[at, cols].astype(F32)).astype(BF16)

    kv_copy = remote(kv16.at[chunk(0)], far_kv, kv_send.at[0], kv_recv.at[0], y_peer)
    pass_on(0)
    for copy in loads[:3]:
        copy.wait()
    gathered(0)
    project(0)
    kv_copy.start()
    pass_on(1)
    to_x[2].start()
    to_x[3].start()
    loads[3].wait()
    attend_rows(0)
    sum_start(0, attn16)
    gathered(1)
    project(1)
    sum_cross(0, attn16)
    kv_copy.wait_recv()
    attend_rows(1)
    sum_start(1, attn16)
    pass_on(2)
    pass_on(3)
    sum_cross(1, attn16)
    sum_back(0, attn16)
    for copy in loads[4:]:
        copy.wait()
    middle(0)
    feed(0)
    sum_start(2, ffn16)
    sum_back(1, attn16)
    middle(1)
    sum_cross(2, ffn16)
    feed(1)
    sum_start(3, ffn16)
    gathered(2)
    gathered(3)
    sum_back(2, ffn16)
    sum_cross(3, ffn16)
    finish(0)
    feed_back(0)
    sum_back(3, ffn16)
    finish(1)
    feed_back(1)
    for group in (to_x, to_core, onward[2:], [kv_copy]):
        for copy in group:
            copy.wait_send()
    for s, target in ((0, attn16), (1, attn16), (2, ffn16), (3, ffn16)):
        for copy in sum_copies(s, target)[1 if s < 2 else 0 :]:
            copy.wait_send()


def forward(real_length, tok_t, cot_t, weights, gains, head_gains, cosines, sines):
    features, rows = tok_t.shape
    half = rows // 2
    width = 4 * features
    hidden = weights[-1].shape[0]
    head_dim = weights[1].shape[1]
    whole = pl.BlockSpec(memory_space=pltpu.VMEM)
    there = pl.BlockSpec(memory_space=pl.ANY)

    def low(*shape):
        return jax.ShapeDtypeStruct(shape, BF16)

    return pl.pallas_call(
        forward_kernel,
        out_shape=(
            low(features, rows), low(rows, width), low(rows, width), low(rows, width),
            jax.ShapeDtypeStruct((rows, 2 * head_dim), F32), low(rows, head_dim),
            low(rows, 2 * head_dim), low(half, 2 * head_dim), low(rows, head_dim),
            low(rows, width), low(rows, width), low(rows, hidden), low(rows, width),
            low(rows, hidden), low(rows, hidden), jax.ShapeDtypeStruct((8, width), F32),
        ),
        in_specs=[pl.BlockSpec(memory_space=pltpu.SMEM)] + [there] * 9 + [whole] * 4,
        out_specs=[whole] * 16,
        scratch_shapes=[
            pltpu.VMEM((4, width, half), BF16),
            pltpu.VMEM((width, 3 * head_dim), BF16),
            pltpu.VMEM((head_dim, width), BF16),
            pltpu.VMEM((hidden, width), BF16),
            pltpu.VMEM((hidden, width), BF16),
            pltpu.VMEM((hidden, width), BF16),
            pltpu.VMEM((4, half, width), BF16),
            pltpu.VMEM((4, half // 2, width), BF16),
            pltpu.VMEM((4, half // 2, width), BF16),
            pltpu.VMEM((rows, width), BF16),
            pltpu.SemaphoreType.DMA((7,)),
            pltpu.SemaphoreType.DMA((4,)),
            pltpu.SemaphoreType.DMA((3, 4)),
            pltpu.SemaphoreType.DMA((3, 4)),
            pltpu.SemaphoreType.DMA((1,)),
            pltpu.SemaphoreType.DMA((1,)),
            pltpu.SemaphoreType.DMA((3, 4)),
            pltpu.SemaphoreType.DMA((3, 4)),
        ],
        name="forward",
        compiler_params=pltpu.CompilerParams(
            collective_id=2, has_side_effects=True, vmem_limit_bytes=63 << 20
        ),
    )(real_length, tok_t, cot_t, *weights, gains, head_gains, cosines, sines)


def backward_kernel(
    step_rows, steps, ring, gate_hidden,
    real_length, tok, x_in, cot_in, n_in, q_in, kv_in, far_in, att_in, attn_in, mid_in, hid_in,
    dffn_in, dg_in, du_in, gain_ffn, w_q, w_k, w_v, w_o, w_g, w_u, gains, head_gains, gain_col,
    cosines, sines,
    out, xg_t, gain_rows, gain_cols,
    g, y2, z2, m2, z1, m1, y1, hid, dg, du, mid, dffn, w_tiles, acc, part, near, far, dm, cot, attn,
    v_o, v_qkv, dkv_new, norm_near, norm_far, row_part,
    row_near, kv_near, kv_far, turned, head_sums, row_sums, sum_slots, sum_new, col_slots,
    col_new,
    load_sem, tile_sem, keep_sem, chain_send, chain_recv, peer_send, peer_recv,
):
    dp, ctx, tp = lax.axis_index("dp"), lax.axis_index("ctx"), lax.axis_index("tp")
    s, K = step_rows, steps
    upper = dp // 2
    odd = tp % 2
    outer = (dp == 0) | (dp == 3)
    inner = jnp.logical_not(outer)
    yes = dp >= 0
    core_index = tp + 1 - 2 * odd
    x_index = (tp + 2) % 4
    cross_index = (core_index + 2) % 4
    z_index = dp + 1 - 2 * (dp % 2)
    core_peer, x_peer = (dp, ctx, core_index), (dp, ctx, x_index)
    y_peer, z_peer, m_peer = (dp, 1 - ctx, tp), (z_index, ctx, tp), (3 - dp, ctx, tp)
    features, rows = tok.shape[0], tok.shape[1] // 2
    width = 4 * features
    hidden = w_g.shape[0]
    head_dim = w_k.shape[1]
    half = rows // 2
    kv_rows = head_dim // 2
    score_scale = head_dim ** (-0.5)

    def remote(source, target, send, recv, peer):
        return pltpu.make_async_remote_copy(
            src_ref=source, dst_ref=target, send_sem=send, recv_sem=recv,
            device_id=peer, device_id_type=MESH,
        )

    def chunk(c):
        return pl.ds(c * rows, rows)

    def multiple(start, size):
        return pl.ds(pl.multiple_of(start, size), size)

    dqkv, kv16 = dg.at[:, 0 : 3 * head_dim], dg.at[:, 3 * head_dim : 5 * head_dim]
    dkv, dkv_far = du.at[:, 0 : 2 * head_dim], du.at[0:rows, 2 * head_dim : 4 * head_dim]
    far_kv = du.at[rows : 2 * rows, 2 * head_dim : 4 * head_dim]
    q16, att = du.at[:, 4 * head_dim : 5 * head_dim], du.at[:, 5 * head_dim : 6 * head_dim]

    tok_own = dm.at[0:features, 0 : 2 * rows]

    pairs = (
        (hid_in, hid), (dffn_in, dffn), (dg_in, dg), (mid_in, mid), (du_in, du), (cot_in, cot),
        (attn_in, attn), (w_o, v_o),
        (w_q, v_qkv.at[:, 0:head_dim]), (w_k, v_qkv.at[:, head_dim : 2 * head_dim]),
        (w_v, v_qkv.at[:, 2 * head_dim : 3 * head_dim]),
    )
    count = len(pairs)

    def load(j):
        return pltpu.make_async_copy(pairs[j][0], pairs[j][1], load_sem.at[j])

    late_pairs = (
        (x_in, dffn), (n_in, mid), (q_in, q16), (kv_in, kv16), (far_in, far_kv), (att_in, att),
    )

    def load_tok():
        return pltpu.make_async_copy(tok, tok_own, load_sem.at[count + len(late_pairs)])

    def late_load(j):
        return pltpu.make_async_copy(late_pairs[j][0], late_pairs[j][1], load_sem.at[count + j])

    for j in range(count):
        load(j).start()
    barrier = pltpu.get_barrier_semaphore()
    for peer in (core_peer, x_peer, y_peer, z_peer, m_peer):
        pl.semaphore_signal(barrier, inc=1, device_id=peer, device_id_type=MESH)
    pl.semaphore_wait(barrier, 5)

    base = 2 * s * K

    def rows2(k, h):
        return multiple((2 * k + h) * s, s)

    def rows1(k, h):
        return multiple(base + (2 * k + h) * s, s)

    def pair1(k):
        return pl.ds(pl.multiple_of(base + 2 * k * s, s), 2 * s)

    def slot(k):
        return multiple((k % ring) * s, s)

    def slot_pair(k):
        return multiple((k % ring) * 2 * s, 2 * s)

    def slot_half(k, h):
        return multiple(((k % ring) * 2 + h) * s, s)

    def chain(j, k, source, target, peer):
        return remote(source, target, chain_send.at[j, k], chain_recv.at[j, k], peer)

    def keep(j, k, source, target):
        return pltpu.make_async_copy(source, target, keep_sem.at[j, k])

    def c_y2(k):
        return chain(0, k, g.at[rows2(k, 1 - ctx)], y2.at[slot(k)], y_peer)

    def c_z2(k):
        return chain(1, k, y2.at[slot(k)], z2.at[slot(k)], z_peer)

    def c_m2(k):
        return chain(2, k, z2.at[slot(k)], m2.at[slot(k)], m_peer)

    def c_fo(k):
        return chain(3, k, m2.at[slot(k)], out.at[rows2(k, ctx)], z_peer)

    def c_fy(k):
        return chain(4, k, m2.at[slot(k)], out.at[rows2(k, ctx)], y_peer)

    def c_fy_outer(k):
        return chain(4, k, out.at[rows2(k, ctx)], out.at[rows2(k, ctx)], y_peer)

    def c_z1(k):
        return chain(5, k, g.at[pair1(k)], z1.at[slot_pair(k)], z_peer)

    def c_m1(k):
        return chain(6, k, z1.at[slot_half(k, 1 - upper)], m1.at[slot(k)], m_peer)

    def c_y1(k):
        return chain(7, k, m1.at[slot(k)], y1.at[slot(k)], y_peer)

    def c_fm(k):
        return chain(8, k, y1.at[slot(k)], out.at[rows1(k, upper)], m_peer)

    def c_fa(k):
        return chain(9, k, y1.at[slot(k)], out.at[rows1(k, upper)], z_peer)

    def c_fb(k):
        return chain(10, k, out.at[rows1(k, 1 - upper)], out.at[rows1(k, 1 - upper)], z_peer)

    def keep2(k):
        return keep(0, k, m2.at[slot(k)], out.at[rows2(k, ctx)])

    def keep1(k):
        return keep(1, k, y1.at[slot(k)], out.at[rows1(k, upper)])

    def b2(k):
        c_y2(k).wait_recv()
        y2[slot(k), :] = add16(y2[slot(k), :], g[rows2(k, ctx), :])
        pl.when(outer)(lambda: c_z2(k).start())

    def b1(k):
        c_z1(k).wait_recv()
        z1[slot_pair(k), :] = add16(z1[slot_pair(k), :], g[pair1(k), :])
        c_m1(k).start()

    def c2(k):
        c_z2(k).wait_recv()
        z2[slot(k), :] = add16(z2[slot(k), :], y2[slot(k), :])
        c_m2(k).start()

    def c1(k):
        c_m1(k).wait_recv()
        m1[slot(k), :] = add16(m1[slot(k), :], z1[slot_half(k, upper), :])
        c_y1(k).start()

    def d2(k):
        c_m2(k).wait_recv()
        m2[slot(k), :] = add16(m2[slot(k), :], z2[slot(k), :])
        c_fo(k).start()
        c_fy(k).start()
        keep2(k).start()

    def d1(k):
        c_y1(k).wait_recv()
        y1[slot(k), :] = add16(y1[slot(k), :], m1[slot(k), :])
        c_fm(k).start()
        c_fa(k).start()
        keep1(k).start()

    def e2(k):
        c_fo(k).wait_recv()
        c_fy_outer(k).start()

    def e1(k):
        c_fm(k).wait_recv()
        c_fb(k).start()

    def f2(k):
        c_fy(k).wait_recv()
        c_y2(k).wait_send()

    def f_outer(k):
        c_z2(k).wait_send()
        c_fy_outer(k).wait_send()
        c_fa(k).wait_recv()
        c_fb(k).wait_recv()
        c_z1(k).wait_send()

    def f_inner(k):
        keep2(k).wait()
        keep1(k).wait()
        for copy in (c_m2, c_fo, c_fy, c_m1, c_y1, c_fm, c_fa, c_fb):
            copy(k).wait_send()

    hops = (
        (5, yes, f2), (5, outer, f_outer), (5, inner, f_inner), (4, outer, e2), (4, inner, e1),
        (3, inner, d2), (3, inner, d1), (2, inner, c2), (2, inner, c1), (1, yes, b2), (1, inner, b1),
        (0, yes, lambda k: c_y2(k).start()), (0, outer, lambda k: c_z1(k).start()),
    )

    def grad_tile(index, first, size):
        left, right = ((hid, dffn), (dg, mid), (du, mid))[index]
        at = first if isinstance(first, int) else pl.multiple_of(first, 256)
        tile = contract(left[:, pl.ds(at, size)], right[...], 0, 0)
        start = index * hidden + first
        g[pl.ds(start if isinstance(start, int) else pl.multiple_of(start, 64), size), :] = (
            tile.astype(BF16)
        )

    full = hidden // 256
    tail = hidden - 256 * full

    def mid_part(c):
        tiles = column_tiles(hidden, 256)

        def fetch(j):
            first, size = tiles[j]
            return [
                pltpu.make_async_copy(
                    w.at[pl.ds(first, size)], w_tiles.at[i, j % 2, pl.ds(0, size)],
                    tile_sem.at[i, j % 2],
                )
                for i, w in enumerate((w_g, w_u))
            ]

        for copy in fetch(0):
            copy.start()
        for j, (first, size) in enumerate(tiles):
            if j + 1 < len(tiles):
                for copy in fetch(j + 1):
                    copy.start()
            for copy in fetch(j):
                copy.wait()
            cols = pl.ds(first, size)
            term = dot_nn(dg[chunk(c), cols], w_tiles[0, j % 2, 0:size, :]) + dot_nn(
                du[chunk(c), cols], w_tiles[1, j % 2, 0:size, :]
            )
            if j == 0:
                acc[...] = term
            else:
                acc[...] += term
        part[c] = acc[...].astype(BF16)

    def own_half(index):
        return multiple(index * half, half)

    def peer_copy(j, source, target, peer):
        return remote(source, target, peer_send.at[j], peer_recv.at[j], peer)

    def sum_copies(c):
        final = dm.at[multiple(c * rows + odd * half, half)]
        return (
            peer_copy(3 * c, part.at[c, own_half(1 - odd)], near.at[c], core_peer),
            peer_copy(3 * c + 1, near.at[c], far.at[c], x_peer),
            peer_copy(3 * c + 2, final, final, core_peer),
        )

    def sum_begin(c):
        mid_part(c)
        sum_copies(c)[0].start()

    def sum_cross(c):
        copies = sum_copies(c)
        copies[0].wait_recv()
        near[c] = add16(part[c, own_half(odd)], near[c])
        copies[1].start()

    def sum_back(c):
        copies = sum_copies(c)
        copies[1].wait_recv()
        dm[multiple(c * rows + odd * half, half), :] = add16(near[c], far[c])
        copies[2].start()

    def norms_back(c):
        sum_copies(c)[2].wait_recv()

        def body(block, state):
            at = pl.ds(c * rows + block.start, block.size)
            branch = attn[at, :].astype(F32)
            scale_a = scale_of(branch)
            unit_a = branch * scale_a
            resid = dffn[at, :].astype(F32) + unit_a * gains[1:2, :]
            scale_r = scale_of(resid)
            unit_r = resid * scale_r
            grad = dm[at, :].astype(F32)
            weighted = grad * gains[2:3, :]
            mean = jnp.mean(unit_r * weighted, axis=-1, keepdims=True)
            d_resid = cot[at, :].astype(F32) + scale_r * (weighted - unit_r * mean)
            weighted = d_resid * gains[1:2, :]
            mean = jnp.mean(unit_a * weighted, axis=-1, keepdims=True)
            cot[at, :] = d_resid.astype(BF16)
            attn[at, :] = (scale_a * (weighted - unit_a * mean)).astype(BF16)
            return (
                state[0] + (d_resid * unit_a).reshape(-1, 8, width).sum(axis=0),
                state[1] + (grad * unit_r).reshape(-1, 8, width).sum(axis=0),
            )

        zero = jnp.zeros((8, width), F32)
        sum_a, sum_r = row_blocks(rows, 16, body, (zero, zero))
        if c == 1:
            row_sums[0], row_sums[1] = sum_a, sum_r
        else:
            row_sums[0] += sum_a
            row_sums[1] += sum_r

    def head_back(grad, at, j):
        cosine, sine = cosines[at, :], sines[at, :]
        low, high = grad[:, : head_dim // 2], grad[:, head_dim // 2 :]
        grad = jnp.concatenate([low * cosine + high * sine, high * cosine - low * sine], axis=1)
        cols = pl.ds(j * head_dim, head_dim)
        raw = dot_nn(mid[at, :], v_qkv[:, cols])
        scale = scale_of(raw)
        unit = raw * scale
        weighted = grad * head_gains[j : j + 1, :]
        mean = jnp.mean(unit * weighted, axis=-1, keepdims=True)
        dqkv[at, cols] = (scale * (weighted - unit * mean)).astype(BF16)
        head_sums[j] += (grad * unit).reshape(-1, 8, head_dim).sum(axis=0)

    def attend_back_rows(c):
        d_keys, d_values = [0.0, 0.0], [0.0, 0.0]
        for first in range(0, rows, half):
            at = pl.ds(c * rows + first, half)
            query = q16[at, :]
            d_out = dot_nt(attn[at, :], v_o[...]).astype(BF16)
            row_id = first + lax.broadcasted_iota(jnp.int32, (half, rows), 0)
            key_id = lax.broadcasted_iota(jnp.int32, (half, rows), 1)
            allowed = key_id <= row_id
            if c == 1:
                allowed = allowed & (rows + key_id < real_length[0, 0])
            keys = [(kv16[chunk(c), :head_dim], kv16[chunk(c), head_dim:], allowed)]
            if c == 1:
                keys.append((far_kv[:, :head_dim], far_kv[:, head_dim:], None))
            scores = []
            for key, _, mask in keys:
                score = dot_nt(query, key) * score_scale
                scores.append(score if mask is None else jnp.where(mask, score, MASKED))
            most = scores[0].max(axis=1, keepdims=True)
            for score in scores[1:]:
                most = jnp.maximum(most, score.max(axis=1, keepdims=True))
            exps = [jnp.exp(score - most) for score in scores]
            total = sum(e.sum(axis=1, keepdims=True) for e in exps)
            probs = [e / total for e in exps]
            d_probs = [dot_nt(d_out, key[1]) for key in keys]
            mean = sum((p * d).sum(axis=1, keepdims=True) for p, d in zip(probs, d_probs))
            d_query = 0.0
            for i, key in enumerate(keys):
                d_score = (probs[i] * (d_probs[i] - mean)).astype(BF16)
                d_query += dot_nn(d_score, key[0])
                d_keys[i] += contract(d_score, query, 0, 0)
                d_values[i] += contract(probs[i].astype(BF16), d_out, 0, 0)
            head_back(d_query * score_scale, at, 0)
        dkv[chunk(c), :head_dim] = (d_keys[0] * score_scale).astype(BF16)
        dkv[chunk(c), head_dim:] = d_values[0].astype(BF16)
        if c == 1:
            dkv_far[:, :head_dim] = (d_keys[1] * score_scale).astype(BF16)
            dkv_far[:, head_dim:] = d_values[1].astype(BF16)
            far_copy().start()

    def far_copy():
        return peer_copy(6, dkv_far, dkv_new, y_peer)

    def keys_back(c):
        if c == 0:
            far_copy().wait_recv()
        for first in range(0, rows, half):
            at = pl.ds(c * rows + first, half)
            grad = dkv[at, :].astype(F32)
            if c == 0:
                grad = grad + dkv_new[pl.ds(first, half), :].astype(F32)
            head_back(grad[:, :head_dim], at, 1)
            dqkv[at, 2 * head_dim :] = grad[:, head_dim:].astype(BF16)

    def cell(c, j):
        index = 4 * c + j
        return hid.at[pl.ds(index // 3 * features, features), pl.ds(index % 3 * rows, rows)]

    owners = (tp, core_index, x_index, cross_index)

    def scatter_copies(c):
        return (
            peer_copy(7 + 6 * c, cell(c, 1), norm_near.at[c, 0], core_peer),
            peer_copy(8 + 6 * c, cell(c, 3), norm_near.at[c, 1], core_peer),
            peer_copy(9 + 6 * c, row_part.at[c, 0], row_near.at[c, 0], core_peer),
            peer_copy(10 + 6 * c, cell(c, 2), norm_far.at[c], x_peer),
            peer_copy(11 + 6 * c, row_part.at[c, 1], row_near.at[c, 1], x_peer),
        )

    def scatter_begin(c):
        for j in range(4):
            weights = v_qkv[multiple(owners[j] * features, features), :]
            cell(c, j)[...] = dot_nt(weights, dqkv[chunk(c), :]).astype(BF16)
        for first in range(0, rows, half):
            at = pl.ds(c * rows + first, half)
            raw = dot_nn(mid[at, :], v_qkv[...])
            inner_sum = (raw * dqkv[at, :].astype(F32)).sum(axis=1, keepdims=True)
            scale = scale_of(dffn[at, :].astype(F32))
            lane = lax.broadcasted_iota(jnp.int32, (half, 128), 1)
            both = jnp.where(lane == 0, inner_sum, scale)
            row_part[c, 0, :, pl.ds(first, half)] = both.T[0:8, :]
        for copy in scatter_copies(c)[:3]:
            copy.start()

    def scatter_cross(c):
        copies = scatter_copies(c)
        for copy in copies[:3]:
            copy.wait_recv()
        cell(c, 0)[...] = add16(cell(c, 0)[...], norm_near[c, 0])
        cell(c, 2)[...] = add16(cell(c, 2)[...], norm_near[c, 1])
        row_part[c, 1] = row_part[c, 0] + row_near[c, 0]
        copies[3].start()
        copies[4].start()

    def scatter_end(c):
        copies = scatter_copies(c)
        copies[3].wait_recv()
        copies[4].wait_recv()
        for first in range(0, width, 128):
            turned[first : first + 128, :] = cot[chunk(c), first : first + 128].T
        lane = (ctx if c == 0 else 1 - ctx) * rows
        lanes = pl.ds(pl.multiple_of(lane, rows), rows)
        grad = cell(c, 0)[...].astype(F32) + norm_far[c].astype(F32)
        values = tok_own[:, lanes].astype(F32)
        scale = row_part[c, 0, 1:2, :]
        inner_sum = row_part[c, 1, 0:1, :] + row_near[c, 1, 0:1, :]
        d_in = scale * (grad * gain_col[:, 0:1]) - values * (
            scale * scale * inner_sum * (1.0 / width)
        )
        d_resid = turned[multiple(tp * features, features), :].astype(F32)
        xg_t[:, lanes] = (d_resid + d_in).astype(BF16)
        column = jnp.sum(grad * values * scale, axis=1, keepdims=True)
        column = jnp.broadcast_to(column, (features, 128))
        if c == 1:
            col_slots[0] = column
        else:
            col_slots[0] += column

    at_out = 3 * hidden
    at_query = at_out + head_dim
    at_kv = at_query + head_dim

    def small_grads():
        g[pl.ds(at_out, head_dim), :] = contract(att[...], attn[...], 0, 0).astype(BF16)
        g[pl.ds(at_query, head_dim), :] = contract(dqkv[:, :head_dim], mid[...], 0, 0).astype(BF16)
        spare = g.shape[0] - at_kv - kv_rows
        g[pl.ds(at_kv + kv_rows, spare), :] = jnp.zeros((spare, width), BF16)
        sum_copies(1)[0].wait_send()
        for j in range(4):
            cols = multiple(head_dim + owners[j] * kv_rows, kv_rows)
            part[1, pl.ds(j * kv_rows, kv_rows), :] = contract(dqkv[:, cols], mid[...], 0, 0).astype(
                BF16
            )
        for copy in kv_copies()[:2]:
            copy.start()

    def kv_copies():
        return (
            peer_copy(19, part.at[1, pl.ds(kv_rows, kv_rows)], kv_near.at[0], core_peer),
            peer_copy(20, part.at[1, pl.ds(3 * kv_rows, kv_rows)], kv_near.at[1], core_peer),
            peer_copy(21, part.at[1, pl.ds(2 * kv_rows, kv_rows)], kv_far, x_peer),
        )

    def kv_cross():
        copies = kv_copies()
        copies[0].wait_recv()
        copies[1].wait_recv()
        for j in range(2):
            at = pl.ds(2 * j * kv_rows, kv_rows)
            part[1, at, :] = add16(part[1, at, :], kv_near[j])
        copies[2].start()

    def kv_end():
        kv_copies()[2].wait_recv()
        g[pl.ds(at_kv, kv_rows), :] = add16(part[1, pl.ds(0, kv_rows), :], kv_far[...])

    sum_peers = (core_peer, x_peer, y_peer, z_peer, m_peer)

    def sum_copy(j):
        return peer_copy(22 + j, sum_slots.at[j], sum_new.at[j], sum_peers[j])

    def col_copy(j):
        return peer_copy(27 + j, col_slots.at[j], col_new.at[j], sum_peers[2 + j])

    def gains_begin():
        sum_slots[0] = jnp.zeros((8, width), F32)
        for j, values in enumerate((row_sums[0], row_sums[1], gain_ffn[...])):
            sum_slots[0, j : j + 1, :] = 0.25 * values.sum(axis=0, keepdims=True)
        for j in range(2):
            sum_slots[0, 3:4, j * head_dim : (j + 1) * head_dim] = head_sums[j].sum(
                axis=0, keepdims=True
            )
        sum_copy(0).start()
        col_copy(0).start()

    def gains_hop(j):
        sum_copy(j).wait_recv()
        if j < 4:
            sum_slots[j + 1] = sum_slots[j] + sum_new[j]
            sum_copy(j + 1).start()
        else:
            gain_rows[...] = sum_slots[j] + sum_new[j]
        if j < 3:
            col_copy(j).wait_recv()
        if j < 2:
            col_slots[j + 1] = col_slots[j] + col_new[j]
            col_copy(j + 1).start()
        if j == 2:
            mine = multiple(tp * features, features)
            gain_cols[mine, :] = col_slots[2] + col_new[2]
            gather_copies()[0].start()
            gather_copies()[1].start()
        if j == 3:
            gather_copies()[1].wait_recv()
            gather_copies()[2].start()
        if j == 4:
            gather_copies()[0].wait_recv()
            gather_copies()[2].wait_recv()

    def gather_copies():
        mine = gain_cols.at[multiple(tp * features, features)]
        theirs = gain_cols.at[multiple(x_index * features, features)]
        return (
            peer_copy(30, mine, mine, core_peer),
            peer_copy(31, mine, mine, x_peer),
            peer_copy(32, theirs, theirs, core_peer),
        )

    def load_late():
        for j in range(len(late_pairs)):
            late_load(j).start()

    def wait_late():
        for j in range(len(late_pairs)):
            late_load(j).wait()
        for j in range(5, count):
            load(j).wait()
        head_sums[...] = jnp.zeros(head_sums.shape, F32)

    gate_tiles = gate_hidden // 256
    load(0).wait()
    load(1).wait()
    grad_tile(0, 0, 256)
    load(2).wait()
    load(3).wait()
    for j in range(gate_tiles, full):
        grad_tile(1, 256 * j, 256)
    if tail:
        grad_tile(1, 256 * full, tail)
    load(4).wait()

    last_up = 1 + full
    stages = (
        (last_up + gate_tiles + 1, load_late),
        (2, lambda: sum_begin(1)),
        (3, lambda: sum_cross(1)),
        (4, lambda: sum_begin(0)),
        (5, lambda: sum_cross(0)),
        (6, lambda: sum_back(1)),
        (8, lambda: sum_back(0)),
        (last_up + gate_tiles + 2, wait_late),
    )
    first_back = last_up + gate_tiles + 2
    stages += tuple(
        (first_back + j, action)
        for j, action in enumerate(
            (
                lambda: norms_back(1),
                lambda: attend_back_rows(1),
                lambda: norms_back(0),
                lambda: (sum_copies(0)[2].wait_send(), load_tok().start(), attend_back_rows(0)),
                lambda: keys_back(1),
                lambda: scatter_begin(1),
                lambda: keys_back(0),
                lambda: (scatter_cross(1), scatter_begin(0)),
                small_grads,
                lambda: (scatter_cross(0), kv_cross()),
                lambda: (load_tok().wait(), scatter_end(1)),
                lambda: (scatter_end(0), kv_end()),
                gains_begin,
            )
        )
    )
    at_gains = first_back + 13
    stages += tuple((at_gains + j, partial(gains_hop, j)) for j in range(5))

    def body(t, carry):
        pl.when(t < full - 1)(lambda: grad_tile(0, 256 * (t + 1), 256))
        if tail:
            pl.when(t == full - 1)(lambda: grad_tile(0, 256 * full, tail))
        pl.when((t >= 1) & (t < last_up))(lambda: grad_tile(2, 256 * (t - 1), 256))
        if tail:
            pl.when(t == last_up)(lambda: grad_tile(2, 256 * full, tail))
        late = t - last_up - 1
        pl.when((late >= 0) & (late < gate_tiles))(lambda: grad_tile(1, 256 * late, 256))
        for lag, who, action in hops:
            k = t - lag
            pl.when(who & (k >= 0) & (k < K))(partial(action, k))
        for step, action in stages:
            pl.when(t == step)(lambda action=action: action() and None)
        return carry

    lax.fori_loop(0, K + 5, body, 0)
    done = [sum_copies(0)[j] for j in (0, 1)] + [sum_copies(1)[j] for j in (1, 2)]
    done += [far_copy(), *scatter_copies(0), *scatter_copies(1), *kv_copies()]
    done += [sum_copy(j) for j in range(5)] + [col_copy(j) for j in range(3)]
    for copy in done + list(gather_copies()):
        copy.wait_send()


def backward(real_length, tok_t, forward_outs, gain_ffn, weights, gains, head_gains, gain_col, tables):
    features, rows = tok_t.shape
    half = rows // 2
    width = 4 * features
    w_q, w_k, w_v, w_o, w_g, w_u = weights
    hidden, head_dim = w_g.shape[0], w_k.shape[1]
    kv_rows = head_dim // 2
    step_rows, ring = 48, 6
    needed = 3 * hidden + 2 * head_dim + kv_rows
    steps = -(-needed // (4 * step_rows))
    total = 4 * step_rows * steps
    gate_hidden = total // 2 - hidden
    whole = pl.BlockSpec(memory_space=pltpu.VMEM)
    there = pl.BlockSpec(memory_space=pl.ANY)

    def low(*shape):
        return pltpu.VMEM(shape, BF16)

    def high(*shape):
        return pltpu.VMEM(shape, F32)

    slots = [low(n * step_rows * ring, width) for n in (1, 1, 1, 2, 1, 1)]
    return pl.pallas_call(
        partial(backward_kernel, step_rows, steps, ring, gate_hidden),
        out_shape=(
            jax.ShapeDtypeStruct((total, width), BF16),
            jax.ShapeDtypeStruct((features, rows), BF16),
            jax.ShapeDtypeStruct((8, width), F32),
            jax.ShapeDtypeStruct((width, 128), F32),
        ),
        in_specs=[pl.BlockSpec(memory_space=pltpu.SMEM)] + [there] * 14 + [whole] + [there] * 6
        + [whole] * 5,
        out_specs=[there, whole, whole, whole],
        scratch_shapes=[
            low(total, width), *slots,
            low(rows, hidden), low(rows, hidden), low(rows, hidden), low(rows, width),
            low(rows, width), low(2, 2, 256, width), high(half, width), low(2, half, width),
            low(2, half // 2, width), low(2, half // 2, width), low(rows, width), low(rows, width),
            low(rows, width), low(head_dim, width), low(width, 3 * head_dim),
            low(half, 2 * head_dim), low(2, 2, features, half), low(2, features, half),
            high(2, 2, 8, half), high(2, 2, 8, half), low(2, kv_rows, width), low(kv_rows, width),
            low(width, half), high(2, 8, head_dim), high(2, 8, width),
            high(5, 8, width), high(5, 8, width), high(3, features, 128), high(3, features, 128),
            pltpu.SemaphoreType.DMA((20,)), pltpu.SemaphoreType.DMA((2, 2)),
            pltpu.SemaphoreType.DMA((2, steps)), pltpu.SemaphoreType.DMA((11, steps)),
            pltpu.SemaphoreType.DMA((11, steps)), pltpu.SemaphoreType.DMA((33,)),
            pltpu.SemaphoreType.DMA((33,)),
        ],
        name="backward",
        compiler_params=pltpu.CompilerParams(
            collective_id=1, has_side_effects=True, vmem_limit_bytes=63 << 20
        ),
    )(real_length, tok_t, *forward_outs, gain_ffn, *weights, gains, head_gains, gain_col, *tables)


def paired_shards(
    tokens,
    out_grad,
    w_query,
    w_key,
    w_value,
    w_out,
    w_gate,
    w_up,
    w_down,
    gain_in,
    gain_post_attn,
    gain_pre_ffn,
    gain_post_ffn,
    gain_query,
    gain_key,
    bucket_lengths,
    true_lengths,
):
    ctx_index, tp_index = lax.axis_index("ctx"), lax.axis_index("tp")
    rows = tokens.shape[0] // 2
    feature_cols = tokens.shape[1]
    head_dim = w_key.shape[1]
    score_scale = head_dim ** (-0.5)
    g_in, g_pa, g_pf, g_pff, g_q, g_k = [
        gain.astype(F32)
        for gain in (gain_in, gain_post_attn, gain_pre_ffn, gain_post_ffn, gain_query, gain_key)
    ]
    width = 4 * feature_cols
    seq_pos = jnp.arange(2 * rows, dtype=jnp.int32)
    cosines, sines = [table[:, : head_dim // 2] for table in rope_tables(seq_pos, head_dim)]
    real_length = lax.dynamic_slice_in_dim(true_lengths, 1 - ctx_index, 1, 1)
    gains = jnp.stack([g_in, g_pa, g_pf, g_pff])
    head_gains = jnp.stack([g_q, g_k])
    weights = (w_query, w_key, w_value, w_out, w_gate.T, w_up.T, w_down)
    (
        out_t, x16, cot16, n16, raw, q16, kv16, far_kv, att16, attn16, mid16, hid16, dffn16, dg16,
        du16, gain_sum,
    ) = forward(
        real_length, tokens.T, out_grad.T, weights, gains, head_gains, cosines, sines
    )

    gain_col = lax.dynamic_slice_in_dim(g_in, tp_index * feature_cols, feature_cols)
    sums, xg_t, gain_rows, gain_cols = backward(
        real_length, tokens.T,
        (x16, cot16, n16, q16, kv16, far_kv, att16, attn16, mid16, hid16, dffn16, dg16, du16),
        gain_sum, weights[:-1], gains, head_gains, gain_col[:, None], (cosines, sines),
    )
    hidden = w_down.shape[0]
    ends = [hidden, 2 * hidden, 3 * hidden, 3 * hidden + head_dim, 3 * hidden + 2 * head_dim]
    down_sum, gate_sum, up_sum, out_sum, query_sum, mine = [
        sums[start:end] for start, end in zip([0] + ends, ends + [ends[-1] + head_dim // 2])
    ]
    far = lax.ppermute(mine, "tp", XOR2)
    near = lax.ppermute(jnp.stack([mine, far]), "tp", XOR1)
    kv_all = (mine, near[0], far, near[1])
    kv_sum = jnp.concatenate(
        [lax.select_n(tp_index ^ j, *kv_all) for j in range(4)], axis=0
    ).astype(F32).T
    return (
        out_t.T,
        xg_t.T,
        query_sum.astype(F32).T,
        kv_sum[:, :head_dim],
        kv_sum[:, head_dim:],
        out_sum.astype(F32),
        gate_sum.astype(F32).T,
        up_sum.astype(F32).T,
        down_sum.astype(F32),
        gain_cols[:, 0],
        gain_rows[0],
        gain_rows[1],
        gain_rows[2],
        gain_rows[3, :head_dim],
        gain_rows[3, head_dim : 2 * head_dim],
    )


def solution(mesh):
    def layer(*args):
        tokens, bucket_lengths = args[0], args[-2]
        sizes = mesh.shape
        group_rows = tokens.shape[0] // sizes["dp"]
        paired = (sizes["dp"], sizes["ctx"], sizes["tp"]) == (4, 2, 4) and (
            group_rows == 1024 * bucket_lengths.shape[1] == 2048
        )
        return mapped(paired_shards if paired else shards)(*args)

    def mapped(body):
        return jax.shard_map(
            body,
            mesh=mesh,
            in_specs=(
                P(("dp", "ctx"), "tp"),
                P(("dp", "ctx"), "tp"),
                P(None, "tp"),
                P(),
                P(),
                P("tp", None),
                P(None, "tp"),
                P(None, "tp"),
                P("tp", None),
                P(),
                P(),
                P(),
                P(),
                P(),
                P(),
                P("dp", None),
                P("dp", None),
            ),
            out_specs=(
                P(("dp", "ctx"), "tp"),
                P(("dp", "ctx"), "tp"),
                P(None, "tp"),
                P(),
                P(),
                P("tp", None),
                P(None, "tp"),
                P(None, "tp"),
                P("tp", None),
                P(),
                P(),
                P(),
                P(),
                P(),
                P(),
            ),
            check_vma=False,
        )

    return layer
```

```python
import math
from functools import partial

import jax
import jax.numpy as jnp
import numpy as np
from jax import lax
from jax.experimental import pallas as pl
from jax.experimental.pallas import tpu as pltpu
from jax.sharding import PartitionSpec as P

QBLK = 512


EPSILON = 1e-06
ROPE_BASE = 1000000.0
MASKED = -1e30


def contract(left, right, left_dim, right_dim):
    return lax.dot_general(
        left, right, (((left_dim,), (right_dim,)), ((), ())), preferred_element_type=jnp.float32
    )


def rms_norm(values, gain):
    return values * lax.rsqrt(jnp.mean(values * values, axis=-1, keepdims=True) + EPSILON) * gain


def rotate(values, cosine_table, sine_table):
    half_dim = values.shape[-1] // 2
    turned = jnp.concatenate([-values[..., half_dim:], values[..., :half_dim]], axis=-1)
    return values * cosine_table + turned * sine_table


def rope_tables(seq_pos, head_dim):
    freq_index = jnp.arange(head_dim // 2, dtype=jnp.float32)
    inverse = ROPE_BASE ** (-2.0 * freq_index / head_dim)
    angles = seq_pos.astype(jnp.float32)[:, None] * inverse[None, :]
    angles = jnp.concatenate([angles, angles], axis=-1)
    return (jnp.cos(angles), jnp.sin(angles))


def stream_layout(bucket_row, true_row, tok_dev, n_ctx):
    group_rows = tok_dev * n_ctx
    half_shard = tok_dev // 2
    row_ids = jnp.arange(group_rows, dtype=jnp.int32)
    device = row_ids // tok_dev
    half_index = row_ids % tok_dev // half_shard
    block_ids = jnp.where(half_index == 0, device, 2 * n_ctx - 1 - device)
    stream_pos = block_ids * half_shard + row_ids % half_shard
    starts = jnp.cumsum(bucket_row) - bucket_row
    ends = starts + bucket_row
    inside = (
        (stream_pos[:, None] >= starts[None, :]) & (stream_pos[:, None] < ends[None, :])
    ).astype(jnp.int32)
    slot_ids = jnp.arange(bucket_row.shape[0], dtype=jnp.int32)
    seq_ids = jnp.sum(inside * slot_ids[None, :], axis=1)
    seq_pos = stream_pos - jnp.sum(inside * starts[None, :], axis=1)
    is_valid = (seq_pos < jnp.sum(inside * true_row[None, :], axis=1)).astype(jnp.int32)
    return (seq_ids, stream_pos, seq_pos, is_valid)


def shape_heads(query_raw, key_raw, gain_q, gain_k, cosine_table, sine_table):
    query_heads = query_raw.reshape(query_raw.shape[0], -1, key_raw.shape[1])
    query_rot = rotate(
        rms_norm(query_heads, gain_q), cosine_table[:, None, :], sine_table[:, None, :]
    )
    key_rot = rotate(rms_norm(key_raw, gain_k), cosine_table, sine_table)
    return (query_rot, key_rot)


def geglu(gate_in, up_in):
    return jax.nn.gelu(gate_in, approximate=True) * up_in


def shards(
    tokens,
    out_grad,
    w_query,
    w_key,
    w_value,
    w_out,
    w_gate,
    w_up,
    w_down,
    gain_in,
    gain_post_attn,
    gain_pre_ffn,
    gain_post_ffn,
    gain_query,
    gain_key,
    bucket_lengths,
    true_lengths,
):
    n_ctx = lax.axis_size("ctx")
    ctx_index = lax.axis_index("ctx")
    tp_index = lax.axis_index("tp")
    rows_dev = tokens.shape[0]
    feature_cols = tokens.shape[1]
    head_dim = w_key.shape[1]
    head_count = w_query.shape[1] // head_dim
    group_rows = rows_dev * n_ctx
    blocks = rows_dev // QBLK
    score_scale = head_dim ** (-0.5)
    gain_in32, gain_pa32, gain_pf32, gain_pff32, gain_q32, gain_k32 = [
        tensor.astype(jnp.float32)
        for tensor in (gain_in, gain_post_attn, gain_pre_ffn, gain_post_ffn, gain_query, gain_key)
    ]
    input_full, cot_full = (
        lax.all_gather(tokens, "tp", axis=1, tiled=True),
        lax.all_gather(out_grad, "tp", axis=1, tiled=True),
    )
    inputs = input_full.astype(jnp.float32)
    seq_all, spos_all, rpos_all, valid_all = stream_layout(
        bucket_lengths[0], true_lengths[0], rows_dev, n_ctx
    )
    first_row = ctx_index * rows_dev
    seq_local = lax.dynamic_slice_in_dim(seq_all, first_row, rows_dev)
    spos_local = lax.dynamic_slice_in_dim(spos_all, first_row, rows_dev)
    rpos_local = lax.dynamic_slice_in_dim(rpos_all, first_row, rows_dev)
    cosine_table, sine_table = rope_tables(rpos_local, head_dim)
    normed_in, pull_in = jax.vjp(rms_norm, inputs, gain_in32)
    normed_in16 = normed_in.astype(jnp.bfloat16)
    query_raw = jnp.dot(normed_in16, w_query, preferred_element_type=jnp.float32)
    key_raw = jnp.dot(normed_in16, w_key, preferred_element_type=jnp.float32)
    value_raw = jnp.dot(normed_in16, w_value, preferred_element_type=jnp.float32)
    (query_rot, key_rot), rope_pull = jax.vjp(
        partial(shape_heads, cosine_table=cosine_table, sine_table=sine_table),
        query_raw,
        key_raw,
        gain_q32,
        gain_k32,
    )
    query16 = query_rot.astype(jnp.bfloat16)
    key16 = key_rot.astype(jnp.bfloat16)
    value16 = value_raw.astype(jnp.bfloat16)
    key_group, value_group = (
        lax.all_gather(key16, "ctx", axis=0, tiled=True),
        lax.all_gather(value16, "ctx", axis=0, tiled=True),
    )

    def allowed_mask(seq_rows, spos_rows):
        return (
            (valid_all[None, :] == 1)
            & (seq_all[None, :] == seq_rows[:, None])
            & (spos_all[None, :] <= spos_rows[:, None])
        )

    query_blocks = query16.reshape(blocks, QBLK, head_count, head_dim)
    seq_blocks = seq_local.reshape(blocks, QBLK)
    spos_blocks = spos_local.reshape(blocks, QBLK)

    def forward_block(block_item):
        query_block, seq_rows, spos_rows = block_item
        scores = (
            jnp.einsum("qhd,kd->hqk", query_block, key_group, preferred_element_type=jnp.float32)
            * score_scale
        )
        scores = jnp.where(allowed_mask(seq_rows, spos_rows)[None], scores, MASKED)
        row_max = jnp.max(scores, axis=-1, keepdims=True)
        exp_scores = jnp.exp(scores - row_max)
        row_total = jnp.sum(exp_scores, axis=-1, keepdims=True)
        prob_rows = (exp_scores / row_total).astype(jnp.bfloat16)
        output = jnp.einsum(
            "hqk,kd->qhd", prob_rows, value_group, preferred_element_type=jnp.float32
        )
        return (output, (row_max + jnp.log(row_total))[..., 0])

    attended, log_norm = lax.map(forward_block, (query_blocks, seq_blocks, spos_blocks))
    attended16 = attended.reshape(rows_dev, head_count * head_dim).astype(jnp.bfloat16)
    attention = lax.psum(
        jnp.dot(attended16, w_out, preferred_element_type=jnp.float32).astype(jnp.bfloat16), "tp"
    ).astype(jnp.float32)
    post_attn, pull_post_attn = jax.vjp(rms_norm, attention, gain_pa32)
    residual = inputs + post_attn
    normed_mid, pull_pre_ffn = jax.vjp(rms_norm, residual, gain_pf32)
    mid16 = normed_mid.astype(jnp.bfloat16)
    gate_out = jnp.dot(mid16, w_gate, preferred_element_type=jnp.float32)
    up_out = jnp.dot(mid16, w_up, preferred_element_type=jnp.float32)
    hidden, pull_geglu = jax.vjp(geglu, gate_out, up_out)
    hidden16 = hidden.astype(jnp.bfloat16)
    ffn_branch = lax.psum(
        jnp.dot(hidden16, w_down, preferred_element_type=jnp.float32).astype(jnp.bfloat16), "tp"
    ).astype(jnp.float32)
    post_ffn, pull_post_ffn = jax.vjp(rms_norm, ffn_branch, gain_pff32)
    outputs = residual + post_ffn
    out_rows = lax.dynamic_slice_in_dim(outputs, tp_index * feature_cols, feature_cols, 1).astype(
        jnp.bfloat16
    )
    cotangent = cot_full.astype(jnp.float32)
    d_ffn, d_gain_post_ffn = pull_post_ffn(cotangent)
    d_ffn16 = d_ffn.astype(jnp.bfloat16)
    d_hidden = contract(d_ffn16, w_down, 1, 1)
    grad_down = contract(hidden16, d_ffn16, 0, 0)
    d_gate, d_up = pull_geglu(d_hidden)
    d_gate16 = d_gate.astype(jnp.bfloat16)
    d_up16 = d_up.astype(jnp.bfloat16)
    grad_gate = contract(mid16, d_gate16, 0, 0)
    grad_up = contract(mid16, d_up16, 0, 0)
    d_mid = lax.psum(
        (contract(d_gate16, w_gate, 1, 1) + contract(d_up16, w_up, 1, 1)).astype(jnp.bfloat16), "tp"
    ).astype(jnp.float32)
    d_res_norm, d_gain_pre_ffn = pull_pre_ffn(d_mid)
    d_resid = cotangent + d_res_norm
    d_attn, d_gain_post_attn = pull_post_attn(d_resid)
    d_attn16 = d_attn.astype(jnp.bfloat16)
    d_attended16 = contract(d_attn16, w_out, 1, 1).astype(jnp.bfloat16)
    grad_out = contract(attended16, d_attn16, 0, 0)
    key_back, value_back = (key_group, value_group)

    def backward_block(running, block_item):
        key_sum, value_sum = running
        query_block, dout_block, lse_block, seq_rows, spos_rows = block_item
        scores = (
            jnp.einsum("qhd,kd->hqk", query_block, key_back, preferred_element_type=jnp.float32)
            * score_scale
        )
        scores = jnp.where(allowed_mask(seq_rows, spos_rows)[None], scores, MASKED)
        prob_rows = jnp.exp(scores - lse_block[..., None])
        prob16 = prob_rows.astype(jnp.bfloat16)
        d_probs = jnp.einsum(
            "qhd,kd->hqk", dout_block, value_back, preferred_element_type=jnp.float32
        )
        row_inner = jnp.sum(prob_rows * d_probs, axis=-1, keepdims=True)
        d_scores16 = (prob_rows * (d_probs - row_inner)).astype(jnp.bfloat16)
        d_query = (
            jnp.einsum("hqk,kd->qhd", d_scores16, key_back, preferred_element_type=jnp.float32)
            * score_scale
        )
        key_sum = (
            key_sum
            + jnp.einsum("hqk,qhd->kd", d_scores16, query_block, preferred_element_type=jnp.float32)
            * score_scale
        )
        value_sum = value_sum + jnp.einsum(
            "hqk,qhd->kd", prob16, dout_block, preferred_element_type=jnp.float32
        )
        return ((key_sum, value_sum), d_query)

    zero_rows = jnp.zeros((group_rows, head_dim), jnp.float32)
    (key_sum, value_sum), d_query_blocks = lax.scan(
        backward_block,
        (zero_rows, zero_rows),
        (
            query_blocks,
            d_attended16.reshape(blocks, QBLK, head_count, head_dim),
            log_norm,
            seq_blocks,
            spos_blocks,
        ),
    )
    d_key_rot, d_value = (
        lax.psum_scatter(
            key_sum.astype(jnp.bfloat16), "ctx", scatter_dimension=0, tiled=True
        ).astype(jnp.float32),
        lax.psum_scatter(
            value_sum.astype(jnp.bfloat16), "ctx", scatter_dimension=0, tiled=True
        ).astype(jnp.float32),
    )
    d_query_raw, d_key_raw, d_gain_query, d_gain_key = rope_pull(
        (d_query_blocks.reshape(rows_dev, head_count, head_dim), d_key_rot)
    )
    d_query16 = d_query_raw.astype(jnp.bfloat16)
    d_key16 = d_key_raw.astype(jnp.bfloat16)
    d_value16 = d_value.astype(jnp.bfloat16)
    grad_query = contract(normed_in16, d_query16, 0, 0)
    grad_key = contract(normed_in16, d_key16, 0, 0)
    grad_value = contract(normed_in16, d_value16, 0, 0)
    d_normed_part = (
        contract(d_query16, w_query, 1, 1)
        + contract(d_key16, w_key, 1, 1)
        + contract(d_value16, w_value, 1, 1)
    )
    d_normed_in = lax.psum(d_normed_part.astype(jnp.bfloat16), "tp").astype(jnp.float32)
    d_in_norm, d_gain_in = pull_in(d_normed_in)
    d_inputs = d_resid + d_in_norm
    grad_rows = lax.dynamic_slice_in_dim(d_inputs, tp_index * feature_cols, feature_cols, 1).astype(
        jnp.bfloat16
    )
    sharded = (
        grad_query,
        grad_out,
        grad_gate,
        grad_up,
        grad_down,
        d_gain_in,
        d_gain_post_attn,
        d_gain_pre_ffn,
        d_gain_post_ffn,
    )
    reduced = (
        lax.psum_scatter(
            sharded[0].astype(jnp.bfloat16), ("dp", "ctx"), scatter_dimension=0, tiled=True
        ).astype(jnp.float32),
        lax.psum_scatter(
            sharded[1].astype(jnp.bfloat16), ("dp", "ctx"), scatter_dimension=1, tiled=True
        ).astype(jnp.float32),
        lax.psum_scatter(
            sharded[2].astype(jnp.bfloat16), ("dp", "ctx"), scatter_dimension=0, tiled=True
        ).astype(jnp.float32),
        lax.psum_scatter(
            sharded[3].astype(jnp.bfloat16), ("dp", "ctx"), scatter_dimension=0, tiled=True
        ).astype(jnp.float32),
        lax.psum_scatter(
            sharded[4].astype(jnp.bfloat16), ("dp", "ctx"), scatter_dimension=1, tiled=True
        ).astype(jnp.float32),
        lax.psum_scatter(
            sharded[5].astype(jnp.bfloat16), ("dp", "ctx"), scatter_dimension=0, tiled=True
        ).astype(jnp.float32),
        lax.psum_scatter(
            sharded[6].astype(jnp.bfloat16), ("dp", "ctx"), scatter_dimension=0, tiled=True
        ).astype(jnp.float32),
        lax.psum_scatter(
            sharded[7].astype(jnp.bfloat16), ("dp", "ctx"), scatter_dimension=0, tiled=True
        ).astype(jnp.float32),
        lax.psum_scatter(
            sharded[8].astype(jnp.bfloat16), ("dp", "ctx"), scatter_dimension=0, tiled=True
        ).astype(jnp.float32),
    )
    summed = (
        lax.all_gather(reduced[0].astype(jnp.bfloat16), ("dp", "ctx"), axis=0, tiled=True).astype(
            jnp.float32
        ),
        lax.all_gather(reduced[1].astype(jnp.bfloat16), ("dp", "ctx"), axis=1, tiled=True).astype(
            jnp.float32
        ),
        lax.all_gather(reduced[2].astype(jnp.bfloat16), ("dp", "ctx"), axis=0, tiled=True).astype(
            jnp.float32
        ),
        lax.all_gather(reduced[3].astype(jnp.bfloat16), ("dp", "ctx"), axis=0, tiled=True).astype(
            jnp.float32
        ),
        lax.all_gather(reduced[4].astype(jnp.bfloat16), ("dp", "ctx"), axis=1, tiled=True).astype(
            jnp.float32
        ),
        lax.all_gather(reduced[5].astype(jnp.bfloat16), ("dp", "ctx"), axis=0, tiled=True).astype(
            jnp.float32
        ),
        lax.all_gather(reduced[6].astype(jnp.bfloat16), ("dp", "ctx"), axis=0, tiled=True).astype(
            jnp.float32
        ),
        lax.all_gather(reduced[7].astype(jnp.bfloat16), ("dp", "ctx"), axis=0, tiled=True).astype(
            jnp.float32
        ),
        lax.all_gather(reduced[8].astype(jnp.bfloat16), ("dp", "ctx"), axis=0, tiled=True).astype(
            jnp.float32
        ),
    )
    shared = lax.psum((grad_key, grad_value, d_gain_query, d_gain_key), ("dp", "ctx", "tp"))
    return (
        out_rows,
        grad_rows,
        summed[0],
        shared[0],
        shared[1],
        summed[1],
        summed[2],
        summed[3],
        summed[4],
        summed[5],
        summed[6],
        summed[7],
        summed[8],
        shared[2],
        shared[3],
    )


XOR1 = ((0, 1), (1, 0), (2, 3), (3, 2))
XOR2 = ((0, 2), (2, 0), (1, 3), (3, 1))
MESH = pl.DeviceIdType.MESH
GELU_SCALE = math.sqrt(2.0 / math.pi)
F32 = jnp.float32
BF16 = jnp.bfloat16


def add16(left, right):
    return (left.astype(F32) + right.astype(F32)).astype(BF16)


def block_tables(length, head_dim):
    freq_index = np.arange(head_dim // 2, dtype=np.float32)
    inverse = np.float32(ROPE_BASE) ** (np.float32(-2.0) * freq_index / np.float32(head_dim))
    angles = np.arange(length, dtype=np.float32)[:, None] * inverse.astype(np.float32)[None, :]
    angles = angles.astype(np.float64)
    return np.cos(angles).astype(np.float32), np.sin(angles).astype(np.float32)


def scale_of(values):
    return lax.rsqrt(jnp.mean(values * values, axis=-1, keepdims=True) + EPSILON)


STORED = 13


def row_blocks(base, rows, size, body, carry=None):
    def step(i, state):
        at = pl.ds(pl.multiple_of(base + i * size, size), size)
        return body(at, pl.ds(pl.multiple_of(i * size, size), size), state)

    return lax.fori_loop(0, rows // size, step, carry)


def spread_gains(packed, gains, head_gains):
    columns = gains.shape[1] // 128
    for j in range(4):
        for i in range(columns):
            at = j * columns + i
            gains[j : j + 1, 128 * i : 128 * i + 128] = packed[at : at + 1, :]
    head_columns = head_gains.shape[1] // 128
    for j in range(2):
        for i in range(head_columns):
            at = 4 * columns + j * head_columns + i
            head_gains[j : j + 1, 128 * i : 128 * i + 128] = packed[at : at + 1, :]


def turn_in(source, target, rows):
    for first in range(0, source.shape[0], 128):
        target[rows, first : first + 128] = source[first : first + 128, :].T


def column_tiles(total, size):
    return [(first, min(size, total - first)) for first in range(0, total, size)]


def dot_nn(left, right):
    return jnp.dot(left, right, preferred_element_type=F32)


def dot_nt(left, right):
    return contract(left, right, 1, 1)


def gelu_parts(gate):
    square = gate * gate
    tanh = jnp.tanh(GELU_SCALE * gate * (1.0 + 0.044715 * square))
    half = 0.5 + 0.5 * tanh
    slope = GELU_SCALE * (1.0 + 3.0 * 0.044715 * square)
    return gate * half, half + 0.5 * gate * (1.0 - tanh * tanh) * slope


def forward_kernel(
    real_lengths, tok, cot, w_q, w_k, w_v, w_o, w_g, w_u, w_d, packed, cosines, sines,
    out_t, gain_sum, *refs,
):
    stored, refs = refs[:STORED], refs[STORED:]
    kept, refs = refs[:STORED], refs[STORED:]
    x16, cot16, n16, q16, kv16, far_kv, att16, attn16, mid16, hid16, dffn16, dg16, du16 = kept
    blocks, v_qkv, v_o, v_g, v_u, v_d, part, near, far, ffn16, gains, head_gains = refs[:12]
    load_sem, own_sem, store_sem, g_send, g_recv, kv_send, kv_recv, s_send, s_recv = refs[12:]
    dp, ctx, tp = lax.axis_index("dp"), lax.axis_index("ctx"), lax.axis_index("tp")
    core_peer = (dp, ctx, tp + 1 - 2 * (tp % 2))
    x_index = (tp + 2) % 4
    x_peer = (dp, ctx, x_index)
    y_peer = (dp, 1 - ctx, tp)
    features, rows = tok.shape[0], tok.shape[1] // 2
    width = 4 * features
    hidden = w_d.shape[0]
    head_dim = w_k.shape[1]
    half = rows // 2
    odd = tp % 2

    loads = [
        pltpu.make_async_copy(source, target, load_sem.at[j])
        for j, (source, target) in enumerate(
            (
                (w_q, v_qkv.at[:, 0:head_dim]),
                (w_k, v_qkv.at[:, head_dim : 2 * head_dim]),
                (w_v, v_qkv.at[:, 2 * head_dim : 3 * head_dim]),
                (w_o, v_o), (w_g, v_g), (w_u, v_u), (w_d, v_d),
            )
        )
    ]
    for copy in loads:
        copy.start()

    def half_of(source, index):
        lane = (ctx if index % 2 == 0 else 1 - ctx) * rows
        return source.at[:, pl.ds(pl.multiple_of(lane, rows), rows)]

    def place(index, owner):
        return blocks.at[index, pl.ds(pl.multiple_of(owner * features, features), features)]

    sources = [half_of(tok, 0), half_of(tok, 1), half_of(cot, 0), half_of(cot, 1)]

    def remote(source, target, send, recv, peer):
        return pltpu.make_async_remote_copy(
            src_ref=source, dst_ref=target, send_sem=send, recv_sem=recv,
            device_id=peer, device_id_type=MESH,
        )

    own = [pltpu.make_async_copy(sources[j], place(j, tp), own_sem.at[j]) for j in range(4)]
    to_x = [
        remote(sources[j], place(j, tp), g_send.at[0, j], g_recv.at[0, j], x_peer) for j in range(4)
    ]
    to_core = [
        remote(sources[j], place(j, tp), g_send.at[1, j], g_recv.at[1, j], core_peer)
        for j in range(4)
    ]
    onward = [
        remote(place(j, x_index), place(j, x_index), g_send.at[2, j], g_recv.at[2, j], core_peer)
        for j in range(4)
    ]
    for copy in own:
        copy.start()
    barrier = pltpu.get_barrier_semaphore()
    for peer in (core_peer, x_peer, y_peer):
        pl.semaphore_signal(barrier, inc=1, device_id=peer, device_id_type=MESH)
    pl.semaphore_wait(barrier, 3)

    for j in range(4):
        to_core[j].start()
    to_x[0].start()
    to_x[1].start()

    spread_gains(packed, gains, head_gains)

    def store(j, c):
        at = slice(None) if c is None else chunk(c)
        return pltpu.make_async_copy(kept[j].at[at], stored[j].at[at], store_sem.at[j, c or 0])

    def pass_on(j):
        to_x[j].wait_recv()
        onward[j].start()

    def gathered(j):
        own[j].wait()
        to_core[j].wait_recv()
        onward[j].wait_recv()

    def chunk(c):
        return pl.ds(c * rows, rows)

    def project(c):
        turn_in(blocks.at[c], x16, chunk(c))

        def norm(at, _, carry):
            values = x16[at, :].astype(F32)
            n16[at, :] = (values * scale_of(values) * gains[0:1, :]).astype(BF16)

        row_blocks(c * rows, rows, 64, norm)
        for first in range(0, rows, half):
            at = pl.ds(c * rows + first, half)
            tables = pl.ds(c * rows + first, half)
            values = dot_nn(n16[at, :], v_qkv[...])
            cosine, sine = cosines[tables, :], sines[tables, :]
            for j, target in ((0, q16.at[at, :]), (1, kv16.at[at, 0:head_dim])):
                head = values[:, j * head_dim : (j + 1) * head_dim]
                head = head * scale_of(head) * head_gains[j : j + 1, :]
                low, high = head[:, : head_dim // 2], head[:, head_dim // 2 :]
                target[:, : head_dim // 2] = (low * cosine - high * sine).astype(BF16)
                target[:, head_dim // 2 :] = (high * cosine + low * sine).astype(BF16)
            kv16[at, head_dim:] = values[:, 2 * head_dim :].astype(BF16)

    score_scale = head_dim ** (-0.5)

    def attend_rows(c):
        for first in range(0, rows, half):
            at = pl.ds(c * rows + first, half)
            query = q16[at, :]
            row_id = first + lax.broadcasted_iota(jnp.int32, (half, rows), 0)
            key_id = lax.broadcasted_iota(jnp.int32, (half, rows), 1)
            allowed = key_id <= row_id
            if c == 1:
                allowed = allowed & (rows + key_id < real_lengths[0, 1 - ctx])
            keys = [(kv16[chunk(c), :head_dim], kv16[chunk(c), head_dim:], allowed)]
            if c == 1:
                keys.append((far_kv[:, :head_dim], far_kv[:, head_dim:], None))
            scores = []
            for key, _, mask in keys:
                score = dot_nt(query, key) * score_scale
                scores.append(score if mask is None else jnp.where(mask, score, MASKED))
            most = scores[0].max(axis=1, keepdims=True)
            for score in scores[1:]:
                most = jnp.maximum(most, score.max(axis=1, keepdims=True))
            exps = [jnp.exp(score - most) for score in scores]
            total = sum(e.sum(axis=1, keepdims=True) for e in exps)
            out = sum(dot_nn((e / total).astype(BF16), k[1]) for e, k in zip(exps, keys))
            att16[at, :] = out.astype(BF16)
        part[c] = dot_nn(att16[chunk(c), :], v_o[...]).astype(BF16)

    def rows_of(index):
        return pl.ds(pl.multiple_of(index * half, half), half)

    def sum_copies(s, target):
        start = pl.multiple_of((s % 2) * rows + odd * half, half)
        final = target.at[pl.ds(start, half)]
        return (
            remote(part.at[s, rows_of(1 - odd)], near.at[s], s_send.at[0, s], s_recv.at[0, s], core_peer),
            remote(near.at[s], far.at[s], s_send.at[1, s], s_recv.at[1, s], x_peer),
            remote(final, final, s_send.at[2, s], s_recv.at[2, s], core_peer),
        )

    def sum_start(s, target):
        sum_copies(s, target)[0].start()

    def sum_cross(s, target):
        copies = sum_copies(s, target)
        copies[0].wait_recv()
        near[s] = add16(part[s, rows_of(odd)], near[s])
        copies[1].start()

    def sum_back(s, target):
        copies = sum_copies(s, target)
        copies[1].wait_recv()
        start = pl.multiple_of((s % 2) * rows + odd * half, half)
        target[pl.ds(start, half), :] = add16(near[s], far[s])
        copies[2].start()
        copies[2].wait_recv()

    def residual(at):
        branch = attn16[at, :].astype(F32)
        return x16[at, :].astype(F32) + branch * scale_of(branch) * gains[1:2, :]

    def middle(c):
        def body(at, _, carry):
            values = residual(at)
            mid16[at, :] = (values * scale_of(values) * gains[2:3, :]).astype(BF16)

        row_blocks(c * rows, rows, 64, body)

    def feed(c):
        for first, size in column_tiles(hidden, 256):
            for low in range(0, rows, half):
                at = pl.ds(c * rows + low, half)
                cols = pl.ds(first, size)
                gate = dot_nt(mid16[at, :], v_g[cols, :])
                up = dot_nt(mid16[at, :], v_u[cols, :])
                act, slope = gelu_parts(gate)
                hid16[at, cols] = (act * up).astype(BF16)
                dg16[at, cols] = (slope * up).astype(BF16)
                du16[at, cols] = act.astype(BF16)
        for first, size in column_tiles(width, 256):
            cols = pl.ds(first, size)
            part[2 + c, :, cols] = dot_nn(hid16[chunk(c), :], v_d[:, cols]).astype(BF16)

    def finish(c):
        turn_in(blocks.at[2 + c], cot16, chunk(c))
        sum_copies(c, attn16)[0].wait_send()
        onward[c].wait_send()

        def body(at, block, total):
            branch = ffn16[at, :].astype(F32)
            scale = scale_of(branch)
            unit = branch * scale
            grad = cot16[at, :].astype(F32)
            part[c, block, :] = (residual(at) + unit * gains[3:4, :]).astype(BF16)
            weighted = grad * gains[3:4, :]
            inner = jnp.mean(unit * weighted, axis=-1, keepdims=True)
            dffn16[at, :] = (scale * (weighted - unit * inner)).astype(BF16)
            return total + (grad * unit).reshape(-1, 8, width).sum(axis=0)

        total = row_blocks(c * rows, rows, 64, body, jnp.zeros((8, width), F32))
        if c == 0:
            gain_sum[...] = total
        else:
            gain_sum[...] += total
        for first in range(0, width, 128):
            blocks[c, first : first + 128, :] = part[c, :, first : first + 128].T
        lane = (ctx if c == 0 else 1 - ctx) * rows
        mine = blocks[c, pl.ds(pl.multiple_of(tp * features, features), features), :]
        out_t[:, pl.ds(pl.multiple_of(lane, rows), rows)] = mine

    def feed_back(c):
        for first, size in column_tiles(hidden, 256):
            for low in range(0, rows, half):
                at = pl.ds(c * rows + low, half)
                cols = pl.ds(first, size)
                d_hidden = dot_nt(dffn16[at, :], v_d[cols, :])
                dg16[at, cols] = (d_hidden * dg16[at, cols].astype(F32)).astype(BF16)
                du16[at, cols] = (d_hidden * du16[at, cols].astype(F32)).astype(BF16)

    kv_copy = remote(kv16.at[chunk(0)], far_kv, kv_send.at[0], kv_recv.at[0], y_peer)
    X, COT, N, Q, KV, FAR, ATT, ATTN, MID, HID, DFFN, DG, DU = range(STORED)
    started = []

    def store_all(c, *which):
        for j in which:
            store(j, c).start()
            started.append((j, c))

    pass_on(0)
    for copy in loads[:3]:
        copy.wait()
    gathered(0)
    project(0)
    kv_copy.start()
    store_all(0, X, N, Q, KV)
    pass_on(1)
    to_x[2].start()
    to_x[3].start()
    loads[3].wait()
    attend_rows(0)
    sum_start(0, attn16)
    gathered(1)
    project(1)
    store_all(1, X, N, Q, KV)
    sum_cross(0, attn16)
    kv_copy.wait_recv()
    attend_rows(1)
    sum_start(1, attn16)
    store_all(None, FAR)
    store_all(0, ATT)
    store_all(1, ATT)
    pass_on(2)
    pass_on(3)
    sum_cross(1, attn16)
    sum_back(0, attn16)
    for copy in loads[4:]:
        copy.wait()
    middle(0)
    store_all(0, ATTN, MID)
    feed(0)
    sum_start(2, ffn16)
    store_all(0, HID)
    sum_back(1, attn16)
    middle(1)
    store_all(1, ATTN, MID)
    sum_cross(2, ffn16)
    feed(1)
    sum_start(3, ffn16)
    store_all(1, HID)
    gathered(2)
    gathered(3)
    sum_back(2, ffn16)
    sum_cross(3, ffn16)
    finish(0)
    store_all(0, COT, DFFN)
    feed_back(0)
    store_all(0, DG, DU)
    sum_back(3, ffn16)
    finish(1)
    store_all(1, COT, DFFN)
    feed_back(1)
    store_all(1, DG, DU)
    for group in (to_x, to_core, onward[2:], [kv_copy]):
        for copy in group:
            copy.wait_send()
    for s, target in ((0, attn16), (1, attn16), (2, ffn16), (3, ffn16)):
        for copy in sum_copies(s, target)[1 if s < 2 else 0 :]:
            copy.wait_send()
    for j, c in started:
        store(j, c).wait()


def forward(real_lengths, tok_t, cot_t, weights, packed, tables):
    features, rows = tok_t.shape
    half = rows // 2
    width = 4 * features
    hidden = weights[-1].shape[0]
    head_dim = weights[1].shape[1]
    whole = pl.BlockSpec(memory_space=pltpu.VMEM)
    there = pl.BlockSpec(memory_space=pl.ANY)
    kept = [
        (rows, width), (rows, width), (rows, width), (rows, head_dim), (rows, 2 * head_dim),
        (half, 2 * head_dim), (rows, head_dim), (rows, width), (rows, width), (rows, hidden),
        (rows, width), (rows, hidden), (rows, hidden),
    ]

    return pl.pallas_call(
        forward_kernel,
        out_shape=(
            jax.ShapeDtypeStruct((features, rows), BF16), jax.ShapeDtypeStruct((8, width), F32),
            *[jax.ShapeDtypeStruct(shape, BF16) for shape in kept],
        ),
        in_specs=[pl.BlockSpec(memory_space=pltpu.SMEM)] + [there] * 9 + [whole] * 3,
        out_specs=[whole] * 2 + [there] * STORED,
        scratch_shapes=[pltpu.VMEM(shape, BF16) for shape in kept]
        + [
            pltpu.VMEM((4, width, half), BF16),
            pltpu.VMEM((width, 3 * head_dim), BF16),
            pltpu.VMEM((head_dim, width), BF16),
            pltpu.VMEM((hidden, width), BF16),
            pltpu.VMEM((hidden, width), BF16),
            pltpu.VMEM((hidden, width), BF16),
            pltpu.VMEM((4, half, width), BF16),
            pltpu.VMEM((4, half // 2, width), BF16),
            pltpu.VMEM((4, half // 2, width), BF16),
            pltpu.VMEM((rows, width), BF16),
            pltpu.VMEM((4, width), F32),
            pltpu.VMEM((2, head_dim), F32),
            pltpu.SemaphoreType.DMA((7,)),
            pltpu.SemaphoreType.DMA((4,)),
            pltpu.SemaphoreType.DMA((STORED, 2)),
            pltpu.SemaphoreType.DMA((3, 4)),
            pltpu.SemaphoreType.DMA((3, 4)),
            pltpu.SemaphoreType.DMA((1,)),
            pltpu.SemaphoreType.DMA((1,)),
            pltpu.SemaphoreType.DMA((3, 4)),
            pltpu.SemaphoreType.DMA((3, 4)),
        ],
        name="forward",
        compiler_params=pltpu.CompilerParams(
            collective_id=2, has_side_effects=True, vmem_limit_bytes=63 << 20
        ),
    )(real_lengths, tok_t, cot_t, *weights, packed, *tables)


def backward_kernel(
    step_rows, steps, steps_low, lag, ring, gate_hidden,
    real_lengths, tok, x_in, cot_in, n_in, q_in, kv_in, far_in, att_in, attn_in, mid_in, hid_in,
    dffn_in, dg_in, du_in, gain_ffn, w_q, w_k, w_v, w_o, w_g, w_u, packed, cosines, sines,
    out, xg_t, gain_rows, gain_cols,
    g, y2, z2, m2, z1, m1, y1, hid, dg, du, mid, dffn, w_tiles, part, near, far, dm, cot, attn,
    v_o, v_qkv, dkv_new, norm_near, norm_far, row_part,
    row_near, kv_near, kv_far, turned, head_sums, row_sums, sum_slots, sum_new, col_slots,
    col_new, gains, head_gains, gain_col,
    load_sem, tile_sem, keep_sem, chain_send, chain_recv, peer_send, peer_recv,
):
    dp, ctx, tp = lax.axis_index("dp"), lax.axis_index("ctx"), lax.axis_index("tp")
    s, K, low_steps = step_rows, steps, steps_low
    upper = dp // 2
    odd = tp % 2
    outer = (dp == 0) | (dp == 3)
    inner = jnp.logical_not(outer)
    yes = dp >= 0
    core_index = tp + 1 - 2 * odd
    x_index = (tp + 2) % 4
    cross_index = (core_index + 2) % 4
    z_index = dp + 1 - 2 * (dp % 2)
    core_peer, x_peer = (dp, ctx, core_index), (dp, ctx, x_index)
    y_peer, z_peer, m_peer = (dp, 1 - ctx, tp), (z_index, ctx, tp), (3 - dp, ctx, tp)
    features, rows = tok.shape[0], tok.shape[1] // 2
    width = 4 * features
    hidden = w_g.shape[0]
    head_dim = w_k.shape[1]
    half = rows // 2
    kv_rows = head_dim // 2
    score_scale = head_dim ** (-0.5)

    def remote(source, target, send, recv, peer):
        return pltpu.make_async_remote_copy(
            src_ref=source, dst_ref=target, send_sem=send, recv_sem=recv,
            device_id=peer, device_id_type=MESH,
        )

    def chunk(c):
        return pl.ds(c * rows, rows)

    def multiple(start, size):
        return pl.ds(pl.multiple_of(start, size), size)

    dqkv, kv16 = dg.at[:, 0 : 3 * head_dim], dg.at[:, 3 * head_dim : 5 * head_dim]
    dkv, dkv_far = du.at[:, 0 : 2 * head_dim], du.at[0:rows, 2 * head_dim : 4 * head_dim]
    far_kv = du.at[rows : 2 * rows, 2 * head_dim : 4 * head_dim]
    q16, att = du.at[:, 4 * head_dim : 5 * head_dim], du.at[:, 5 * head_dim : 6 * head_dim]

    tok_own = dm.at[0:features, 0 : 2 * rows]

    pairs = (
        (hid_in, hid), (dffn_in, dffn), (dg_in, dg), (mid_in, mid), (du_in, du), (cot_in, cot),
        (attn_in, attn), (w_o, v_o),
        (w_q, v_qkv.at[:, 0:head_dim]), (w_k, v_qkv.at[:, head_dim : 2 * head_dim]),
        (w_v, v_qkv.at[:, 2 * head_dim : 3 * head_dim]),
    )
    count = len(pairs)

    def load(j):
        return pltpu.make_async_copy(pairs[j][0], pairs[j][1], load_sem.at[j])

    late_pairs = (
        (x_in, dffn), (n_in, mid), (q_in, q16), (kv_in, kv16), (far_in, far_kv), (att_in, att),
    )

    def load_tok():
        return pltpu.make_async_copy(tok, tok_own, load_sem.at[count + len(late_pairs)])

    def late_load(j):
        return pltpu.make_async_copy(late_pairs[j][0], late_pairs[j][1], load_sem.at[count + j])

    for j in range(count):
        load(j).start()
    barrier = pltpu.get_barrier_semaphore()
    for peer in (core_peer, x_peer, y_peer, z_peer, m_peer):
        pl.semaphore_signal(barrier, inc=1, device_id=peer, device_id_type=MESH)
    pl.semaphore_wait(barrier, 5)

    base = 2 * s * K

    def rows2(k, h):
        return multiple((2 * k + h) * s, s)

    def rows1(k, h):
        return multiple(base + (2 * k + h) * s, s)

    def pair1(k):
        return pl.ds(pl.multiple_of(base + 2 * k * s, s), 2 * s)

    def slot(k):
        return multiple((k % ring) * s, s)

    def slot_pair(k):
        return multiple((k % ring) * 2 * s, 2 * s)

    def slot_half(k, h):
        return multiple(((k % ring) * 2 + h) * s, s)

    def chain(j, k, source, target, peer):
        return remote(source, target, chain_send.at[j, k], chain_recv.at[j, k], peer)

    def keep(j, k, source, target):
        return pltpu.make_async_copy(source, target, keep_sem.at[j, k])

    def c_y2(k):
        return chain(0, k, g.at[rows2(k, 1 - ctx)], y2.at[slot(k)], y_peer)

    def c_z2(k):
        return chain(1, k, y2.at[slot(k)], z2.at[slot(k)], z_peer)

    def c_m2(k):
        return chain(2, k, z2.at[slot(k)], m2.at[slot(k)], m_peer)

    def c_fo(k):
        return chain(3, k, m2.at[slot(k)], out.at[rows2(k, ctx)], z_peer)

    def c_fy(k):
        return chain(4, k, m2.at[slot(k)], out.at[rows2(k, ctx)], y_peer)

    def c_fy_outer(k):
        return chain(4, k, out.at[rows2(k, ctx)], out.at[rows2(k, ctx)], y_peer)

    def c_z1(k):
        return chain(5, k, g.at[pair1(k)], z1.at[slot_pair(k)], z_peer)

    def c_m1(k):
        return chain(6, k, z1.at[slot_half(k, 1 - upper)], m1.at[slot(k)], m_peer)

    def c_y1(k):
        return chain(7, k, m1.at[slot(k)], y1.at[slot(k)], y_peer)

    def c_fm(k):
        return chain(8, k, y1.at[slot(k)], out.at[rows1(k, upper)], m_peer)

    def c_fa(k):
        return chain(9, k, y1.at[slot(k)], out.at[rows1(k, upper)], z_peer)

    def c_fb(k):
        return chain(10, k, out.at[rows1(k, 1 - upper)], out.at[rows1(k, 1 - upper)], z_peer)

    def keep2(k):
        return keep(0, k, m2.at[slot(k)], out.at[rows2(k, ctx)])

    def keep1(k):
        return keep(1, k, y1.at[slot(k)], out.at[rows1(k, upper)])

    def b2(k):
        c_y2(k).wait_recv()
        y2[slot(k), :] = add16(y2[slot(k), :], g[rows2(k, ctx), :])
        pl.when(outer)(lambda: c_z2(k).start())

    def b1(k):
        c_z1(k).wait_recv()
        z1[slot_pair(k), :] = add16(z1[slot_pair(k), :], g[pair1(k), :])
        c_m1(k).start()

    def c2(k):
        c_z2(k).wait_recv()
        z2[slot(k), :] = add16(z2[slot(k), :], y2[slot(k), :])
        c_m2(k).start()

    def c1(k):
        c_m1(k).wait_recv()
        m1[slot(k), :] = add16(m1[slot(k), :], z1[slot_half(k, upper), :])
        c_y1(k).start()

    def d2(k):
        c_m2(k).wait_recv()
        m2[slot(k), :] = add16(m2[slot(k), :], z2[slot(k), :])
        c_fo(k).start()
        c_fy(k).start()
        keep2(k).start()

    def d1(k):
        c_y1(k).wait_recv()
        y1[slot(k), :] = add16(y1[slot(k), :], m1[slot(k), :])
        c_fm(k).start()
        c_fa(k).start()
        keep1(k).start()

    def e2(k):
        c_fo(k).wait_recv()
        c_fy_outer(k).start()

    def e1(k):
        c_fm(k).wait_recv()
        c_fb(k).start()

    def f2(k):
        c_fy(k).wait_recv()
        c_y2(k).wait_send()

    def f2_outer(k):
        c_fy_outer(k).wait_send()

    def f1_outer(k):
        c_fa(k).wait_recv()
        c_fb(k).wait_recv()
        c_z1(k).wait_send()

    def f2_inner(k):
        keep2(k).wait()
        c_fo(k).wait_send()
        c_fy(k).wait_send()

    def f1_inner(k):
        keep1(k).wait()
        for copy in (c_fm, c_fa, c_fb):
            copy(k).wait_send()

    hops = (
        (5, yes, K, f2), (5, outer, K, f2_outer), (5, outer, low_steps, f1_outer),
        (5, inner, K, f2_inner), (5, inner, low_steps, f1_inner),
        (4, inner, K, lambda k: c_m2(k).wait_send()),
        (4, inner, low_steps, lambda k: c_y1(k).wait_send()),
        (3, outer, K, lambda k: c_z2(k).wait_send()),
        (3, inner, low_steps, lambda k: c_m1(k).wait_send()),
        (4, outer, K, e2),
        (4, inner, low_steps, e1), (3, inner, K, d2), (3, inner, low_steps, d1), (2, inner, K, c2),
        (2, inner, low_steps, c1), (1, yes, K, b2), (1, inner, low_steps, b1),
        (0, yes, K, lambda k: c_y2(k).start()), (0, outer, low_steps, lambda k: c_z1(k).start()),
    )

    def grad_tile(index, first, size):
        left, right = ((hid, dffn), (dg, mid), (du, mid))[index]
        at = first if isinstance(first, int) else pl.multiple_of(first, 256)
        tile = contract(left[:, pl.ds(at, size)], right[...], 0, 0)
        start = index * hidden + first
        g[pl.ds(start if isinstance(start, int) else pl.multiple_of(start, 64), size), :] = (
            tile.astype(BF16)
        )

    full = hidden // 256
    tail = hidden - 256 * full

    mid_tiles = column_tiles(width, 256)

    def fetch(j):
        first, size = mid_tiles[j % len(mid_tiles)]
        return [
            pltpu.make_async_copy(
                w.at[:, pl.ds(first, size)], w_tiles.at[i, j % 2, :, pl.ds(0, size)],
                tile_sem.at[i, j % 2],
            )
            for i, w in enumerate((w_g, w_u))
        ]

    def mid_part(c, low, high):
        base = (1 - c) * len(mid_tiles)
        for j in range(base + low, base + high):
            first, size = mid_tiles[j - base]
            if j + 1 < 2 * len(mid_tiles):
                for copy in fetch(j + 1):
                    copy.start()
            for copy in fetch(j):
                copy.wait()
            term = dot_nn(dg[chunk(c), :], w_tiles[0, j % 2, :, 0:size]) + dot_nn(
                du[chunk(c), :], w_tiles[1, j % 2, :, 0:size]
            )
            part[c, :, pl.ds(first, size)] = term.astype(BF16)

    def own_half(index):
        return multiple(index * half, half)

    def peer_copy(j, source, target, peer):
        return remote(source, target, peer_send.at[j], peer_recv.at[j], peer)

    def sum_copies(c):
        final = dm.at[multiple(c * rows + odd * half, half)]
        return (
            peer_copy(3 * c, part.at[c, own_half(1 - odd)], near.at[c], core_peer),
            peer_copy(3 * c + 1, near.at[c], far.at[c], x_peer),
            peer_copy(3 * c + 2, final, final, core_peer),
        )

    mid_split = (len(mid_tiles) + 1) // 2

    def sum_begin(c):
        mid_part(c, mid_split, len(mid_tiles))
        sum_copies(c)[0].start()

    def sum_cross(c):
        copies = sum_copies(c)
        copies[0].wait_recv()
        near[c] = add16(part[c, own_half(odd)], near[c])
        copies[1].start()

    def sum_back(c):
        copies = sum_copies(c)
        copies[1].wait_recv()
        dm[multiple(c * rows + odd * half, half), :] = add16(near[c], far[c])
        copies[2].start()

    def norms_back(c, second):
        if not second:
            sum_copies(c)[2].wait_recv()

        def body(at, _, state):
            branch = attn[at, :].astype(F32)
            scale_a = scale_of(branch)
            unit_a = branch * scale_a
            resid = dffn[at, :].astype(F32) + unit_a * gains[1:2, :]
            scale_r = scale_of(resid)
            unit_r = resid * scale_r
            grad = dm[at, :].astype(F32)
            weighted = grad * gains[2:3, :]
            mean = jnp.mean(unit_r * weighted, axis=-1, keepdims=True)
            d_resid = cot[at, :].astype(F32) + scale_r * (weighted - unit_r * mean)
            weighted = d_resid * gains[1:2, :]
            mean = jnp.mean(unit_a * weighted, axis=-1, keepdims=True)
            cot[at, :] = d_resid.astype(BF16)
            attn[at, :] = (scale_a * (weighted - unit_a * mean)).astype(BF16)
            return (
                state[0] + (d_resid * unit_a).reshape(-1, 8, width).sum(axis=0),
                state[1] + (grad * unit_r).reshape(-1, 8, width).sum(axis=0),
            )

        zero = jnp.zeros((8, width), F32)
        sum_a, sum_r = row_blocks(c * rows + second * half, half, 64, body, (zero, zero))
        if c == 1 and not second:
            row_sums[0], row_sums[1] = sum_a, sum_r
        else:
            row_sums[0] += sum_a
            row_sums[1] += sum_r

    def head_back(grad, at, j):
        cosine, sine = cosines[at, :], sines[at, :]
        low, high = grad[:, : head_dim // 2], grad[:, head_dim // 2 :]
        grad = jnp.concatenate([low * cosine + high * sine, high * cosine - low * sine], axis=1)
        cols = pl.ds(j * head_dim, head_dim)
        raw = dot_nn(mid[at, :], v_qkv[:, cols])
        scale = scale_of(raw)
        unit = raw * scale
        weighted = grad * head_gains[j : j + 1, :]
        mean = jnp.mean(unit * weighted, axis=-1, keepdims=True)
        dqkv[at, cols] = (scale * (weighted - unit * mean)).astype(BF16)
        head_sums[j] += (grad * unit).reshape(-1, 8, head_dim).sum(axis=0)

    def attend_back_rows(c, second):
        d_keys, d_values = [0.0, 0.0], [0.0, 0.0]
        for first in (second * half,):
            at = pl.ds(c * rows + first, half)
            query = q16[at, :]
            d_out = dot_nt(attn[at, :], v_o[...]).astype(BF16)
            row_id = first + lax.broadcasted_iota(jnp.int32, (half, rows), 0)
            key_id = lax.broadcasted_iota(jnp.int32, (half, rows), 1)
            allowed = key_id <= row_id
            if c == 1:
                allowed = allowed & (rows + key_id < real_lengths[0, 1 - ctx])
            keys = [(kv16[chunk(c), :head_dim], kv16[chunk(c), head_dim:], allowed)]
            if c == 1:
                keys.append((far_kv[:, :head_dim], far_kv[:, head_dim:], None))
            scores = []
            for key, _, mask in keys:
                score = dot_nt(query, key) * score_scale
                scores.append(score if mask is None else jnp.where(mask, score, MASKED))
            most = scores[0].max(axis=1, keepdims=True)
            for score in scores[1:]:
                most = jnp.maximum(most, score.max(axis=1, keepdims=True))
            exps = [jnp.exp(score - most) for score in scores]
            total = sum(e.sum(axis=1, keepdims=True) for e in exps)
            probs = [e / total for e in exps]
            d_probs = [dot_nt(d_out, key[1]) for key in keys]
            mean = sum((p * d).sum(axis=1, keepdims=True) for p, d in zip(probs, d_probs))
            d_query = 0.0
            for i, key in enumerate(keys):
                d_score = (probs[i] * (d_probs[i] - mean)).astype(BF16)
                d_query += dot_nn(d_score, key[0])
                d_keys[i] += contract(d_score, query, 0, 0)
                d_values[i] += contract(probs[i].astype(BF16), d_out, 0, 0)
            head_back(d_query * score_scale, at, 0)
        places = [dkv.at[chunk(c), :]] + [dkv_far] * c
        for i, place in enumerate(places):
            for cols, term in (
                (pl.ds(0, head_dim), d_keys[i] * score_scale),
                (pl.ds(head_dim, head_dim), d_values[i]),
            ):
                if second:
                    term = term + place[:, cols].astype(F32)
                place[:, cols] = term.astype(BF16)
        if c == 1 and second:
            far_copies()[0].start()

    quarter = half // 2
    far_rows = multiple(odd * half + tp // 2 * quarter, quarter)

    def far_copies():
        given = dkv_far.at[multiple(odd * half + (1 - tp // 2) * quarter, quarter), :]
        return (
            peer_copy(33, dkv_far.at[own_half(1 - odd), :], dkv_new.at[0:half], core_peer),
            peer_copy(34, given, dkv_new.at[half : half + quarter], x_peer),
            peer_copy(6, dkv_far.at[far_rows, :], dkv_new.at[half + quarter : 2 * half], y_peer),
        )

    def far_cross():
        copies = far_copies()
        copies[0].wait_recv()
        dkv_far[own_half(odd), :] = add16(dkv_far[own_half(odd), :], dkv_new[0:half, :])
        copies[1].start()

    def far_up():
        copies = far_copies()
        copies[1].wait_recv()
        dkv_far[far_rows, :] = add16(dkv_far[far_rows, :], dkv_new[half : half + quarter, :])
        copies[2].start()

    def keys_back(c):
        if c == 0:
            far_copies()[2].wait_recv()
            dkv[far_rows, :] = add16(dkv[far_rows, :], dkv_new[half + quarter : 2 * half, :])
        for first in range(0, rows, half):
            at = pl.ds(c * rows + first, half)
            grad = dkv[at, :].astype(F32)
            head_back(grad[:, :head_dim], at, 1)
            dqkv[at, 2 * head_dim :] = grad[:, head_dim:].astype(BF16)

    def cell(c, j):
        index = 4 * c + j
        return hid.at[pl.ds(index // 3 * features, features), pl.ds(index % 3 * rows, rows)]

    owners = (tp, core_index, x_index, cross_index)

    def scatter_copies(c):
        return (
            peer_copy(7 + 6 * c, cell(c, 1), norm_near.at[c, 0], core_peer),
            peer_copy(8 + 6 * c, cell(c, 3), norm_near.at[c, 1], core_peer),
            peer_copy(9 + 6 * c, row_part.at[c, 0], row_near.at[c, 0], core_peer),
            peer_copy(10 + 6 * c, cell(c, 2), norm_far.at[c], x_peer),
            peer_copy(11 + 6 * c, row_part.at[c, 1], row_near.at[c, 1], x_peer),
        )

    def scatter_begin(c):
        for j in range(4):
            weights = v_qkv[multiple(owners[j] * features, features), :]
            cell(c, j)[...] = dot_nt(weights, dqkv[chunk(c), :]).astype(BF16)
        for first in range(0, rows, half):
            at = pl.ds(c * rows + first, half)
            raw = dot_nn(mid[at, :], v_qkv[...])
            inner_sum = (raw * dqkv[at, :].astype(F32)).sum(axis=1, keepdims=True)
            scale = scale_of(dffn[at, :].astype(F32))
            lane = lax.broadcasted_iota(jnp.int32, (half, 128), 1)
            both = jnp.where(lane == 0, inner_sum, scale)
            row_part[c, 0, :, pl.ds(first, half)] = both.T[0:8, :]
        for copy in scatter_copies(c)[:3]:
            copy.start()

    def scatter_cross(c):
        copies = scatter_copies(c)
        for copy in copies[:3]:
            copy.wait_recv()
        cell(c, 0)[...] = add16(cell(c, 0)[...], norm_near[c, 0])
        cell(c, 2)[...] = add16(cell(c, 2)[...], norm_near[c, 1])
        row_part[c, 1] = row_part[c, 0] + row_near[c, 0]
        copies[3].start()
        copies[4].start()

    def scatter_end(c):
        copies = scatter_copies(c)
        copies[3].wait_recv()
        copies[4].wait_recv()
        for first in range(0, width, 128):
            turned[first : first + 128, :] = cot[chunk(c), first : first + 128].T
        lane = (ctx if c == 0 else 1 - ctx) * rows
        lanes = pl.ds(pl.multiple_of(lane, rows), rows)
        grad = cell(c, 0)[...].astype(F32) + norm_far[c].astype(F32)
        values = tok_own[:, lanes].astype(F32)
        scale = row_part[c, 0, 1:2, :]
        inner_sum = row_part[c, 1, 0:1, :] + row_near[c, 1, 0:1, :]
        d_in = scale * (grad * gain_col[:, 0:1]) - values * (
            scale * scale * inner_sum * (1.0 / width)
        )
        d_resid = turned[multiple(tp * features, features), :].astype(F32)
        xg_t[:, lanes] = (d_resid + d_in).astype(BF16)
        column = jnp.sum(grad * values * scale, axis=1, keepdims=True)
        column = jnp.broadcast_to(column, (features, 128))
        if c == 1:
            col_slots[0] = column
        else:
            col_slots[0] += column

    at_out = 3 * hidden
    at_query = at_out + head_dim
    at_kv = at_query + head_dim

    def out_grad():
        g[pl.ds(at_out, head_dim), :] = contract(att[...], attn[...], 0, 0).astype(BF16)

    def query_grad():
        g[pl.ds(at_query, head_dim), :] = contract(dqkv[:, :head_dim], mid[...], 0, 0).astype(BF16)

    def kv_grads():
        spare = g.shape[0] - at_kv - kv_rows
        g[pl.ds(at_kv + kv_rows, spare), :] = jnp.zeros((spare, width), BF16)
        sum_copies(1)[0].wait_send()
        for j in range(4):
            cols = multiple(head_dim + owners[j] * kv_rows, kv_rows)
            part[1, pl.ds(j * kv_rows, kv_rows), :] = contract(dqkv[:, cols], mid[...], 0, 0).astype(
                BF16
            )
        for copy in kv_copies()[:2]:
            copy.start()

    def kv_copies():
        return (
            peer_copy(19, part.at[1, pl.ds(kv_rows, kv_rows)], kv_near.at[0], core_peer),
            peer_copy(20, part.at[1, pl.ds(3 * kv_rows, kv_rows)], kv_near.at[1], core_peer),
            peer_copy(21, part.at[1, pl.ds(2 * kv_rows, kv_rows)], kv_far, x_peer),
        )

    def kv_cross():
        copies = kv_copies()
        copies[0].wait_recv()
        copies[1].wait_recv()
        for j in range(2):
            at = pl.ds(2 * j * kv_rows, kv_rows)
            part[1, at, :] = add16(part[1, at, :], kv_near[j])
        copies[2].start()

    def kv_end():
        kv_copies()[2].wait_recv()
        g[pl.ds(at_kv, kv_rows), :] = add16(part[1, pl.ds(0, kv_rows), :], kv_far[...])

    sum_peers = (core_peer, x_peer, y_peer, z_peer, m_peer)

    def sum_copy(j):
        return peer_copy(22 + j, sum_slots.at[j], sum_new.at[j], sum_peers[j])

    def col_copy(j):
        return peer_copy(27 + j, col_slots.at[j], col_new.at[j], sum_peers[2 + j])

    def gains_begin():
        sum_slots[0] = jnp.zeros((8, width), F32)
        for j, values in enumerate((row_sums[0], row_sums[1], gain_ffn[...])):
            sum_slots[0, j : j + 1, :] = 0.25 * values.sum(axis=0, keepdims=True)
        for j in range(2):
            sum_slots[0, 3:4, j * head_dim : (j + 1) * head_dim] = head_sums[j].sum(
                axis=0, keepdims=True
            )
        sum_copy(0).start()
        col_copy(0).start()

    def gains_hop(j):
        sum_copy(j).wait_recv()
        if j < 4:
            sum_slots[j + 1] = sum_slots[j] + sum_new[j]
            sum_copy(j + 1).start()
        else:
            gain_rows[...] = sum_slots[j] + sum_new[j]
        if j < 3:
            col_copy(j).wait_recv()
        if j < 2:
            col_slots[j + 1] = col_slots[j] + col_new[j]
            col_copy(j + 1).start()
        if j == 2:
            mine = multiple(tp * features, features)
            gain_cols[mine, :] = col_slots[2] + col_new[2]
            gather_copies()[0].start()
            gather_copies()[1].start()
        if j == 3:
            gather_copies()[1].wait_recv()
            gather_copies()[2].start()
        if j == 4:
            gather_copies()[0].wait_recv()
            gather_copies()[2].wait_recv()

    def gather_copies():
        mine = gain_cols.at[multiple(tp * features, features)]
        theirs = gain_cols.at[multiple(x_index * features, features)]
        return (
            peer_copy(30, mine, mine, core_peer),
            peer_copy(31, mine, mine, x_peer),
            peer_copy(32, theirs, theirs, core_peer),
        )

    def late(low, high):
        for j in range(low, high):
            late_load(j).start()

    def wait_late(low, high):
        for j in range(low, high):
            late_load(j).wait()

    def wait_rest():
        for j in range(5, count):
            load(j).wait()
        head_sums[...] = jnp.zeros(head_sums.shape, F32)

    gate_tiles = gate_hidden // 256
    load(0).wait()
    load(1).wait()
    grad_tile(0, 0, 256)
    load(2).wait()
    load(3).wait()
    grad_tile(1, 256 * gate_tiles, 256)
    for copy in fetch(0):
        copy.start()
    spread_gains(packed, gains, head_gains)
    for first in range(0, width, 128):
        row = gains[0:1, first : first + 128]
        gain_cols[first : first + 128, :] = jnp.broadcast_to(row, (128, 128)).T
    gain_col[...] = gain_cols[multiple(tp * features, features), :]

    first_up = full + 1
    first_gate = first_up + full + 1
    freed = first_gate + gate_tiles
    stages = [
        (0, load(4).wait),
        (0, lambda: [grad_tile(1, 256 * j, 256) for j in range(gate_tiles + 1, full)]),
        (1, lambda: mid_part(1, 0, mid_split)),
        (2, lambda: sum_begin(1)),
        (3, lambda: (sum_cross(1), mid_part(0, 0, mid_split))),
        (4, lambda: sum_begin(0)),
        (5, lambda: sum_cross(0)),
        (7, lambda: (late(0, 1), sum_back(1))),
        (9, lambda: (wait_late(0, 1), wait_rest())),
        (9, lambda: norms_back(1, 0)),
        (10, lambda: norms_back(1, 1)),
        (11, lambda: sum_back(0)),
        (13, lambda: norms_back(0, 0)),
        (14, lambda: norms_back(0, 1)),
        (freed, lambda: late(1, len(late_pairs))),
    ]
    chain_stages = (
        (1, lambda: wait_late(1, len(late_pairs))),
        (1, lambda: attend_back_rows(1, 0)),
        (2, lambda: attend_back_rows(1, 1)),
        (3, lambda: (sum_copies(0)[2].wait_send(), load_tok().start())),
        (3, lambda: attend_back_rows(0, 0)),
        (4, lambda: attend_back_rows(0, 1)),
        (5, lambda: (far_cross(), keys_back(1))),
        (6, lambda: scatter_begin(1)),
        (7, lambda: scatter_cross(1)),
        (8, lambda: (far_up(), out_grad())),
        (11, lambda: (load_tok().wait(), scatter_end(1))),
        (14, lambda: keys_back(0)),
        (15, lambda: scatter_begin(0)),
        (16, query_grad),
        (17, lambda: (scatter_cross(0), kv_grads())),
        (18, kv_cross),
        (20, lambda: scatter_end(0)),
        (21, gains_begin),
        (22, kv_end),
    )
    stages += [(freed + j, action) for j, action in chain_stages]
    stages += [(freed + 23 + 2 * j, partial(gains_hop, j)) for j in range(5)]

    def body(t, carry):
        pl.when((t < full) & (t != 2))(
            lambda: grad_tile(0, 256 * (t + 1 - jnp.minimum(t // 2, 1)), 256)
        )
        if tail:
            pl.when(t == 2)(lambda: grad_tile(1, 256 * full, tail))
            pl.when(t == full)(lambda: grad_tile(0, 256 * full, tail))
            pl.when(t == first_gate - 1)(lambda: grad_tile(2, 256 * full, tail))
        up = t - first_up
        pl.when((up >= 0) & (up < full))(lambda: grad_tile(2, 256 * up, 256))
        gate = t - first_gate
        pl.when((gate >= 0) & (gate < gate_tiles))(lambda: grad_tile(1, 256 * gate, 256))
        for stage, who, limit, action in hops:
            k = t - stage * lag
            pl.when(who & (k >= 0) & (k < limit))(partial(action, k))
        for step, action in stages:
            pl.when(t == step)(lambda action=action: action() and None)
        return carry

    lax.fori_loop(0, K + 5 * lag, body, 0)
    done = [sum_copies(0)[j] for j in (0, 1)] + [sum_copies(1)[j] for j in (1, 2)]
    done += [*far_copies(), *scatter_copies(0), *scatter_copies(1), *kv_copies()]
    done += [sum_copy(j) for j in range(5)] + [col_copy(j) for j in range(3)]
    for copy in done + list(gather_copies()):
        copy.wait_send()


def backward(real_lengths, tok_t, forward_outs, gain_ffn, weights, packed, tables):
    features, rows = tok_t.shape
    half = rows // 2
    width = 4 * features
    w_q, w_k, w_v, w_o, w_g, w_u = weights
    hidden, head_dim = w_g.shape[0], w_k.shape[1]
    kv_rows = head_dim // 2
    step_rows, lag = 32, 2
    ring = 4 * lag + 1
    needed = 3 * hidden + 2 * head_dim + kv_rows
    steps = -(-needed // (4 * step_rows))
    total = 4 * step_rows * steps
    gate_hidden = total // 2 - hidden
    steps_low = -(-(needed - total // 2) // (2 * step_rows))
    whole = pl.BlockSpec(memory_space=pltpu.VMEM)
    there = pl.BlockSpec(memory_space=pl.ANY)

    def low(*shape):
        return pltpu.VMEM(shape, BF16)

    def high(*shape):
        return pltpu.VMEM(shape, F32)

    slots = [low(n * step_rows * ring, width) for n in (1, 1, 1, 2, 1, 1)]
    return pl.pallas_call(
        partial(backward_kernel, step_rows, steps, steps_low, lag, ring, gate_hidden),
        out_shape=(
            jax.ShapeDtypeStruct((total, width), BF16),
            jax.ShapeDtypeStruct((features, rows), BF16),
            jax.ShapeDtypeStruct((8, width), F32),
            jax.ShapeDtypeStruct((width, 128), F32),
        ),
        in_specs=[pl.BlockSpec(memory_space=pltpu.SMEM)] + [there] * 14 + [whole] + [there] * 6
        + [whole] * 3,
        out_specs=[there, whole, whole, whole],
        scratch_shapes=[
            low(total, width), *slots,
            low(rows, hidden), low(rows, hidden), low(rows, hidden), low(rows, width),
            low(rows, width), low(2, 2, hidden, 256), low(2, half, width),
            low(2, half // 2, width), low(2, half // 2, width), low(rows, width), low(rows, width),
            low(rows, width), low(head_dim, width), low(width, 3 * head_dim),
            low(half, 2 * head_dim), low(2, 2, features, half), low(2, features, half),
            high(2, 2, 8, half), high(2, 2, 8, half), low(2, kv_rows, width), low(kv_rows, width),
            low(width, half), high(2, 8, head_dim), high(2, 8, width),
            high(5, 8, width), high(5, 8, width), high(3, features, 128), high(3, features, 128),
            high(4, width), high(2, head_dim), high(features, 128),
            pltpu.SemaphoreType.DMA((20,)), pltpu.SemaphoreType.DMA((2, 2)),
            pltpu.SemaphoreType.DMA((2, steps)), pltpu.SemaphoreType.DMA((11, steps)),
            pltpu.SemaphoreType.DMA((11, steps)), pltpu.SemaphoreType.DMA((35,)),
            pltpu.SemaphoreType.DMA((35,)),
        ],
        name="backward",
        compiler_params=pltpu.CompilerParams(
            collective_id=1, has_side_effects=True, vmem_limit_bytes=63 << 20
        ),
    )(real_lengths, tok_t, *forward_outs, gain_ffn, *weights, packed, *tables)


def paired_shards(
    tokens,
    out_grad,
    w_query,
    w_key,
    w_value,
    w_out,
    w_gate,
    w_up,
    w_down,
    gain_in,
    gain_post_attn,
    gain_pre_ffn,
    gain_post_ffn,
    gain_query,
    gain_key,
    bucket_lengths,
    true_lengths,
):
    tp_index = lax.axis_index("tp")
    rows = tokens.shape[0] // 2
    head_dim = w_key.shape[1]
    score_scale = head_dim ** (-0.5)
    tables = block_tables(2 * rows, head_dim)
    packed = jnp.concatenate(
        [gain_in, gain_post_attn, gain_pre_ffn, gain_post_ffn, gain_query, gain_key]
    ).astype(F32).reshape(-1, 128)
    weights = (w_query, w_key, w_value, w_out, w_gate.T, w_up.T, w_down)
    out_t, gain_sum, *kept = forward(
        true_lengths, tokens.T, out_grad.T, weights, packed, tables
    )
    sums, xg_t, gain_rows, gain_cols = backward(
        true_lengths, tokens.T, kept, gain_sum, weights[:-1], packed, tables
    )
    hidden = w_down.shape[0]
    ends = [hidden, 2 * hidden, 3 * hidden, 3 * hidden + head_dim, 3 * hidden + 2 * head_dim]
    down_sum, gate_sum, up_sum, out_sum, query_sum, mine = [
        sums[start:end] for start, end in zip([0] + ends, ends + [ends[-1] + head_dim // 2])
    ]
    far = lax.ppermute(mine, "tp", XOR2)
    near = lax.ppermute(jnp.stack([mine, far]), "tp", XOR1)
    kv_all = (mine, near[0], far, near[1])
    kv_sum = jnp.concatenate(
        [lax.select_n(tp_index ^ j, *kv_all) for j in range(4)], axis=0
    ).astype(F32).T
    return (
        out_t.T,
        xg_t.T,
        query_sum.astype(F32).T,
        kv_sum[:, :head_dim],
        kv_sum[:, head_dim:],
        out_sum.astype(F32),
        gate_sum.astype(F32).T,
        up_sum.astype(F32).T,
        down_sum.astype(F32),
        gain_cols[:, 0],
        gain_rows[0],
        gain_rows[1],
        gain_rows[2],
        gain_rows[3, :head_dim],
        gain_rows[3, head_dim : 2 * head_dim],
    )


def solution(mesh):
    def layer(*args):
        tokens, bucket_lengths = args[0], args[-2]
        sizes = mesh.shape
        group_rows = tokens.shape[0] // sizes["dp"]
        paired = (sizes["dp"], sizes["ctx"], sizes["tp"]) == (4, 2, 4) and (
            group_rows == 1024 * bucket_lengths.shape[1] == 2048
        )
        return mapped(paired_shards if paired else shards)(*args)

    def mapped(body):
        return jax.shard_map(
            body,
            mesh=mesh,
            in_specs=(
                P(("dp", "ctx"), "tp"),
                P(("dp", "ctx"), "tp"),
                P(None, "tp"),
                P(),
                P(),
                P("tp", None),
                P(None, "tp"),
                P(None, "tp"),
                P("tp", None),
                P(),
                P(),
                P(),
                P(),
                P(),
                P(),
                P("dp", None),
                P("dp", None),
            ),
            out_specs=(
                P(("dp", "ctx"), "tp"),
                P(("dp", "ctx"), "tp"),
                P(None, "tp"),
                P(),
                P(),
                P("tp", None),
                P(None, "tp"),
                P(None, "tp"),
                P("tp", None),
                P(),
                P(),
                P(),
                P(),
                P(),
                P(),
            ),
            check_vma=False,
        )

    return layer
```

```python
import math
from functools import partial

import jax
import jax.numpy as jnp
import numpy as np
from jax import lax
from jax.experimental import pallas as pl
from jax.experimental.pallas import tpu as pltpu
from jax.sharding import PartitionSpec as P

QBLK = 512


EPSILON = 1e-06
ROPE_BASE = 1000000.0
MASKED = -1e30


def contract(left, right, left_dim, right_dim):
    return lax.dot_general(
        left, right, (((left_dim,), (right_dim,)), ((), ())), preferred_element_type=jnp.float32
    )


def rms_norm(values, gain):
    return values * lax.rsqrt(jnp.mean(values * values, axis=-1, keepdims=True) + EPSILON) * gain


def rotate(values, cosine_table, sine_table):
    half_dim = values.shape[-1] // 2
    turned = jnp.concatenate([-values[..., half_dim:], values[..., :half_dim]], axis=-1)
    return values * cosine_table + turned * sine_table


def rope_tables(seq_pos, head_dim):
    freq_index = jnp.arange(head_dim // 2, dtype=jnp.float32)
    inverse = ROPE_BASE ** (-2.0 * freq_index / head_dim)
    angles = seq_pos.astype(jnp.float32)[:, None] * inverse[None, :]
    angles = jnp.concatenate([angles, angles], axis=-1)
    return (jnp.cos(angles), jnp.sin(angles))


def stream_layout(bucket_row, true_row, tok_dev, n_ctx):
    group_rows = tok_dev * n_ctx
    half_shard = tok_dev // 2
    row_ids = jnp.arange(group_rows, dtype=jnp.int32)
    device = row_ids // tok_dev
    half_index = row_ids % tok_dev // half_shard
    block_ids = jnp.where(half_index == 0, device, 2 * n_ctx - 1 - device)
    stream_pos = block_ids * half_shard + row_ids % half_shard
    starts = jnp.cumsum(bucket_row) - bucket_row
    ends = starts + bucket_row
    inside = (
        (stream_pos[:, None] >= starts[None, :]) & (stream_pos[:, None] < ends[None, :])
    ).astype(jnp.int32)
    slot_ids = jnp.arange(bucket_row.shape[0], dtype=jnp.int32)
    seq_ids = jnp.sum(inside * slot_ids[None, :], axis=1)
    seq_pos = stream_pos - jnp.sum(inside * starts[None, :], axis=1)
    is_valid = (seq_pos < jnp.sum(inside * true_row[None, :], axis=1)).astype(jnp.int32)
    return (seq_ids, stream_pos, seq_pos, is_valid)


def shape_heads(query_raw, key_raw, gain_q, gain_k, cosine_table, sine_table):
    query_heads = query_raw.reshape(query_raw.shape[0], -1, key_raw.shape[1])
    query_rot = rotate(
        rms_norm(query_heads, gain_q), cosine_table[:, None, :], sine_table[:, None, :]
    )
    key_rot = rotate(rms_norm(key_raw, gain_k), cosine_table, sine_table)
    return (query_rot, key_rot)


def geglu(gate_in, up_in):
    return jax.nn.gelu(gate_in, approximate=True) * up_in


def shards(
    tokens,
    out_grad,
    w_query,
    w_key,
    w_value,
    w_out,
    w_gate,
    w_up,
    w_down,
    gain_in,
    gain_post_attn,
    gain_pre_ffn,
    gain_post_ffn,
    gain_query,
    gain_key,
    bucket_lengths,
    true_lengths,
):
    n_ctx = lax.axis_size("ctx")
    ctx_index = lax.axis_index("ctx")
    tp_index = lax.axis_index("tp")
    rows_dev = tokens.shape[0]
    feature_cols = tokens.shape[1]
    head_dim = w_key.shape[1]
    head_count = w_query.shape[1] // head_dim
    group_rows = rows_dev * n_ctx
    blocks = rows_dev // QBLK
    score_scale = head_dim ** (-0.5)
    gain_in32, gain_pa32, gain_pf32, gain_pff32, gain_q32, gain_k32 = [
        tensor.astype(jnp.float32)
        for tensor in (gain_in, gain_post_attn, gain_pre_ffn, gain_post_ffn, gain_query, gain_key)
    ]
    input_full, cot_full = (
        lax.all_gather(tokens, "tp", axis=1, tiled=True),
        lax.all_gather(out_grad, "tp", axis=1, tiled=True),
    )
    inputs = input_full.astype(jnp.float32)
    seq_all, spos_all, rpos_all, valid_all = stream_layout(
        bucket_lengths[0], true_lengths[0], rows_dev, n_ctx
    )
    first_row = ctx_index * rows_dev
    seq_local = lax.dynamic_slice_in_dim(seq_all, first_row, rows_dev)
    spos_local = lax.dynamic_slice_in_dim(spos_all, first_row, rows_dev)
    rpos_local = lax.dynamic_slice_in_dim(rpos_all, first_row, rows_dev)
    cosine_table, sine_table = rope_tables(rpos_local, head_dim)
    normed_in, pull_in = jax.vjp(rms_norm, inputs, gain_in32)
    normed_in16 = normed_in.astype(jnp.bfloat16)
    query_raw = jnp.dot(normed_in16, w_query, preferred_element_type=jnp.float32)
    key_raw = jnp.dot(normed_in16, w_key, preferred_element_type=jnp.float32)
    value_raw = jnp.dot(normed_in16, w_value, preferred_element_type=jnp.float32)
    (query_rot, key_rot), rope_pull = jax.vjp(
        partial(shape_heads, cosine_table=cosine_table, sine_table=sine_table),
        query_raw,
        key_raw,
        gain_q32,
        gain_k32,
    )
    query16 = query_rot.astype(jnp.bfloat16)
    key16 = key_rot.astype(jnp.bfloat16)
    value16 = value_raw.astype(jnp.bfloat16)
    key_group, value_group = (
        lax.all_gather(key16, "ctx", axis=0, tiled=True),
        lax.all_gather(value16, "ctx", axis=0, tiled=True),
    )

    def allowed_mask(seq_rows, spos_rows):
        return (
            (valid_all[None, :] == 1)
            & (seq_all[None, :] == seq_rows[:, None])
            & (spos_all[None, :] <= spos_rows[:, None])
        )

    query_blocks = query16.reshape(blocks, QBLK, head_count, head_dim)
    seq_blocks = seq_local.reshape(blocks, QBLK)
    spos_blocks = spos_local.reshape(blocks, QBLK)

    def forward_block(block_item):
        query_block, seq_rows, spos_rows = block_item
        scores = (
            jnp.einsum("qhd,kd->hqk", query_block, key_group, preferred_element_type=jnp.float32)
            * score_scale
        )
        scores = jnp.where(allowed_mask(seq_rows, spos_rows)[None], scores, MASKED)
        row_max = jnp.max(scores, axis=-1, keepdims=True)
        exp_scores = jnp.exp(scores - row_max)
        row_total = jnp.sum(exp_scores, axis=-1, keepdims=True)
        prob_rows = (exp_scores / row_total).astype(jnp.bfloat16)
        output = jnp.einsum(
            "hqk,kd->qhd", prob_rows, value_group, preferred_element_type=jnp.float32
        )
        return (output, (row_max + jnp.log(row_total))[..., 0])

    attended, log_norm = lax.map(forward_block, (query_blocks, seq_blocks, spos_blocks))
    attended16 = attended.reshape(rows_dev, head_count * head_dim).astype(jnp.bfloat16)
    attention = lax.psum(
        jnp.dot(attended16, w_out, preferred_element_type=jnp.float32).astype(jnp.bfloat16), "tp"
    ).astype(jnp.float32)
    post_attn, pull_post_attn = jax.vjp(rms_norm, attention, gain_pa32)
    residual = inputs + post_attn
    normed_mid, pull_pre_ffn = jax.vjp(rms_norm, residual, gain_pf32)
    mid16 = normed_mid.astype(jnp.bfloat16)
    gate_out = jnp.dot(mid16, w_gate, preferred_element_type=jnp.float32)
    up_out = jnp.dot(mid16, w_up, preferred_element_type=jnp.float32)
    hidden, pull_geglu = jax.vjp(geglu, gate_out, up_out)
    hidden16 = hidden.astype(jnp.bfloat16)
    ffn_branch = lax.psum(
        jnp.dot(hidden16, w_down, preferred_element_type=jnp.float32).astype(jnp.bfloat16), "tp"
    ).astype(jnp.float32)
    post_ffn, pull_post_ffn = jax.vjp(rms_norm, ffn_branch, gain_pff32)
    outputs = residual + post_ffn
    out_rows = lax.dynamic_slice_in_dim(outputs, tp_index * feature_cols, feature_cols, 1).astype(
        jnp.bfloat16
    )
    cotangent = cot_full.astype(jnp.float32)
    d_ffn, d_gain_post_ffn = pull_post_ffn(cotangent)
    d_ffn16 = d_ffn.astype(jnp.bfloat16)
    d_hidden = contract(d_ffn16, w_down, 1, 1)
    grad_down = contract(hidden16, d_ffn16, 0, 0)
    d_gate, d_up = pull_geglu(d_hidden)
    d_gate16 = d_gate.astype(jnp.bfloat16)
    d_up16 = d_up.astype(jnp.bfloat16)
    grad_gate = contract(mid16, d_gate16, 0, 0)
    grad_up = contract(mid16, d_up16, 0, 0)
    d_mid = lax.psum(
        (contract(d_gate16, w_gate, 1, 1) + contract(d_up16, w_up, 1, 1)).astype(jnp.bfloat16), "tp"
    ).astype(jnp.float32)
    d_res_norm, d_gain_pre_ffn = pull_pre_ffn(d_mid)
    d_resid = cotangent + d_res_norm
    d_attn, d_gain_post_attn = pull_post_attn(d_resid)
    d_attn16 = d_attn.astype(jnp.bfloat16)
    d_attended16 = contract(d_attn16, w_out, 1, 1).astype(jnp.bfloat16)
    grad_out = contract(attended16, d_attn16, 0, 0)
    key_back, value_back = (key_group, value_group)

    def backward_block(running, block_item):
        key_sum, value_sum = running
        query_block, dout_block, lse_block, seq_rows, spos_rows = block_item
        scores = (
            jnp.einsum("qhd,kd->hqk", query_block, key_back, preferred_element_type=jnp.float32)
            * score_scale
        )
        scores = jnp.where(allowed_mask(seq_rows, spos_rows)[None], scores, MASKED)
        prob_rows = jnp.exp(scores - lse_block[..., None])
        prob16 = prob_rows.astype(jnp.bfloat16)
        d_probs = jnp.einsum(
            "qhd,kd->hqk", dout_block, value_back, preferred_element_type=jnp.float32
        )
        row_inner = jnp.sum(prob_rows * d_probs, axis=-1, keepdims=True)
        d_scores16 = (prob_rows * (d_probs - row_inner)).astype(jnp.bfloat16)
        d_query = (
            jnp.einsum("hqk,kd->qhd", d_scores16, key_back, preferred_element_type=jnp.float32)
            * score_scale
        )
        key_sum = (
            key_sum
            + jnp.einsum("hqk,qhd->kd", d_scores16, query_block, preferred_element_type=jnp.float32)
            * score_scale
        )
        value_sum = value_sum + jnp.einsum(
            "hqk,qhd->kd", prob16, dout_block, preferred_element_type=jnp.float32
        )
        return ((key_sum, value_sum), d_query)

    zero_rows = jnp.zeros((group_rows, head_dim), jnp.float32)
    (key_sum, value_sum), d_query_blocks = lax.scan(
        backward_block,
        (zero_rows, zero_rows),
        (
            query_blocks,
            d_attended16.reshape(blocks, QBLK, head_count, head_dim),
            log_norm,
            seq_blocks,
            spos_blocks,
        ),
    )
    d_key_rot, d_value = (
        lax.psum_scatter(
            key_sum.astype(jnp.bfloat16), "ctx", scatter_dimension=0, tiled=True
        ).astype(jnp.float32),
        lax.psum_scatter(
            value_sum.astype(jnp.bfloat16), "ctx", scatter_dimension=0, tiled=True
        ).astype(jnp.float32),
    )
    d_query_raw, d_key_raw, d_gain_query, d_gain_key = rope_pull(
        (d_query_blocks.reshape(rows_dev, head_count, head_dim), d_key_rot)
    )
    d_query16 = d_query_raw.astype(jnp.bfloat16)
    d_key16 = d_key_raw.astype(jnp.bfloat16)
    d_value16 = d_value.astype(jnp.bfloat16)
    grad_query = contract(normed_in16, d_query16, 0, 0)
    grad_key = contract(normed_in16, d_key16, 0, 0)
    grad_value = contract(normed_in16, d_value16, 0, 0)
    d_normed_part = (
        contract(d_query16, w_query, 1, 1)
        + contract(d_key16, w_key, 1, 1)
        + contract(d_value16, w_value, 1, 1)
    )
    d_normed_in = lax.psum(d_normed_part.astype(jnp.bfloat16), "tp").astype(jnp.float32)
    d_in_norm, d_gain_in = pull_in(d_normed_in)
    d_inputs = d_resid + d_in_norm
    grad_rows = lax.dynamic_slice_in_dim(d_inputs, tp_index * feature_cols, feature_cols, 1).astype(
        jnp.bfloat16
    )
    sharded = (
        grad_query,
        grad_out,
        grad_gate,
        grad_up,
        grad_down,
        d_gain_in,
        d_gain_post_attn,
        d_gain_pre_ffn,
        d_gain_post_ffn,
    )
    reduced = (
        lax.psum_scatter(
            sharded[0].astype(jnp.bfloat16), ("dp", "ctx"), scatter_dimension=0, tiled=True
        ).astype(jnp.float32),
        lax.psum_scatter(
            sharded[1].astype(jnp.bfloat16), ("dp", "ctx"), scatter_dimension=1, tiled=True
        ).astype(jnp.float32),
        lax.psum_scatter(
            sharded[2].astype(jnp.bfloat16), ("dp", "ctx"), scatter_dimension=0, tiled=True
        ).astype(jnp.float32),
        lax.psum_scatter(
            sharded[3].astype(jnp.bfloat16), ("dp", "ctx"), scatter_dimension=0, tiled=True
        ).astype(jnp.float32),
        lax.psum_scatter(
            sharded[4].astype(jnp.bfloat16), ("dp", "ctx"), scatter_dimension=1, tiled=True
        ).astype(jnp.float32),
        lax.psum_scatter(
            sharded[5].astype(jnp.bfloat16), ("dp", "ctx"), scatter_dimension=0, tiled=True
        ).astype(jnp.float32),
        lax.psum_scatter(
            sharded[6].astype(jnp.bfloat16), ("dp", "ctx"), scatter_dimension=0, tiled=True
        ).astype(jnp.float32),
        lax.psum_scatter(
            sharded[7].astype(jnp.bfloat16), ("dp", "ctx"), scatter_dimension=0, tiled=True
        ).astype(jnp.float32),
        lax.psum_scatter(
            sharded[8].astype(jnp.bfloat16), ("dp", "ctx"), scatter_dimension=0, tiled=True
        ).astype(jnp.float32),
    )
    summed = (
        lax.all_gather(reduced[0].astype(jnp.bfloat16), ("dp", "ctx"), axis=0, tiled=True).astype(
            jnp.float32
        ),
        lax.all_gather(reduced[1].astype(jnp.bfloat16), ("dp", "ctx"), axis=1, tiled=True).astype(
            jnp.float32
        ),
        lax.all_gather(reduced[2].astype(jnp.bfloat16), ("dp", "ctx"), axis=0, tiled=True).astype(
            jnp.float32
        ),
        lax.all_gather(reduced[3].astype(jnp.bfloat16), ("dp", "ctx"), axis=0, tiled=True).astype(
            jnp.float32
        ),
        lax.all_gather(reduced[4].astype(jnp.bfloat16), ("dp", "ctx"), axis=1, tiled=True).astype(
            jnp.float32
        ),
        lax.all_gather(reduced[5].astype(jnp.bfloat16), ("dp", "ctx"), axis=0, tiled=True).astype(
            jnp.float32
        ),
        lax.all_gather(reduced[6].astype(jnp.bfloat16), ("dp", "ctx"), axis=0, tiled=True).astype(
            jnp.float32
        ),
        lax.all_gather(reduced[7].astype(jnp.bfloat16), ("dp", "ctx"), axis=0, tiled=True).astype(
            jnp.float32
        ),
        lax.all_gather(reduced[8].astype(jnp.bfloat16), ("dp", "ctx"), axis=0, tiled=True).astype(
            jnp.float32
        ),
    )
    shared = lax.psum((grad_key, grad_value, d_gain_query, d_gain_key), ("dp", "ctx", "tp"))
    return (
        out_rows,
        grad_rows,
        summed[0],
        shared[0],
        shared[1],
        summed[1],
        summed[2],
        summed[3],
        summed[4],
        summed[5],
        summed[6],
        summed[7],
        summed[8],
        shared[2],
        shared[3],
    )


XOR1 = ((0, 1), (1, 0), (2, 3), (3, 2))
XOR2 = ((0, 2), (2, 0), (1, 3), (3, 1))
MESH = pl.DeviceIdType.MESH
GELU_SCALE = math.sqrt(2.0 / math.pi)
F32 = jnp.float32
BF16 = jnp.bfloat16


def add16(left, right):
    return (left.astype(F32) + right.astype(F32)).astype(BF16)


def block_tables(length, head_dim):
    freq_index = np.arange(head_dim // 2, dtype=np.float32)
    inverse = np.float32(ROPE_BASE) ** (np.float32(-2.0) * freq_index / np.float32(head_dim))
    angles = np.arange(length, dtype=np.float32)[:, None] * inverse.astype(np.float32)[None, :]
    angles = angles.astype(np.float64)
    return np.cos(angles).astype(np.float32), np.sin(angles).astype(np.float32)


def scale_of(values):
    return lax.rsqrt(jnp.mean(values * values, axis=-1, keepdims=True) + EPSILON)


STORED = 13


def row_blocks(base, rows, size, body, carry=None):
    def step(i, state):
        at = pl.ds(pl.multiple_of(base + i * size, size), size)
        return body(at, pl.ds(pl.multiple_of(i * size, size), size), state)

    return lax.fori_loop(0, rows // size, step, carry)


def spread_gains(packed, gains, head_gains):
    columns = gains.shape[1] // 128
    for j in range(4):
        for i in range(columns):
            at = j * columns + i
            gains[j : j + 1, 128 * i : 128 * i + 128] = packed[at : at + 1, :]
    head_columns = head_gains.shape[1] // 128
    for j in range(2):
        for i in range(head_columns):
            at = 4 * columns + j * head_columns + i
            head_gains[j : j + 1, 128 * i : 128 * i + 128] = packed[at : at + 1, :]


def turn_in(source, target, rows):
    for first in range(0, source.shape[0], 128):
        target[rows, first : first + 128] = source[first : first + 128, :].T


def column_tiles(total, size):
    return [(first, min(size, total - first)) for first in range(0, total, size)]


def dot_nn(left, right):
    return jnp.dot(left, right, preferred_element_type=F32)


def dot_nt(left, right):
    return contract(left, right, 1, 1)


def gelu_parts(gate):
    square = gate * gate
    tanh = jnp.tanh(GELU_SCALE * gate * (1.0 + 0.044715 * square))
    half = 0.5 + 0.5 * tanh
    slope = GELU_SCALE * (1.0 + 3.0 * 0.044715 * square)
    return gate * half, half + 0.5 * gate * (1.0 - tanh * tanh) * slope


def forward_kernel(
    real_lengths, tok, cot, w_q, w_k, w_v, w_o, w_g, w_u, w_d, packed, cosines, sines,
    out_t, gain_sum, *refs,
):
    stored, refs = refs[:STORED], refs[STORED:]
    kept, refs = refs[:STORED], refs[STORED:]
    x16, cot16, n16, q16, kv16, far_kv, att16, attn16, mid16, hid16, dffn16, dg16, du16 = kept
    blocks, v_qkv, v_o, v_g, v_u, v_d, part, near, far, ffn16, gains, head_gains = refs[:12]
    load_sem, own_sem, store_sem, g_send, g_recv, kv_send, kv_recv, s_send, s_recv = refs[12:]
    dp, ctx, tp = lax.axis_index("dp"), lax.axis_index("ctx"), lax.axis_index("tp")
    core_peer = (dp, ctx, tp + 1 - 2 * (tp % 2))
    x_index = (tp + 2) % 4
    x_peer = (dp, ctx, x_index)
    y_peer = (dp, 1 - ctx, tp)
    features, rows = tok.shape[0], tok.shape[1] // 2
    width = 4 * features
    hidden = w_d.shape[0]
    head_dim = w_k.shape[1]
    half = rows // 2
    odd = tp % 2

    loads = [
        pltpu.make_async_copy(source, target, load_sem.at[j])
        for j, (source, target) in enumerate(
            (
                (w_q, v_qkv.at[:, 0:head_dim]),
                (w_k, v_qkv.at[:, head_dim : 2 * head_dim]),
                (w_v, v_qkv.at[:, 2 * head_dim : 3 * head_dim]),
                (w_o, v_o), (w_g, v_g), (w_u, v_u), (w_d, v_d),
            )
        )
    ]
    for copy in loads:
        copy.start()

    def half_of(source, index):
        lane = (ctx if index % 2 == 0 else 1 - ctx) * rows
        return source.at[:, pl.ds(pl.multiple_of(lane, rows), rows)]

    def place(index, owner):
        return blocks.at[index, pl.ds(pl.multiple_of(owner * features, features), features)]

    sources = [half_of(tok, 0), half_of(tok, 1), half_of(cot, 0), half_of(cot, 1)]

    def remote(source, target, send, recv, peer):
        return pltpu.make_async_remote_copy(
            src_ref=source, dst_ref=target, send_sem=send, recv_sem=recv,
            device_id=peer, device_id_type=MESH,
        )

    own = [pltpu.make_async_copy(sources[j], place(j, tp), own_sem.at[j]) for j in range(4)]
    to_x = [
        remote(sources[j], place(j, tp), g_send.at[0, j], g_recv.at[0, j], x_peer) for j in range(4)
    ]
    to_core = [
        remote(sources[j], place(j, tp), g_send.at[1, j], g_recv.at[1, j], core_peer)
        for j in range(4)
    ]
    onward = [
        remote(place(j, x_index), place(j, x_index), g_send.at[2, j], g_recv.at[2, j], core_peer)
        for j in range(4)
    ]
    for copy in own:
        copy.start()
    barrier = pltpu.get_barrier_semaphore()
    for peer in (core_peer, x_peer, y_peer):
        pl.semaphore_signal(barrier, inc=1, device_id=peer, device_id_type=MESH)
    pl.semaphore_wait(barrier, 3)

    for j in range(4):
        to_core[j].start()
    to_x[0].start()
    to_x[1].start()

    spread_gains(packed, gains, head_gains)

    def store(j, c):
        at = slice(None) if c is None else chunk(c)
        return pltpu.make_async_copy(kept[j].at[at], stored[j].at[at], store_sem.at[j, c or 0])

    def pass_on(j):
        to_x[j].wait_recv()
        onward[j].start()

    def gathered(j):
        own[j].wait()
        to_core[j].wait_recv()
        onward[j].wait_recv()

    def chunk(c):
        return pl.ds(c * rows, rows)

    def normalise(c):
        turn_in(blocks.at[c], x16, chunk(c))

        def norm(at, _, carry):
            values = x16[at, :].astype(F32)
            n16[at, :] = (values * scale_of(values) * gains[0:1, :]).astype(BF16)

        row_blocks(c * rows, rows, 64, norm)

    def project(c):
        for first in range(0, rows, half):
            at = pl.ds(c * rows + first, half)
            tables = pl.ds(c * rows + first, half)
            values = dot_nn(n16[at, :], v_qkv[...])
            cosine, sine = cosines[tables, :], sines[tables, :]
            for j, target in ((0, q16.at[at, :]), (1, kv16.at[at, 0:head_dim])):
                head = values[:, j * head_dim : (j + 1) * head_dim]
                head = head * scale_of(head) * head_gains[j : j + 1, :]
                low, high = head[:, : head_dim // 2], head[:, head_dim // 2 :]
                target[:, : head_dim // 2] = (low * cosine - high * sine).astype(BF16)
                target[:, head_dim // 2 :] = (high * cosine + low * sine).astype(BF16)
            kv16[at, head_dim:] = values[:, 2 * head_dim :].astype(BF16)

    score_scale = head_dim ** (-0.5)

    def attend_rows(c):
        for first in range(0, rows, half):
            at = pl.ds(c * rows + first, half)
            query = q16[at, :]
            row_id = first + lax.broadcasted_iota(jnp.int32, (half, rows), 0)
            key_id = lax.broadcasted_iota(jnp.int32, (half, rows), 1)
            allowed = key_id <= row_id
            if c == 1:
                allowed = allowed & (rows + key_id < real_lengths[0, 1 - ctx])
            keys = [(kv16[chunk(c), :head_dim], kv16[chunk(c), head_dim:], allowed)]
            if c == 1:
                keys.append((far_kv[:, :head_dim], far_kv[:, head_dim:], None))
            scores = []
            for key, _, mask in keys:
                score = dot_nt(query, key) * score_scale
                scores.append(score if mask is None else jnp.where(mask, score, MASKED))
            most = scores[0].max(axis=1, keepdims=True)
            for score in scores[1:]:
                most = jnp.maximum(most, score.max(axis=1, keepdims=True))
            exps = [jnp.exp(score - most) for score in scores]
            total = sum(e.sum(axis=1, keepdims=True) for e in exps)
            out = sum(dot_nn((e / total).astype(BF16), k[1]) for e, k in zip(exps, keys))
            att16[at, :] = out.astype(BF16)
        part[c] = dot_nn(att16[chunk(c), :], v_o[...]).astype(BF16)

    def rows_of(index):
        return pl.ds(pl.multiple_of(index * half, half), half)

    def sum_copies(s, target):
        start = pl.multiple_of((s % 2) * rows + odd * half, half)
        final = target.at[pl.ds(start, half)]
        return (
            remote(part.at[s, rows_of(1 - odd)], near.at[s], s_send.at[0, s], s_recv.at[0, s], core_peer),
            remote(near.at[s], far.at[s], s_send.at[1, s], s_recv.at[1, s], x_peer),
            remote(final, final, s_send.at[2, s], s_recv.at[2, s], core_peer),
        )

    def sum_start(s, target):
        sum_copies(s, target)[0].start()

    def sum_cross(s, target):
        copies = sum_copies(s, target)
        copies[0].wait_recv()
        near[s] = add16(part[s, rows_of(odd)], near[s])
        copies[1].start()

    def sum_back(s, target):
        copies = sum_copies(s, target)
        copies[1].wait_recv()
        start = pl.multiple_of((s % 2) * rows + odd * half, half)
        target[pl.ds(start, half), :] = add16(near[s], far[s])
        copies[2].start()
        copies[2].wait_recv()

    def residual(at):
        branch = attn16[at, :].astype(F32)
        return x16[at, :].astype(F32) + branch * scale_of(branch) * gains[1:2, :]

    def middle(c):
        def body(at, _, carry):
            values = residual(at)
            mid16[at, :] = (values * scale_of(values) * gains[2:3, :]).astype(BF16)

        row_blocks(c * rows, rows, 64, body)

    def feed(c):
        for first, size in column_tiles(hidden, 256):
            for low in range(0, rows, half):
                at = pl.ds(c * rows + low, half)
                cols = pl.ds(first, size)
                gate = dot_nt(mid16[at, :], v_g[cols, :])
                up = dot_nt(mid16[at, :], v_u[cols, :])
                act, slope = gelu_parts(gate)
                hid16[at, cols] = (act * up).astype(BF16)
                dg16[at, cols] = (slope * up).astype(BF16)
                du16[at, cols] = act.astype(BF16)
        for first, size in column_tiles(width, 256):
            cols = pl.ds(first, size)
            part[2 + c, :, cols] = dot_nn(hid16[chunk(c), :], v_d[:, cols]).astype(BF16)

    def finish(c):
        turn_in(blocks.at[2 + c], cot16, chunk(c))
        sum_copies(c, attn16)[0].wait_send()
        onward[c].wait_send()

        def body(at, block, total):
            branch = ffn16[at, :].astype(F32)
            scale = scale_of(branch)
            unit = branch * scale
            grad = cot16[at, :].astype(F32)
            part[c, block, :] = (residual(at) + unit * gains[3:4, :]).astype(BF16)
            weighted = grad * gains[3:4, :]
            inner = jnp.mean(unit * weighted, axis=-1, keepdims=True)
            dffn16[at, :] = (scale * (weighted - unit * inner)).astype(BF16)
            return total + (grad * unit).reshape(-1, 8, width).sum(axis=0)

        total = row_blocks(c * rows, rows, 64, body, jnp.zeros((8, width), F32))
        if c == 0:
            gain_sum[...] = total
        else:
            gain_sum[...] += total
        for first in range(0, width, 128):
            blocks[c, first : first + 128, :] = part[c, :, first : first + 128].T
        lane = (ctx if c == 0 else 1 - ctx) * rows
        mine = blocks[c, pl.ds(pl.multiple_of(tp * features, features), features), :]
        out_t[:, pl.ds(pl.multiple_of(lane, rows), rows)] = mine

    def feed_back(c):
        for first, size in column_tiles(hidden, 256):
            for low in range(0, rows, half):
                at = pl.ds(c * rows + low, half)
                cols = pl.ds(first, size)
                d_hidden = dot_nt(dffn16[at, :], v_d[cols, :])
                dg16[at, cols] = (d_hidden * dg16[at, cols].astype(F32)).astype(BF16)
                du16[at, cols] = (d_hidden * du16[at, cols].astype(F32)).astype(BF16)

    kv_copy = remote(kv16.at[chunk(0)], far_kv, kv_send.at[0], kv_recv.at[0], y_peer)
    X, COT, N, Q, KV, FAR, ATT, ATTN, MID, HID, DFFN, DG, DU = range(STORED)
    started = []

    def store_all(c, *which):
        for j in which:
            store(j, c).start()
            started.append((j, c))

    pass_on(0)
    for copy in loads[:3]:
        copy.wait()
    gathered(0)
    normalise(0)
    project(0)
    kv_copy.start()
    store_all(0, X, N, Q, KV)
    pass_on(1)
    to_x[2].start()
    loads[3].wait()
    attend_rows(0)
    sum_start(0, attn16)
    gathered(1)
    normalise(1)
    sum_cross(0, attn16)
    project(1)
    store_all(1, X, N, Q, KV)
    kv_copy.wait_recv()
    attend_rows(1)
    sum_start(1, attn16)
    store_all(None, FAR)
    store_all(0, ATT)
    store_all(1, ATT)
    pass_on(2)
    sum_cross(1, attn16)
    sum_back(0, attn16)
    for copy in loads[4:]:
        copy.wait()
    middle(0)
    to_x[3].start()
    store_all(0, ATTN, MID)
    feed(0)
    sum_start(2, ffn16)
    store_all(0, HID)
    sum_back(1, attn16)
    middle(1)
    store_all(1, ATTN, MID)
    sum_cross(2, ffn16)
    pass_on(3)
    feed(1)
    sum_start(3, ffn16)
    store_all(1, HID)
    gathered(2)
    sum_cross(3, ffn16)
    sum_back(2, ffn16)
    finish(0)
    store_all(0, COT, DFFN)
    feed_back(0)
    store_all(0, DG, DU)
    gathered(3)
    sum_back(3, ffn16)
    finish(1)
    store_all(1, COT, DFFN)
    feed_back(1)
    store_all(1, DG, DU)
    for group in (to_x, to_core, onward[2:], [kv_copy]):
        for copy in group:
            copy.wait_send()
    for s, target in ((0, attn16), (1, attn16), (2, ffn16), (3, ffn16)):
        for copy in sum_copies(s, target)[1 if s < 2 else 0 :]:
            copy.wait_send()
    for j, c in started:
        store(j, c).wait()


def forward(real_lengths, tok_t, cot_t, weights, packed, tables):
    features, rows = tok_t.shape
    half = rows // 2
    width = 4 * features
    hidden = weights[-1].shape[0]
    head_dim = weights[1].shape[1]
    whole = pl.BlockSpec(memory_space=pltpu.VMEM)
    there = pl.BlockSpec(memory_space=pl.ANY)
    kept = [
        (rows, width), (rows, width), (rows, width), (rows, head_dim), (rows, 2 * head_dim),
        (half, 2 * head_dim), (rows, head_dim), (rows, width), (rows, width), (rows, hidden),
        (rows, width), (rows, hidden), (rows, hidden),
    ]

    return pl.pallas_call(
        forward_kernel,
        out_shape=(
            jax.ShapeDtypeStruct((features, rows), BF16), jax.ShapeDtypeStruct((8, width), F32),
            *[jax.ShapeDtypeStruct(shape, BF16) for shape in kept],
        ),
        in_specs=[pl.BlockSpec(memory_space=pltpu.SMEM)] + [there] * 9 + [whole] * 3,
        out_specs=[whole] * 2 + [there] * STORED,
        scratch_shapes=[pltpu.VMEM(shape, BF16) for shape in kept]
        + [
            pltpu.VMEM((4, width, half), BF16),
            pltpu.VMEM((width, 3 * head_dim), BF16),
            pltpu.VMEM((head_dim, width), BF16),
            pltpu.VMEM((hidden, width), BF16),
            pltpu.VMEM((hidden, width), BF16),
            pltpu.VMEM((hidden, width), BF16),
            pltpu.VMEM((4, half, width), BF16),
            pltpu.VMEM((4, half // 2, width), BF16),
            pltpu.VMEM((4, half // 2, width), BF16),
            pltpu.VMEM((rows, width), BF16),
            pltpu.VMEM((4, width), F32),
            pltpu.VMEM((2, head_dim), F32),
            pltpu.SemaphoreType.DMA((7,)),
            pltpu.SemaphoreType.DMA((4,)),
            pltpu.SemaphoreType.DMA((STORED, 2)),
            pltpu.SemaphoreType.DMA((3, 4)),
            pltpu.SemaphoreType.DMA((3, 4)),
            pltpu.SemaphoreType.DMA((1,)),
            pltpu.SemaphoreType.DMA((1,)),
            pltpu.SemaphoreType.DMA((3, 4)),
            pltpu.SemaphoreType.DMA((3, 4)),
        ],
        name="forward",
        compiler_params=pltpu.CompilerParams(
            collective_id=2, has_side_effects=True, vmem_limit_bytes=63 << 20
        ),
    )(real_lengths, tok_t, cot_t, *weights, packed, *tables)


def backward_kernel(
    step_rows, steps, few, lag,
    real_lengths, tok, x_in, cot_in, n_in, q_in, kv_in, far_in, att_in, attn_in, mid_in, hid_in,
    dffn_in, dg_in, du_in, gain_ffn, w_q, w_k, w_v, w_o, w_g, w_u, packed, cosines, sines,
    out, xg_t, gain_rows, gain_cols,
    g, y2, z2, m2, z1, m1, y1, a3, b3, hid, dg, du, mid, dffn, w_tiles, part, near, far, dm, cot, attn,
    v_o, v_qkv, dkv_new, norm_near, norm_far, row_part,
    row_near, kv_near, kv_far, turned, head_sums, row_sums, sum_slots, sum_new, col_slots,
    col_new, gains, head_gains, gain_col, col_part,
    load_sem, tile_sem, keep_sem, keep_few, chain_send, chain_recv, few_send, few_recv, peer_send,
    peer_recv,
):
    dp, ctx, tp = lax.axis_index("dp"), lax.axis_index("ctx"), lax.axis_index("tp")
    s, K = step_rows, steps
    upper = dp // 2
    odd = tp % 2
    outer = (dp == 0) | (dp == 3)
    inner = jnp.logical_not(outer)
    yes = dp >= 0
    core_index = tp + 1 - 2 * odd
    x_index = (tp + 2) % 4
    cross_index = (core_index + 2) % 4
    z_index = dp + 1 - 2 * (dp % 2)
    core_peer, x_peer = (dp, ctx, core_index), (dp, ctx, x_index)
    y_peer, z_peer, m_peer = (dp, 1 - ctx, tp), (z_index, ctx, tp), (3 - dp, ctx, tp)
    features, rows = tok.shape[0], tok.shape[1] // 2
    width = 4 * features
    hidden = w_g.shape[0]
    head_dim = w_k.shape[1]
    half = rows // 2
    kv_rows = head_dim // 2
    score_scale = head_dim ** (-0.5)

    def remote(source, target, send, recv, peer):
        return pltpu.make_async_remote_copy(
            src_ref=source, dst_ref=target, send_sem=send, recv_sem=recv,
            device_id=peer, device_id_type=MESH,
        )

    def chunk(c):
        return pl.ds(c * rows, rows)

    def multiple(start, size):
        return pl.ds(pl.multiple_of(start, size), size)

    dqkv, kv16 = dg.at[:, 0 : 3 * head_dim], dg.at[:, 3 * head_dim : 5 * head_dim]
    dkv, dkv_far = du.at[:, 0 : 2 * head_dim], du.at[0:rows, 2 * head_dim : 4 * head_dim]
    far_kv = du.at[rows : 2 * rows, 2 * head_dim : 4 * head_dim]
    q16, att = du.at[:, 4 * head_dim : 5 * head_dim], du.at[:, 5 * head_dim : 6 * head_dim]

    tok_own = dm.at[0:features, 0 : 2 * rows]

    pairs = (
        (hid_in, hid), (dffn_in, dffn), (du_in, du), (mid_in, mid), (dg_in, dg), (cot_in, cot),
        (attn_in, attn), (w_o, v_o),
        (w_q, v_qkv.at[:, 0:head_dim]), (w_k, v_qkv.at[:, head_dim : 2 * head_dim]),
        (w_v, v_qkv.at[:, 2 * head_dim : 3 * head_dim]),
    )
    count = len(pairs)

    def load(j):
        return pltpu.make_async_copy(pairs[j][0], pairs[j][1], load_sem.at[j])

    late_pairs = (
        (x_in, dffn), (n_in, mid), (q_in, q16), (kv_in, kv16), (far_in, far_kv), (att_in, att),
    )

    def load_tok():
        return pltpu.make_async_copy(tok, tok_own, load_sem.at[count + len(late_pairs)])

    def late_load(j):
        return pltpu.make_async_copy(late_pairs[j][0], late_pairs[j][1], load_sem.at[count + j])

    for j in range(count):
        load(j).start()
    barrier = pltpu.get_barrier_semaphore()
    for peer in (core_peer, x_peer, y_peer, z_peer, m_peer):
        pl.semaphore_signal(barrier, inc=1, device_id=peer, device_id_type=MESH)
    pl.semaphore_wait(barrier, 5)

    third = 3
    enter1, enter3 = 2 * lag, 0
    base3 = 2 * s * K
    base = base3 + 2 * s * few
    ring, ring_few = 4 * lag + 1, -(-(4 * lag + 1) // third) + 1

    def rows2(k, h):
        return multiple((2 * k + h) * s, s)

    def rows1(k, h):
        return multiple(base + (2 * k + h) * s, s)

    def rows3(k, h):
        return multiple(base3 + (2 * k + h) * s, s)

    def pair1(k):
        return pl.ds(pl.multiple_of(base + 2 * k * s, s), 2 * s)

    def slot(k):
        return multiple((k % ring) * s, s)

    def slot_few(k):
        return multiple((k % ring_few) * s, s)

    def slot_pair(k):
        return multiple((k % ring_few) * 2 * s, 2 * s)

    def slot_half(k, h):
        return multiple(((k % ring_few) * 2 + h) * s, s)

    def chain(j, k, source, target, peer):
        if j < 5:
            return remote(source, target, chain_send.at[j, k], chain_recv.at[j, k], peer)
        return remote(source, target, few_send.at[j - 5, k], few_recv.at[j - 5, k], peer)

    def c_y2(k):
        return chain(0, k, g.at[rows2(k, 1 - ctx)], y2.at[slot(k)], y_peer)

    def c_z2(k):
        return chain(1, k, y2.at[slot(k)], z2.at[slot(k)], z_peer)

    def c_m2(k):
        return chain(2, k, z2.at[slot(k)], m2.at[slot(k)], m_peer)

    def c_fo(k):
        return chain(3, k, m2.at[slot(k)], out.at[rows2(k, ctx)], z_peer)

    def c_fy(k):
        return chain(4, k, m2.at[slot(k)], out.at[rows2(k, ctx)], y_peer)

    def c_fy_outer(k):
        return chain(4, k, out.at[rows2(k, ctx)], out.at[rows2(k, ctx)], y_peer)

    def c_z1(k):
        return chain(5, k, g.at[pair1(k)], z1.at[slot_pair(k)], z_peer)

    def c_m1(k):
        return chain(6, k, z1.at[slot_half(k, 1 - upper)], m1.at[slot_few(k)], m_peer)

    def c_y1(k):
        return chain(7, k, m1.at[slot_few(k)], y1.at[slot_few(k)], y_peer)

    def c_fm(k):
        return chain(8, k, y1.at[slot_few(k)], out.at[rows1(k, upper)], m_peer)

    def c_fa(k):
        return chain(9, k, y1.at[slot_few(k)], out.at[rows1(k, upper)], z_peer)

    def c_fb(k):
        return chain(10, k, out.at[rows1(k, 1 - upper)], out.at[rows1(k, 1 - upper)], z_peer)

    def c_3up(k):
        return chain(11, k, g.at[rows3(k, 1 - upper)], a3.at[slot_few(k)], z_peer)

    def c_3mid(k):
        return chain(12, k, a3.at[slot_few(k)], b3.at[slot_few(k)], m_peer)

    def c_3end(k):
        return chain(13, k, b3.at[slot_few(k)], a3.at[slot_few(k)], z_peer)

    def c_3y(k):
        return chain(14, k, a3.at[slot_few(k)], b3.at[slot_few(k)], y_peer)

    def c_3back(k):
        return chain(15, k, b3.at[slot_few(k)], out.at[rows3(k, upper)], z_peer)

    def c_3over(k):
        return chain(16, k, out.at[rows3(k, upper)], out.at[rows3(k, upper)], m_peer)

    def c_3last(k):
        return chain(17, k, out.at[rows3(k, 1 - upper)], out.at[rows3(k, 1 - upper)], z_peer)

    def keep2(k):
        return pltpu.make_async_copy(m2.at[slot(k)], out.at[rows2(k, ctx)], keep_sem.at[k])

    def keep1(k):
        return pltpu.make_async_copy(y1.at[slot_few(k)], out.at[rows1(k, upper)], keep_few.at[0, k])

    def keep3(k):
        return pltpu.make_async_copy(b3.at[slot_few(k)], out.at[rows3(k, upper)], keep_few.at[1, k])

    def inner3_mid(k):
        c_3up(k).wait_recv()
        a3[slot_few(k), :] = add16(a3[slot_few(k), :], g[rows3(k, 1 - upper), :])
        c_3mid(k).start()

    def inner3_end(k):
        c_3mid(k).wait_recv()
        b3[slot_few(k), :] = add16(b3[slot_few(k), :], g[rows3(k, upper), :])
        c_3end(k).start()

    def outer3_y(k):
        c_3end(k).wait_recv()
        a3[slot_few(k), :] = add16(a3[slot_few(k), :], g[rows3(k, upper), :])
        c_3y(k).start()

    def outer3_back(k):
        c_3y(k).wait_recv()
        b3[slot_few(k), :] = add16(b3[slot_few(k), :], a3[slot_few(k), :])
        c_3back(k).start()
        keep3(k).start()

    def inner3_over(k):
        c_3back(k).wait_recv()
        c_3over(k).start()

    def inner3_last(k):
        c_3over(k).wait_recv()
        c_3last(k).start()

    def outer3_done(k):
        c_3last(k).wait_recv()
        c_3up(k).wait_send()

    def inner3_done(k):
        c_3over(k).wait_send()
        c_3last(k).wait_send()

    def outer3_sent(k):
        c_3back(k).wait_send()
        keep3(k).wait()

    def b2(k):
        c_y2(k).wait_recv()
        y2[slot(k), :] = add16(y2[slot(k), :], g[rows2(k, ctx), :])
        pl.when(outer)(lambda: c_z2(k).start())

    def b1(k):
        c_z1(k).wait_recv()
        z1[slot_pair(k), :] = add16(z1[slot_pair(k), :], g[pair1(k), :])
        c_m1(k).start()

    def c2(k):
        c_z2(k).wait_recv()
        z2[slot(k), :] = add16(z2[slot(k), :], y2[slot(k), :])
        c_m2(k).start()

    def c1(k):
        c_m1(k).wait_recv()
        m1[slot_few(k), :] = add16(m1[slot_few(k), :], z1[slot_half(k, upper), :])
        c_y1(k).start()

    def d2(k):
        c_m2(k).wait_recv()
        m2[slot(k), :] = add16(m2[slot(k), :], z2[slot(k), :])
        c_fo(k).start()
        c_fy(k).start()
        keep2(k).start()

    def d1(k):
        c_y1(k).wait_recv()
        y1[slot_few(k), :] = add16(y1[slot_few(k), :], m1[slot_few(k), :])
        c_fm(k).start()
        c_fa(k).start()
        keep1(k).start()

    def e2(k):
        c_fo(k).wait_recv()
        c_fy_outer(k).start()

    def e1(k):
        c_fm(k).wait_recv()
        c_fb(k).start()

    def f2(k):
        c_fy(k).wait_recv()
        c_y2(k).wait_send()

    def f2_outer(k):
        c_fy_outer(k).wait_send()

    def f1_outer(k):
        c_fa(k).wait_recv()
        c_fb(k).wait_recv()
        c_z1(k).wait_send()

    def f2_inner(k):
        keep2(k).wait()
        c_fo(k).wait_send()
        c_fy(k).wait_send()

    def f1_inner(k):
        keep1(k).wait()
        for copy in (c_fm, c_fa, c_fb):
            copy(k).wait_send()

    two, one, three = (K, 1, 0), (few, third, enter1), (few, third, enter3)
    hops = (
        (5, yes, two, f2), (5, outer, two, f2_outer), (5, outer, one, f1_outer),
        (5, inner, two, f2_inner), (5, inner, one, f1_inner),
        (7, outer, three, outer3_done), (7, inner, three, inner3_done),
        (6, outer, three, outer3_sent),
        (5, outer, three, lambda k: c_3y(k).wait_send()),
        (4, inner, two, lambda k: c_m2(k).wait_send()),
        (4, inner, one, lambda k: c_y1(k).wait_send()),
        (3, outer, two, lambda k: c_z2(k).wait_send()),
        (3, inner, one, lambda k: c_m1(k).wait_send()),
        (3, inner, three, lambda k: c_3mid(k).wait_send()),
        (3, inner, three, lambda k: c_3end(k).wait_send()),
        (6, inner, three, inner3_last), (5, inner, three, inner3_over),
        (4, outer, two, e2), (4, inner, one, e1), (4, outer, three, outer3_back),
        (3, inner, two, d2), (3, inner, one, d1), (3, outer, three, outer3_y),
        (2, inner, two, c2), (2, inner, one, c1), (2, inner, three, inner3_end),
        (1, yes, two, b2), (1, inner, one, b1), (1, inner, three, inner3_mid),
        (0, yes, two, lambda k: c_y2(k).start()), (0, outer, one, lambda k: c_z1(k).start()),
        (0, outer, three, lambda k: c_3up(k).start()),
    )

    def grad_tile(index, first, size):
        left, right = ((hid, dffn), (dg, mid), (du, mid))[index]
        at = first if isinstance(first, int) else pl.multiple_of(first, 256)
        tile = contract(left[:, pl.ds(at, size)], right[...], 0, 0)
        start = index * hidden + first
        g[pl.ds(start if isinstance(start, int) else pl.multiple_of(start, 64), size), :] = (
            tile.astype(BF16)
        )

    full = hidden // 256
    tail = hidden - 256 * full

    mid_tiles = column_tiles(width, 256)

    def fetch(j):
        first, size = mid_tiles[j % len(mid_tiles)]
        return [
            pltpu.make_async_copy(
                w.at[:, pl.ds(first, size)], w_tiles.at[i, j % 2, :, pl.ds(0, size)],
                tile_sem.at[i, j % 2],
            )
            for i, w in enumerate((w_g, w_u))
        ]

    def mid_part(c, low, high):
        base = (1 - c) * len(mid_tiles)
        for j in range(base + low, base + high):
            first, size = mid_tiles[j - base]
            if j + 1 < 2 * len(mid_tiles):
                for copy in fetch(j + 1):
                    copy.start()
            for copy in fetch(j):
                copy.wait()
            term = dot_nn(dg[chunk(c), :], w_tiles[0, j % 2, :, 0:size]) + dot_nn(
                du[chunk(c), :], w_tiles[1, j % 2, :, 0:size]
            )
            part[c, :, pl.ds(first, size)] = term.astype(BF16)

    def own_half(index):
        return multiple(index * half, half)

    def peer_copy(j, source, target, peer):
        return remote(source, target, peer_send.at[j], peer_recv.at[j], peer)

    def sum_copies(c):
        final = dm.at[multiple(c * rows + odd * half, half)]
        return (
            peer_copy(3 * c, part.at[c, own_half(1 - odd)], near.at[c], core_peer),
            peer_copy(3 * c + 1, near.at[c], far.at[c], x_peer),
            peer_copy(3 * c + 2, final, final, core_peer),
        )

    def sum_begin(c):
        mid_part(c, cuts[2], tiles)
        sum_copies(c)[0].start()

    def sum_cross(c):
        copies = sum_copies(c)
        copies[0].wait_recv()
        near[c] = add16(part[c, own_half(odd)], near[c])
        copies[1].start()

    def sum_back(c):
        copies = sum_copies(c)
        copies[1].wait_recv()
        dm[multiple(c * rows + odd * half, half), :] = add16(near[c], far[c])
        copies[2].start()

    def norms_back(c, second):
        if not second:
            sum_copies(c)[2].wait_recv()

        def body(at, _, state):
            branch = attn[at, :].astype(F32)
            scale_a = scale_of(branch)
            unit_a = branch * scale_a
            resid = dffn[at, :].astype(F32) + unit_a * gains[1:2, :]
            scale_r = scale_of(resid)
            unit_r = resid * scale_r
            grad = dm[at, :].astype(F32)
            weighted = grad * gains[2:3, :]
            mean = jnp.mean(unit_r * weighted, axis=-1, keepdims=True)
            d_resid = cot[at, :].astype(F32) + scale_r * (weighted - unit_r * mean)
            weighted = d_resid * gains[1:2, :]
            mean = jnp.mean(unit_a * weighted, axis=-1, keepdims=True)
            cot[at, :] = d_resid.astype(BF16)
            attn[at, :] = (scale_a * (weighted - unit_a * mean)).astype(BF16)
            return (
                state[0] + (d_resid * unit_a).reshape(-1, 8, width).sum(axis=0),
                state[1] + (grad * unit_r).reshape(-1, 8, width).sum(axis=0),
            )

        zero = jnp.zeros((8, width), F32)
        sum_a, sum_r = row_blocks(c * rows + second * half, half, 64, body, (zero, zero))
        if c == 1 and not second:
            row_sums[0], row_sums[1] = sum_a, sum_r
        else:
            row_sums[0] += sum_a
            row_sums[1] += sum_r

    def head_back(grad, at, j):
        cosine, sine = cosines[at, :], sines[at, :]
        low, high = grad[:, : head_dim // 2], grad[:, head_dim // 2 :]
        grad = jnp.concatenate([low * cosine + high * sine, high * cosine - low * sine], axis=1)
        cols = pl.ds(j * head_dim, head_dim)
        raw = dot_nn(mid[at, :], v_qkv[:, cols])
        scale = scale_of(raw)
        unit = raw * scale
        weighted = grad * head_gains[j : j + 1, :]
        mean = jnp.mean(unit * weighted, axis=-1, keepdims=True)
        dqkv[at, cols] = (scale * (weighted - unit * mean)).astype(BF16)
        head_sums[j] += (grad * unit).reshape(-1, 8, head_dim).sum(axis=0)

    def attend_back_rows(c, second):
        d_keys, d_values = [0.0, 0.0], [0.0, 0.0]
        for first in (second * half,):
            at = pl.ds(c * rows + first, half)
            query = q16[at, :]
            d_out = dot_nt(attn[at, :], v_o[...]).astype(BF16)
            row_id = first + lax.broadcasted_iota(jnp.int32, (half, rows), 0)
            key_id = lax.broadcasted_iota(jnp.int32, (half, rows), 1)
            allowed = key_id <= row_id
            if c == 1:
                allowed = allowed & (rows + key_id < real_lengths[0, 1 - ctx])
            keys = [(kv16[chunk(c), :head_dim], kv16[chunk(c), head_dim:], allowed)]
            if c == 1:
                keys.append((far_kv[:, :head_dim], far_kv[:, head_dim:], None))
            scores = []
            for key, _, mask in keys:
                score = dot_nt(query, key) * score_scale
                scores.append(score if mask is None else jnp.where(mask, score, MASKED))
            most = scores[0].max(axis=1, keepdims=True)
            for score in scores[1:]:
                most = jnp.maximum(most, score.max(axis=1, keepdims=True))
            exps = [jnp.exp(score - most) for score in scores]
            total = sum(e.sum(axis=1, keepdims=True) for e in exps)
            probs = [e / total for e in exps]
            d_probs = [dot_nt(d_out, key[1]) for key in keys]
            mean = sum((p * d).sum(axis=1, keepdims=True) for p, d in zip(probs, d_probs))
            d_query = 0.0
            for i, key in enumerate(keys):
                d_score = (probs[i] * (d_probs[i] - mean)).astype(BF16)
                d_query += dot_nn(d_score, key[0])
                d_keys[i] += contract(d_score, query, 0, 0)
                d_values[i] += contract(probs[i].astype(BF16), d_out, 0, 0)
            head_back(d_query * score_scale, at, 0)
        places = [dkv.at[chunk(c), :]] + [dkv_far] * c
        for i, place in enumerate(places):
            for cols, term in (
                (pl.ds(0, head_dim), d_keys[i] * score_scale),
                (pl.ds(head_dim, head_dim), d_values[i]),
            ):
                if second:
                    term = term + place[:, cols].astype(F32)
                place[:, cols] = term.astype(BF16)
        if c == 1 and second:
            far_copies()[0].start()

    quarter = half // 2
    far_rows = multiple(odd * half + tp // 2 * quarter, quarter)

    def far_copies():
        given = dkv_far.at[multiple(odd * half + (1 - tp // 2) * quarter, quarter), :]
        return (
            peer_copy(33, dkv_far.at[own_half(1 - odd), :], dkv_new.at[0:half], core_peer),
            peer_copy(34, given, dkv_new.at[half : half + quarter], x_peer),
            peer_copy(6, dkv_far.at[far_rows, :], dkv_new.at[half + quarter : 2 * half], y_peer),
        )

    def far_cross():
        copies = far_copies()
        copies[0].wait_recv()
        dkv_far[own_half(odd), :] = add16(dkv_far[own_half(odd), :], dkv_new[0:half, :])
        copies[1].start()

    def far_up():
        copies = far_copies()
        copies[1].wait_recv()
        dkv_far[far_rows, :] = add16(dkv_far[far_rows, :], dkv_new[half : half + quarter, :])
        copies[2].start()

    def keys_back(c):
        if c == 0:
            far_copies()[2].wait_recv()
            dkv[far_rows, :] = add16(dkv[far_rows, :], dkv_new[half + quarter : 2 * half, :])
        for first in range(0, rows, half):
            at = pl.ds(c * rows + first, half)
            grad = dkv[at, :].astype(F32)
            head_back(grad[:, :head_dim], at, 1)
            dqkv[at, 2 * head_dim :] = grad[:, head_dim:].astype(BF16)

    def cell(c, j):
        index = 4 * c + j
        return hid.at[pl.ds(index // 3 * features, features), pl.ds(index % 3 * rows, rows)]

    owners = (tp, core_index, x_index, cross_index)

    def scatter_copies(c):
        return (
            peer_copy(7 + 6 * c, cell(c, 1), norm_near.at[c, 0], core_peer),
            peer_copy(8 + 6 * c, cell(c, 3), norm_near.at[c, 1], core_peer),
            peer_copy(9 + 6 * c, row_part.at[c, 0], row_near.at[c, 0], core_peer),
            peer_copy(10 + 6 * c, cell(c, 2), norm_far.at[c], x_peer),
            peer_copy(11 + 6 * c, row_part.at[c, 1], row_near.at[c, 1], x_peer),
        )

    def scatter_begin(c):
        for j in range(4):
            weights = v_qkv[multiple(owners[j] * features, features), :]
            cell(c, j)[...] = dot_nt(weights, dqkv[chunk(c), :]).astype(BF16)
        for first in range(0, rows, half):
            at = pl.ds(c * rows + first, half)
            raw = dot_nn(mid[at, :], v_qkv[...])
            inner_sum = (raw * dqkv[at, :].astype(F32)).sum(axis=1, keepdims=True)
            scale = scale_of(dffn[at, :].astype(F32))
            lane = lax.broadcasted_iota(jnp.int32, (half, 128), 1)
            both = jnp.where(lane == 0, inner_sum, scale)
            row_part[c, 0, :, pl.ds(first, half)] = both.T[0:8, :]
        for copy in scatter_copies(c)[:3]:
            copy.start()

    def scatter_cross(c):
        copies = scatter_copies(c)
        for copy in copies[:3]:
            copy.wait_recv()
        cell(c, 0)[...] = add16(cell(c, 0)[...], norm_near[c, 0])
        cell(c, 2)[...] = add16(cell(c, 2)[...], norm_near[c, 1])
        row_part[c, 1] = row_part[c, 0] + row_near[c, 0]
        copies[3].start()
        copies[4].start()

    def scatter_end(c):
        copies = scatter_copies(c)
        copies[3].wait_recv()
        copies[4].wait_recv()
        for first in range(0, width, 128):
            turned[first : first + 128, :] = cot[chunk(c), first : first + 128].T
        lane = (ctx if c == 0 else 1 - ctx) * rows
        lanes = pl.ds(pl.multiple_of(lane, rows), rows)
        grad = cell(c, 0)[...].astype(F32) + norm_far[c].astype(F32)
        values = tok_own[:, lanes].astype(F32)
        scale = row_part[c, 0, 1:2, :]
        inner_sum = row_part[c, 1, 0:1, :] + row_near[c, 1, 0:1, :]
        d_in = scale * (grad * gain_col[:, 0:1]) - values * (
            scale * scale * inner_sum * (1.0 / width)
        )
        d_resid = turned[multiple(tp * features, features), :].astype(F32)
        xg_t[:, lanes] = (d_resid + d_in).astype(BF16)
        column = jnp.sum(grad * values * scale, axis=1, keepdims=True)
        column = jnp.broadcast_to(column, (features, 128))
        for first, size in column_tiles(features, 128):
            block = column[first : first + size, :]
            if size < 128:
                block = jnp.concatenate([block, jnp.zeros((128 - size, 128), F32)], axis=0)
            cols = pl.ds(first, 128)
            if c == 1:
                col_slots[0, :, cols] = block.T[0:8, :]
            else:
                col_slots[0, :, cols] += block.T[0:8, :]

    at_out = 3 * hidden
    at_query = at_out + head_dim
    at_kv = at_query + head_dim

    def out_grad():
        g[pl.ds(at_out, head_dim), :] = contract(att[...], attn[...], 0, 0).astype(BF16)

    def query_grad():
        g[pl.ds(at_query, head_dim), :] = contract(dqkv[:, :head_dim], mid[...], 0, 0).astype(BF16)

    def kv_grads():
        sum_copies(1)[0].wait_send()
        for j in range(4):
            cols = multiple(head_dim + owners[j] * kv_rows, kv_rows)
            part[1, pl.ds(j * kv_rows, kv_rows), :] = contract(dqkv[:, cols], mid[...], 0, 0).astype(
                BF16
            )
        for copy in kv_copies()[:2]:
            copy.start()

    def kv_copies():
        return (
            peer_copy(19, part.at[1, pl.ds(kv_rows, kv_rows)], kv_near.at[0], core_peer),
            peer_copy(20, part.at[1, pl.ds(3 * kv_rows, kv_rows)], kv_near.at[1], core_peer),
            peer_copy(21, part.at[1, pl.ds(2 * kv_rows, kv_rows)], kv_far, x_peer),
        )

    def kv_cross():
        copies = kv_copies()
        copies[0].wait_recv()
        copies[1].wait_recv()
        for j in range(2):
            at = pl.ds(2 * j * kv_rows, kv_rows)
            part[1, at, :] = add16(part[1, at, :], kv_near[j])
        copies[2].start()

    def kv_end():
        kv_copies()[2].wait_recv()
        g[pl.ds(at_kv, kv_rows), :] = add16(part[1, pl.ds(0, kv_rows), :], kv_far[...])

    sum_peers = (core_peer, x_peer, y_peer, z_peer, m_peer)

    def sum_copy(j):
        return peer_copy(22 + j, sum_slots.at[j], sum_new.at[j], sum_peers[j])

    def col_copy(j):
        return peer_copy(27 + j, col_slots.at[j], col_new.at[j], sum_peers[2 + j])

    def gains_begin():
        sum_slots[0] = jnp.zeros((8, width), F32)
        for j, values in enumerate((row_sums[0], row_sums[1], gain_ffn[...])):
            sum_slots[0, j : j + 1, :] = 0.25 * values.sum(axis=0, keepdims=True)
        for j in range(2):
            sum_slots[0, 3:4, j * head_dim : (j + 1) * head_dim] = head_sums[j].sum(
                axis=0, keepdims=True
            )
        sum_copy(0).start()
        col_copy(0).start()

    def gains_hop(j):
        sum_copy(j).wait_recv()
        if j < 4:
            sum_slots[j + 1] = sum_slots[j] + sum_new[j]
            sum_copy(j + 1).start()
        else:
            gain_rows[...] = sum_slots[j] + sum_new[j]
        if j < 3:
            col_copy(j).wait_recv()
        if j < 2:
            col_slots[j + 1] = col_slots[j] + col_new[j]
            col_copy(j + 1).start()
        if j == 2:
            gain_cols[tp] = col_slots[2] + col_new[2]
            gather_copies()[0].start()
            gather_copies()[1].start()
        if j == 3:
            gather_copies()[1].wait_recv()
            gather_copies()[2].start()
        if j == 4:
            gather_copies()[0].wait_recv()
            gather_copies()[2].wait_recv()

    def gather_copies():
        mine, theirs = gain_cols.at[tp], gain_cols.at[x_index]
        return (
            peer_copy(30, mine, mine, core_peer),
            peer_copy(31, mine, mine, x_peer),
            peer_copy(32, theirs, theirs, core_peer),
        )

    def late(low, high):
        for j in range(low, high):
            late_load(j).start()

    def wait_late(low, high):
        for j in range(low, high):
            late_load(j).wait()

    def wait_rest():
        for j in range(5, count):
            load(j).wait()
        head_sums[...] = jnp.zeros(head_sums.shape, F32)

    load(0).wait()
    load(1).wait()
    grad_tile(0, 0, 256)
    load(2).wait()
    load(3).wait()
    grad_tile(2, 0, 256)
    for copy in fetch(0):
        copy.start()
    spread_gains(packed, gains, head_gains)
    for first in range(0, width, 128):
        row = gains[0:1, first : first + 128]
        col_part[first : first + 128, :] = jnp.broadcast_to(row, (128, 128)).T
    gain_col[...] = col_part[multiple(tp * features, features), :]

    lone = full - 2
    order = [(0, 1), (2, lone), (0, 2), (2, lone + 1), (2, 1)] + [(0, j) for j in range(3, full + 1)]
    order += [(2, full)] + [(2, j) for j in range(2, lone)]
    first_gate = len(order) + 1
    freed = first_gate + full + 1
    tiles = len(mid_tiles)
    cuts = [0, tiles // 3, tiles // 3 + (tiles + 1) // 3]

    order += [(1, j) for j in range(full + 1)]

    def tiles_at(t):
        for index in range(3):
            steps_of = [(1 + i, j) for i, (which, j) in enumerate(order) if which == index]
            part_of = [(step, j) for step, j in steps_of if j < full]
            if not isinstance(t, int):
                number = sum(jnp.where(t == step, j + 1, 0) for step, j in part_of)
                pl.when(number > 0)(partial(grad_tile, index, 256 * (number - 1), 256))
            for step, j in steps_of:
                if j == full and tail:
                    pl.when(t == step)(partial(grad_tile, index, 256 * full, tail))

    def choose(t, table):
        middle = len(table) // 2
        if middle == 0:
            pl.when(t == table[0][0])(lambda: [action() for action in table[0][1]] and None)
        else:
            pl.when(t < table[middle][0])(lambda: choose(t, table[:middle]))
            pl.when(t >= table[middle][0])(lambda: choose(t, table[middle:]))

    stages = [(1, load(4).wait)]
    after = [
        (4, lambda: mid_part(1, cuts[0], cuts[1])),
        (5, lambda: mid_part(1, cuts[1], cuts[2])),
        (6, lambda: sum_begin(1)),
        (7, lambda: (sum_cross(1), mid_part(0, cuts[0], cuts[1]))),
        (8, lambda: mid_part(0, cuts[1], cuts[2])),
        (9, lambda: (late(0, 1), sum_begin(0))),
        (10, lambda: sum_cross(0)),
        (11, lambda: sum_back(1)),
        (12, lambda: (wait_late(0, 1), wait_rest())),
        (13, lambda: norms_back(1, 0)),
        (14, lambda: norms_back(1, 1)),
        (15, lambda: sum_back(0)),
        (17, lambda: norms_back(0, 0)),
        (18, lambda: norms_back(0, 1)),
        (freed, lambda: late(1, len(late_pairs))),
    ]
    chain_stages = (
        (1, lambda: wait_late(1, len(late_pairs))),
        (1, lambda: attend_back_rows(1, 0)),
        (2, lambda: attend_back_rows(1, 1)),
        (3, lambda: (sum_copies(0)[2].wait_send(), load_tok().start())),
        (3, lambda: attend_back_rows(0, 0)),
        (4, lambda: attend_back_rows(0, 1)),
        (5, lambda: (far_cross(), keys_back(1))),
        (6, lambda: scatter_begin(1)),
        (7, lambda: (scatter_cross(1), out_grad())),
        (8, far_up),
        (11, lambda: (load_tok().wait(), scatter_end(1))),
        (14, lambda: keys_back(0)),
        (15, lambda: scatter_begin(0)),
        (16, query_grad),
        (17, lambda: (scatter_cross(0), kv_grads())),
        (18, kv_cross),
        (20, lambda: scatter_end(0)),
        (21, gains_begin),
        (22, kv_end),
    )
    stages += after + [(freed + j, action) for j, action in chain_stages]
    stages += [(freed + 23 + 2 * j, partial(gains_hop, j)) for j in range(5)]

    table = [
        (step, [action for at, action in stages if at == step])
        for step in sorted({at for at, _ in stages})
    ]

    def body(t, carry):
        pl.when(t <= len(order))(lambda: tiles_at(t))
        for hop, who, (limit, spacing, first), action in hops:
            entered = t - hop * lag - first
            k = entered // spacing
            now = who & (entered >= 0) & (k < limit)
            if spacing > 1:
                now = now & (entered % spacing == 0)
            pl.when(now)(partial(action, k))
        choose(t, table)
        return carry

    last = max(K + 5 * lag, third * (few - 1) + 1 + max(enter1 + 5 * lag, enter3 + 7 * lag))
    lax.fori_loop(0, last, body, 0)
    done = [sum_copies(0)[j] for j in (0, 1)] + [sum_copies(1)[j] for j in (1, 2)]
    done += [*far_copies(), *scatter_copies(0), *scatter_copies(1), *kv_copies()]
    done += [sum_copy(j) for j in range(5)] + [col_copy(j) for j in range(3)]
    for copy in done + list(gather_copies()):
        copy.wait_send()


def backward(real_lengths, tok_t, forward_outs, gain_ffn, weights, packed, tables):
    features, rows = tok_t.shape
    half = rows // 2
    width = 4 * features
    w_q, w_k, w_v, w_o, w_g, w_u = weights
    hidden, head_dim = w_g.shape[0], w_k.shape[1]
    kv_rows = head_dim // 2
    step_rows, lag = 32, 2
    total = 3 * hidden + 2 * head_dim + kv_rows
    few = total // (10 * step_rows)
    steps = total // (2 * step_rows) - 2 * few
    ring, ring_few = 4 * lag + 1, -(-(4 * lag + 1) // 3) + 1
    spread = -(-features // 128) * 128
    whole = pl.BlockSpec(memory_space=pltpu.VMEM)
    there = pl.BlockSpec(memory_space=pl.ANY)

    def low(*shape):
        return pltpu.VMEM(shape, BF16)

    def high(*shape):
        return pltpu.VMEM(shape, F32)

    slots = [low(step_rows * ring, width)] * 3
    slots += [low(n * step_rows * ring_few, width) for n in (2, 1, 1, 1, 1)]
    return pl.pallas_call(
        partial(backward_kernel, step_rows, steps, few, lag),
        out_shape=(
            jax.ShapeDtypeStruct((total, width), BF16),
            jax.ShapeDtypeStruct((features, rows), BF16),
            jax.ShapeDtypeStruct((8, width), F32),
            jax.ShapeDtypeStruct((4, 8, spread), F32),
        ),
        in_specs=[pl.BlockSpec(memory_space=pltpu.SMEM)] + [there] * 14 + [whole] + [there] * 6
        + [whole] * 3,
        out_specs=[there, whole, whole, whole],
        scratch_shapes=[
            low(total, width), *slots,
            low(rows, hidden), low(rows, hidden), low(rows, hidden), low(rows, width),
            low(rows, width), low(2, 2, hidden, 256), low(2, half, width),
            low(2, half // 2, width), low(2, half // 2, width), low(rows, width), low(rows, width),
            low(rows, width), low(head_dim, width), low(width, 3 * head_dim),
            low(half, 2 * head_dim), low(2, 2, features, half), low(2, features, half),
            high(2, 2, 8, half), high(2, 2, 8, half), low(2, kv_rows, width), low(kv_rows, width),
            low(width, half), high(2, 8, head_dim), high(2, 8, width),
            high(5, 8, width), high(5, 8, width), high(3, 8, spread), high(3, 8, spread),
            high(4, width), high(2, head_dim), high(features, 128), high(width, 128),
            pltpu.SemaphoreType.DMA((20,)), pltpu.SemaphoreType.DMA((2, 2)),
            pltpu.SemaphoreType.DMA((steps,)), pltpu.SemaphoreType.DMA((2, few)),
            pltpu.SemaphoreType.DMA((5, steps)), pltpu.SemaphoreType.DMA((5, steps)),
            pltpu.SemaphoreType.DMA((13, few)), pltpu.SemaphoreType.DMA((13, few)),
            pltpu.SemaphoreType.DMA((35,)),
            pltpu.SemaphoreType.DMA((35,)),
        ],
        name="backward",
        compiler_params=pltpu.CompilerParams(
            collective_id=1, has_side_effects=True, vmem_limit_bytes=63 << 20
        ),
    )(real_lengths, tok_t, *forward_outs, gain_ffn, *weights, packed, *tables)


def paired_shards(
    tokens,
    out_grad,
    w_query,
    w_key,
    w_value,
    w_out,
    w_gate,
    w_up,
    w_down,
    gain_in,
    gain_post_attn,
    gain_pre_ffn,
    gain_post_ffn,
    gain_query,
    gain_key,
    bucket_lengths,
    true_lengths,
):
    tp_index = lax.axis_index("tp")
    rows = tokens.shape[0] // 2
    head_dim = w_key.shape[1]
    score_scale = head_dim ** (-0.5)
    tables = block_tables(2 * rows, head_dim)
    packed, offset = 0.0, 0
    all_gains = (gain_in, gain_post_attn, gain_pre_ffn, gain_post_ffn, gain_query, gain_key)
    length = sum(gain.size for gain in all_gains)
    for gain in all_gains:
        placed = jnp.pad(gain.astype(F32), (offset, length - offset - gain.size))
        packed, offset = packed + placed, offset + gain.size
    packed = packed.reshape(-1, 128)
    weights = (w_query, w_key, w_value, w_out, w_gate.T, w_up.T, w_down)
    out_t, gain_sum, *kept = forward(
        true_lengths, tokens.T, out_grad.T, weights, packed, tables
    )
    sums, xg_t, gain_rows, gain_cols = backward(
        true_lengths, tokens.T, kept, gain_sum, weights[:-1], packed, tables
    )
    hidden = w_down.shape[0]
    sizes = [hidden, hidden, hidden, head_dim, head_dim, head_dim // 2]
    ends = [sum(sizes[: j + 1]) for j in range(len(sizes))]
    down_sum, gate_sum, up_sum, out_sum, query_sum, mine = [
        sums[end - size : end] for size, end in zip(sizes, ends)
    ]
    far = lax.ppermute(mine, "tp", XOR2)
    near = lax.ppermute(jnp.stack([mine, far]), "tp", XOR1)
    kv_all = (mine, near[0], far, near[1])
    kv_sum = jnp.concatenate(
        [lax.select_n(tp_index ^ j, *kv_all) for j in range(4)], axis=0
    ).astype(F32).T
    return (
        out_t.T,
        xg_t.T,
        query_sum.astype(F32).T,
        kv_sum[:, :head_dim],
        kv_sum[:, head_dim:],
        out_sum.astype(F32),
        gate_sum.astype(F32).T,
        up_sum.astype(F32).T,
        down_sum.astype(F32),
        gain_cols[:, 0, : tokens.shape[1]].reshape(-1),
        gain_rows[0],
        gain_rows[1],
        gain_rows[2],
        gain_rows[3, :head_dim],
        gain_rows[3, head_dim : 2 * head_dim],
    )


def solution(mesh):
    def layer(*args):
        tokens, bucket_lengths = args[0], args[-2]
        sizes = mesh.shape
        group_rows = tokens.shape[0] // sizes["dp"]
        paired = (sizes["dp"], sizes["ctx"], sizes["tp"]) == (4, 2, 4) and (
            group_rows == 1024 * bucket_lengths.shape[1] == 2048
        )
        return mapped(paired_shards if paired else shards)(*args)

    def mapped(body):
        return jax.shard_map(
            body,
            mesh=mesh,
            in_specs=(
                P(("dp", "ctx"), "tp"),
                P(("dp", "ctx"), "tp"),
                P(None, "tp"),
                P(),
                P(),
                P("tp", None),
                P(None, "tp"),
                P(None, "tp"),
                P("tp", None),
                P(),
                P(),
                P(),
                P(),
                P(),
                P(),
                P("dp", None),
                P("dp", None),
            ),
            out_specs=(
                P(("dp", "ctx"), "tp"),
                P(("dp", "ctx"), "tp"),
                P(None, "tp"),
                P(),
                P(),
                P("tp", None),
                P(None, "tp"),
                P(None, "tp"),
                P("tp", None),
                P(),
                P(),
                P(),
                P(),
                P(),
                P(),
            ),
            check_vma=False,
        )

    return layer
```

```python
import math
from functools import partial

import jax
import jax.numpy as jnp
import numpy as np
from jax import lax
from jax.experimental import pallas as pl
from jax.experimental.pallas import tpu as pltpu
from jax.sharding import PartitionSpec as P

QBLK = 512


EPSILON = 1e-06
ROPE_BASE = 1000000.0
MASKED = -1e30


def contract(left, right, left_dim, right_dim):
    return lax.dot_general(
        left, right, (((left_dim,), (right_dim,)), ((), ())), preferred_element_type=jnp.float32
    )


def rms_norm(values, gain):
    return values * lax.rsqrt(jnp.mean(values * values, axis=-1, keepdims=True) + EPSILON) * gain


def rotate(values, cosine_table, sine_table):
    half_dim = values.shape[-1] // 2
    turned = jnp.concatenate([-values[..., half_dim:], values[..., :half_dim]], axis=-1)
    return values * cosine_table + turned * sine_table


def rope_tables(seq_pos, head_dim):
    freq_index = jnp.arange(head_dim // 2, dtype=jnp.float32)
    inverse = ROPE_BASE ** (-2.0 * freq_index / head_dim)
    angles = seq_pos.astype(jnp.float32)[:, None] * inverse[None, :]
    angles = jnp.concatenate([angles, angles], axis=-1)
    return (jnp.cos(angles), jnp.sin(angles))


def stream_layout(bucket_row, true_row, tok_dev, n_ctx):
    group_rows = tok_dev * n_ctx
    half_shard = tok_dev // 2
    row_ids = jnp.arange(group_rows, dtype=jnp.int32)
    device = row_ids // tok_dev
    half_index = row_ids % tok_dev // half_shard
    block_ids = jnp.where(half_index == 0, device, 2 * n_ctx - 1 - device)
    stream_pos = block_ids * half_shard + row_ids % half_shard
    starts = jnp.cumsum(bucket_row) - bucket_row
    ends = starts + bucket_row
    inside = (
        (stream_pos[:, None] >= starts[None, :]) & (stream_pos[:, None] < ends[None, :])
    ).astype(jnp.int32)
    slot_ids = jnp.arange(bucket_row.shape[0], dtype=jnp.int32)
    seq_ids = jnp.sum(inside * slot_ids[None, :], axis=1)
    seq_pos = stream_pos - jnp.sum(inside * starts[None, :], axis=1)
    is_valid = (seq_pos < jnp.sum(inside * true_row[None, :], axis=1)).astype(jnp.int32)
    return (seq_ids, stream_pos, seq_pos, is_valid)


def shape_heads(query_raw, key_raw, gain_q, gain_k, cosine_table, sine_table):
    query_heads = query_raw.reshape(query_raw.shape[0], -1, key_raw.shape[1])
    query_rot = rotate(
        rms_norm(query_heads, gain_q), cosine_table[:, None, :], sine_table[:, None, :]
    )
    key_rot = rotate(rms_norm(key_raw, gain_k), cosine_table, sine_table)
    return (query_rot, key_rot)


def geglu(gate_in, up_in):
    return jax.nn.gelu(gate_in, approximate=True) * up_in


def shards(
    tokens,
    out_grad,
    w_query,
    w_key,
    w_value,
    w_out,
    w_gate,
    w_up,
    w_down,
    gain_in,
    gain_post_attn,
    gain_pre_ffn,
    gain_post_ffn,
    gain_query,
    gain_key,
    bucket_lengths,
    true_lengths,
):
    n_ctx = lax.axis_size("ctx")
    ctx_index = lax.axis_index("ctx")
    tp_index = lax.axis_index("tp")
    rows_dev = tokens.shape[0]
    feature_cols = tokens.shape[1]
    head_dim = w_key.shape[1]
    head_count = w_query.shape[1] // head_dim
    group_rows = rows_dev * n_ctx
    blocks = rows_dev // QBLK
    score_scale = head_dim ** (-0.5)
    gain_in32, gain_pa32, gain_pf32, gain_pff32, gain_q32, gain_k32 = [
        tensor.astype(jnp.float32)
        for tensor in (gain_in, gain_post_attn, gain_pre_ffn, gain_post_ffn, gain_query, gain_key)
    ]
    input_full, cot_full = (
        lax.all_gather(tokens, "tp", axis=1, tiled=True),
        lax.all_gather(out_grad, "tp", axis=1, tiled=True),
    )
    inputs = input_full.astype(jnp.float32)
    seq_all, spos_all, rpos_all, valid_all = stream_layout(
        bucket_lengths[0], true_lengths[0], rows_dev, n_ctx
    )
    first_row = ctx_index * rows_dev
    seq_local = lax.dynamic_slice_in_dim(seq_all, first_row, rows_dev)
    spos_local = lax.dynamic_slice_in_dim(spos_all, first_row, rows_dev)
    rpos_local = lax.dynamic_slice_in_dim(rpos_all, first_row, rows_dev)
    cosine_table, sine_table = rope_tables(rpos_local, head_dim)
    normed_in, pull_in = jax.vjp(rms_norm, inputs, gain_in32)
    normed_in16 = normed_in.astype(jnp.bfloat16)
    query_raw = jnp.dot(normed_in16, w_query, preferred_element_type=jnp.float32)
    key_raw = jnp.dot(normed_in16, w_key, preferred_element_type=jnp.float32)
    value_raw = jnp.dot(normed_in16, w_value, preferred_element_type=jnp.float32)
    (query_rot, key_rot), rope_pull = jax.vjp(
        partial(shape_heads, cosine_table=cosine_table, sine_table=sine_table),
        query_raw,
        key_raw,
        gain_q32,
        gain_k32,
    )
    query16 = query_rot.astype(jnp.bfloat16)
    key16 = key_rot.astype(jnp.bfloat16)
    value16 = value_raw.astype(jnp.bfloat16)
    key_group, value_group = (
        lax.all_gather(key16, "ctx", axis=0, tiled=True),
        lax.all_gather(value16, "ctx", axis=0, tiled=True),
    )

    def allowed_mask(seq_rows, spos_rows):
        return (
            (valid_all[None, :] == 1)
            & (seq_all[None, :] == seq_rows[:, None])
            & (spos_all[None, :] <= spos_rows[:, None])
        )

    query_blocks = query16.reshape(blocks, QBLK, head_count, head_dim)
    seq_blocks = seq_local.reshape(blocks, QBLK)
    spos_blocks = spos_local.reshape(blocks, QBLK)

    def forward_block(block_item):
        query_block, seq_rows, spos_rows = block_item
        scores = (
            jnp.einsum("qhd,kd->hqk", query_block, key_group, preferred_element_type=jnp.float32)
            * score_scale
        )
        scores = jnp.where(allowed_mask(seq_rows, spos_rows)[None], scores, MASKED)
        row_max = jnp.max(scores, axis=-1, keepdims=True)
        exp_scores = jnp.exp(scores - row_max)
        row_total = jnp.sum(exp_scores, axis=-1, keepdims=True)
        prob_rows = (exp_scores / row_total).astype(jnp.bfloat16)
        output = jnp.einsum(
            "hqk,kd->qhd", prob_rows, value_group, preferred_element_type=jnp.float32
        )
        return (output, (row_max + jnp.log(row_total))[..., 0])

    attended, log_norm = lax.map(forward_block, (query_blocks, seq_blocks, spos_blocks))
    attended16 = attended.reshape(rows_dev, head_count * head_dim).astype(jnp.bfloat16)
    attention = lax.psum(
        jnp.dot(attended16, w_out, preferred_element_type=jnp.float32).astype(jnp.bfloat16), "tp"
    ).astype(jnp.float32)
    post_attn, pull_post_attn = jax.vjp(rms_norm, attention, gain_pa32)
    residual = inputs + post_attn
    normed_mid, pull_pre_ffn = jax.vjp(rms_norm, residual, gain_pf32)
    mid16 = normed_mid.astype(jnp.bfloat16)
    gate_out = jnp.dot(mid16, w_gate, preferred_element_type=jnp.float32)
    up_out = jnp.dot(mid16, w_up, preferred_element_type=jnp.float32)
    hidden, pull_geglu = jax.vjp(geglu, gate_out, up_out)
    hidden16 = hidden.astype(jnp.bfloat16)
    ffn_branch = lax.psum(
        jnp.dot(hidden16, w_down, preferred_element_type=jnp.float32).astype(jnp.bfloat16), "tp"
    ).astype(jnp.float32)
    post_ffn, pull_post_ffn = jax.vjp(rms_norm, ffn_branch, gain_pff32)
    outputs = residual + post_ffn
    out_rows = lax.dynamic_slice_in_dim(outputs, tp_index * feature_cols, feature_cols, 1).astype(
        jnp.bfloat16
    )
    cotangent = cot_full.astype(jnp.float32)
    d_ffn, d_gain_post_ffn = pull_post_ffn(cotangent)
    d_ffn16 = d_ffn.astype(jnp.bfloat16)
    d_hidden = contract(d_ffn16, w_down, 1, 1)
    grad_down = contract(hidden16, d_ffn16, 0, 0)
    d_gate, d_up = pull_geglu(d_hidden)
    d_gate16 = d_gate.astype(jnp.bfloat16)
    d_up16 = d_up.astype(jnp.bfloat16)
    grad_gate = contract(mid16, d_gate16, 0, 0)
    grad_up = contract(mid16, d_up16, 0, 0)
    d_mid = lax.psum(
        (contract(d_gate16, w_gate, 1, 1) + contract(d_up16, w_up, 1, 1)).astype(jnp.bfloat16), "tp"
    ).astype(jnp.float32)
    d_res_norm, d_gain_pre_ffn = pull_pre_ffn(d_mid)
    d_resid = cotangent + d_res_norm
    d_attn, d_gain_post_attn = pull_post_attn(d_resid)
    d_attn16 = d_attn.astype(jnp.bfloat16)
    d_attended16 = contract(d_attn16, w_out, 1, 1).astype(jnp.bfloat16)
    grad_out = contract(attended16, d_attn16, 0, 0)
    key_back, value_back = (key_group, value_group)

    def backward_block(running, block_item):
        key_sum, value_sum = running
        query_block, dout_block, lse_block, seq_rows, spos_rows = block_item
        scores = (
            jnp.einsum("qhd,kd->hqk", query_block, key_back, preferred_element_type=jnp.float32)
            * score_scale
        )
        scores = jnp.where(allowed_mask(seq_rows, spos_rows)[None], scores, MASKED)
        prob_rows = jnp.exp(scores - lse_block[..., None])
        prob16 = prob_rows.astype(jnp.bfloat16)
        d_probs = jnp.einsum(
            "qhd,kd->hqk", dout_block, value_back, preferred_element_type=jnp.float32
        )
        row_inner = jnp.sum(prob_rows * d_probs, axis=-1, keepdims=True)
        d_scores16 = (prob_rows * (d_probs - row_inner)).astype(jnp.bfloat16)
        d_query = (
            jnp.einsum("hqk,kd->qhd", d_scores16, key_back, preferred_element_type=jnp.float32)
            * score_scale
        )
        key_sum = (
            key_sum
            + jnp.einsum("hqk,qhd->kd", d_scores16, query_block, preferred_element_type=jnp.float32)
            * score_scale
        )
        value_sum = value_sum + jnp.einsum(
            "hqk,qhd->kd", prob16, dout_block, preferred_element_type=jnp.float32
        )
        return ((key_sum, value_sum), d_query)

    zero_rows = jnp.zeros((group_rows, head_dim), jnp.float32)
    (key_sum, value_sum), d_query_blocks = lax.scan(
        backward_block,
        (zero_rows, zero_rows),
        (
            query_blocks,
            d_attended16.reshape(blocks, QBLK, head_count, head_dim),
            log_norm,
            seq_blocks,
            spos_blocks,
        ),
    )
    d_key_rot, d_value = (
        lax.psum_scatter(
            key_sum.astype(jnp.bfloat16), "ctx", scatter_dimension=0, tiled=True
        ).astype(jnp.float32),
        lax.psum_scatter(
            value_sum.astype(jnp.bfloat16), "ctx", scatter_dimension=0, tiled=True
        ).astype(jnp.float32),
    )
    d_query_raw, d_key_raw, d_gain_query, d_gain_key = rope_pull(
        (d_query_blocks.reshape(rows_dev, head_count, head_dim), d_key_rot)
    )
    d_query16 = d_query_raw.astype(jnp.bfloat16)
    d_key16 = d_key_raw.astype(jnp.bfloat16)
    d_value16 = d_value.astype(jnp.bfloat16)
    grad_query = contract(normed_in16, d_query16, 0, 0)
    grad_key = contract(normed_in16, d_key16, 0, 0)
    grad_value = contract(normed_in16, d_value16, 0, 0)
    d_normed_part = (
        contract(d_query16, w_query, 1, 1)
        + contract(d_key16, w_key, 1, 1)
        + contract(d_value16, w_value, 1, 1)
    )
    d_normed_in = lax.psum(d_normed_part.astype(jnp.bfloat16), "tp").astype(jnp.float32)
    d_in_norm, d_gain_in = pull_in(d_normed_in)
    d_inputs = d_resid + d_in_norm
    grad_rows = lax.dynamic_slice_in_dim(d_inputs, tp_index * feature_cols, feature_cols, 1).astype(
        jnp.bfloat16
    )
    sharded = (
        grad_query,
        grad_out,
        grad_gate,
        grad_up,
        grad_down,
        d_gain_in,
        d_gain_post_attn,
        d_gain_pre_ffn,
        d_gain_post_ffn,
    )
    reduced = (
        lax.psum_scatter(
            sharded[0].astype(jnp.bfloat16), ("dp", "ctx"), scatter_dimension=0, tiled=True
        ).astype(jnp.float32),
        lax.psum_scatter(
            sharded[1].astype(jnp.bfloat16), ("dp", "ctx"), scatter_dimension=1, tiled=True
        ).astype(jnp.float32),
        lax.psum_scatter(
            sharded[2].astype(jnp.bfloat16), ("dp", "ctx"), scatter_dimension=0, tiled=True
        ).astype(jnp.float32),
        lax.psum_scatter(
            sharded[3].astype(jnp.bfloat16), ("dp", "ctx"), scatter_dimension=0, tiled=True
        ).astype(jnp.float32),
        lax.psum_scatter(
            sharded[4].astype(jnp.bfloat16), ("dp", "ctx"), scatter_dimension=1, tiled=True
        ).astype(jnp.float32),
        lax.psum_scatter(
            sharded[5].astype(jnp.bfloat16), ("dp", "ctx"), scatter_dimension=0, tiled=True
        ).astype(jnp.float32),
        lax.psum_scatter(
            sharded[6].astype(jnp.bfloat16), ("dp", "ctx"), scatter_dimension=0, tiled=True
        ).astype(jnp.float32),
        lax.psum_scatter(
            sharded[7].astype(jnp.bfloat16), ("dp", "ctx"), scatter_dimension=0, tiled=True
        ).astype(jnp.float32),
        lax.psum_scatter(
            sharded[8].astype(jnp.bfloat16), ("dp", "ctx"), scatter_dimension=0, tiled=True
        ).astype(jnp.float32),
    )
    summed = (
        lax.all_gather(reduced[0].astype(jnp.bfloat16), ("dp", "ctx"), axis=0, tiled=True).astype(
            jnp.float32
        ),
        lax.all_gather(reduced[1].astype(jnp.bfloat16), ("dp", "ctx"), axis=1, tiled=True).astype(
            jnp.float32
        ),
        lax.all_gather(reduced[2].astype(jnp.bfloat16), ("dp", "ctx"), axis=0, tiled=True).astype(
            jnp.float32
        ),
        lax.all_gather(reduced[3].astype(jnp.bfloat16), ("dp", "ctx"), axis=0, tiled=True).astype(
            jnp.float32
        ),
        lax.all_gather(reduced[4].astype(jnp.bfloat16), ("dp", "ctx"), axis=1, tiled=True).astype(
            jnp.float32
        ),
        lax.all_gather(reduced[5].astype(jnp.bfloat16), ("dp", "ctx"), axis=0, tiled=True).astype(
            jnp.float32
        ),
        lax.all_gather(reduced[6].astype(jnp.bfloat16), ("dp", "ctx"), axis=0, tiled=True).astype(
            jnp.float32
        ),
        lax.all_gather(reduced[7].astype(jnp.bfloat16), ("dp", "ctx"), axis=0, tiled=True).astype(
            jnp.float32
        ),
        lax.all_gather(reduced[8].astype(jnp.bfloat16), ("dp", "ctx"), axis=0, tiled=True).astype(
            jnp.float32
        ),
    )
    shared = lax.psum((grad_key, grad_value, d_gain_query, d_gain_key), ("dp", "ctx", "tp"))
    return (
        out_rows,
        grad_rows,
        summed[0],
        shared[0],
        shared[1],
        summed[1],
        summed[2],
        summed[3],
        summed[4],
        summed[5],
        summed[6],
        summed[7],
        summed[8],
        shared[2],
        shared[3],
    )


XOR1 = ((0, 1), (1, 0), (2, 3), (3, 2))
XOR2 = ((0, 2), (2, 0), (1, 3), (3, 1))
MESH = pl.DeviceIdType.MESH
GELU_SCALE = math.sqrt(2.0 / math.pi)
F32 = jnp.float32
BF16 = jnp.bfloat16


def add16(left, right):
    return (left.astype(F32) + right.astype(F32)).astype(BF16)


def block_tables(length, head_dim):
    freq_index = np.arange(head_dim // 2, dtype=np.float32)
    inverse = np.float32(ROPE_BASE) ** (np.float32(-2.0) * freq_index / np.float32(head_dim))
    angles = np.arange(length, dtype=np.float32)[:, None] * inverse.astype(np.float32)[None, :]
    angles = angles.astype(np.float64)
    return np.cos(angles).astype(np.float32), np.sin(angles).astype(np.float32)


def scale_of(values):
    return lax.rsqrt(jnp.mean(values * values, axis=-1, keepdims=True) + EPSILON)


STORED = 13


def row_blocks(base, rows, size, body, carry=None):
    def step(i, state):
        at = pl.ds(pl.multiple_of(base + i * size, size), size)
        return body(at, pl.ds(pl.multiple_of(i * size, size), size), state)

    return lax.fori_loop(0, rows // size, step, carry)


def spread_gains(packed, gains, head_gains):
    columns = gains.shape[1] // 128
    for j in range(4):
        for i in range(columns):
            at = j * columns + i
            gains[j : j + 1, 128 * i : 128 * i + 128] = packed[at : at + 1, :]
    head_columns = head_gains.shape[1] // 128
    for j in range(2):
        for i in range(head_columns):
            at = 4 * columns + j * head_columns + i
            head_gains[j : j + 1, 128 * i : 128 * i + 128] = packed[at : at + 1, :]


def turn_in(source, target, rows):
    for first in range(0, source.shape[0], 128):
        target[rows, first : first + 128] = source[first : first + 128, :].T


def column_tiles(total, size):
    return [(first, min(size, total - first)) for first in range(0, total, size)]


def dot_nn(left, right):
    return jnp.dot(left, right, preferred_element_type=F32)


def dot_nt(left, right):
    return contract(left, right, 1, 1)


def gelu_parts(gate):
    square = gate * gate
    tanh = jnp.tanh(GELU_SCALE * gate * (1.0 + 0.044715 * square))
    half = 0.5 + 0.5 * tanh
    slope = GELU_SCALE * (1.0 + 3.0 * 0.044715 * square)
    return gate * half, half + 0.5 * gate * (1.0 - tanh * tanh) * slope


def forward_kernel(
    real_lengths, tok, cot, w_q, w_k, w_v, w_o, w_g, w_u, w_d, packed, cosines, sines,
    out_t, gain_sum, *refs,
):
    stored, refs = refs[:STORED], refs[STORED:]
    kept, refs = refs[:STORED], refs[STORED:]
    x16, cot16, n16, q16, kv16, far_kv, att16, attn16, mid16, hid16, dffn16, dg16, du16 = kept
    blocks, v_qkv, v_o, v_g, v_u, v_d, part, near, far, ffn16, gains, head_gains = refs[:12]
    load_sem, own_sem, store_sem, g_send, g_recv, kv_send, kv_recv, s_send, s_recv = refs[12:]
    dp, ctx, tp = lax.axis_index("dp"), lax.axis_index("ctx"), lax.axis_index("tp")
    core_peer = (dp, ctx, tp + 1 - 2 * (tp % 2))
    x_index = (tp + 2) % 4
    x_peer = (dp, ctx, x_index)
    y_peer = (dp, 1 - ctx, tp)
    features, rows = tok.shape[0], tok.shape[1] // 2
    width = 4 * features
    hidden = w_d.shape[0]
    head_dim = w_k.shape[1]
    half = rows // 2
    odd = tp % 2

    loads = [
        pltpu.make_async_copy(source, target, load_sem.at[j])
        for j, (source, target) in enumerate(
            (
                (w_q, v_qkv.at[:, 0:head_dim]),
                (w_k, v_qkv.at[:, head_dim : 2 * head_dim]),
                (w_v, v_qkv.at[:, 2 * head_dim : 3 * head_dim]),
                (w_o, v_o), (w_g, v_g), (w_u, v_u), (w_d, v_d),
            )
        )
    ]
    for copy in loads:
        copy.start()

    def half_of(source, index):
        lane = (ctx if index % 2 == 0 else 1 - ctx) * rows
        return source.at[:, pl.ds(pl.multiple_of(lane, rows), rows)]

    def place(index, owner):
        return blocks.at[index, pl.ds(pl.multiple_of(owner * features, features), features)]

    sources = [half_of(tok, 0), half_of(tok, 1), half_of(cot, 0), half_of(cot, 1)]

    def remote(source, target, send, recv, peer):
        return pltpu.make_async_remote_copy(
            src_ref=source, dst_ref=target, send_sem=send, recv_sem=recv,
            device_id=peer, device_id_type=MESH,
        )

    own = [pltpu.make_async_copy(sources[j], place(j, tp), own_sem.at[j]) for j in range(4)]
    to_x = [
        remote(sources[j], place(j, tp), g_send.at[0, j], g_recv.at[0, j], x_peer) for j in range(4)
    ]
    to_core = [
        remote(sources[j], place(j, tp), g_send.at[1, j], g_recv.at[1, j], core_peer)
        for j in range(4)
    ]
    onward = [
        remote(place(j, x_index), place(j, x_index), g_send.at[2, j], g_recv.at[2, j], core_peer)
        for j in range(4)
    ]
    for copy in own:
        copy.start()
    barrier = pltpu.get_barrier_semaphore()
    for peer in (core_peer, x_peer, y_peer):
        pl.semaphore_signal(barrier, inc=1, device_id=peer, device_id_type=MESH)
    pl.semaphore_wait(barrier, 3)

    for j in range(4):
        to_core[j].start()
    to_x[0].start()
    to_x[1].start()

    spread_gains(packed, gains, head_gains)

    def store(j, c):
        at = slice(None) if c is None else chunk(c)
        return pltpu.make_async_copy(kept[j].at[at], stored[j].at[at], store_sem.at[j, c or 0])

    def pass_on(j):
        to_x[j].wait_recv()
        onward[j].start()

    def gathered(j):
        own[j].wait()
        to_core[j].wait_recv()
        onward[j].wait_recv()

    def chunk(c):
        return pl.ds(c * rows, rows)

    def normalise(c):
        turn_in(blocks.at[c], x16, chunk(c))

        def norm(at, _, carry):
            values = x16[at, :].astype(F32)
            n16[at, :] = (values * scale_of(values) * gains[0:1, :]).astype(BF16)

        row_blocks(c * rows, rows, 64, norm)

    def project(c):
        for first in range(0, rows, half):
            at = pl.ds(c * rows + first, half)
            tables = pl.ds(c * rows + first, half)
            values = dot_nn(n16[at, :], v_qkv[...])
            cosine, sine = cosines[tables, :], sines[tables, :]
            for j, target in ((0, q16.at[at, :]), (1, kv16.at[at, 0:head_dim])):
                head = values[:, j * head_dim : (j + 1) * head_dim]
                head = head * scale_of(head) * head_gains[j : j + 1, :]
                low, high = head[:, : head_dim // 2], head[:, head_dim // 2 :]
                target[:, : head_dim // 2] = (low * cosine - high * sine).astype(BF16)
                target[:, head_dim // 2 :] = (high * cosine + low * sine).astype(BF16)
            kv16[at, head_dim:] = values[:, 2 * head_dim :].astype(BF16)

    score_scale = head_dim ** (-0.5)

    def attend_rows(c):
        for first in range(0, rows, half):
            at = pl.ds(c * rows + first, half)
            query = q16[at, :]
            row_id = first + lax.broadcasted_iota(jnp.int32, (half, rows), 0)
            key_id = lax.broadcasted_iota(jnp.int32, (half, rows), 1)
            allowed = key_id <= row_id
            if c == 1:
                allowed = allowed & (rows + key_id < real_lengths[0, 1 - ctx])
            keys = [(kv16[chunk(c), :head_dim], kv16[chunk(c), head_dim:], allowed)]
            if c == 1:
                keys.append((far_kv[:, :head_dim], far_kv[:, head_dim:], None))
            scores = []
            for key, _, mask in keys:
                score = dot_nt(query, key) * score_scale
                scores.append(score if mask is None else jnp.where(mask, score, MASKED))
            most = scores[0].max(axis=1, keepdims=True)
            for score in scores[1:]:
                most = jnp.maximum(most, score.max(axis=1, keepdims=True))
            exps = [jnp.exp(score - most) for score in scores]
            total = sum(e.sum(axis=1, keepdims=True) for e in exps)
            out = sum(dot_nn((e / total).astype(BF16), k[1]) for e, k in zip(exps, keys))
            att16[at, :] = out.astype(BF16)
        part[c] = dot_nn(att16[chunk(c), :], v_o[...]).astype(BF16)

    def rows_of(index):
        return pl.ds(pl.multiple_of(index * half, half), half)

    def sum_copies(s, target):
        start = pl.multiple_of((s % 2) * rows + odd * half, half)
        final = target.at[pl.ds(start, half)]
        return (
            remote(part.at[s, rows_of(1 - odd)], near.at[s], s_send.at[0, s], s_recv.at[0, s], core_peer),
            remote(near.at[s], far.at[s], s_send.at[1, s], s_recv.at[1, s], x_peer),
            remote(final, final, s_send.at[2, s], s_recv.at[2, s], core_peer),
        )

    def sum_start(s, target):
        sum_copies(s, target)[0].start()

    def sum_cross(s, target):
        copies = sum_copies(s, target)
        copies[0].wait_recv()
        near[s] = add16(part[s, rows_of(odd)], near[s])
        copies[1].start()

    def sum_back(s, target):
        copies = sum_copies(s, target)
        copies[1].wait_recv()
        start = pl.multiple_of((s % 2) * rows + odd * half, half)
        target[pl.ds(start, half), :] = add16(near[s], far[s])
        copies[2].start()
        copies[2].wait_recv()

    def residual(at):
        branch = attn16[at, :].astype(F32)
        return x16[at, :].astype(F32) + branch * scale_of(branch) * gains[1:2, :]

    def middle(c):
        def body(at, _, carry):
            values = residual(at)
            mid16[at, :] = (values * scale_of(values) * gains[2:3, :]).astype(BF16)

        row_blocks(c * rows, rows, 64, body)

    def feed(c):
        for first, size in column_tiles(hidden, 256):
            for low in range(0, rows, half):
                at = pl.ds(c * rows + low, half)
                cols = pl.ds(first, size)
                gate = dot_nt(mid16[at, :], v_g[cols, :])
                up = dot_nt(mid16[at, :], v_u[cols, :])
                act, slope = gelu_parts(gate)
                hid16[at, cols] = (act * up).astype(BF16)
                dg16[at, cols] = (slope * up).astype(BF16)
                du16[at, cols] = act.astype(BF16)
        for first, size in column_tiles(width, 256):
            cols = pl.ds(first, size)
            part[2 + c, :, cols] = dot_nn(hid16[chunk(c), :], v_d[:, cols]).astype(BF16)

    def finish(c):
        turn_in(blocks.at[2 + c], cot16, chunk(c))
        sum_copies(c, attn16)[0].wait_send()
        onward[c].wait_send()

        def body(at, block, total):
            branch = ffn16[at, :].astype(F32)
            scale = scale_of(branch)
            unit = branch * scale
            grad = cot16[at, :].astype(F32)
            part[c, block, :] = (residual(at) + unit * gains[3:4, :]).astype(BF16)
            weighted = grad * gains[3:4, :]
            inner = jnp.mean(unit * weighted, axis=-1, keepdims=True)
            dffn16[at, :] = (scale * (weighted - unit * inner)).astype(BF16)
            return total + (grad * unit).reshape(-1, 8, width).sum(axis=0)

        total = row_blocks(c * rows, rows, 64, body, jnp.zeros((8, width), F32))
        if c == 0:
            gain_sum[...] = total
        else:
            gain_sum[...] += total
        for first in range(0, width, 128):
            blocks[c, first : first + 128, :] = part[c, :, first : first + 128].T
        lane = (ctx if c == 0 else 1 - ctx) * rows
        mine = blocks[c, pl.ds(pl.multiple_of(tp * features, features), features), :]
        out_t[:, pl.ds(pl.multiple_of(lane, rows), rows)] = mine

    def feed_back(c):
        for first, size in column_tiles(hidden, 256):
            for low in range(0, rows, half):
                at = pl.ds(c * rows + low, half)
                cols = pl.ds(first, size)
                d_hidden = dot_nt(dffn16[at, :], v_d[cols, :])
                dg16[at, cols] = (d_hidden * dg16[at, cols].astype(F32)).astype(BF16)
                du16[at, cols] = (d_hidden * du16[at, cols].astype(F32)).astype(BF16)

    kv_copy = remote(kv16.at[chunk(0)], far_kv, kv_send.at[0], kv_recv.at[0], y_peer)
    X, COT, N, Q, KV, FAR, ATT, ATTN, MID, HID, DFFN, DG, DU = range(STORED)
    started = []

    def store_all(c, *which):
        for j in which:
            store(j, c).start()
            started.append((j, c))

    pass_on(0)
    for copy in loads[:3]:
        copy.wait()
    gathered(0)
    normalise(0)
    project(0)
    kv_copy.start()
    store_all(0, X, N, Q, KV)
    pass_on(1)
    to_x[2].start()
    loads[3].wait()
    attend_rows(0)
    sum_start(0, attn16)
    gathered(1)
    normalise(1)
    sum_cross(0, attn16)
    project(1)
    store_all(1, X, N, Q, KV)
    kv_copy.wait_recv()
    attend_rows(1)
    sum_start(1, attn16)
    store_all(None, FAR)
    store_all(0, ATT)
    store_all(1, ATT)
    pass_on(2)
    sum_cross(1, attn16)
    sum_back(0, attn16)
    for copy in loads[4:]:
        copy.wait()
    middle(0)
    to_x[3].start()
    store_all(0, ATTN, MID)
    feed(0)
    sum_start(2, ffn16)
    store_all(0, HID)
    sum_back(1, attn16)
    middle(1)
    store_all(1, ATTN, MID)
    sum_cross(2, ffn16)
    pass_on(3)
    feed(1)
    sum_start(3, ffn16)
    store_all(1, HID)
    gathered(2)
    sum_cross(3, ffn16)
    sum_back(2, ffn16)
    finish(0)
    store_all(0, COT, DFFN)
    feed_back(0)
    store_all(0, DG, DU)
    gathered(3)
    sum_back(3, ffn16)
    finish(1)
    store_all(1, COT, DFFN)
    feed_back(1)
    store_all(1, DG, DU)
    for group in (to_x, to_core, onward[2:], [kv_copy]):
        for copy in group:
            copy.wait_send()
    for s, target in ((0, attn16), (1, attn16), (2, ffn16), (3, ffn16)):
        for copy in sum_copies(s, target)[1 if s < 2 else 0 :]:
            copy.wait_send()
    for j, c in started:
        store(j, c).wait()


def forward(real_lengths, tok_t, cot_t, weights, packed, tables):
    features, rows = tok_t.shape
    half = rows // 2
    width = 4 * features
    hidden = weights[-1].shape[0]
    head_dim = weights[1].shape[1]
    whole = pl.BlockSpec(memory_space=pltpu.VMEM)
    there = pl.BlockSpec(memory_space=pl.ANY)
    kept = [
        (rows, width), (rows, width), (rows, width), (rows, head_dim), (rows, 2 * head_dim),
        (half, 2 * head_dim), (rows, head_dim), (rows, width), (rows, width), (rows, hidden),
        (rows, width), (rows, hidden), (rows, hidden),
    ]

    return pl.pallas_call(
        forward_kernel,
        out_shape=(
            jax.ShapeDtypeStruct((features, rows), BF16), jax.ShapeDtypeStruct((8, width), F32),
            *[jax.ShapeDtypeStruct(shape, BF16) for shape in kept],
        ),
        in_specs=[pl.BlockSpec(memory_space=pltpu.SMEM)] + [there] * 9 + [whole] * 3,
        out_specs=[whole] * 2 + [there] * STORED,
        scratch_shapes=[pltpu.VMEM(shape, BF16) for shape in kept]
        + [
            pltpu.VMEM((4, width, half), BF16),
            pltpu.VMEM((width, 3 * head_dim), BF16),
            pltpu.VMEM((head_dim, width), BF16),
            pltpu.VMEM((hidden, width), BF16),
            pltpu.VMEM((hidden, width), BF16),
            pltpu.VMEM((hidden, width), BF16),
            pltpu.VMEM((4, half, width), BF16),
            pltpu.VMEM((4, half // 2, width), BF16),
            pltpu.VMEM((4, half // 2, width), BF16),
            pltpu.VMEM((rows, width), BF16),
            pltpu.VMEM((4, width), F32),
            pltpu.VMEM((2, head_dim), F32),
            pltpu.SemaphoreType.DMA((7,)),
            pltpu.SemaphoreType.DMA((4,)),
            pltpu.SemaphoreType.DMA((STORED, 2)),
            pltpu.SemaphoreType.DMA((3, 4)),
            pltpu.SemaphoreType.DMA((3, 4)),
            pltpu.SemaphoreType.DMA((1,)),
            pltpu.SemaphoreType.DMA((1,)),
            pltpu.SemaphoreType.DMA((3, 4)),
            pltpu.SemaphoreType.DMA((3, 4)),
        ],
        name="forward",
        compiler_params=pltpu.CompilerParams(
            collective_id=2, has_side_effects=True, vmem_limit_bytes=63 << 20
        ),
    )(real_lengths, tok_t, cot_t, *weights, packed, *tables)


def backward_kernel(
    step_rows, steps, few, lag,
    real_lengths, tok, x_in, cot_in, n_in, q_in, kv_in, far_in, att_in, attn_in, mid_in, hid_in,
    dffn_in, dg_in, du_in, gain_ffn, w_q, w_k, w_v, w_o, w_g, w_u, packed, cosines, sines,
    out, xg_t, gain_rows, gain_cols,
    g, y2, z2, m2, z1, m1, y1, a3, b3, hid, dg, du, mid, dffn, w_tiles, part, near, far, dm, cot, attn,
    v_o, v_qkv, dkv_new, norm_near, norm_far, row_part,
    row_near, kv_near, kv_far, turned, head_sums, row_sums, sum_slots, sum_new, col_slots,
    col_new, gains, head_gains, gain_col, col_part,
    load_sem, tile_sem, keep_sem, keep_few, chain_send, chain_recv, few_send, few_recv, peer_send,
    peer_recv,
):
    dp, ctx, tp = lax.axis_index("dp"), lax.axis_index("ctx"), lax.axis_index("tp")
    s, K = step_rows, steps
    upper = dp // 2
    odd = tp % 2
    outer = (dp == 0) | (dp == 3)
    inner = jnp.logical_not(outer)
    yes = dp >= 0
    core_index = tp + 1 - 2 * odd
    x_index = (tp + 2) % 4
    z_index = dp + 1 - 2 * (dp % 2)
    core_peer, x_peer = (dp, ctx, core_index), (dp, ctx, x_index)
    y_peer, z_peer, m_peer = (dp, 1 - ctx, tp), (z_index, ctx, tp), (3 - dp, ctx, tp)
    features, rows = tok.shape[0], tok.shape[1] // 2
    width = 4 * features
    hidden = w_g.shape[0]
    head_dim = w_k.shape[1]
    half = rows // 2
    kv_rows = head_dim // 2
    score_scale = head_dim ** (-0.5)

    def remote(source, target, send, recv, peer):
        return pltpu.make_async_remote_copy(
            src_ref=source, dst_ref=target, send_sem=send, recv_sem=recv,
            device_id=peer, device_id_type=MESH,
        )

    def chunk(c):
        return pl.ds(c * rows, rows)

    def multiple(start, size):
        return pl.ds(pl.multiple_of(start, size), size)

    dqkv, kv16 = dg.at[:, 0 : 3 * head_dim], dg.at[:, 3 * head_dim : 5 * head_dim]
    dkv, dkv_far = du.at[:, 0 : 2 * head_dim], du.at[0:rows, 2 * head_dim : 4 * head_dim]
    far_kv = du.at[rows : 2 * rows, 2 * head_dim : 4 * head_dim]
    q16, att = du.at[:, 4 * head_dim : 5 * head_dim], du.at[:, 5 * head_dim : 6 * head_dim]

    tok_own = dm.at[0:features, 0 : 2 * rows]

    pairs = (
        (hid_in, hid), (dffn_in, dffn), (du_in, du), (mid_in, mid), (dg_in, dg), (cot_in, cot),
        (attn_in, attn), (w_o, v_o),
        (w_q, v_qkv.at[:, 0:head_dim]), (w_k, v_qkv.at[:, head_dim : 2 * head_dim]),
        (w_v, v_qkv.at[:, 2 * head_dim : 3 * head_dim]),
    )
    count = len(pairs)

    def load(j):
        return pltpu.make_async_copy(pairs[j][0], pairs[j][1], load_sem.at[j])

    late_pairs = (
        (x_in, dffn), (n_in, mid), (q_in, q16), (kv_in, kv16), (far_in, far_kv), (att_in, att),
    )

    def load_tok():
        return pltpu.make_async_copy(tok, tok_own, load_sem.at[count + len(late_pairs)])

    def late_load(j):
        return pltpu.make_async_copy(late_pairs[j][0], late_pairs[j][1], load_sem.at[count + j])

    for j in range(count):
        load(j).start()
    barrier = pltpu.get_barrier_semaphore()
    for peer in (core_peer, x_peer, y_peer, z_peer, m_peer):
        pl.semaphore_signal(barrier, inc=1, device_id=peer, device_id_type=MESH)
    pl.semaphore_wait(barrier, 5)

    third = 3
    enter1, enter3 = 2 * lag, 0
    base3 = 2 * s * K
    base = base3 + 2 * s * few
    ring, ring_few = 4 * lag + 1, -(-(4 * lag + 1) // third) + 1

    def rows2(k, h):
        return multiple((2 * k + h) * s, s)

    def rows1(k, h):
        return multiple(base + (2 * k + h) * s, s)

    def rows3(k, h):
        return multiple(base3 + (2 * k + h) * s, s)

    def pair1(k):
        return pl.ds(pl.multiple_of(base + 2 * k * s, s), 2 * s)

    def slot(k):
        return multiple((k % ring) * s, s)

    def slot_few(k):
        return multiple((k % ring_few) * s, s)

    def slot_pair(k):
        return multiple((k % ring_few) * 2 * s, 2 * s)

    def slot_half(k, h):
        return multiple(((k % ring_few) * 2 + h) * s, s)

    def chain(j, k, source, target, peer):
        if j < 5:
            return remote(source, target, chain_send.at[j, k], chain_recv.at[j, k], peer)
        return remote(source, target, few_send.at[j - 5, k], few_recv.at[j - 5, k], peer)

    def c_y2(k):
        return chain(0, k, g.at[rows2(k, 1 - ctx)], y2.at[slot(k)], y_peer)

    def c_z2(k):
        return chain(1, k, y2.at[slot(k)], z2.at[slot(k)], z_peer)

    def c_m2(k):
        return chain(2, k, z2.at[slot(k)], m2.at[slot(k)], m_peer)

    def c_fo(k):
        return chain(3, k, m2.at[slot(k)], out.at[rows2(k, ctx)], z_peer)

    def c_fy(k):
        return chain(4, k, m2.at[slot(k)], out.at[rows2(k, ctx)], y_peer)

    def c_fy_outer(k):
        return chain(4, k, out.at[rows2(k, ctx)], out.at[rows2(k, ctx)], y_peer)

    def c_z1(k):
        return chain(5, k, g.at[pair1(k)], z1.at[slot_pair(k)], z_peer)

    def c_m1(k):
        return chain(6, k, z1.at[slot_half(k, 1 - upper)], m1.at[slot_few(k)], m_peer)

    def c_y1(k):
        return chain(7, k, m1.at[slot_few(k)], y1.at[slot_few(k)], y_peer)

    def c_fm(k):
        return chain(8, k, y1.at[slot_few(k)], out.at[rows1(k, upper)], m_peer)

    def c_fa(k):
        return chain(9, k, y1.at[slot_few(k)], out.at[rows1(k, upper)], z_peer)

    def c_fb(k):
        return chain(10, k, out.at[rows1(k, 1 - upper)], out.at[rows1(k, 1 - upper)], z_peer)

    def c_3up(k):
        return chain(11, k, g.at[rows3(k, 1 - upper)], a3.at[slot_few(k)], z_peer)

    def c_3mid(k):
        return chain(12, k, a3.at[slot_few(k)], b3.at[slot_few(k)], m_peer)

    def c_3end(k):
        return chain(13, k, b3.at[slot_few(k)], a3.at[slot_few(k)], z_peer)

    def c_3y(k):
        return chain(14, k, a3.at[slot_few(k)], b3.at[slot_few(k)], y_peer)

    def c_3back(k):
        return chain(15, k, b3.at[slot_few(k)], out.at[rows3(k, upper)], z_peer)

    def c_3over(k):
        return chain(16, k, out.at[rows3(k, upper)], out.at[rows3(k, upper)], m_peer)

    def c_3last(k):
        return chain(17, k, out.at[rows3(k, 1 - upper)], out.at[rows3(k, 1 - upper)], z_peer)

    def keep2(k):
        return pltpu.make_async_copy(m2.at[slot(k)], out.at[rows2(k, ctx)], keep_sem.at[k])

    def keep1(k):
        return pltpu.make_async_copy(y1.at[slot_few(k)], out.at[rows1(k, upper)], keep_few.at[0, k])

    def keep3(k):
        return pltpu.make_async_copy(b3.at[slot_few(k)], out.at[rows3(k, upper)], keep_few.at[1, k])

    def inner3_mid(k):
        c_3up(k).wait_recv()
        a3[slot_few(k), :] = add16(a3[slot_few(k), :], g[rows3(k, 1 - upper), :])
        c_3mid(k).start()

    def inner3_end(k):
        c_3mid(k).wait_recv()
        b3[slot_few(k), :] = add16(b3[slot_few(k), :], g[rows3(k, upper), :])
        c_3end(k).start()

    def outer3_y(k):
        c_3end(k).wait_recv()
        a3[slot_few(k), :] = add16(a3[slot_few(k), :], g[rows3(k, upper), :])
        c_3y(k).start()

    def outer3_back(k):
        c_3y(k).wait_recv()
        b3[slot_few(k), :] = add16(b3[slot_few(k), :], a3[slot_few(k), :])
        c_3back(k).start()
        keep3(k).start()

    def inner3_over(k):
        c_3back(k).wait_recv()
        c_3over(k).start()

    def inner3_last(k):
        c_3over(k).wait_recv()
        c_3last(k).start()

    def outer3_done(k):
        c_3last(k).wait_recv()
        c_3up(k).wait_send()

    def inner3_done(k):
        c_3over(k).wait_send()
        c_3last(k).wait_send()

    def outer3_sent(k):
        c_3back(k).wait_send()
        keep3(k).wait()

    def b2(k):
        c_y2(k).wait_recv()
        y2[slot(k), :] = add16(y2[slot(k), :], g[rows2(k, ctx), :])
        pl.when(outer)(lambda: c_z2(k).start())

    def b1(k):
        c_z1(k).wait_recv()
        z1[slot_pair(k), :] = add16(z1[slot_pair(k), :], g[pair1(k), :])
        c_m1(k).start()

    def c2(k):
        c_z2(k).wait_recv()
        z2[slot(k), :] = add16(z2[slot(k), :], y2[slot(k), :])
        c_m2(k).start()

    def c1(k):
        c_m1(k).wait_recv()
        m1[slot_few(k), :] = add16(m1[slot_few(k), :], z1[slot_half(k, upper), :])
        c_y1(k).start()

    def d2(k):
        c_m2(k).wait_recv()
        m2[slot(k), :] = add16(m2[slot(k), :], z2[slot(k), :])
        c_fo(k).start()
        c_fy(k).start()
        keep2(k).start()

    def d1(k):
        c_y1(k).wait_recv()
        y1[slot_few(k), :] = add16(y1[slot_few(k), :], m1[slot_few(k), :])
        c_fm(k).start()
        c_fa(k).start()
        keep1(k).start()

    def e2(k):
        c_fo(k).wait_recv()
        c_fy_outer(k).start()

    def e1(k):
        c_fm(k).wait_recv()
        c_fb(k).start()

    def f2(k):
        c_fy(k).wait_recv()
        c_y2(k).wait_send()

    def f2_outer(k):
        c_fy_outer(k).wait_send()

    def f1_outer(k):
        c_fa(k).wait_recv()
        c_fb(k).wait_recv()
        c_z1(k).wait_send()

    def f2_inner(k):
        keep2(k).wait()
        c_fo(k).wait_send()
        c_fy(k).wait_send()

    def f1_inner(k):
        keep1(k).wait()
        for copy in (c_fm, c_fa, c_fb):
            copy(k).wait_send()

    two, one, three = (K, 1, 0), (few, third, enter1), (few, third, enter3)
    hops = (
        (5, yes, two, f2), (5, outer, two, f2_outer), (5, outer, one, f1_outer),
        (5, inner, two, f2_inner), (5, inner, one, f1_inner),
        (7, outer, three, outer3_done), (7, inner, three, inner3_done),
        (6, outer, three, outer3_sent),
        (5, outer, three, lambda k: c_3y(k).wait_send()),
        (4, inner, two, lambda k: c_m2(k).wait_send()),
        (4, inner, one, lambda k: c_y1(k).wait_send()),
        (3, outer, two, lambda k: c_z2(k).wait_send()),
        (3, inner, one, lambda k: c_m1(k).wait_send()),
        (3, inner, three, lambda k: c_3mid(k).wait_send()),
        (3, inner, three, lambda k: c_3end(k).wait_send()),
        (6, inner, three, inner3_last), (5, inner, three, inner3_over),
        (4, outer, two, e2), (4, inner, one, e1), (4, outer, three, outer3_back),
        (3, inner, two, d2), (3, inner, one, d1), (3, outer, three, outer3_y),
        (2, inner, two, c2), (2, inner, one, c1), (2, inner, three, inner3_end),
        (1, yes, two, b2), (1, inner, one, b1), (1, inner, three, inner3_mid),
        (0, yes, two, lambda k: c_y2(k).start()), (0, outer, one, lambda k: c_z1(k).start()),
        (0, outer, three, lambda k: c_3up(k).start()),
    )

    def grad_tile(index, first, size):
        left, right = ((hid, dffn), (dg, mid), (du, mid))[index]
        at = first if isinstance(first, int) else pl.multiple_of(first, 256)
        tile = contract(left[:, pl.ds(at, size)], right[...], 0, 0)
        start = index * hidden + first
        g[pl.ds(start if isinstance(start, int) else pl.multiple_of(start, 64), size), :] = (
            tile.astype(BF16)
        )

    full = hidden // 256
    tail = hidden - 256 * full

    wide = width // 256
    rest = width - 256 * wide
    tiles = wide + (rest > 0)

    def fetch(slot, first, size):
        return [
            pltpu.make_async_copy(
                w.at[:, pl.ds(first, size)], w_tiles.at[i, slot, :, pl.ds(0, size)],
                tile_sem.at[i, slot],
            )
            for i, w in enumerate((w_g, w_u))
        ]

    def fetch_start(slot, first, size):
        for copy in fetch(slot, first, size):
            copy.start()

    def mid_term(c, slot, first, size):
        for copy in fetch(slot, first, size):
            copy.wait()
        at = multiple(c * rows, rows)
        term = dot_nn(dg[at, :], w_tiles[0, slot, :, 0:size]) + dot_nn(
            du[at, :], w_tiles[1, slot, :, 0:size]
        )
        part[c, :, pl.ds(first, size)] = term.astype(BF16)

    mid_first, mid_each = 4, (wide + 1) // 2

    def mid_at(t):
        since = t - mid_first
        c = 1 - since // (mid_each + 1)
        turn = since % (mid_each + 1)

        def tile(i, carry):
            n = 2 * turn + i
            slot = ((1 - c) * tiles + n) % 2
            pl.when(n + 1 < wide)(
                lambda: fetch_start(1 - slot, pl.multiple_of(256 * (n + 1), 256), 256)
            )
            if rest:
                pl.when(n + 1 == wide)(lambda: fetch_start(1 - slot, 256 * wide, rest))
            mid_term(c, slot, pl.multiple_of(256 * n, 256), 256)
            return carry

        def full_tiles():
            lax.fori_loop(0, 2, tile, 0)

        pl.when(turn < mid_each)(full_tiles)

        def last_tile():
            slot = ((1 - c) * tiles + wide) % 2
            pl.when(c == 1)(lambda: fetch_start(1 - slot, 0, 256))
            if rest:
                mid_term(c, slot, 256 * wide, rest)

        pl.when(turn == mid_each)(last_tile)

    def own_half(index):
        return multiple(index * half, half)

    def peer_copy(j, source, target, peer):
        return remote(source, target, peer_send.at[j], peer_recv.at[j], peer)

    def sum_copies(c):
        final = dm.at[multiple(c * rows + odd * half, half)]
        return (
            peer_copy(3 * c, part.at[c, own_half(1 - odd)], near.at[c], core_peer),
            peer_copy(3 * c + 1, near.at[c], far.at[c], x_peer),
            peer_copy(3 * c + 2, final, final, core_peer),
        )

    def sum_cross(c):
        copies = sum_copies(c)
        copies[0].wait_recv()
        near[c] = add16(part[c, own_half(odd)], near[c])
        copies[1].start()

    def sum_back(c):
        copies = sum_copies(c)
        copies[1].wait_recv()
        dm[multiple(c * rows + odd * half, half), :] = add16(near[c], far[c])
        copies[2].start()

    def norms_back(base):
        def body(at, _, state):
            branch = attn[at, :].astype(F32)
            scale_a = scale_of(branch)
            unit_a = branch * scale_a
            resid = dffn[at, :].astype(F32) + unit_a * gains[1:2, :]
            scale_r = scale_of(resid)
            unit_r = resid * scale_r
            grad = dm[at, :].astype(F32)
            weighted = grad * gains[2:3, :]
            mean = jnp.mean(unit_r * weighted, axis=-1, keepdims=True)
            d_resid = cot[at, :].astype(F32) + scale_r * (weighted - unit_r * mean)
            weighted = d_resid * gains[1:2, :]
            mean = jnp.mean(unit_a * weighted, axis=-1, keepdims=True)
            cot[at, :] = d_resid.astype(BF16)
            attn[at, :] = (scale_a * (weighted - unit_a * mean)).astype(BF16)
            return (
                state[0] + (d_resid * unit_a).reshape(-1, 8, width).sum(axis=0),
                state[1] + (grad * unit_r).reshape(-1, 8, width).sum(axis=0),
            )

        zero = jnp.zeros((8, width), F32)
        sum_a, sum_r = row_blocks(base, half, 64, body, (zero, zero))
        row_sums[0] += sum_a
        row_sums[1] += sum_r

    norm_steps = ((13, rows), (14, rows + half), (17, 0), (18, half))

    def norms_at(t):
        base = sum(jnp.where(t == step, start, 0) for step, start in norm_steps)
        now = sum(jnp.where(t == step, 1, 0) for step, _ in norm_steps)
        pl.when(now > 0)(lambda: norms_back(base))

    def head_back(grad, at, j):
        cosine, sine = cosines[at, :], sines[at, :]
        low, high = grad[:, : head_dim // 2], grad[:, head_dim // 2 :]
        grad = jnp.concatenate([low * cosine + high * sine, high * cosine - low * sine], axis=1)
        cols = pl.ds(j * head_dim, head_dim)
        raw = dot_nn(mid[at, :], v_qkv[:, cols])
        scale = scale_of(raw)
        unit = raw * scale
        weighted = grad * head_gains[j : j + 1, :]
        mean = jnp.mean(unit * weighted, axis=-1, keepdims=True)
        dqkv[at, cols] = (scale * (weighted - unit * mean)).astype(BF16)
        head_sums[j] += (grad * unit).reshape(-1, 8, head_dim).sum(axis=0)

    block_rows = 128

    def over_rows(low, high, body):
        def step(i, carry):
            body(pl.multiple_of(low + i * block_rows, block_rows))
            return carry

        lax.fori_loop(0, (high - low) // block_rows, step, 0)

    def attend_back_rows(c, second):
        def block(first):
            d_keys, d_values = [0.0, 0.0], [0.0, 0.0]
            at = multiple(c * rows + first, block_rows)
            query = q16[at, :]
            d_out = dot_nt(attn[at, :], v_o[...]).astype(BF16)
            row_id = first + lax.broadcasted_iota(jnp.int32, (block_rows, rows), 0)
            key_id = lax.broadcasted_iota(jnp.int32, (block_rows, rows), 1)
            allowed = key_id <= row_id
            if c == 1:
                allowed = allowed & (rows + key_id < real_lengths[0, 1 - ctx])
            keys = [(kv16[chunk(c), :head_dim], kv16[chunk(c), head_dim:], allowed)]
            if c == 1:
                keys.append((far_kv[:, :head_dim], far_kv[:, head_dim:], None))
            scores = []
            for key, _, mask in keys:
                score = dot_nt(query, key) * score_scale
                scores.append(score if mask is None else jnp.where(mask, score, MASKED))
            most = scores[0].max(axis=1, keepdims=True)
            for score in scores[1:]:
                most = jnp.maximum(most, score.max(axis=1, keepdims=True))
            exps = [jnp.exp(score - most) for score in scores]
            total = sum(e.sum(axis=1, keepdims=True) for e in exps)
            probs = [e / total for e in exps]
            d_probs = [dot_nt(d_out, key[1]) for key in keys]
            mean = sum((p * d).sum(axis=1, keepdims=True) for p, d in zip(probs, d_probs))
            d_query = 0.0
            for i, key in enumerate(keys):
                d_score = (probs[i] * (d_probs[i] - mean)).astype(BF16)
                d_query += dot_nn(d_score, key[0])
                d_keys[i] += contract(d_score, query, 0, 0)
                d_values[i] += contract(probs[i].astype(BF16), d_out, 0, 0)
            head_back(d_query * score_scale, at, 0)
            places = [dkv.at[chunk(c), :]] + [dkv_far] * c
            for i, place in enumerate(places):
                for cols, term in (
                    (pl.ds(0, head_dim), d_keys[i] * score_scale),
                    (pl.ds(head_dim, head_dim), d_values[i]),
                ):
                    place[:, cols] = (place[:, cols].astype(F32) + term).astype(BF16)

        if c == 1 and not second:
            dkv[...] = jnp.zeros((2 * rows, 2 * head_dim), BF16)
            dkv_far[...] = jnp.zeros((rows, 2 * head_dim), BF16)
        over_rows(second * half, second * half + half, block)
        if c == 1 and second:
            far_copies()[0].start()

    quarter = half // 2
    far_rows = multiple(odd * half + tp // 2 * quarter, quarter)

    def far_copies():
        given = dkv_far.at[multiple(odd * half + (1 - tp // 2) * quarter, quarter), :]
        return (
            peer_copy(33, dkv_far.at[own_half(1 - odd), :], dkv_new.at[0:half], core_peer),
            peer_copy(34, given, dkv_new.at[half : half + quarter], x_peer),
            peer_copy(6, dkv_far.at[far_rows, :], dkv_new.at[half + quarter : 2 * half], y_peer),
        )

    def far_cross():
        copies = far_copies()
        copies[0].wait_recv()
        dkv_far[own_half(odd), :] = add16(dkv_far[own_half(odd), :], dkv_new[0:half, :])
        copies[1].start()

    def far_up():
        copies = far_copies()
        copies[1].wait_recv()
        dkv_far[far_rows, :] = add16(dkv_far[far_rows, :], dkv_new[half : half + quarter, :])
        copies[2].start()

    def keys_back(c):
        if c == 0:
            far_copies()[2].wait_recv()
            dkv[far_rows, :] = add16(dkv[far_rows, :], dkv_new[half + quarter : 2 * half, :])
        def block(first):
            at = multiple(c * rows + first, block_rows)
            grad = dkv[at, :].astype(F32)
            head_back(grad[:, :head_dim], at, 1)
            dqkv[at, 2 * head_dim :] = grad[:, head_dim:].astype(BF16)

        over_rows(0, rows, block)

    def cell(c, j):
        index = 4 * c + j
        return hid.at[pl.ds(index // 3 * features, features), pl.ds(index % 3 * rows, rows)]

    def owner_of(j):
        near_one = tp + (j % 2) * (1 - 2 * odd)
        return (near_one + 2 * (j // 2)) % 4

    def cell_at(index):
        return hid.at[
            multiple(index // 3 * features, features), multiple(index % 3 * rows, rows)
        ]

    def scatter_copies(c):
        return (
            peer_copy(7 + 6 * c, cell(c, 1), norm_near.at[c, 0], core_peer),
            peer_copy(8 + 6 * c, cell(c, 3), norm_near.at[c, 1], core_peer),
            peer_copy(9 + 6 * c, row_part.at[c, 0], row_near.at[c, 0], core_peer),
            peer_copy(10 + 6 * c, cell(c, 2), norm_far.at[c], x_peer),
            peer_copy(11 + 6 * c, row_part.at[c, 1], row_near.at[c, 1], x_peer),
        )

    def scatter_begin(c):
        def features_of(j, carry):
            weights = v_qkv[multiple(owner_of(j) * features, features), :]
            cell_at(4 * c + j)[...] = dot_nt(weights, dqkv[chunk(c), :]).astype(BF16)
            return carry

        lax.fori_loop(0, 4, features_of, 0)
        def block(first):
            at = multiple(c * rows + first, block_rows)
            raw = dot_nn(mid[at, :], v_qkv[...])
            inner_sum = (raw * dqkv[at, :].astype(F32)).sum(axis=1, keepdims=True)
            scale = scale_of(dffn[at, :].astype(F32))
            lane = lax.broadcasted_iota(jnp.int32, (block_rows, 128), 1)
            both = jnp.where(lane == 0, inner_sum, scale)
            row_part[c, 0, :, pl.ds(first, block_rows)] = both.T[0:8, :]

        over_rows(0, rows, block)
        for copy in scatter_copies(c)[:3]:
            copy.start()

    def scatter_cross(c):
        copies = scatter_copies(c)
        for copy in copies[:3]:
            copy.wait_recv()
        cell(c, 0)[...] = add16(cell(c, 0)[...], norm_near[c, 0])
        cell(c, 2)[...] = add16(cell(c, 2)[...], norm_near[c, 1])
        row_part[c, 1] = row_part[c, 0] + row_near[c, 0]
        copies[3].start()
        copies[4].start()

    def scatter_end(c):
        copies = scatter_copies(c)
        copies[3].wait_recv()
        copies[4].wait_recv()
        for first in range(0, width, 128):
            turned[first : first + 128, :] = cot[chunk(c), first : first + 128].T
        lane = (ctx if c == 0 else 1 - ctx) * rows
        lanes = pl.ds(pl.multiple_of(lane, rows), rows)
        grad = cell(c, 0)[...].astype(F32) + norm_far[c].astype(F32)
        values = tok_own[:, lanes].astype(F32)
        scale = row_part[c, 0, 1:2, :]
        inner_sum = row_part[c, 1, 0:1, :] + row_near[c, 1, 0:1, :]
        d_in = scale * (grad * gain_col[:, 0:1]) - values * (
            scale * scale * inner_sum * (1.0 / width)
        )
        d_resid = turned[multiple(tp * features, features), :].astype(F32)
        xg_t[:, lanes] = (d_resid + d_in).astype(BF16)
        column = jnp.sum(grad * values * scale, axis=1, keepdims=True)
        column = jnp.broadcast_to(column, (features, 128))
        for first, size in column_tiles(features, 128):
            block = column[first : first + size, :]
            if size < 128:
                block = jnp.concatenate([block, jnp.zeros((128 - size, 128), F32)], axis=0)
            cols = pl.ds(first, 128)
            if c == 1:
                col_slots[0, :, cols] = block.T[0:8, :]
            else:
                col_slots[0, :, cols] += block.T[0:8, :]

    at_out = 3 * hidden
    at_query = at_out + head_dim
    at_kv = at_query + head_dim

    def out_grad():
        g[pl.ds(at_out, head_dim), :] = contract(att[...], attn[...], 0, 0).astype(BF16)

    def query_grad():
        g[pl.ds(at_query, head_dim), :] = contract(dqkv[:, :head_dim], mid[...], 0, 0).astype(BF16)

    def kv_grads():
        sum_copies(1)[0].wait_send()

        def block(j, carry):
            cols = multiple(head_dim + owner_of(j) * kv_rows, kv_rows)
            term = contract(dqkv[:, cols], mid[...], 0, 0)
            part[1, multiple(j * kv_rows, kv_rows), :] = term.astype(BF16)
            return carry

        lax.fori_loop(0, 4, block, 0)
        for copy in kv_copies()[:2]:
            copy.start()

    def kv_copies():
        return (
            peer_copy(19, part.at[1, pl.ds(kv_rows, kv_rows)], kv_near.at[0], core_peer),
            peer_copy(20, part.at[1, pl.ds(3 * kv_rows, kv_rows)], kv_near.at[1], core_peer),
            peer_copy(21, part.at[1, pl.ds(2 * kv_rows, kv_rows)], kv_far, x_peer),
        )

    def kv_cross():
        copies = kv_copies()
        copies[0].wait_recv()
        copies[1].wait_recv()
        for j in range(2):
            at = pl.ds(2 * j * kv_rows, kv_rows)
            part[1, at, :] = add16(part[1, at, :], kv_near[j])
        copies[2].start()

    def kv_end():
        kv_copies()[2].wait_recv()
        g[pl.ds(at_kv, kv_rows), :] = add16(part[1, pl.ds(0, kv_rows), :], kv_far[...])

    sum_peers = (core_peer, x_peer, y_peer, z_peer, m_peer)

    def sum_copy(j):
        return peer_copy(22 + j, sum_slots.at[j], sum_new.at[j], sum_peers[j])

    def col_copy(j):
        return peer_copy(27 + j, col_slots.at[j], col_new.at[j], sum_peers[2 + j])

    def gains_begin():
        sum_slots[0] = jnp.zeros((8, width), F32)
        for j, values in enumerate((row_sums[0], row_sums[1], gain_ffn[...])):
            sum_slots[0, j : j + 1, :] = 0.25 * values.sum(axis=0, keepdims=True)
        for j in range(2):
            sum_slots[0, 3:4, j * head_dim : (j + 1) * head_dim] = head_sums[j].sum(
                axis=0, keepdims=True
            )
        sum_copy(0).start()
        col_copy(0).start()

    def gains_hop(j):
        sum_copy(j).wait_recv()
        if j < 4:
            sum_slots[j + 1] = sum_slots[j] + sum_new[j]
            sum_copy(j + 1).start()
        else:
            gain_rows[...] = sum_slots[j] + sum_new[j]
        if j < 3:
            col_copy(j).wait_recv()
        if j < 2:
            col_slots[j + 1] = col_slots[j] + col_new[j]
            col_copy(j + 1).start()
        if j == 2:
            gain_cols[tp] = col_slots[2] + col_new[2]
            gather_copies()[0].start()
            gather_copies()[1].start()
        if j == 3:
            gather_copies()[1].wait_recv()
            gather_copies()[2].start()
        if j == 4:
            gather_copies()[0].wait_recv()
            gather_copies()[2].wait_recv()

    def gather_copies():
        mine, theirs = gain_cols.at[tp], gain_cols.at[x_index]
        return (
            peer_copy(30, mine, mine, core_peer),
            peer_copy(31, mine, mine, x_peer),
            peer_copy(32, theirs, theirs, core_peer),
        )

    def late(low, high):
        for j in range(low, high):
            late_load(j).start()

    def wait_late(low, high):
        for j in range(low, high):
            late_load(j).wait()

    def wait_rest():
        for j in range(5, count):
            load(j).wait()
        head_sums[...] = jnp.zeros(head_sums.shape, F32)
        row_sums[...] = jnp.zeros(row_sums.shape, F32)

    load(0).wait()
    load(1).wait()
    grad_tile(0, 0, 256)
    load(2).wait()
    load(3).wait()
    grad_tile(2, 0, 256)
    fetch_start(0, 0, 256)
    spread_gains(packed, gains, head_gains)
    for first in range(0, width, 128):
        row = gains[0:1, first : first + 128]
        col_part[first : first + 128, :] = jnp.broadcast_to(row, (128, 128)).T
    gain_col[...] = col_part[multiple(tp * features, features), :]

    lone = full - 2
    order = [(0, 1), (2, lone), (0, 2), (2, lone + 1), (2, 1)] + [(0, j) for j in range(3, full + 1)]
    order += [(2, full)] + [(2, j) for j in range(2, lone)]
    first_gate = len(order) + 1
    freed = first_gate + full + 1

    order += [(1, j) for j in range(full + 1)]

    def tiles_at(t):
        for index in range(3):
            steps_of = [(1 + i, j) for i, (which, j) in enumerate(order) if which == index]
            part_of = [(step, j) for step, j in steps_of if j < full]
            if not isinstance(t, int):
                number = sum(jnp.where(t == step, j + 1, 0) for step, j in part_of)
                pl.when(number > 0)(partial(grad_tile, index, 256 * (number - 1), 256))
            for step, j in steps_of:
                if j == full and tail:
                    pl.when(t == step)(partial(grad_tile, index, 256 * full, tail))

    def choose(t, table):
        middle = len(table) // 2
        if middle == 0:
            pl.when(t == table[0][0])(lambda: [action() for action in table[0][1]] and None)
        else:
            pl.when(t < table[middle][0])(lambda: choose(t, table[:middle]))
            pl.when(t >= table[middle][0])(lambda: choose(t, table[middle:]))

    stages = [(1, load(4).wait)]
    after = [
        (6, lambda: sum_copies(1)[0].start()),
        (7, lambda: sum_cross(1)),
        (9, lambda: (late(0, 1), sum_copies(0)[0].start())),
        (10, lambda: sum_cross(0)),
        (11, lambda: sum_back(1)),
        (12, lambda: (wait_late(0, 1), wait_rest())),
        (13, lambda: sum_copies(1)[2].wait_recv()),
        (15, lambda: sum_back(0)),
        (17, lambda: sum_copies(0)[2].wait_recv()),
        (freed, lambda: late(1, len(late_pairs))),
    ]
    chain_stages = (
        (1, lambda: wait_late(1, len(late_pairs))),
        (1, lambda: attend_back_rows(1, 0)),
        (2, lambda: attend_back_rows(1, 1)),
        (3, lambda: (sum_copies(0)[2].wait_send(), load_tok().start())),
        (3, lambda: attend_back_rows(0, 0)),
        (4, lambda: attend_back_rows(0, 1)),
        (5, lambda: (far_cross(), keys_back(1))),
        (6, lambda: scatter_begin(1)),
        (7, lambda: (scatter_cross(1), out_grad())),
        (8, far_up),
        (11, lambda: (load_tok().wait(), scatter_end(1))),
        (14, lambda: keys_back(0)),
        (15, lambda: scatter_begin(0)),
        (16, query_grad),
        (17, lambda: (scatter_cross(0), kv_grads())),
        (18, kv_cross),
        (20, lambda: scatter_end(0)),
        (21, gains_begin),
        (22, kv_end),
    )
    stages += after + [(freed + j, action) for j, action in chain_stages]
    stages += [(freed + 23 + 2 * j, partial(gains_hop, j)) for j in range(5)]

    table = [
        (step, [action for at, action in stages if at == step])
        for step in sorted({at for at, _ in stages})
    ]

    def body(t, carry):
        pl.when(t <= len(order))(lambda: tiles_at(t))
        for hop, who, (limit, spacing, first), action in hops:
            entered = t - hop * lag - first
            k = entered // spacing
            now = who & (entered >= 0) & (k < limit)
            if spacing > 1:
                now = now & (entered % spacing == 0)
            pl.when(now)(partial(action, k))
        pl.when((t >= mid_first) & (t < mid_first + 2 * (mid_each + 1)))(lambda: mid_at(t))
        choose(t, table)
        pl.when((t >= norm_steps[0][0]) & (t <= norm_steps[-1][0]))(lambda: norms_at(t))
        return carry

    last = max(K + 5 * lag, third * (few - 1) + 1 + max(enter1 + 5 * lag, enter3 + 7 * lag))
    lax.fori_loop(0, last, body, 0)
    done = [sum_copies(0)[j] for j in (0, 1)] + [sum_copies(1)[j] for j in (1, 2)]
    done += [*far_copies(), *scatter_copies(0), *scatter_copies(1), *kv_copies()]
    done += [sum_copy(j) for j in range(5)] + [col_copy(j) for j in range(3)]
    for copy in done + list(gather_copies()):
        copy.wait_send()


def backward(real_lengths, tok_t, forward_outs, gain_ffn, weights, packed, tables):
    features, rows = tok_t.shape
    half = rows // 2
    width = 4 * features
    w_q, w_k, w_v, w_o, w_g, w_u = weights
    hidden, head_dim = w_g.shape[0], w_k.shape[1]
    kv_rows = head_dim // 2
    step_rows, lag = 32, 2
    total = 3 * hidden + 2 * head_dim + kv_rows
    few = total // (10 * step_rows)
    steps = total // (2 * step_rows) - 2 * few
    ring, ring_few = 4 * lag + 1, -(-(4 * lag + 1) // 3) + 1
    spread = -(-features // 128) * 128
    whole = pl.BlockSpec(memory_space=pltpu.VMEM)
    there = pl.BlockSpec(memory_space=pl.ANY)

    def low(*shape):
        return pltpu.VMEM(shape, BF16)

    def high(*shape):
        return pltpu.VMEM(shape, F32)

    slots = [low(step_rows * ring, width)] * 3
    slots += [low(n * step_rows * ring_few, width) for n in (2, 1, 1, 1, 1)]
    return pl.pallas_call(
        partial(backward_kernel, step_rows, steps, few, lag),
        out_shape=(
            jax.ShapeDtypeStruct((total, width), BF16),
            jax.ShapeDtypeStruct((features, rows), BF16),
            jax.ShapeDtypeStruct((8, width), F32),
            jax.ShapeDtypeStruct((4, 8, spread), F32),
        ),
        in_specs=[pl.BlockSpec(memory_space=pltpu.SMEM)] + [there] * 14 + [whole] + [there] * 6
        + [whole] * 3,
        out_specs=[there, whole, whole, whole],
        scratch_shapes=[
            low(total, width), *slots,
            low(rows, hidden), low(rows, hidden), low(rows, hidden), low(rows, width),
            low(rows, width), low(2, 2, hidden, 256), low(2, half, width),
            low(2, half // 2, width), low(2, half // 2, width), low(rows, width), low(rows, width),
            low(rows, width), low(head_dim, width), low(width, 3 * head_dim),
            low(half, 2 * head_dim), low(2, 2, features, half), low(2, features, half),
            high(2, 2, 8, half), high(2, 2, 8, half), low(2, kv_rows, width), low(kv_rows, width),
            low(width, half), high(2, 8, head_dim), high(2, 8, width),
            high(5, 8, width), high(5, 8, width), high(3, 8, spread), high(3, 8, spread),
            high(4, width), high(2, head_dim), high(features, 128), high(width, 128),
            pltpu.SemaphoreType.DMA((20,)), pltpu.SemaphoreType.DMA((2, 2)),
            pltpu.SemaphoreType.DMA((steps,)), pltpu.SemaphoreType.DMA((2, few)),
            pltpu.SemaphoreType.DMA((5, steps)), pltpu.SemaphoreType.DMA((5, steps)),
            pltpu.SemaphoreType.DMA((13, few)), pltpu.SemaphoreType.DMA((13, few)),
            pltpu.SemaphoreType.DMA((35,)),
            pltpu.SemaphoreType.DMA((35,)),
        ],
        name="backward",
        compiler_params=pltpu.CompilerParams(
            collective_id=1, has_side_effects=True, vmem_limit_bytes=63 << 20
        ),
    )(real_lengths, tok_t, *forward_outs, gain_ffn, *weights, packed, *tables)


def paired_shards(
    tokens,
    out_grad,
    w_query,
    w_key,
    w_value,
    w_out,
    w_gate,
    w_up,
    w_down,
    gain_in,
    gain_post_attn,
    gain_pre_ffn,
    gain_post_ffn,
    gain_query,
    gain_key,
    bucket_lengths,
    true_lengths,
):
    tp_index = lax.axis_index("tp")
    rows = tokens.shape[0] // 2
    head_dim = w_key.shape[1]
    score_scale = head_dim ** (-0.5)
    tables = block_tables(2 * rows, head_dim)
    packed, offset = 0.0, 0
    all_gains = (gain_in, gain_post_attn, gain_pre_ffn, gain_post_ffn, gain_query, gain_key)
    length = sum(gain.size for gain in all_gains)
    for gain in all_gains:
        placed = jnp.pad(gain.astype(F32), (offset, length - offset - gain.size))
        packed, offset = packed + placed, offset + gain.size
    packed = packed.reshape(-1, 128)
    weights = (w_query, w_key, w_value, w_out, w_gate.T, w_up.T, w_down)
    out_t, gain_sum, *kept = forward(
        true_lengths, tokens.T, out_grad.T, weights, packed, tables
    )
    sums, xg_t, gain_rows, gain_cols = backward(
        true_lengths, tokens.T, kept, gain_sum, weights[:-1], packed, tables
    )
    hidden = w_down.shape[0]
    sizes = [hidden, hidden, hidden, head_dim, head_dim, head_dim // 2]
    ends = [sum(sizes[: j + 1]) for j in range(len(sizes))]
    down_sum, gate_sum, up_sum, out_sum, query_sum, mine = [
        sums[end - size : end] for size, end in zip(sizes, ends)
    ]
    far = lax.ppermute(mine, "tp", XOR2)
    near = lax.ppermute(jnp.stack([mine, far]), "tp", XOR1)
    kv_all = (mine, near[0], far, near[1])
    kv_sum = jnp.concatenate(
        [lax.select_n(tp_index ^ j, *kv_all) for j in range(4)], axis=0
    ).astype(F32).T
    return (
        out_t.T,
        xg_t.T,
        query_sum.astype(F32).T,
        kv_sum[:, :head_dim],
        kv_sum[:, head_dim:],
        out_sum.astype(F32),
        gate_sum.astype(F32).T,
        up_sum.astype(F32).T,
        down_sum.astype(F32),
        gain_cols[:, 0, : tokens.shape[1]].reshape(-1),
        gain_rows[0],
        gain_rows[1],
        gain_rows[2],
        gain_rows[3, :head_dim],
        gain_rows[3, head_dim : 2 * head_dim],
    )


def solution(mesh):
    def layer(*args):
        tokens, bucket_lengths = args[0], args[-2]
        sizes = mesh.shape
        group_rows = tokens.shape[0] // sizes["dp"]
        paired = (sizes["dp"], sizes["ctx"], sizes["tp"]) == (4, 2, 4) and (
            group_rows == 1024 * bucket_lengths.shape[1] == 2048
        )
        return mapped(paired_shards if paired else shards)(*args)

    def mapped(body):
        return jax.shard_map(
            body,
            mesh=mesh,
            in_specs=(
                P(("dp", "ctx"), "tp"),
                P(("dp", "ctx"), "tp"),
                P(None, "tp"),
                P(),
                P(),
                P("tp", None),
                P(None, "tp"),
                P(None, "tp"),
                P("tp", None),
                P(),
                P(),
                P(),
                P(),
                P(),
                P(),
                P("dp", None),
                P("dp", None),
            ),
            out_specs=(
                P(("dp", "ctx"), "tp"),
                P(("dp", "ctx"), "tp"),
                P(None, "tp"),
                P(),
                P(),
                P("tp", None),
                P(None, "tp"),
                P(None, "tp"),
                P("tp", None),
                P(),
                P(),
                P(),
                P(),
                P(),
                P(),
            ),
            check_vma=False,
        )

    return layer
```

```python
import math
from functools import partial

import jax
import jax.numpy as jnp
import numpy as np
from jax import lax
from jax.experimental import pallas as pl
from jax.experimental.pallas import tpu as pltpu
from jax.sharding import PartitionSpec as P

QBLK = 512


EPSILON = 1e-06
ROPE_BASE = 1000000.0
MASKED = -1e30


def contract(left, right, left_dim, right_dim):
    return lax.dot_general(
        left, right, (((left_dim,), (right_dim,)), ((), ())), preferred_element_type=jnp.float32
    )


def rms_norm(values, gain):
    return values * lax.rsqrt(jnp.mean(values * values, axis=-1, keepdims=True) + EPSILON) * gain


def rotate(values, cosine_table, sine_table):
    half_dim = values.shape[-1] // 2
    turned = jnp.concatenate([-values[..., half_dim:], values[..., :half_dim]], axis=-1)
    return values * cosine_table + turned * sine_table


def rope_tables(seq_pos, head_dim):
    freq_index = jnp.arange(head_dim // 2, dtype=jnp.float32)
    inverse = ROPE_BASE ** (-2.0 * freq_index / head_dim)
    angles = seq_pos.astype(jnp.float32)[:, None] * inverse[None, :]
    angles = jnp.concatenate([angles, angles], axis=-1)
    return (jnp.cos(angles), jnp.sin(angles))


def stream_layout(bucket_row, true_row, tok_dev, n_ctx):
    group_rows = tok_dev * n_ctx
    half_shard = tok_dev // 2
    row_ids = jnp.arange(group_rows, dtype=jnp.int32)
    device = row_ids // tok_dev
    half_index = row_ids % tok_dev // half_shard
    block_ids = jnp.where(half_index == 0, device, 2 * n_ctx - 1 - device)
    stream_pos = block_ids * half_shard + row_ids % half_shard
    starts = jnp.cumsum(bucket_row) - bucket_row
    ends = starts + bucket_row
    inside = (
        (stream_pos[:, None] >= starts[None, :]) & (stream_pos[:, None] < ends[None, :])
    ).astype(jnp.int32)
    slot_ids = jnp.arange(bucket_row.shape[0], dtype=jnp.int32)
    seq_ids = jnp.sum(inside * slot_ids[None, :], axis=1)
    seq_pos = stream_pos - jnp.sum(inside * starts[None, :], axis=1)
    is_valid = (seq_pos < jnp.sum(inside * true_row[None, :], axis=1)).astype(jnp.int32)
    return (seq_ids, stream_pos, seq_pos, is_valid)


def shape_heads(query_raw, key_raw, gain_q, gain_k, cosine_table, sine_table):
    query_heads = query_raw.reshape(query_raw.shape[0], -1, key_raw.shape[1])
    query_rot = rotate(
        rms_norm(query_heads, gain_q), cosine_table[:, None, :], sine_table[:, None, :]
    )
    key_rot = rotate(rms_norm(key_raw, gain_k), cosine_table, sine_table)
    return (query_rot, key_rot)


def geglu(gate_in, up_in):
    return jax.nn.gelu(gate_in, approximate=True) * up_in


def shards(
    tokens,
    out_grad,
    w_query,
    w_key,
    w_value,
    w_out,
    w_gate,
    w_up,
    w_down,
    gain_in,
    gain_post_attn,
    gain_pre_ffn,
    gain_post_ffn,
    gain_query,
    gain_key,
    bucket_lengths,
    true_lengths,
):
    n_ctx = lax.axis_size("ctx")
    ctx_index = lax.axis_index("ctx")
    tp_index = lax.axis_index("tp")
    rows_dev = tokens.shape[0]
    feature_cols = tokens.shape[1]
    head_dim = w_key.shape[1]
    head_count = w_query.shape[1] // head_dim
    group_rows = rows_dev * n_ctx
    blocks = rows_dev // QBLK
    score_scale = head_dim ** (-0.5)
    gain_in32, gain_pa32, gain_pf32, gain_pff32, gain_q32, gain_k32 = [
        tensor.astype(jnp.float32)
        for tensor in (gain_in, gain_post_attn, gain_pre_ffn, gain_post_ffn, gain_query, gain_key)
    ]
    input_full, cot_full = (
        lax.all_gather(tokens, "tp", axis=1, tiled=True),
        lax.all_gather(out_grad, "tp", axis=1, tiled=True),
    )
    inputs = input_full.astype(jnp.float32)
    seq_all, spos_all, rpos_all, valid_all = stream_layout(
        bucket_lengths[0], true_lengths[0], rows_dev, n_ctx
    )
    first_row = ctx_index * rows_dev
    seq_local = lax.dynamic_slice_in_dim(seq_all, first_row, rows_dev)
    spos_local = lax.dynamic_slice_in_dim(spos_all, first_row, rows_dev)
    rpos_local = lax.dynamic_slice_in_dim(rpos_all, first_row, rows_dev)
    cosine_table, sine_table = rope_tables(rpos_local, head_dim)
    normed_in, pull_in = jax.vjp(rms_norm, inputs, gain_in32)
    normed_in16 = normed_in.astype(jnp.bfloat16)
    query_raw = jnp.dot(normed_in16, w_query, preferred_element_type=jnp.float32)
    key_raw = jnp.dot(normed_in16, w_key, preferred_element_type=jnp.float32)
    value_raw = jnp.dot(normed_in16, w_value, preferred_element_type=jnp.float32)
    (query_rot, key_rot), rope_pull = jax.vjp(
        partial(shape_heads, cosine_table=cosine_table, sine_table=sine_table),
        query_raw,
        key_raw,
        gain_q32,
        gain_k32,
    )
    query16 = query_rot.astype(jnp.bfloat16)
    key16 = key_rot.astype(jnp.bfloat16)
    value16 = value_raw.astype(jnp.bfloat16)
    key_group, value_group = (
        lax.all_gather(key16, "ctx", axis=0, tiled=True),
        lax.all_gather(value16, "ctx", axis=0, tiled=True),
    )

    def allowed_mask(seq_rows, spos_rows):
        return (
            (valid_all[None, :] == 1)
            & (seq_all[None, :] == seq_rows[:, None])
            & (spos_all[None, :] <= spos_rows[:, None])
        )

    query_blocks = query16.reshape(blocks, QBLK, head_count, head_dim)
    seq_blocks = seq_local.reshape(blocks, QBLK)
    spos_blocks = spos_local.reshape(blocks, QBLK)

    def forward_block(block_item):
        query_block, seq_rows, spos_rows = block_item
        scores = (
            jnp.einsum("qhd,kd->hqk", query_block, key_group, preferred_element_type=jnp.float32)
            * score_scale
        )
        scores = jnp.where(allowed_mask(seq_rows, spos_rows)[None], scores, MASKED)
        row_max = jnp.max(scores, axis=-1, keepdims=True)
        exp_scores = jnp.exp(scores - row_max)
        row_total = jnp.sum(exp_scores, axis=-1, keepdims=True)
        prob_rows = (exp_scores / row_total).astype(jnp.bfloat16)
        output = jnp.einsum(
            "hqk,kd->qhd", prob_rows, value_group, preferred_element_type=jnp.float32
        )
        return (output, (row_max + jnp.log(row_total))[..., 0])

    attended, log_norm = lax.map(forward_block, (query_blocks, seq_blocks, spos_blocks))
    attended16 = attended.reshape(rows_dev, head_count * head_dim).astype(jnp.bfloat16)
    attention = lax.psum(
        jnp.dot(attended16, w_out, preferred_element_type=jnp.float32).astype(jnp.bfloat16), "tp"
    ).astype(jnp.float32)
    post_attn, pull_post_attn = jax.vjp(rms_norm, attention, gain_pa32)
    residual = inputs + post_attn
    normed_mid, pull_pre_ffn = jax.vjp(rms_norm, residual, gain_pf32)
    mid16 = normed_mid.astype(jnp.bfloat16)
    gate_out = jnp.dot(mid16, w_gate, preferred_element_type=jnp.float32)
    up_out = jnp.dot(mid16, w_up, preferred_element_type=jnp.float32)
    hidden, pull_geglu = jax.vjp(geglu, gate_out, up_out)
    hidden16 = hidden.astype(jnp.bfloat16)
    ffn_branch = lax.psum(
        jnp.dot(hidden16, w_down, preferred_element_type=jnp.float32).astype(jnp.bfloat16), "tp"
    ).astype(jnp.float32)
    post_ffn, pull_post_ffn = jax.vjp(rms_norm, ffn_branch, gain_pff32)
    outputs = residual + post_ffn
    out_rows = lax.dynamic_slice_in_dim(outputs, tp_index * feature_cols, feature_cols, 1).astype(
        jnp.bfloat16
    )
    cotangent = cot_full.astype(jnp.float32)
    d_ffn, d_gain_post_ffn = pull_post_ffn(cotangent)
    d_ffn16 = d_ffn.astype(jnp.bfloat16)
    d_hidden = contract(d_ffn16, w_down, 1, 1)
    grad_down = contract(hidden16, d_ffn16, 0, 0)
    d_gate, d_up = pull_geglu(d_hidden)
    d_gate16 = d_gate.astype(jnp.bfloat16)
    d_up16 = d_up.astype(jnp.bfloat16)
    grad_gate = contract(mid16, d_gate16, 0, 0)
    grad_up = contract(mid16, d_up16, 0, 0)
    d_mid = lax.psum(
        (contract(d_gate16, w_gate, 1, 1) + contract(d_up16, w_up, 1, 1)).astype(jnp.bfloat16), "tp"
    ).astype(jnp.float32)
    d_res_norm, d_gain_pre_ffn = pull_pre_ffn(d_mid)
    d_resid = cotangent + d_res_norm
    d_attn, d_gain_post_attn = pull_post_attn(d_resid)
    d_attn16 = d_attn.astype(jnp.bfloat16)
    d_attended16 = contract(d_attn16, w_out, 1, 1).astype(jnp.bfloat16)
    grad_out = contract(attended16, d_attn16, 0, 0)
    key_back, value_back = (key_group, value_group)

    def backward_block(running, block_item):
        key_sum, value_sum = running
        query_block, dout_block, lse_block, seq_rows, spos_rows = block_item
        scores = (
            jnp.einsum("qhd,kd->hqk", query_block, key_back, preferred_element_type=jnp.float32)
            * score_scale
        )
        scores = jnp.where(allowed_mask(seq_rows, spos_rows)[None], scores, MASKED)
        prob_rows = jnp.exp(scores - lse_block[..., None])
        prob16 = prob_rows.astype(jnp.bfloat16)
        d_probs = jnp.einsum(
            "qhd,kd->hqk", dout_block, value_back, preferred_element_type=jnp.float32
        )
        row_inner = jnp.sum(prob_rows * d_probs, axis=-1, keepdims=True)
        d_scores16 = (prob_rows * (d_probs - row_inner)).astype(jnp.bfloat16)
        d_query = (
            jnp.einsum("hqk,kd->qhd", d_scores16, key_back, preferred_element_type=jnp.float32)
            * score_scale
        )
        key_sum = (
            key_sum
            + jnp.einsum("hqk,qhd->kd", d_scores16, query_block, preferred_element_type=jnp.float32)
            * score_scale
        )
        value_sum = value_sum + jnp.einsum(
            "hqk,qhd->kd", prob16, dout_block, preferred_element_type=jnp.float32
        )
        return ((key_sum, value_sum), d_query)

    zero_rows = jnp.zeros((group_rows, head_dim), jnp.float32)
    (key_sum, value_sum), d_query_blocks = lax.scan(
        backward_block,
        (zero_rows, zero_rows),
        (
            query_blocks,
            d_attended16.reshape(blocks, QBLK, head_count, head_dim),
            log_norm,
            seq_blocks,
            spos_blocks,
        ),
    )
    d_key_rot, d_value = (
        lax.psum_scatter(
            key_sum.astype(jnp.bfloat16), "ctx", scatter_dimension=0, tiled=True
        ).astype(jnp.float32),
        lax.psum_scatter(
            value_sum.astype(jnp.bfloat16), "ctx", scatter_dimension=0, tiled=True
        ).astype(jnp.float32),
    )
    d_query_raw, d_key_raw, d_gain_query, d_gain_key = rope_pull(
        (d_query_blocks.reshape(rows_dev, head_count, head_dim), d_key_rot)
    )
    d_query16 = d_query_raw.astype(jnp.bfloat16)
    d_key16 = d_key_raw.astype(jnp.bfloat16)
    d_value16 = d_value.astype(jnp.bfloat16)
    grad_query = contract(normed_in16, d_query16, 0, 0)
    grad_key = contract(normed_in16, d_key16, 0, 0)
    grad_value = contract(normed_in16, d_value16, 0, 0)
    d_normed_part = (
        contract(d_query16, w_query, 1, 1)
        + contract(d_key16, w_key, 1, 1)
        + contract(d_value16, w_value, 1, 1)
    )
    d_normed_in = lax.psum(d_normed_part.astype(jnp.bfloat16), "tp").astype(jnp.float32)
    d_in_norm, d_gain_in = pull_in(d_normed_in)
    d_inputs = d_resid + d_in_norm
    grad_rows = lax.dynamic_slice_in_dim(d_inputs, tp_index * feature_cols, feature_cols, 1).astype(
        jnp.bfloat16
    )
    sharded = (
        grad_query,
        grad_out,
        grad_gate,
        grad_up,
        grad_down,
        d_gain_in,
        d_gain_post_attn,
        d_gain_pre_ffn,
        d_gain_post_ffn,
    )
    reduced = (
        lax.psum_scatter(
            sharded[0].astype(jnp.bfloat16), ("dp", "ctx"), scatter_dimension=0, tiled=True
        ).astype(jnp.float32),
        lax.psum_scatter(
            sharded[1].astype(jnp.bfloat16), ("dp", "ctx"), scatter_dimension=1, tiled=True
        ).astype(jnp.float32),
        lax.psum_scatter(
            sharded[2].astype(jnp.bfloat16), ("dp", "ctx"), scatter_dimension=0, tiled=True
        ).astype(jnp.float32),
        lax.psum_scatter(
            sharded[3].astype(jnp.bfloat16), ("dp", "ctx"), scatter_dimension=0, tiled=True
        ).astype(jnp.float32),
        lax.psum_scatter(
            sharded[4].astype(jnp.bfloat16), ("dp", "ctx"), scatter_dimension=1, tiled=True
        ).astype(jnp.float32),
        lax.psum_scatter(
            sharded[5].astype(jnp.bfloat16), ("dp", "ctx"), scatter_dimension=0, tiled=True
        ).astype(jnp.float32),
        lax.psum_scatter(
            sharded[6].astype(jnp.bfloat16), ("dp", "ctx"), scatter_dimension=0, tiled=True
        ).astype(jnp.float32),
        lax.psum_scatter(
            sharded[7].astype(jnp.bfloat16), ("dp", "ctx"), scatter_dimension=0, tiled=True
        ).astype(jnp.float32),
        lax.psum_scatter(
            sharded[8].astype(jnp.bfloat16), ("dp", "ctx"), scatter_dimension=0, tiled=True
        ).astype(jnp.float32),
    )
    summed = (
        lax.all_gather(reduced[0].astype(jnp.bfloat16), ("dp", "ctx"), axis=0, tiled=True).astype(
            jnp.float32
        ),
        lax.all_gather(reduced[1].astype(jnp.bfloat16), ("dp", "ctx"), axis=1, tiled=True).astype(
            jnp.float32
        ),
        lax.all_gather(reduced[2].astype(jnp.bfloat16), ("dp", "ctx"), axis=0, tiled=True).astype(
            jnp.float32
        ),
        lax.all_gather(reduced[3].astype(jnp.bfloat16), ("dp", "ctx"), axis=0, tiled=True).astype(
            jnp.float32
        ),
        lax.all_gather(reduced[4].astype(jnp.bfloat16), ("dp", "ctx"), axis=1, tiled=True).astype(
            jnp.float32
        ),
        lax.all_gather(reduced[5].astype(jnp.bfloat16), ("dp", "ctx"), axis=0, tiled=True).astype(
            jnp.float32
        ),
        lax.all_gather(reduced[6].astype(jnp.bfloat16), ("dp", "ctx"), axis=0, tiled=True).astype(
            jnp.float32
        ),
        lax.all_gather(reduced[7].astype(jnp.bfloat16), ("dp", "ctx"), axis=0, tiled=True).astype(
            jnp.float32
        ),
        lax.all_gather(reduced[8].astype(jnp.bfloat16), ("dp", "ctx"), axis=0, tiled=True).astype(
            jnp.float32
        ),
    )
    shared = lax.psum((grad_key, grad_value, d_gain_query, d_gain_key), ("dp", "ctx", "tp"))
    return (
        out_rows,
        grad_rows,
        summed[0],
        shared[0],
        shared[1],
        summed[1],
        summed[2],
        summed[3],
        summed[4],
        summed[5],
        summed[6],
        summed[7],
        summed[8],
        shared[2],
        shared[3],
    )


XOR1 = ((0, 1), (1, 0), (2, 3), (3, 2))
XOR2 = ((0, 2), (2, 0), (1, 3), (3, 1))
MESH = pl.DeviceIdType.MESH
GELU_SCALE = math.sqrt(2.0 / math.pi)
F32 = jnp.float32
BF16 = jnp.bfloat16


def add16(left, right):
    return (left.astype(F32) + right.astype(F32)).astype(BF16)


def block_tables(length, head_dim):
    freq_index = np.arange(head_dim // 2, dtype=np.float32)
    inverse = np.float32(ROPE_BASE) ** (np.float32(-2.0) * freq_index / np.float32(head_dim))
    angles = np.arange(length, dtype=np.float32)[:, None] * inverse.astype(np.float32)[None, :]
    angles = angles.astype(np.float64)
    return np.cos(angles).astype(np.float32), np.sin(angles).astype(np.float32)


def scale_of(values):
    return lax.rsqrt(jnp.mean(values * values, axis=-1, keepdims=True) + EPSILON)


STORED = 13


def row_blocks(base, rows, size, body, carry=None):
    def step(i, state):
        at = pl.ds(pl.multiple_of(base + i * size, size), size)
        return body(at, pl.ds(pl.multiple_of(i * size, size), size), state)

    return lax.fori_loop(0, rows // size, step, carry)


def spread_gains(packed, gains, head_gains):
    columns = gains.shape[1] // 128
    for j in range(4):
        for i in range(columns):
            at = j * columns + i
            gains[j : j + 1, 128 * i : 128 * i + 128] = packed[at : at + 1, :]
    head_columns = head_gains.shape[1] // 128
    for j in range(2):
        for i in range(head_columns):
            at = 4 * columns + j * head_columns + i
            head_gains[j : j + 1, 128 * i : 128 * i + 128] = packed[at : at + 1, :]


def turn_in(source, target, rows):
    for first in range(0, source.shape[0], 128):
        target[rows, first : first + 128] = source[first : first + 128, :].T


def column_tiles(total, size):
    return [(first, min(size, total - first)) for first in range(0, total, size)]


def dot_nn(left, right):
    return jnp.dot(left, right, preferred_element_type=F32)


def dot_nt(left, right):
    return contract(left, right, 1, 1)


def gelu_parts(gate):
    square = gate * gate
    tanh = jnp.tanh(GELU_SCALE * gate * (1.0 + 0.044715 * square))
    half = 0.5 + 0.5 * tanh
    slope = GELU_SCALE * (1.0 + 3.0 * 0.044715 * square)
    return gate * half, half + 0.5 * gate * (1.0 - tanh * tanh) * slope


def forward_kernel(
    real_lengths, tok, cot, w_q, w_k, w_v, w_o, w_g, w_u, w_d, packed, cosines, sines,
    out_t, gain_sum, *refs,
):
    stored, refs = refs[:STORED], refs[STORED:]
    kept, refs = refs[:STORED], refs[STORED:]
    x16, cot16, n16, q16, kv16, far_kv, att16, attn16, mid16, hid16, dffn16, dg16, du16 = kept
    blocks, v_qkv, v_o, v_g, v_u, v_d, part, near, far, ffn16, gains, head_gains = refs[:12]
    load_sem, own_sem, store_sem, g_send, g_recv, kv_send, kv_recv, s_send, s_recv = refs[12:]
    dp, ctx, tp = lax.axis_index("dp"), lax.axis_index("ctx"), lax.axis_index("tp")
    core_peer = (dp, ctx, tp + 1 - 2 * (tp % 2))
    x_index = (tp + 2) % 4
    x_peer = (dp, ctx, x_index)
    y_peer = (dp, 1 - ctx, tp)
    features, rows = tok.shape[0], tok.shape[1] // 2
    width = 4 * features
    hidden = w_d.shape[0]
    head_dim = w_k.shape[1]
    half = rows // 2
    odd = tp % 2

    loads = [
        pltpu.make_async_copy(source, target, load_sem.at[j])
        for j, (source, target) in enumerate(
            (
                (w_q, v_qkv.at[:, 0:head_dim]),
                (w_k, v_qkv.at[:, head_dim : 2 * head_dim]),
                (w_v, v_qkv.at[:, 2 * head_dim : 3 * head_dim]),
                (w_o, v_o), (w_g, v_g), (w_u, v_u), (w_d, v_d),
            )
        )
    ]
    for copy in loads:
        copy.start()

    def half_of(source, index):
        lane = (ctx if index % 2 == 0 else 1 - ctx) * rows
        return source.at[:, pl.ds(pl.multiple_of(lane, rows), rows)]

    def place(index, owner):
        return blocks.at[index, pl.ds(pl.multiple_of(owner * features, features), features)]

    sources = [half_of(tok, 0), half_of(tok, 1), half_of(cot, 0), half_of(cot, 1)]

    def remote(source, target, send, recv, peer):
        return pltpu.make_async_remote_copy(
            src_ref=source, dst_ref=target, send_sem=send, recv_sem=recv,
            device_id=peer, device_id_type=MESH,
        )

    own = [pltpu.make_async_copy(sources[j], place(j, tp), own_sem.at[j]) for j in range(4)]
    to_x = [
        remote(sources[j], place(j, tp), g_send.at[0, j], g_recv.at[0, j], x_peer) for j in range(4)
    ]
    to_core = [
        remote(sources[j], place(j, tp), g_send.at[1, j], g_recv.at[1, j], core_peer)
        for j in range(4)
    ]
    onward = [
        remote(place(j, x_index), place(j, x_index), g_send.at[2, j], g_recv.at[2, j], core_peer)
        for j in range(4)
    ]
    for copy in own:
        copy.start()
    barrier = pltpu.get_barrier_semaphore()
    for peer in (core_peer, x_peer, y_peer):
        pl.semaphore_signal(barrier, inc=1, device_id=peer, device_id_type=MESH)
    pl.semaphore_wait(barrier, 3)

    for j in range(4):
        to_core[j].start()
    to_x[0].start()
    to_x[1].start()

    spread_gains(packed, gains, head_gains)

    def store(j, c):
        at = slice(None) if c is None else chunk(c)
        return pltpu.make_async_copy(kept[j].at[at], stored[j].at[at], store_sem.at[j, c or 0])

    def pass_on(j):
        to_x[j].wait_recv()
        onward[j].start()

    def gathered(j):
        own[j].wait()
        to_core[j].wait_recv()
        onward[j].wait_recv()

    def chunk(c):
        return pl.ds(c * rows, rows)

    def normalise(c):
        turn_in(blocks.at[c], x16, chunk(c))

        def norm(at, _, carry):
            values = x16[at, :].astype(F32)
            n16[at, :] = (values * scale_of(values) * gains[0:1, :]).astype(BF16)

        row_blocks(c * rows, rows, 64, norm)

    def project(c):
        for first in range(0, rows, half):
            at = pl.ds(c * rows + first, half)
            tables = pl.ds(c * rows + first, half)
            values = dot_nn(n16[at, :], v_qkv[...])
            cosine, sine = cosines[tables, :], sines[tables, :]
            for j, target in ((0, q16.at[at, :]), (1, kv16.at[at, 0:head_dim])):
                head = values[:, j * head_dim : (j + 1) * head_dim]
                head = head * scale_of(head) * head_gains[j : j + 1, :]
                low, high = head[:, : head_dim // 2], head[:, head_dim // 2 :]
                target[:, : head_dim // 2] = (low * cosine - high * sine).astype(BF16)
                target[:, head_dim // 2 :] = (high * cosine + low * sine).astype(BF16)
            kv16[at, head_dim:] = values[:, 2 * head_dim :].astype(BF16)

    score_scale = head_dim ** (-0.5)

    def attend_rows(c):
        for first in range(0, rows, half):
            at = pl.ds(c * rows + first, half)
            query = q16[at, :]
            row_id = first + lax.broadcasted_iota(jnp.int32, (half, rows), 0)
            key_id = lax.broadcasted_iota(jnp.int32, (half, rows), 1)
            allowed = key_id <= row_id
            if c == 1:
                allowed = allowed & (rows + key_id < real_lengths[0, 1 - ctx])
            keys = [(kv16[chunk(c), :head_dim], kv16[chunk(c), head_dim:], allowed)]
            if c == 1:
                keys.append((far_kv[:, :head_dim], far_kv[:, head_dim:], None))
            scores = []
            for key, _, mask in keys:
                score = dot_nt(query, key) * score_scale
                scores.append(score if mask is None else jnp.where(mask, score, MASKED))
            most = scores[0].max(axis=1, keepdims=True)
            for score in scores[1:]:
                most = jnp.maximum(most, score.max(axis=1, keepdims=True))
            exps = [jnp.exp(score - most) for score in scores]
            total = sum(e.sum(axis=1, keepdims=True) for e in exps)
            out = sum(dot_nn((e / total).astype(BF16), k[1]) for e, k in zip(exps, keys))
            att16[at, :] = out.astype(BF16)
        part[c] = dot_nn(att16[chunk(c), :], v_o[...]).astype(BF16)

    def rows_of(index):
        return pl.ds(pl.multiple_of(index * half, half), half)

    def sum_copies(s, target):
        start = pl.multiple_of((s % 2) * rows + odd * half, half)
        final = target.at[pl.ds(start, half)]
        return (
            remote(part.at[s, rows_of(1 - odd)], near.at[s], s_send.at[0, s], s_recv.at[0, s], core_peer),
            remote(near.at[s], far.at[s], s_send.at[1, s], s_recv.at[1, s], x_peer),
            remote(final, final, s_send.at[2, s], s_recv.at[2, s], core_peer),
        )

    def sum_start(s, target):
        sum_copies(s, target)[0].start()

    def sum_cross(s, target):
        copies = sum_copies(s, target)
        copies[0].wait_recv()
        near[s] = add16(part[s, rows_of(odd)], near[s])
        copies[1].start()

    def sum_back(s, target):
        copies = sum_copies(s, target)
        copies[1].wait_recv()
        start = pl.multiple_of((s % 2) * rows + odd * half, half)
        target[pl.ds(start, half), :] = add16(near[s], far[s])
        copies[2].start()
        copies[2].wait_recv()

    def residual(at):
        branch = attn16[at, :].astype(F32)
        return x16[at, :].astype(F32) + branch * scale_of(branch) * gains[1:2, :]

    def middle(c):
        def body(at, _, carry):
            values = residual(at)
            mid16[at, :] = (values * scale_of(values) * gains[2:3, :]).astype(BF16)

        row_blocks(c * rows, rows, 64, body)

    def feed(c):
        for first, size in column_tiles(hidden, 256):
            for low in range(0, rows, half):
                at = pl.ds(c * rows + low, half)
                cols = pl.ds(first, size)
                gate = dot_nt(mid16[at, :], v_g[cols, :])
                up = dot_nt(mid16[at, :], v_u[cols, :])
                act, slope = gelu_parts(gate)
                hid16[at, cols] = (act * up).astype(BF16)
                dg16[at, cols] = (slope * up).astype(BF16)
                du16[at, cols] = act.astype(BF16)
        for first, size in column_tiles(width, 256):
            cols = pl.ds(first, size)
            part[2 + c, :, cols] = dot_nn(hid16[chunk(c), :], v_d[:, cols]).astype(BF16)

    def finish(c):
        turn_in(blocks.at[2 + c], cot16, chunk(c))
        sum_copies(c, attn16)[0].wait_send()
        onward[c].wait_send()

        def body(at, block, total):
            branch = ffn16[at, :].astype(F32)
            scale = scale_of(branch)
            unit = branch * scale
            grad = cot16[at, :].astype(F32)
            part[c, block, :] = (residual(at) + unit * gains[3:4, :]).astype(BF16)
            weighted = grad * gains[3:4, :]
            inner = jnp.mean(unit * weighted, axis=-1, keepdims=True)
            dffn16[at, :] = (scale * (weighted - unit * inner)).astype(BF16)
            return total + (grad * unit).reshape(-1, 8, width).sum(axis=0)

        total = row_blocks(c * rows, rows, 64, body, jnp.zeros((8, width), F32))
        if c == 0:
            gain_sum[...] = total
        else:
            gain_sum[...] += total
        for first in range(0, width, 128):
            blocks[c, first : first + 128, :] = part[c, :, first : first + 128].T
        lane = (ctx if c == 0 else 1 - ctx) * rows
        mine = blocks[c, pl.ds(pl.multiple_of(tp * features, features), features), :]
        out_t[:, pl.ds(pl.multiple_of(lane, rows), rows)] = mine

    def feed_back(c):
        for first, size in column_tiles(hidden, 256):
            for low in range(0, rows, half):
                at = pl.ds(c * rows + low, half)
                cols = pl.ds(first, size)
                d_hidden = dot_nt(dffn16[at, :], v_d[cols, :])
                dg16[at, cols] = (d_hidden * dg16[at, cols].astype(F32)).astype(BF16)
                du16[at, cols] = (d_hidden * du16[at, cols].astype(F32)).astype(BF16)

    kv_copy = remote(kv16.at[chunk(0)], far_kv, kv_send.at[0], kv_recv.at[0], y_peer)
    X, COT, N, Q, KV, FAR, ATT, ATTN, MID, HID, DFFN, DG, DU = range(STORED)
    started = []

    def store_all(c, *which):
        for j in which:
            store(j, c).start()
            started.append((j, c))

    pass_on(0)
    for copy in loads[:3]:
        copy.wait()
    gathered(0)
    normalise(0)
    project(0)
    kv_copy.start()
    store_all(0, X, N, Q, KV)
    pass_on(1)
    to_x[2].start()
    loads[3].wait()
    attend_rows(0)
    sum_start(0, attn16)
    gathered(1)
    normalise(1)
    sum_cross(0, attn16)
    project(1)
    store_all(1, X, N, Q, KV)
    kv_copy.wait_recv()
    attend_rows(1)
    sum_start(1, attn16)
    store_all(None, FAR)
    store_all(0, ATT)
    store_all(1, ATT)
    pass_on(2)
    sum_cross(1, attn16)
    sum_back(0, attn16)
    for copy in loads[4:]:
        copy.wait()
    middle(0)
    to_x[3].start()
    store_all(0, ATTN, MID)
    feed(0)
    sum_start(2, ffn16)
    store_all(0, HID)
    sum_back(1, attn16)
    middle(1)
    store_all(1, ATTN, MID)
    sum_cross(2, ffn16)
    pass_on(3)
    feed(1)
    sum_start(3, ffn16)
    store_all(1, HID)
    gathered(2)
    sum_cross(3, ffn16)
    sum_back(2, ffn16)
    finish(0)
    store_all(0, COT, DFFN)
    feed_back(0)
    store_all(0, DG, DU)
    gathered(3)
    sum_back(3, ffn16)
    finish(1)
    store_all(1, COT, DFFN)
    feed_back(1)
    store_all(1, DG, DU)
    for group in (to_x, to_core, onward[2:], [kv_copy]):
        for copy in group:
            copy.wait_send()
    for s, target in ((0, attn16), (1, attn16), (2, ffn16), (3, ffn16)):
        for copy in sum_copies(s, target)[1 if s < 2 else 0 :]:
            copy.wait_send()
    for j, c in started:
        store(j, c).wait()


def forward(real_lengths, tok_t, cot_t, weights, packed, tables):
    features, rows = tok_t.shape
    half = rows // 2
    width = 4 * features
    hidden = weights[-1].shape[0]
    head_dim = weights[1].shape[1]
    whole = pl.BlockSpec(memory_space=pltpu.VMEM)
    there = pl.BlockSpec(memory_space=pl.ANY)
    kept = [
        (rows, width), (rows, width), (rows, width), (rows, head_dim), (rows, 2 * head_dim),
        (half, 2 * head_dim), (rows, head_dim), (rows, width), (rows, width), (rows, hidden),
        (rows, width), (rows, hidden), (rows, hidden),
    ]

    return pl.pallas_call(
        forward_kernel,
        out_shape=(
            jax.ShapeDtypeStruct((features, rows), BF16), jax.ShapeDtypeStruct((8, width), F32),
            *[jax.ShapeDtypeStruct(shape, BF16) for shape in kept],
        ),
        in_specs=[pl.BlockSpec(memory_space=pltpu.SMEM)] + [there] * 9 + [whole] * 3,
        out_specs=[whole] * 2 + [there] * STORED,
        scratch_shapes=[pltpu.VMEM(shape, BF16) for shape in kept]
        + [
            pltpu.VMEM((4, width, half), BF16),
            pltpu.VMEM((width, 3 * head_dim), BF16),
            pltpu.VMEM((head_dim, width), BF16),
            pltpu.VMEM((hidden, width), BF16),
            pltpu.VMEM((hidden, width), BF16),
            pltpu.VMEM((hidden, width), BF16),
            pltpu.VMEM((4, half, width), BF16),
            pltpu.VMEM((4, half // 2, width), BF16),
            pltpu.VMEM((4, half // 2, width), BF16),
            pltpu.VMEM((rows, width), BF16),
            pltpu.VMEM((4, width), F32),
            pltpu.VMEM((2, head_dim), F32),
            pltpu.SemaphoreType.DMA((7,)),
            pltpu.SemaphoreType.DMA((4,)),
            pltpu.SemaphoreType.DMA((STORED, 2)),
            pltpu.SemaphoreType.DMA((3, 4)),
            pltpu.SemaphoreType.DMA((3, 4)),
            pltpu.SemaphoreType.DMA((1,)),
            pltpu.SemaphoreType.DMA((1,)),
            pltpu.SemaphoreType.DMA((3, 4)),
            pltpu.SemaphoreType.DMA((3, 4)),
        ],
        name="forward",
        compiler_params=pltpu.CompilerParams(
            collective_id=2, has_side_effects=True, vmem_limit_bytes=63 << 20
        ),
    )(real_lengths, tok_t, cot_t, *weights, packed, *tables)


def backward_kernel(
    step_rows, steps, few, lag,
    real_lengths, tok, x_in, cot_in, n_in, q_in, kv_in, far_in, att_in, attn_in, mid_in, hid_in,
    dffn_in, dg_in, du_in, gain_ffn, w_q, w_k, w_v, w_o, w_g, w_u, packed, cosines, sines,
    out, xg_t, gain_rows, gain_cols,
    g, y2, z2, m2, z1, m1, y1, a3, b3, hid, dg, du, mid, dffn, w_tiles, part, near, far, dm, cot, attn,
    v_o, v_qkv, dkv_new, norm_near, norm_far, row_part,
    row_near, kv_near, kv_far, turned, head_sums, row_sums, sum_slots, sum_new, col_slots,
    col_new, gains, head_gains, gain_col, col_part,
    load_sem, tile_sem, keep_sem, keep_few, chain_send, chain_recv, few_send, few_recv, peer_send,
    peer_recv,
):
    dp, ctx, tp = lax.axis_index("dp"), lax.axis_index("ctx"), lax.axis_index("tp")
    s, K = step_rows, steps
    upper = dp // 2
    odd = tp % 2
    outer = (dp == 0) | (dp == 3)
    inner = jnp.logical_not(outer)
    yes = dp >= 0
    core_index = tp + 1 - 2 * odd
    x_index = (tp + 2) % 4
    z_index = dp + 1 - 2 * (dp % 2)
    core_peer, x_peer = (dp, ctx, core_index), (dp, ctx, x_index)
    y_peer, z_peer, m_peer = (dp, 1 - ctx, tp), (z_index, ctx, tp), (3 - dp, ctx, tp)
    features, rows = tok.shape[0], tok.shape[1] // 2
    width = 4 * features
    hidden = w_g.shape[0]
    head_dim = w_k.shape[1]
    half = rows // 2
    kv_rows = head_dim // 2
    score_scale = head_dim ** (-0.5)

    def remote(source, target, send, recv, peer):
        return pltpu.make_async_remote_copy(
            src_ref=source, dst_ref=target, send_sem=send, recv_sem=recv,
            device_id=peer, device_id_type=MESH,
        )

    def chunk(c):
        return pl.ds(c * rows, rows)

    def multiple(start, size):
        return pl.ds(pl.multiple_of(start, size), size)

    dqkv, kv16 = dg.at[:, 0 : 3 * head_dim], dg.at[:, 3 * head_dim : 5 * head_dim]
    dkv, dkv_far = du.at[:, 0 : 2 * head_dim], du.at[0:rows, 2 * head_dim : 4 * head_dim]
    far_kv = du.at[rows : 2 * rows, 2 * head_dim : 4 * head_dim]
    q16, att = du.at[:, 4 * head_dim : 5 * head_dim], du.at[:, 5 * head_dim : 6 * head_dim]

    tok_own = dm.at[0:features, 0 : 2 * rows]

    pairs = (
        (hid_in, hid), (dffn_in, dffn), (du_in, du), (mid_in, mid), (dg_in, dg), (cot_in, cot),
        (attn_in, attn), (w_o, v_o),
        (w_q, v_qkv.at[:, 0:head_dim]), (w_k, v_qkv.at[:, head_dim : 2 * head_dim]),
        (w_v, v_qkv.at[:, 2 * head_dim : 3 * head_dim]),
    )
    count = len(pairs)

    def load(j):
        return pltpu.make_async_copy(pairs[j][0], pairs[j][1], load_sem.at[j])

    late_pairs = (
        (x_in, dffn), (n_in, mid), (q_in, q16), (kv_in, kv16), (far_in, far_kv), (att_in, att),
    )

    def load_tok():
        return pltpu.make_async_copy(tok, tok_own, load_sem.at[count + len(late_pairs)])

    def late_load(j):
        return pltpu.make_async_copy(late_pairs[j][0], late_pairs[j][1], load_sem.at[count + j])

    for j in range(2):
        load(j).start()
    barrier = pltpu.get_barrier_semaphore()
    for peer in (core_peer, x_peer, y_peer, z_peer, m_peer):
        pl.semaphore_signal(barrier, inc=1, device_id=peer, device_id_type=MESH)
    pl.semaphore_wait(barrier, 5)

    third = 3
    enter1, enter3 = 2 * lag, 0
    base3 = 2 * s * K
    base = base3 + 2 * s * few
    ring, ring_few = 4 * lag + 1, -(-(4 * lag + 1) // third) + 1

    def rows2(k, h):
        return multiple((2 * k + h) * s, s)

    def rows1(k, h):
        return multiple(base + (2 * k + h) * s, s)

    def rows3(k, h):
        return multiple(base3 + (2 * k + h) * s, s)

    def pair1(k):
        return pl.ds(pl.multiple_of(base + 2 * k * s, s), 2 * s)

    def slot(k):
        return multiple((k % ring) * s, s)

    def slot_few(k):
        return multiple((k % ring_few) * s, s)

    def slot_pair(k):
        return multiple((k % ring_few) * 2 * s, 2 * s)

    def slot_half(k, h):
        return multiple(((k % ring_few) * 2 + h) * s, s)

    def chain(j, k, source, target, peer):
        if j < 5:
            return remote(source, target, chain_send.at[j, k], chain_recv.at[j, k], peer)
        return remote(source, target, few_send.at[j - 5, k], few_recv.at[j - 5, k], peer)

    def c_y2(k):
        return chain(0, k, g.at[rows2(k, 1 - ctx)], y2.at[slot(k)], y_peer)

    def c_z2(k):
        return chain(1, k, y2.at[slot(k)], z2.at[slot(k)], z_peer)

    def c_m2(k):
        return chain(2, k, z2.at[slot(k)], m2.at[slot(k)], m_peer)

    def c_fo(k):
        return chain(3, k, m2.at[slot(k)], out.at[rows2(k, ctx)], z_peer)

    def c_fy(k):
        return chain(4, k, m2.at[slot(k)], out.at[rows2(k, ctx)], y_peer)

    def c_fy_outer(k):
        return chain(4, k, out.at[rows2(k, ctx)], out.at[rows2(k, ctx)], y_peer)

    def c_z1(k):
        return chain(5, k, g.at[pair1(k)], z1.at[slot_pair(k)], z_peer)

    def c_m1(k):
        return chain(6, k, z1.at[slot_half(k, 1 - upper)], m1.at[slot_few(k)], m_peer)

    def c_y1(k):
        return chain(7, k, m1.at[slot_few(k)], y1.at[slot_few(k)], y_peer)

    def c_fm(k):
        return chain(8, k, y1.at[slot_few(k)], out.at[rows1(k, upper)], m_peer)

    def c_fa(k):
        return chain(9, k, y1.at[slot_few(k)], out.at[rows1(k, upper)], z_peer)

    def c_fb(k):
        return chain(10, k, out.at[rows1(k, 1 - upper)], out.at[rows1(k, 1 - upper)], z_peer)

    def c_3up(k):
        return chain(11, k, g.at[rows3(k, 1 - upper)], a3.at[slot_few(k)], z_peer)

    def c_3mid(k):
        return chain(12, k, a3.at[slot_few(k)], b3.at[slot_few(k)], m_peer)

    def c_3end(k):
        return chain(13, k, b3.at[slot_few(k)], a3.at[slot_few(k)], z_peer)

    def c_3y(k):
        return chain(14, k, a3.at[slot_few(k)], b3.at[slot_few(k)], y_peer)

    def c_3back(k):
        return chain(15, k, b3.at[slot_few(k)], out.at[rows3(k, upper)], z_peer)

    def c_3over(k):
        return chain(16, k, out.at[rows3(k, upper)], out.at[rows3(k, upper)], m_peer)

    def c_3last(k):
        return chain(17, k, out.at[rows3(k, 1 - upper)], out.at[rows3(k, 1 - upper)], z_peer)

    def keep2(k):
        return pltpu.make_async_copy(m2.at[slot(k)], out.at[rows2(k, ctx)], keep_sem.at[k])

    def keep1(k):
        return pltpu.make_async_copy(y1.at[slot_few(k)], out.at[rows1(k, upper)], keep_few.at[0, k])

    def keep3(k):
        return pltpu.make_async_copy(b3.at[slot_few(k)], out.at[rows3(k, upper)], keep_few.at[1, k])

    def inner3_mid(k):
        c_3up(k).wait_recv()
        a3[slot_few(k), :] = add16(a3[slot_few(k), :], g[rows3(k, 1 - upper), :])
        c_3mid(k).start()

    def inner3_end(k):
        c_3mid(k).wait_recv()
        b3[slot_few(k), :] = add16(b3[slot_few(k), :], g[rows3(k, upper), :])
        c_3end(k).start()

    def outer3_y(k):
        c_3end(k).wait_recv()
        a3[slot_few(k), :] = add16(a3[slot_few(k), :], g[rows3(k, upper), :])
        c_3y(k).start()

    def outer3_back(k):
        c_3y(k).wait_recv()
        b3[slot_few(k), :] = add16(b3[slot_few(k), :], a3[slot_few(k), :])
        c_3back(k).start()
        keep3(k).start()

    def inner3_over(k):
        c_3back(k).wait_recv()
        c_3over(k).start()

    def inner3_last(k):
        c_3over(k).wait_recv()
        c_3last(k).start()

    def outer3_done(k):
        c_3last(k).wait_recv()
        c_3up(k).wait_send()

    def inner3_done(k):
        c_3over(k).wait_send()
        c_3last(k).wait_send()

    def outer3_sent(k):
        c_3back(k).wait_send()
        keep3(k).wait()

    def b2(k):
        c_y2(k).wait_recv()
        y2[slot(k), :] = add16(y2[slot(k), :], g[rows2(k, ctx), :])
        pl.when(outer)(lambda: c_z2(k).start())

    def b1(k):
        c_z1(k).wait_recv()
        z1[slot_pair(k), :] = add16(z1[slot_pair(k), :], g[pair1(k), :])
        c_m1(k).start()

    def c2(k):
        c_z2(k).wait_recv()
        z2[slot(k), :] = add16(z2[slot(k), :], y2[slot(k), :])
        c_m2(k).start()

    def c1(k):
        c_m1(k).wait_recv()
        m1[slot_few(k), :] = add16(m1[slot_few(k), :], z1[slot_half(k, upper), :])
        c_y1(k).start()

    def d2(k):
        c_m2(k).wait_recv()
        m2[slot(k), :] = add16(m2[slot(k), :], z2[slot(k), :])
        c_fo(k).start()
        c_fy(k).start()
        keep2(k).start()

    def d1(k):
        c_y1(k).wait_recv()
        y1[slot_few(k), :] = add16(y1[slot_few(k), :], m1[slot_few(k), :])
        c_fm(k).start()
        c_fa(k).start()
        keep1(k).start()

    def e2(k):
        c_fo(k).wait_recv()
        c_fy_outer(k).start()

    def e1(k):
        c_fm(k).wait_recv()
        c_fb(k).start()

    def f2(k):
        c_fy(k).wait_recv()
        c_y2(k).wait_send()

    def f2_outer(k):
        c_fy_outer(k).wait_send()

    def f1_outer(k):
        c_fa(k).wait_recv()
        c_fb(k).wait_recv()
        c_z1(k).wait_send()

    def f2_inner(k):
        keep2(k).wait()
        c_fo(k).wait_send()
        c_fy(k).wait_send()

    def f1_inner(k):
        keep1(k).wait()
        for copy in (c_fm, c_fa, c_fb):
            copy(k).wait_send()

    two, one, three = (K, 1, 0), (few, third, enter1), (few, third, enter3)
    hops = (
        (5, yes, two, f2), (5, outer, two, f2_outer), (5, outer, one, f1_outer),
        (5, inner, two, f2_inner), (5, inner, one, f1_inner),
        (7, outer, three, outer3_done), (7, inner, three, inner3_done),
        (6, outer, three, outer3_sent),
        (5, outer, three, lambda k: c_3y(k).wait_send()),
        (4, inner, two, lambda k: c_m2(k).wait_send()),
        (4, inner, one, lambda k: c_y1(k).wait_send()),
        (3, outer, two, lambda k: c_z2(k).wait_send()),
        (3, inner, one, lambda k: c_m1(k).wait_send()),
        (3, inner, three, lambda k: c_3mid(k).wait_send()),
        (3, inner, three, lambda k: c_3end(k).wait_send()),
        (6, inner, three, inner3_last), (5, inner, three, inner3_over),
        (4, outer, two, e2), (4, inner, one, e1), (4, outer, three, outer3_back),
        (3, inner, two, d2), (3, inner, one, d1), (3, outer, three, outer3_y),
        (2, inner, two, c2), (2, inner, one, c1), (2, inner, three, inner3_end),
        (1, yes, two, b2), (1, inner, one, b1), (1, inner, three, inner3_mid),
        (0, yes, two, lambda k: c_y2(k).start()), (0, outer, one, lambda k: c_z1(k).start()),
        (0, outer, three, lambda k: c_3up(k).start()),
    )

    def grad_tile(index, first, size):
        left, right = ((hid, dffn), (dg, mid), (du, mid))[index]
        at = first if isinstance(first, int) else pl.multiple_of(first, 256)
        tile = contract(left[:, pl.ds(at, size)], right[...], 0, 0)
        start = index * hidden + first
        g[pl.ds(start if isinstance(start, int) else pl.multiple_of(start, 64), size), :] = (
            tile.astype(BF16)
        )

    full = hidden // 256
    tail = hidden - 256 * full

    wide = width // 256
    rest = width - 256 * wide
    tiles = wide + (rest > 0)

    def fetch(slot, first, size):
        return [
            pltpu.make_async_copy(
                w.at[:, pl.ds(first, size)], w_tiles.at[i, slot, :, pl.ds(0, size)],
                tile_sem.at[i, slot],
            )
            for i, w in enumerate((w_g, w_u))
        ]

    def fetch_start(slot, first, size):
        for copy in fetch(slot, first, size):
            copy.start()

    def mid_term(c, slot, first, size):
        for copy in fetch(slot, first, size):
            copy.wait()
        at = multiple(c * rows, rows)
        term = dot_nn(dg[at, :], w_tiles[0, slot, :, 0:size]) + dot_nn(
            du[at, :], w_tiles[1, slot, :, 0:size]
        )
        part[c, :, pl.ds(first, size)] = term.astype(BF16)

    mid_first, mid_each = 4, (wide + 1) // 2

    def mid_at(t):
        since = t - mid_first
        c = 1 - since // (mid_each + 1)
        turn = since % (mid_each + 1)

        def tile(i, carry):
            n = 2 * turn + i
            slot = ((1 - c) * tiles + n) % 2
            pl.when(n + 1 < wide)(
                lambda: fetch_start(1 - slot, pl.multiple_of(256 * (n + 1), 256), 256)
            )
            if rest:
                pl.when(n + 1 == wide)(lambda: fetch_start(1 - slot, 256 * wide, rest))
            mid_term(c, slot, pl.multiple_of(256 * n, 256), 256)
            return carry

        def full_tiles():
            lax.fori_loop(0, 2, tile, 0)

        pl.when(turn < mid_each)(full_tiles)

        def last_tile():
            slot = ((1 - c) * tiles + wide) % 2
            pl.when(c == 1)(lambda: fetch_start(1 - slot, 0, 256))
            if rest:
                mid_term(c, slot, 256 * wide, rest)

        pl.when(turn == mid_each)(last_tile)

    def own_half(index):
        return multiple(index * half, half)

    def peer_copy(j, source, target, peer):
        return remote(source, target, peer_send.at[j], peer_recv.at[j], peer)

    def sum_copies(c):
        final = dm.at[multiple(c * rows + odd * half, half)]
        return (
            peer_copy(3 * c, part.at[c, own_half(1 - odd)], near.at[c], core_peer),
            peer_copy(3 * c + 1, near.at[c], far.at[c], x_peer),
            peer_copy(3 * c + 2, final, final, core_peer),
        )

    def sum_cross(c):
        copies = sum_copies(c)
        copies[0].wait_recv()
        near[c] = add16(part[c, own_half(odd)], near[c])
        copies[1].start()

    def sum_back(c):
        copies = sum_copies(c)
        copies[1].wait_recv()
        dm[multiple(c * rows + odd * half, half), :] = add16(near[c], far[c])
        copies[2].start()

    def norms_back(base):
        def body(at, _, state):
            branch = attn[at, :].astype(F32)
            scale_a = scale_of(branch)
            unit_a = branch * scale_a
            resid = dffn[at, :].astype(F32) + unit_a * gains[1:2, :]
            scale_r = scale_of(resid)
            unit_r = resid * scale_r
            grad = dm[at, :].astype(F32)
            weighted = grad * gains[2:3, :]
            mean = jnp.mean(unit_r * weighted, axis=-1, keepdims=True)
            d_resid = cot[at, :].astype(F32) + scale_r * (weighted - unit_r * mean)
            weighted = d_resid * gains[1:2, :]
            mean = jnp.mean(unit_a * weighted, axis=-1, keepdims=True)
            cot[at, :] = d_resid.astype(BF16)
            attn[at, :] = (scale_a * (weighted - unit_a * mean)).astype(BF16)
            return (
                state[0] + (d_resid * unit_a).reshape(-1, 8, width).sum(axis=0),
                state[1] + (grad * unit_r).reshape(-1, 8, width).sum(axis=0),
            )

        zero = jnp.zeros((8, width), F32)
        sum_a, sum_r = row_blocks(base, half, 64, body, (zero, zero))
        row_sums[0] += sum_a
        row_sums[1] += sum_r

    norm_steps = ((13, rows), (14, rows + half), (17, 0), (18, half))

    def norms_at(t):
        base = sum(jnp.where(t == step, start, 0) for step, start in norm_steps)
        now = sum(jnp.where(t == step, 1, 0) for step, _ in norm_steps)
        pl.when(now > 0)(lambda: norms_back(base))

    def head_back(grad, at, j):
        cosine, sine = cosines[at, :], sines[at, :]
        low, high = grad[:, : head_dim // 2], grad[:, head_dim // 2 :]
        grad = jnp.concatenate([low * cosine + high * sine, high * cosine - low * sine], axis=1)
        cols = pl.ds(j * head_dim, head_dim)
        raw = dot_nn(mid[at, :], v_qkv[:, cols])
        scale = scale_of(raw)
        unit = raw * scale
        weighted = grad * head_gains[j : j + 1, :]
        mean = jnp.mean(unit * weighted, axis=-1, keepdims=True)
        dqkv[at, cols] = (scale * (weighted - unit * mean)).astype(BF16)
        head_sums[j] += (grad * unit).reshape(-1, 8, head_dim).sum(axis=0)

    block_rows = 128

    def over_rows(low, count_rows, body):
        def step(i, carry):
            body(pl.multiple_of(low + i * block_rows, block_rows))
            return carry

        lax.fori_loop(0, count_rows // block_rows, step, 0)

    def attend_back_rows(c, low):
        def block(first):
            d_keys, d_values = [0.0, 0.0], [0.0, 0.0]
            at = multiple(c * rows + first, block_rows)
            query = q16[at, :]
            d_out = dot_nt(attn[at, :], v_o[...]).astype(BF16)
            row_id = first + lax.broadcasted_iota(jnp.int32, (block_rows, rows), 0)
            key_id = lax.broadcasted_iota(jnp.int32, (block_rows, rows), 1)
            allowed = key_id <= row_id
            if c == 1:
                allowed = allowed & (rows + key_id < real_lengths[0, 1 - ctx])
            keys = [(kv16[chunk(c), :head_dim], kv16[chunk(c), head_dim:], allowed)]
            if c == 1:
                keys.append((far_kv[:, :head_dim], far_kv[:, head_dim:], None))
            scores = []
            for key, _, mask in keys:
                score = dot_nt(query, key) * score_scale
                scores.append(score if mask is None else jnp.where(mask, score, MASKED))
            most = scores[0].max(axis=1, keepdims=True)
            for score in scores[1:]:
                most = jnp.maximum(most, score.max(axis=1, keepdims=True))
            exps = [jnp.exp(score - most) for score in scores]
            total = sum(e.sum(axis=1, keepdims=True) for e in exps)
            probs = [e / total for e in exps]
            d_probs = [dot_nt(d_out, key[1]) for key in keys]
            mean = sum((p * d).sum(axis=1, keepdims=True) for p, d in zip(probs, d_probs))
            d_query = 0.0
            for i, key in enumerate(keys):
                d_score = (probs[i] * (d_probs[i] - mean)).astype(BF16)
                d_query += dot_nn(d_score, key[0])
                d_keys[i] += contract(d_score, query, 0, 0)
                d_values[i] += contract(probs[i].astype(BF16), d_out, 0, 0)
            head_back(d_query * score_scale, at, 0)
            places = [dkv.at[chunk(c), :]] + [dkv_far] * c
            for i, place in enumerate(places):
                for cols, term in (
                    (pl.ds(0, head_dim), d_keys[i] * score_scale),
                    (pl.ds(head_dim, head_dim), d_values[i]),
                ):
                    place[:, cols] = (place[:, cols].astype(F32) + term).astype(BF16)

        over_rows(low, half, block)

    attend_steps = ((21, 0), (22, half)), ((23, 0), (24, half))

    def attend_at(t):
        for c, steps_of in ((1, attend_steps[0]), (0, attend_steps[1])):
            low = steps_of[1][1] * (t - steps_of[0][0])
            now = (t >= steps_of[0][0]) & (t <= steps_of[1][0])
            pl.when(now)(partial(attend_back_rows, c, low))

    def clear_keys():
        dkv[...] = jnp.zeros((2 * rows, 2 * head_dim), BF16)
        dkv_far[...] = jnp.zeros((rows, 2 * head_dim), BF16)

    quarter = half // 2
    far_rows = multiple(odd * half + tp // 2 * quarter, quarter)

    def far_copies():
        given = dkv_far.at[multiple(odd * half + (1 - tp // 2) * quarter, quarter), :]
        return (
            peer_copy(33, dkv_far.at[own_half(1 - odd), :], dkv_new.at[0:half], core_peer),
            peer_copy(34, given, dkv_new.at[half : half + quarter], x_peer),
            peer_copy(6, dkv_far.at[far_rows, :], dkv_new.at[half + quarter : 2 * half], y_peer),
        )

    def far_cross():
        copies = far_copies()
        copies[0].wait_recv()
        dkv_far[own_half(odd), :] = add16(dkv_far[own_half(odd), :], dkv_new[0:half, :])
        copies[1].start()

    def far_up():
        copies = far_copies()
        copies[1].wait_recv()
        dkv_far[far_rows, :] = add16(dkv_far[far_rows, :], dkv_new[half : half + quarter, :])
        copies[2].start()

    def far_down():
        far_copies()[2].wait_recv()
        dkv[far_rows, :] = add16(dkv[far_rows, :], dkv_new[half + quarter : 2 * half, :])

    def keys_back(base):
        def block(first):
            at = multiple(base + first, block_rows)
            grad = dkv[at, :].astype(F32)
            head_back(grad[:, :head_dim], at, 1)
            dqkv[at, 2 * head_dim :] = grad[:, head_dim:].astype(BF16)

        over_rows(0, rows, block)

    def cell(c, j):
        index = 4 * c + j
        return hid.at[pl.ds(index // 3 * features, features), pl.ds(index % 3 * rows, rows)]

    def owner_of(j):
        near_one = tp + (j % 2) * (1 - 2 * odd)
        return (near_one + 2 * (j // 2)) % 4

    def cell_at(index):
        return hid.at[
            multiple(index // 3 * features, features), multiple(index % 3 * rows, rows)
        ]

    def scatter_copies(c):
        return (
            peer_copy(7 + 6 * c, cell(c, 1), norm_near.at[c, 0], core_peer),
            peer_copy(8 + 6 * c, cell(c, 3), norm_near.at[c, 1], core_peer),
            peer_copy(9 + 6 * c, row_part.at[c, 0], row_near.at[c, 0], core_peer),
            peer_copy(10 + 6 * c, cell(c, 2), norm_far.at[c], x_peer),
            peer_copy(11 + 6 * c, row_part.at[c, 1], row_near.at[c, 1], x_peer),
        )

    def scatter_begin(c):
        def features_of(j, carry):
            weights = v_qkv[multiple(owner_of(j) * features, features), :]
            values = dqkv[multiple(c * rows, rows), :]
            cell_at(4 * c + j)[...] = dot_nt(weights, values).astype(BF16)
            return carry

        lax.fori_loop(0, 4, features_of, 0)
        def block(first):
            at = multiple(c * rows + first, block_rows)
            raw = dot_nn(mid[at, :], v_qkv[...])
            inner_sum = (raw * dqkv[at, :].astype(F32)).sum(axis=1, keepdims=True)
            scale = scale_of(dffn[at, :].astype(F32))
            lane = lax.broadcasted_iota(jnp.int32, (block_rows, 128), 1)
            both = jnp.where(lane == 0, inner_sum, scale)
            row_part[c, 0, :, pl.ds(first, block_rows)] = both.T[0:8, :]

        over_rows(0, rows, block)

    def scatter_start(c):
        for copy in scatter_copies(c)[:3]:
            copy.start()

    def scatter_cross(c):
        copies = scatter_copies(c)
        for copy in copies[:3]:
            copy.wait_recv()
        cell(c, 0)[...] = add16(cell(c, 0)[...], norm_near[c, 0])
        cell(c, 2)[...] = add16(cell(c, 2)[...], norm_near[c, 1])
        row_part[c, 1] = row_part[c, 0] + row_near[c, 0]
        copies[3].start()
        copies[4].start()

    def scatter_end(c):
        copies = scatter_copies(c)
        copies[3].wait_recv()
        copies[4].wait_recv()
        for first in range(0, width, 128):
            turned[first : first + 128, :] = cot[chunk(c), first : first + 128].T
        lane = (ctx if c == 0 else 1 - ctx) * rows
        lanes = pl.ds(pl.multiple_of(lane, rows), rows)
        grad = cell(c, 0)[...].astype(F32) + norm_far[c].astype(F32)
        values = tok_own[:, lanes].astype(F32)
        scale = row_part[c, 0, 1:2, :]
        inner_sum = row_part[c, 1, 0:1, :] + row_near[c, 1, 0:1, :]
        d_in = scale * (grad * gain_col[:, 0:1]) - values * (
            scale * scale * inner_sum * (1.0 / width)
        )
        d_resid = turned[multiple(tp * features, features), :].astype(F32)
        xg_t[:, lanes] = (d_resid + d_in).astype(BF16)
        column = jnp.sum(grad * values * scale, axis=1, keepdims=True)
        column = jnp.broadcast_to(column, (features, 128))
        for first, size in column_tiles(features, 128):
            block = column[first : first + size, :]
            if size < 128:
                block = jnp.concatenate([block, jnp.zeros((128 - size, 128), F32)], axis=0)
            cols = pl.ds(first, 128)
            if c == 1:
                col_slots[0, :, cols] = block.T[0:8, :]
            else:
                col_slots[0, :, cols] += block.T[0:8, :]

    at_out = 3 * hidden
    at_query = at_out + head_dim
    at_kv = at_query + head_dim

    def out_grad():
        g[pl.ds(at_out, head_dim), :] = contract(att[...], attn[...], 0, 0).astype(BF16)

    def query_grad():
        g[pl.ds(at_query, head_dim), :] = contract(dqkv[:, :head_dim], mid[...], 0, 0).astype(BF16)

    def kv_grads():
        sum_copies(1)[0].wait_send()

        def block(j, carry):
            cols = multiple(head_dim + owner_of(j) * kv_rows, kv_rows)
            term = contract(dqkv[:, cols], mid[...], 0, 0)
            part[1, multiple(j * kv_rows, kv_rows), :] = term.astype(BF16)
            return carry

        lax.fori_loop(0, 4, block, 0)
        for copy in kv_copies()[:2]:
            copy.start()

    def kv_copies():
        return (
            peer_copy(19, part.at[1, pl.ds(kv_rows, kv_rows)], kv_near.at[0], core_peer),
            peer_copy(20, part.at[1, pl.ds(3 * kv_rows, kv_rows)], kv_near.at[1], core_peer),
            peer_copy(21, part.at[1, pl.ds(2 * kv_rows, kv_rows)], kv_far, x_peer),
        )

    def kv_cross():
        copies = kv_copies()
        copies[0].wait_recv()
        copies[1].wait_recv()
        for j in range(2):
            at = pl.ds(2 * j * kv_rows, kv_rows)
            part[1, at, :] = add16(part[1, at, :], kv_near[j])
        copies[2].start()

    def kv_end():
        kv_copies()[2].wait_recv()
        g[pl.ds(at_kv, kv_rows), :] = add16(part[1, pl.ds(0, kv_rows), :], kv_far[...])

    sum_peers = (core_peer, x_peer, y_peer, z_peer, m_peer)

    def sum_copy(j):
        return peer_copy(22 + j, sum_slots.at[j], sum_new.at[j], sum_peers[j])

    def col_copy(j):
        return peer_copy(27 + j, col_slots.at[j], col_new.at[j], sum_peers[2 + j])

    def gains_begin():
        sum_slots[0] = jnp.zeros((8, width), F32)
        for j, values in enumerate((row_sums[0], row_sums[1], gain_ffn[...])):
            sum_slots[0, j : j + 1, :] = 0.25 * values.sum(axis=0, keepdims=True)
        for j in range(2):
            sum_slots[0, 3:4, j * head_dim : (j + 1) * head_dim] = head_sums[j].sum(
                axis=0, keepdims=True
            )
        sum_copy(0).start()
        col_copy(0).start()

    def gains_hop(j):
        sum_copy(j).wait_recv()
        if j < 4:
            sum_slots[j + 1] = sum_slots[j] + sum_new[j]
            sum_copy(j + 1).start()
        else:
            gain_rows[...] = sum_slots[j] + sum_new[j]
        if j < 3:
            col_copy(j).wait_recv()
        if j < 2:
            col_slots[j + 1] = col_slots[j] + col_new[j]
            col_copy(j + 1).start()
        if j == 2:
            gain_cols[tp] = col_slots[2] + col_new[2]
            gather_copies()[0].start()
            gather_copies()[1].start()
        if j == 3:
            gather_copies()[1].wait_recv()
            gather_copies()[2].start()
        if j == 4:
            gather_copies()[0].wait_recv()
            gather_copies()[2].wait_recv()

    def gather_copies():
        mine, theirs = gain_cols.at[tp], gain_cols.at[x_index]
        return (
            peer_copy(30, mine, mine, core_peer),
            peer_copy(31, mine, mine, x_peer),
            peer_copy(32, theirs, theirs, core_peer),
        )

    def late(low, high):
        for j in range(low, high):
            late_load(j).start()

    def wait_late(low, high):
        for j in range(low, high):
            late_load(j).wait()

    def wait_rest():
        for j in range(5, count):
            load(j).wait()
        head_sums[...] = jnp.zeros(head_sums.shape, F32)
        row_sums[...] = jnp.zeros(row_sums.shape, F32)

    load(0).wait()
    load(1).wait()
    for j in range(2, count):
        load(j).start()
    grad_tile(0, 0, 256)
    load(2).wait()
    load(3).wait()
    grad_tile(2, 0, 256)

    def take_gains():
        spread_gains(packed, gains, head_gains)
        for first in range(0, width, 128):
            row = gains[0:1, first : first + 128]
            col_part[first : first + 128, :] = jnp.broadcast_to(row, (128, 128)).T
        gain_col[...] = col_part[multiple(tp * features, features), :]

    lone = full - 2
    order = [(0, 1), (2, lone), (0, 2), (2, lone + 1), (2, 1)] + [(0, j) for j in range(3, full + 1)]
    order += [(2, full)] + [(2, j) for j in range(2, lone)]
    first_gate = len(order) + 1
    freed = first_gate + full + 1

    order += [(1, j) for j in range(full + 1)]

    def tiles_at(t):
        for index in range(3):
            steps_of = [(1 + i, j) for i, (which, j) in enumerate(order) if which == index]
            part_of = [(step, j) for step, j in steps_of if j < full]
            if not isinstance(t, int):
                number = sum(jnp.where(t == step, j + 1, 0) for step, j in part_of)
                pl.when(number > 0)(partial(grad_tile, index, 256 * (number - 1), 256))
            for step, j in steps_of:
                if j == full and tail:
                    pl.when(t == step)(partial(grad_tile, index, 256 * full, tail))

    def choose(t, table):
        middle = len(table) // 2
        if middle == 0:
            pl.when(t == table[0][0])(lambda: [action() for action in table[0][1]] and None)
        else:
            pl.when(t < table[middle][0])(lambda: choose(t, table[:middle]))
            pl.when(t >= table[middle][0])(lambda: choose(t, table[middle:]))

    stages = [(1, load(4).wait), (2, lambda: fetch_start(0, 0, 256)), (11, take_gains)]
    after = [
        (6, lambda: sum_copies(1)[0].start()),
        (7, lambda: sum_cross(1)),
        (9, lambda: (late(0, 1), sum_copies(0)[0].start())),
        (10, lambda: sum_cross(0)),
        (11, lambda: sum_back(1)),
        (12, lambda: (wait_late(0, 1), wait_rest())),
        (13, lambda: sum_copies(1)[2].wait_recv()),
        (15, lambda: sum_back(0)),
        (17, lambda: sum_copies(0)[2].wait_recv()),
        (freed, lambda: late(1, len(late_pairs))),
    ]
    stages += after + [
        (freed, clear_keys),
        (21, lambda: wait_late(1, len(late_pairs))),
        (23, lambda: far_copies()[0].start()),
        (23, lambda: (sum_copies(0)[2].wait_send(), load_tok().start())),
        (25, far_cross),
        (27, lambda: (scatter_start(1), out_grad())),
        (28, far_up),
        (29, lambda: scatter_cross(1)),
        (33, lambda: (load_tok().wait(), scatter_end(1))),
        (34, far_down),
        (36, lambda: (scatter_start(0), query_grad())),
        (37, kv_grads),
        (38, lambda: scatter_cross(0)),
        (39, kv_cross),
        (42, lambda: scatter_end(0)),
        (43, lambda: (gains_begin(), kv_end())),
    ]
    stages += [(45 + 2 * j, partial(gains_hop, j)) for j in range(5)]

    def late_at(t):
        pl.when((t >= attend_steps[0][0][0]) & (t <= attend_steps[1][1][0]))(lambda: attend_at(t))
        pl.when((t == 25) | (t == 34))(lambda: keys_back(jnp.where(t == 25, rows, 0)))
        pl.when((t == 26) | (t == 35))(lambda: scatter_begin(jnp.where(t == 26, 1, 0)))

    table = [
        (step, [action for at, action in stages if at == step])
        for step in sorted({at for at, _ in stages})
    ]

    def body(t, carry):
        pl.when(t <= len(order))(lambda: tiles_at(t))
        for hop, who, (limit, spacing, first), action in hops:
            entered = t - hop * lag - first
            k = entered // spacing
            now = who & (entered >= 0) & (k < limit)
            if spacing > 1:
                now = now & (entered % spacing == 0)
            pl.when(now)(partial(action, k))
        pl.when((t >= mid_first) & (t < mid_first + 2 * (mid_each + 1)))(lambda: mid_at(t))
        choose(t, table)
        pl.when((t >= norm_steps[0][0]) & (t <= norm_steps[-1][0]))(lambda: norms_at(t))
        pl.when((t >= 21) & (t <= 35))(lambda: late_at(t))
        return carry

    last = max(K + 5 * lag, third * (few - 1) + 1 + max(enter1 + 5 * lag, enter3 + 7 * lag))
    lax.fori_loop(0, last, body, 0)
    done = [sum_copies(0)[j] for j in (0, 1)] + [sum_copies(1)[j] for j in (1, 2)]
    done += [*far_copies(), *scatter_copies(0), *scatter_copies(1), *kv_copies()]
    done += [sum_copy(j) for j in range(5)] + [col_copy(j) for j in range(3)]
    for copy in done + list(gather_copies()):
        copy.wait_send()


def backward(real_lengths, tok_t, forward_outs, gain_ffn, weights, packed, tables):
    features, rows = tok_t.shape
    half = rows // 2
    width = 4 * features
    w_q, w_k, w_v, w_o, w_g, w_u = weights
    hidden, head_dim = w_g.shape[0], w_k.shape[1]
    kv_rows = head_dim // 2
    step_rows, lag = 32, 2
    total = 3 * hidden + 2 * head_dim + kv_rows
    few = total // (10 * step_rows)
    steps = total // (2 * step_rows) - 2 * few
    ring, ring_few = 4 * lag + 1, -(-(4 * lag + 1) // 3) + 1
    spread = -(-features // 128) * 128
    whole = pl.BlockSpec(memory_space=pltpu.VMEM)
    there = pl.BlockSpec(memory_space=pl.ANY)

    def low(*shape):
        return pltpu.VMEM(shape, BF16)

    def high(*shape):
        return pltpu.VMEM(shape, F32)

    slots = [low(step_rows * ring, width)] * 3
    slots += [low(n * step_rows * ring_few, width) for n in (2, 1, 1, 1, 1)]
    return pl.pallas_call(
        partial(backward_kernel, step_rows, steps, few, lag),
        out_shape=(
            jax.ShapeDtypeStruct((total, width), BF16),
            jax.ShapeDtypeStruct((features, rows), BF16),
            jax.ShapeDtypeStruct((8, width), F32),
            jax.ShapeDtypeStruct((4, 8, spread), F32),
        ),
        in_specs=[pl.BlockSpec(memory_space=pltpu.SMEM)] + [there] * 14 + [whole] + [there] * 6
        + [whole] * 3,
        out_specs=[there, whole, whole, whole],
        scratch_shapes=[
            low(total, width), *slots,
            low(rows, hidden), low(rows, hidden), low(rows, hidden), low(rows, width),
            low(rows, width), low(2, 2, hidden, 256), low(2, half, width),
            low(2, half // 2, width), low(2, half // 2, width), low(rows, width), low(rows, width),
            low(rows, width), low(head_dim, width), low(width, 3 * head_dim),
            low(half, 2 * head_dim), low(2, 2, features, half), low(2, features, half),
            high(2, 2, 8, half), high(2, 2, 8, half), low(2, kv_rows, width), low(kv_rows, width),
            low(width, half), high(2, 8, head_dim), high(2, 8, width),
            high(5, 8, width), high(5, 8, width), high(3, 8, spread), high(3, 8, spread),
            high(4, width), high(2, head_dim), high(features, 128), high(width, 128),
            pltpu.SemaphoreType.DMA((20,)), pltpu.SemaphoreType.DMA((2, 2)),
            pltpu.SemaphoreType.DMA((steps,)), pltpu.SemaphoreType.DMA((2, few)),
            pltpu.SemaphoreType.DMA((5, steps)), pltpu.SemaphoreType.DMA((5, steps)),
            pltpu.SemaphoreType.DMA((13, few)), pltpu.SemaphoreType.DMA((13, few)),
            pltpu.SemaphoreType.DMA((35,)),
            pltpu.SemaphoreType.DMA((35,)),
        ],
        name="backward",
        compiler_params=pltpu.CompilerParams(
            collective_id=1, has_side_effects=True, vmem_limit_bytes=63 << 20
        ),
    )(real_lengths, tok_t, *forward_outs, gain_ffn, *weights, packed, *tables)


def paired_shards(
    tokens,
    out_grad,
    w_query,
    w_key,
    w_value,
    w_out,
    w_gate,
    w_up,
    w_down,
    gain_in,
    gain_post_attn,
    gain_pre_ffn,
    gain_post_ffn,
    gain_query,
    gain_key,
    bucket_lengths,
    true_lengths,
):
    tp_index = lax.axis_index("tp")
    rows = tokens.shape[0] // 2
    head_dim = w_key.shape[1]
    score_scale = head_dim ** (-0.5)
    tables = block_tables(2 * rows, head_dim)
    packed, offset = 0.0, 0
    all_gains = (gain_in, gain_post_attn, gain_pre_ffn, gain_post_ffn, gain_query, gain_key)
    length = sum(gain.size for gain in all_gains)
    for gain in all_gains:
        placed = jnp.pad(gain.astype(F32), (offset, length - offset - gain.size))
        packed, offset = packed + placed, offset + gain.size
    packed = packed.reshape(-1, 128)
    weights = (w_query, w_key, w_value, w_out, w_gate.T, w_up.T, w_down)
    out_t, gain_sum, *kept = forward(
        true_lengths, tokens.T, out_grad.T, weights, packed, tables
    )
    sums, xg_t, gain_rows, gain_cols = backward(
        true_lengths, tokens.T, kept, gain_sum, weights[:-1], packed, tables
    )
    hidden = w_down.shape[0]
    sizes = [hidden, hidden, hidden, head_dim, head_dim, head_dim // 2]
    ends = [sum(sizes[: j + 1]) for j in range(len(sizes))]
    down_sum, gate_sum, up_sum, out_sum, query_sum, mine = [
        sums[end - size : end] for size, end in zip(sizes, ends)
    ]
    far = lax.ppermute(mine, "tp", XOR2)
    near = lax.ppermute(jnp.stack([mine, far]), "tp", XOR1)
    kv_all = (mine, near[0], far, near[1])
    kv_sum = jnp.concatenate(
        [lax.select_n(tp_index ^ j, *kv_all) for j in range(4)], axis=0
    ).astype(F32).T
    return (
        out_t.T,
        xg_t.T,
        query_sum.astype(F32).T,
        kv_sum[:, :head_dim],
        kv_sum[:, head_dim:],
        out_sum.astype(F32),
        gate_sum.astype(F32).T,
        up_sum.astype(F32).T,
        down_sum.astype(F32),
        gain_cols[:, 0, : tokens.shape[1]].reshape(-1),
        gain_rows[0],
        gain_rows[1],
        gain_rows[2],
        gain_rows[3, :head_dim],
        gain_rows[3, head_dim : 2 * head_dim],
    )


def solution(mesh):
    def layer(*args):
        tokens, bucket_lengths = args[0], args[-2]
        sizes = mesh.shape
        group_rows = tokens.shape[0] // sizes["dp"]
        paired = (sizes["dp"], sizes["ctx"], sizes["tp"]) == (4, 2, 4) and (
            group_rows == 1024 * bucket_lengths.shape[1] == 2048
        )
        return mapped(paired_shards if paired else shards)(*args)

    def mapped(body):
        return jax.shard_map(
            body,
            mesh=mesh,
            in_specs=(
                P(("dp", "ctx"), "tp"),
                P(("dp", "ctx"), "tp"),
                P(None, "tp"),
                P(),
                P(),
                P("tp", None),
                P(None, "tp"),
                P(None, "tp"),
                P("tp", None),
                P(),
                P(),
                P(),
                P(),
                P(),
                P(),
                P("dp", None),
                P("dp", None),
            ),
            out_specs=(
                P(("dp", "ctx"), "tp"),
                P(("dp", "ctx"), "tp"),
                P(None, "tp"),
                P(),
                P(),
                P("tp", None),
                P(None, "tp"),
                P(None, "tp"),
                P("tp", None),
                P(),
                P(),
                P(),
                P(),
                P(),
                P(),
            ),
            check_vma=False,
        )

    return layer
```
